32 devices in a mesh: groups: 2 (over y), blk: 4 (over z), probe: 2 (over x), sub: 2 (over core).
Axes of the slice: x: 2, y: 2, z: 4, core: 2. Of those that a mesh axis runs over, the one named last changes fastest.
Arguments:
- coords: float32 [3, 16384], P(None, ('groups', 'blk')), parts along dimension 1, may hold values from -4 to 4
- noise_var: float32 [16384], P(('groups', 'blk')), parts along dimension 0, may hold values from 0.5 to 2
- probe_signs: int32 [64, 16384], P('probe', ('groups', 'blk')), parts along dimension 1, may hold values from -1 to 1, as said below
- tile_rows: int32 [8, 2, 96], P(('groups', 'blk'), 'sub'), parts along dimension 0, may hold values from 0 to 15
- tile_cols: int32 [8, 2, 96], P(('groups', 'blk'), 'sub'), parts along dimension 0, may hold values from 0 to 31, as said below
- tile_count: int32 [8, 2], P(('groups', 'blk'), 'sub'), parts along dimension 0, may hold values from 24 to 96
Outputs:
- alphas: float32 [3, 128], P(None, ('groups', 'probe')), parts along dimension 1
- betas: float32 [3, 128], P(None, ('groups', 'probe')), parts along dimension 1
- last_basis: float32 [64, 16384], P('probe', ('groups', 'blk')), parts along dimension 1
- coord_grad: float32 [3, 16384], P(None, ('groups', 'blk')), parts along dimension 1
The draws below stay inside these ranges and needn't reach their ends.
There are 2 independent parts, one for each index of `groups`. The reference program is written for one: setup_inputs(seed, part) draws one part's arguments, and reference() takes and returns one part's arrays. A program takes and returns all parts, laid end to end along the dimension named above; each array names one. Nothing has to cross between parts.
Inputs may be any that keep to these rules, and one draw needn't show every extreme that they name: `probe_signs`: every entry is -1 or 1. tile_cols minus tile_rows lies between 0 and 16 in every slot.
All inputs are finite; a program needn't handle non-finite values.
Results may differ from the reference program's by a relative error of at most 0.00025.
Values sent between devices are 32-bit elements; how exact they have to be, the bound alone decides.
No kernel may reach another device: no remote copies, remote signals or barrier semaphores. Data moves between devices by JAX's collectives and lax.ppermute only.
A program may use at most 64 MiB of HBM per device.

```python
import math
import jax
import jax.numpy as jnp
from jax import lax

DIM = 3
BLOCK = 128
PROBES = 64
ITERS = 3
SB = 16
TILES_DEV = 96
NPTS = 8192
N_BLK = 4
N_SUB = 2


def tile_lists(key):
    rows = jax.random.randint(jax.random.fold_in(key, 11), (N_BLK, N_SUB, TILES_DEV), 0, SB)
    offsets = jax.random.randint(jax.random.fold_in(key, 12), (N_BLK, N_SUB, TILES_DEV), 0, SB + 1)
    rows = rows.at[:, :, 0].set(SB - 1).at[:, :, 1].set(0)
    offsets = offsets.at[:, :, 0].set(SB).at[:, :, 1].set(0)
    return (rows.astype(jnp.int32), (rows + offsets).astype(jnp.int32))


def draw_tile_rows(key, part):
    return tile_lists(key)[0]


def draw_tile_cols(key, part):
    return tile_lists(key)[1]


def draw_tile_count(key, part):
    lowest = TILES_DEV // 4
    spread = jax.random.randint(jax.random.fold_in(key, 13), (N_BLK * N_SUB,), 0, 64)
    counts = lowest + (TILES_DEV - lowest) * spread * spread // 3969
    fullest = jax.random.randint(jax.random.fold_in(key, 14), (), 0, N_BLK * N_SUB)
    counts = counts.at[fullest].set(TILES_DEV)
    return counts.reshape(N_BLK, N_SUB).astype(jnp.int32)


def draw_probe_signs(key, part):
    return (2 * jax.random.randint(jax.random.fold_in(key, 15), (PROBES, NPTS), 0, 2) - 1).astype(jnp.int32)


def shard_levels(stream_key, dims, pieces, smallest, top_value):
    def one(dim, blocks):
        draws = jax.random.uniform(jax.random.fold_in(jax.random.fold_in(stream_key, 6), dim), (blocks,), jnp.float32, smallest / len(pieces), top_value / len(pieces))
        return jnp.repeat(jnp.exp(draws), dims[dim] // blocks).reshape((-1,) + (1,) * (len(dims) - dim - 1))

    level = one(*pieces[0])
    for cut in pieces[1:]:
        level = level * one(*cut)
    return level


def bell_draw(rng, extent, scale, limit, pieces=(), held_as=jnp.bfloat16):
    values = jax.random.normal(rng, extent, jnp.float32) * scale
    if len(pieces) > 0:
        values = shard_levels(rng, extent, pieces, -0.22, 0.18) * values
    return jnp.clip(values, min=-limit, max=limit).astype(held_as)


def setup_inputs(seed: int = 0, part: int = 0) -> dict:
    key_list = jax.random.split(jax.random.key(seed), 7)
    part_splits = jax.random.split(jax.random.fold_in(key_list[6], part), 7)
    return {
        "coords": bell_draw(part_splits[0], (DIM, NPTS), 0.7, 4.0, ((1, 4),), jnp.float32),
        "noise_var": jnp.clip(jnp.exp(math.log(2.0) - 1.3862944 * jax.random.uniform(part_splits[1], (NPTS,), jnp.float32) ** shard_levels(part_splits[1], (NPTS,), ((0, 4),), -0.2, 0.2)), 0.5, 2.0),
        "probe_signs": draw_probe_signs(jax.random.fold_in(jax.random.fold_in(key_list[6], part), 71), part),
        "tile_rows": draw_tile_rows(jax.random.fold_in(jax.random.fold_in(key_list[6], part), 71), part),
        "tile_cols": draw_tile_cols(jax.random.fold_in(jax.random.fold_in(key_list[6], part), 71), part),
        "tile_count": draw_tile_count(jax.random.fold_in(jax.random.fold_in(key_list[6], part), 71), part),
    }


SIGNAL_VAR = 0.1
LENGTH_SQ = 2.0
TAPER_SQ = 16.0
WARP_GAIN = 0.4
EPSILON = 1e-06

def tile_kernel(row_pts, col_pts):
    row_warp = row_pts + WARP_GAIN * jnp.tanh(row_pts)
    col_warp = col_pts + WARP_GAIN * jnp.tanh(col_pts)
    dist = jnp.zeros((row_pts.shape[0], row_pts.shape[2], col_pts.shape[2]), row_pts.dtype)
    for coord in range(row_pts.shape[1]):
        differ = row_warp[:, coord, :, None] - col_warp[:, coord, None, :]
        dist = dist + differ * differ
    taper = jnp.maximum(1.0 - dist / TAPER_SQ, 0.0)
    return SIGNAL_VAR * jnp.exp(-dist / (2.0 * LENGTH_SQ)) * taper * taper

def reference(coords, noise_var, probe_signs, tile_rows, tile_cols, tile_count):
    nblocks = SB * N_BLK
    hi = lax.Precision.HIGHEST
    slab = jnp.arange(N_BLK, dtype=jnp.int32)[:, None, None]
    grow = (slab * SB + tile_rows).astype(jnp.int32).reshape(-1, 16)
    gcol = ((slab * SB + tile_cols) % nblocks).astype(jnp.int32).reshape(-1, 16)
    live = jnp.arange(TILES_DEV, dtype=jnp.int32)[None, None, :] < tile_count[:, :, None]
    live = live.astype(coords.dtype).reshape(-1, 16)

    def pts_of(cds, idx):
        blocks = cds.reshape(DIM, nblocks, BLOCK)
        return jnp.transpose(blocks[:, idx, :], (1, 0, 2))

    def apply(vecs):
        vblk = vecs.reshape(PROBES, nblocks, BLOCK)

        def step(acc, item):
            rws, cls, lv = item
            kern = tile_kernel(pts_of(coords, rws), pts_of(coords, cls)) * lv[:, None, None]
            out_row = jnp.einsum('bij,pbj->pbi', kern, vblk[:, cls, :], precision=hi)
            out_col = jnp.einsum('bij,pbi->pbj', kern, vblk[:, rws, :], precision=hi)
            return (acc.at[:, rws, :].add(out_row).at[:, cls, :].add(out_col), None)
        acc, _ = lax.scan(step, jnp.zeros_like(vblk), (grow, gcol, live))
        return acc.reshape(PROBES, -1) + noise_var[None, :] * vecs
    first = probe_signs.astype(coords.dtype)
    current = first
    previous = jnp.zeros_like(first)
    beta = jnp.zeros((PROBES, 1), coords.dtype)
    alpha_list = []
    beta_list = []
    for step_no in range(ITERS):
        work = apply(current) - beta * previous
        alpha = lax.optimization_barrier(jnp.sum(current * work, axis=1)) / NPTS
        work = work - alpha[:, None] * current
        beta = jnp.sqrt(lax.optimization_barrier(jnp.sum(work * work, axis=1)) / NPTS + EPSILON)[:, None]
        previous, current = (current, work / beta)
        alpha_list.append(alpha)
        beta_list.append(beta[:, 0])
    ublk = current.reshape(PROBES, nblocks, BLOCK)
    vblk = first.reshape(PROBES, nblocks, BLOCK)

    def form(cds):

        def step(total, item):
            rws, cls, lv = item
            kern = tile_kernel(pts_of(cds, rws), pts_of(cds, cls)) * lv[:, None, None]
            weight = jnp.einsum('pbi,pbj->bij', ublk[:, rws, :], vblk[:, cls, :], precision=hi)
            weight = weight + jnp.einsum('pbi,pbj->bij', vblk[:, rws, :], ublk[:, cls, :], precision=hi)
            return (total + jnp.sum(kern * weight) / PROBES, None)
        total, _ = lax.scan(jax.checkpoint(step), jnp.zeros((), cds.dtype), (grow, gcol, live))
        return total
    coord_grad = jax.grad(form)(coords)
    return (jnp.stack(alpha_list), jnp.stack(beta_list), current, coord_grad)
```

```python
import functools
import math

import jax
import jax.numpy as jnp
from jax import lax
from jax.experimental import pallas as pl
from jax.experimental.pallas import tpu as pltpu
from jax.sharding import PartitionSpec as P

ITERS = 3
SIGNAL_VAR = 0.1
LENGTH_SQ = 2.0
TAPER_SQ = 16.0
WARP_GAIN = 0.4
EPSILON = 1e-06

BLK = 128
LANES = 128
FEATS = 32
GROUP = 8
LIMIT_MIB = 16
KEPT = 256
WORK_FIRST = 9000000000
WORK_NEXT = 6000000000
WORK_BYTES = 4000000

S_OF_D = -math.log2(math.e) / (2.0 * LENGTH_SQ)
D_OF_S = 1.0 / S_OF_D
ROOT_VAR = math.sqrt(SIGNAL_VAR)
TAPER_STEP = 4.0 * LENGTH_SQ / TAPER_SQ * ROOT_VAR
T_SLOPE = -ROOT_VAR * D_OF_S / TAPER_SQ

F32 = jnp.float32
BF16 = jnp.bfloat16


def split_two(x):
    high = x.astype(BF16)
    low = (x - high.astype(F32)).astype(BF16)
    return high, low


def split_three(x):
    one = x.astype(BF16).astype(F32)
    rest = x - one
    two = rest.astype(BF16).astype(F32)
    three = (rest - two).astype(BF16).astype(F32)
    return one, two, three


def warp(x):
    return x + WARP_GAIN * jnp.tanh(x)


def mxu(a, b):
    return lax.dot_general(a, b, (((1,), (0,)), ((), ())), preferred_element_type=F32)


def features(x):
    scale = -2.0 * S_OF_D
    y = x * scale
    norm = S_OF_D * jnp.sum(x * x, axis=0, keepdims=True)
    x1, x2, x3 = split_three(x)
    y1, y2, y3 = split_three(y)
    n1, n2, n3 = split_three(norm)
    one = jnp.ones_like(norm)
    pad = jnp.zeros((FEATS - 24, x.shape[1]), F32)
    left = jnp.concatenate([x1, x1, x2, x2, x1, x3, n1, n2, n3, one, one, one, pad], axis=0)
    right = jnp.concatenate([y1, y2, y1, y2, y3, y1, one, one, one, n1, n2, n3, pad], axis=0)
    return left, right


def tile_terms(left, right):
    s = mxu(left, right)
    e = jnp.exp2(s)
    t = jnp.maximum(T_SLOPE * s + ROOT_VAR, 0.0)
    return e, t


def put_stats(ref, base, w_of, q_of, qq, qw, blocks):
    alpha_s = qw / jnp.maximum(qq, 1e-30)
    acc = jnp.zeros((qq.shape[0], LANES), F32)
    for b in range(blocks):
        r = w_of(b) - alpha_s * q_of(b)
        acc = acc + r * r
    res = jnp.sum(acc, axis=1, keepdims=True)
    lane = lax.broadcasted_iota(jnp.int32, (qq.shape[0], LANES), 1)
    out = jnp.where(lane == 0, qw, jnp.where(lane == 1, qq, jnp.where(lane == 2, res, 0.0)))
    ref[:, base : base + LANES] = out


def mxu_turned(a, b):
    return lax.dot_general(a, b, (((1,), (1,)), ((), ())), preferred_element_type=F32)


def fold(out, probes):
    if out.shape[0] > probes:
        return out[:probes] + out[probes:]
    return out


def fold_turned(out, probes):
    total = out[:probes, :BLK] + out[:probes, BLK:]
    if out.shape[0] > probes:
        total = total + out[probes:, :BLK]
    return total


def stack_vec(q, exact):
    if exact:
        high = q.astype(BF16)
        return jnp.concatenate([high, high], axis=1)
    high, low = split_two(q)
    return jnp.concatenate(
        [jnp.concatenate([high, high], axis=1), jnp.concatenate([low, jnp.zeros_like(low)], axis=1)], axis=0
    )


def stack_tile(tile):
    return jnp.concatenate(split_two(tile), axis=0)


def kept_and_made(groups, room, group, kept, made):
    first = jnp.minimum(groups, room)
    lax.fori_loop(0, first, lambda g, carry: group(g, kept), 0)
    lax.fori_loop(first, groups, lambda g, carry: group(g, made), 0)


def inner_edges(acc, vecs, rows, cols, groups, kept, made):
    acc[...] = jnp.zeros_like(acc)
    size = acc.shape[1]

    def group(g, tile_of):
        outs = []
        for u in range(GROUP):
            slot = g * GROUP + u
            a = rows[slot]
            c = cols[slot]
            tile = tile_of(slot, a, c)
            outs.append((c, fold(mxu(vecs[a], tile), size)))
            outs.append((a, fold_turned(mxu_turned(vecs[c][:, :BLK], tile), size)))
        for c, out in outs:
            acc[c] = acc[c] + out
        return 0

    kept_and_made(groups, KEPT // GROUP, group, kept, made)


def outer_edges(acc, vecs, src, dst, counts, kept, made):
    size = acc.shape[1]
    base = counts[0] * GROUP

    def group(g, tile_of):
        outs = []
        for u in range(GROUP):
            at = g * GROUP + u
            a = src[at]
            c = dst[at]
            outs.append((c, fold(mxu(vecs[a], tile_of(base + at, a, c)), size)))
        for c, out in outs:
            acc[c] = acc[c] + out
        return 0

    kept_and_made(counts[1], jnp.maximum(KEPT // GROUP - counts[0], 0), group, kept, made)


def maker(tiles, left, right):
    def make(slot, a, c):
        e, t = tile_terms(left[a], right[c])
        tile = stack_tile(e * t * t)
        if tiles is not None:
            tiles[slot] = tile
        return tile

    return make


def keeper(tiles):
    return lambda slot, a, c: tiles[slot]


def groups_of(n):
    return (n + GROUP - 1) // GROUP


def first_inner_kernel(
    blocks, cap, own0, own1, mine,
    rows, cols, src, dst, counts, tiles, z_ref, left, right, acc, vecs,
):
    probes = mine.shape[0] - 3

    def own(lst):
        def step(t, carry):
            n, m = carry
            a = lst[t]
            c = lst[cap + t]
            inside = (c < blocks).astype(jnp.int32)
            rows[n] = a
            cols[n] = c
            src[m] = c - blocks
            dst[m] = a
            return n + inside, m + 1 - inside

        return step

    n, m = lax.fori_loop(0, own0[2 * cap], own(own0), (0, 0))
    n, m = lax.fori_loop(0, own1[2 * cap], own(own1), (n, m))
    for u in range(GROUP):
        rows[n + u] = blocks
        cols[n + u] = blocks
    groups = groups_of(n)
    counts[0] = groups
    counts[1] = m

    for b in range(blocks):
        part = slice(b * BLK, (b + 1) * BLK)
        vecs[b] = stack_vec(mine[:probes, part], True)
        lf, rt = features(warp(mine[probes : probes + 3, part]))
        left[b] = lf.T.astype(BF16)
        right[b] = rt.astype(BF16)
    left[blocks] = jnp.zeros((BLK, FEATS), BF16)
    right[blocks] = jnp.zeros((FEATS, BLK), BF16)
    vecs[blocks] = jnp.zeros((probes, 2 * BLK), BF16)
    inner_edges(acc, vecs, rows, cols, groups, maker(tiles, left, right), maker(None, left, right))
    z_ref[...] = acc[:blocks]


def finish_apply(blocks, acc, z_of, w_ref, q_of, prev_of, beta, noise_ref):
    probes = acc.shape[1]
    qq = jnp.zeros((probes, LANES), F32)
    qw = jnp.zeros((probes, LANES), F32)
    for b in range(blocks):
        q = q_of(b)
        part = slice(b * BLK, (b + 1) * BLK)
        w = acc[b] + z_of(b) + noise_ref[:, part] * q
        if prev_of is not None:
            w = w - beta * prev_of(b)
        w_ref[:, part] = w
        qq = qq + q * q
        qw = qw + q * w
    put_stats(
        w_ref,
        blocks * BLK,
        lambda b: w_ref[:, b * BLK : (b + 1) * BLK],
        q_of,
        jnp.sum(qq, axis=1, keepdims=True),
        jnp.sum(qw, axis=1, keepdims=True),
        blocks,
    )


def first_outer_kernel(
    blocks, cap, low0, low1, old_src, old_dst, old_counts, old_tiles, mine, above, below, noise_ref, z_ref, right,
    src, dst, counts, tiles, w_ref, left, acc, vecs,
):
    probes = mine.shape[0] - 3
    del old_tiles

    def keep(t, carry):
        src[t] = old_src[t]
        dst[t] = old_dst[t]
        return carry

    def lower(lst):
        def step(t, m):
            c = lst[cap + t]
            src[m] = blocks + lst[t]
            dst[m] = c - blocks
            return m + (c >= blocks).astype(jnp.int32)

        return step

    lax.fori_loop(0, old_counts[1], keep, 0)
    m = lax.fori_loop(0, low0[2 * cap], lower(low0), old_counts[1])
    m = lax.fori_loop(0, low1[2 * cap], lower(low1), m)
    for u in range(GROUP):
        src[m + u] = 0
        dst[m + u] = blocks
    counts[0] = old_counts[0]
    counts[1] = groups_of(m)

    for part, ref in enumerate((above, below)):
        for b in range(blocks):
            at = part * blocks + b
            cols = slice(b * BLK, (b + 1) * BLK)
            vecs[at] = stack_vec(ref[:probes, cols], True)
            lf, _ = features(warp(ref[probes : probes + 3, cols]))
            left[at] = lf.T.astype(BF16)
    acc[...] = jnp.zeros_like(acc)
    outer_edges(acc, vecs, src, dst, counts, maker(tiles, left, right), maker(None, left, right))
    finish_apply(
        blocks, acc, lambda b: z_ref[b], w_ref, lambda b: mine[:probes, b * BLK : (b + 1) * BLK], None, None, noise_ref
    )


def inner_kernel(blocks, rows, cols, counts, w_ref, tiles, left, right, z_ref, acc, vecs):
    for b in range(blocks):
        vecs[b] = stack_vec(w_ref[:, b * BLK : (b + 1) * BLK], False)
    vecs[blocks] = jnp.zeros(vecs.shape[1:], BF16)
    inner_edges(acc, vecs, rows, cols, counts[0], keeper(tiles), maker(None, left, right))
    z_ref[...] = acc[:blocks]


def alpha_beta(stats, points):
    qw = [s[:, 0:1] for s in stats]
    qq = [s[:, 1:2] for s in stats]
    res = [s[:, 2:3] for s in stats]
    alpha = functools.reduce(jnp.add, qw) / points
    total = jnp.zeros_like(alpha)
    for w, q, r in zip(qw, qq, res):
        gap = alpha - w / jnp.maximum(q, 1e-30)
        total = total + (r + gap * gap * q)
    return alpha, jnp.sqrt(total / points + EPSILON)


def global_alpha_beta(slabs, points, place, stats_ref):
    order = [stats_ref[lax.rem(slab - place[0] + slabs, slabs)] for slab in range(slabs)]
    return alpha_beta(order, points)


def add_ab(ref, base, old_ab, step, alpha, beta):
    shape = (alpha.shape[0], LANES)
    lane = lax.broadcasted_iota(jnp.int32, shape, 1)
    out = jnp.zeros(shape, F32) if old_ab is None else old_ab[...]
    out = jnp.where(lane == step, alpha, out)
    ref[:, base : base + LANES] = jnp.where(lane == ITERS + step, beta, out)


def block_of(ref, rows, b):
    if len(ref.shape) == 3:
        return ref[b]
    return ref[:rows, b * BLK : (b + 1) * BLK]


def outer_kernel(
    blocks, slabs, points, step, place, src, dst, counts, mine, above, below, stats_ref,
    q_own, q_above, q_below, z_raw, z_old, noise_ref, tiles, left, right, *rest,
):
    probes = mine.shape[0]
    old_ab = None
    if step > 0:
        old_ab = rest[0]
        rest = rest[1:]
    w_ref, own_ref, above_ref, below_ref, z_ref, ab_ref, acc, vecs = rest
    alpha, beta = global_alpha_beta(slabs, points, place, stats_ref)
    scale = 1.0 / beta
    add_ab(ab_ref, 0, old_ab, step, alpha, beta)
    halves = ((mine, q_own, own_ref), (above, q_above, above_ref), (below, q_below, below_ref))
    for part, (w, old, new) in enumerate(halves):
        for b in range(blocks):
            q = (w[:, b * BLK : (b + 1) * BLK] - alpha * block_of(old, probes, b)) * scale
            new[b] = q
            if part > 0:
                vecs[(part - 1) * blocks + b] = stack_vec(q, False)
            else:
                z_ref[b] = (z_raw[b] - alpha * z_old[b]) * scale
    acc[...] = jnp.zeros_like(acc)
    outer_edges(acc, vecs, src, dst, counts, keeper(tiles), maker(None, left, right))
    finish_apply(
        blocks, acc, lambda b: z_ref[b], w_ref, lambda b: own_ref[b], lambda b: block_of(q_own, probes, b), beta, noise_ref
    )


def slope_of(left, right):
    e, t = tile_terms(left, right)
    return (e * t) * (t + TAPER_STEP)


def slope_kernel(rows, cols, src, dst, counts, left_own, left_halo, right, after, slopes):
    del after
    base = counts[0] * GROUP
    room = KEPT // GROUP

    def inner(g, carry):
        for u in range(GROUP):
            slot = g * GROUP + u
            slopes[slot] = slope_of(left_own[rows[slot]], right[cols[slot]])
        return carry

    def outer(g, carry):
        for u in range(GROUP):
            at = g * GROUP + u
            slopes[base + at] = slope_of(left_halo[src[at]], right[dst[at]])
        return carry

    lax.fori_loop(0, jnp.minimum(counts[0], room), inner, 0)
    lax.fori_loop(0, jnp.minimum(counts[1], jnp.maximum(room - counts[0], 0)), outer, 0)


def last_kernel(
    blocks, slabs, points, all_probes, place, rows, cols, src, dst, counts, mine, above, below, stats_ref,
    q_own, q_above, q_below, pts, pts_above, pts_below, old_ab, slopes, left_own, left_out, right,
    basis_ref, grad_ref, acc, form_left, halo_left, form_right, pnts, halo_pnts,
):
    probes = pts.shape[0] - 3
    alpha, beta = global_alpha_beta(slabs, points, place, stats_ref)
    scale = 1.0 / beta
    add_ab(basis_ref, blocks * BLK, old_ab, ITERS - 1, alpha, beta)
    for part, (w, old, ref) in enumerate(((mine, q_own, pts), (above, q_above, pts_above), (below, q_below, pts_below))):
        for b in range(blocks):
            part_cols = slice(b * BLK, (b + 1) * BLK)
            u = (w[:, part_cols] - alpha * block_of(old, probes, b)) * scale
            v = ref[:probes, part_cols]
            high = u.astype(BF16).astype(F32)
            low = u - high
            turned = jnp.concatenate([high, low, v, v], axis=0).T.astype(BF16)
            x = warp(ref[probes : probes + 3, part_cols])
            x1, x2, x3 = split_three(x)
            y = jnp.concatenate([x1, x2, x3, jnp.ones((1, BLK), F32), jnp.zeros((6, BLK), F32)], axis=0).astype(BF16)
            y = jnp.concatenate([y, y], axis=1)
            if part == 0:
                basis_ref[:, part_cols] = u
                form_left[b] = turned
                form_right[b] = jnp.concatenate([v, v, high, low], axis=0).astype(BF16)
                pnts[b] = y
            else:
                halo_left[(part - 1) * blocks + b] = turned
                halo_pnts[(part - 1) * blocks + b] = y
    form_left[blocks] = jnp.zeros((BLK, 4 * probes), BF16)
    form_right[blocks] = jnp.zeros((4 * probes, BLK), BF16)
    pnts[blocks] = jnp.zeros((16, 2 * BLK), BF16)

    def pull(side):
        return lambda slot, a, c: stack_tile(mxu(side[a], form_right[c]) * slopes[slot])

    def pull_made(side, left):
        return lambda slot, a, c: stack_tile(mxu(side[a], form_right[c]) * slope_of(left[a], right[c]))

    inner_edges(acc, pnts, rows, cols, counts[0], pull(form_left), pull_made(form_left, left_own))
    outer_edges(acc, halo_pnts, src, dst, counts, pull(halo_left), pull_made(halo_left, left_out))
    for b in range(blocks):
        part_cols = slice(b * BLK, (b + 1) * BLK)
        raw = pts[probes : probes + 3, part_cols]
        bent = jnp.tanh(raw)
        x = raw + WARP_GAIN * bent
        sums = acc[b]
        moved = sums[0:3] + sums[3:6] + sums[6:9] - x * sums[9:10]
        chain = 1.0 + WARP_GAIN * (1.0 - bent * bent)
        grad_ref[:, part_cols] = moved * chain * (1.0 / (LENGTH_SQ * all_probes))


def close_kernel(peers, place, own, other, grads, basis_ref, alpha_ref, beta_ref, grad_ref):
    probes = own.shape[0]
    width = basis_ref.shape[1]
    lower = place[1] == 0
    mine = own[...]
    theirs = other[...]
    first = jnp.where(lower, mine, theirs)
    second = jnp.where(lower, theirs, mine)
    basis_ref[:probes] = first[:, :width]
    basis_ref[probes:] = second[:, :width]
    ab = jnp.concatenate([first[:, width:], second[:, width:]], axis=0)
    turned = jnp.concatenate([ab, jnp.zeros((LANES - 2 * probes, LANES), F32)], axis=0).T
    alpha_ref[...] = turned[:ITERS, : 2 * probes]
    beta_ref[...] = turned[ITERS : 2 * ITERS, : 2 * probes]
    total = grads[lax.rem(peers - place[2], peers)]
    for k in range(1, peers):
        total = total + grads[lax.rem(k - place[2] + peers, peers)]
    grad_ref[...] = total


def vmem(count):
    return [pl.BlockSpec(memory_space=pltpu.VMEM)] * count


def smem(count):
    return [pl.BlockSpec(memory_space=pltpu.SMEM)] * count


def held(array):
    return pltpu.with_memory_space_constraint(array, pltpu.VMEM)


def call(name, kernel, outs, ins, scratch, work, aliases=None):
    out_shapes, out_scalars = outs
    arrays, scalars = ins
    flops, moved = work
    return pl.pallas_call(
        kernel,
        out_shape=tuple(out_shapes),
        in_specs=smem(scalars) + vmem(len(arrays) - scalars),
        out_specs=tuple(smem(out_scalars) + vmem(len(out_shapes) - out_scalars)),
        scratch_shapes=[pltpu.VMEM(shape, dtype) for shape, dtype in scratch],
        compiler_params=pltpu.CompilerParams(vmem_limit_bytes=LIMIT_MIB * 1024 * 1024),
        cost_estimate=pl.CostEstimate(flops=flops, bytes_accessed=moved, transcendentals=0),
        input_output_aliases=aliases or {},
        name=name,
    )(*arrays)


def shifted(value, axes, count, steps):
    return lax.ppermute(value, axes, [(source, (source + steps) % count) for source in range(count)])


def body(coords, noise_var, probe_signs, tile_rows, tile_cols, tile_count):
    slabs = lax.axis_size("blk")
    subs = lax.axis_size("sub")
    outer = lax.axis_size("probe")
    probes = probe_signs.shape[0] // subs
    width = coords.shape[1]
    blocks = width // BLK
    cap = tile_rows.shape[-1]
    points = float(width * slabs)
    all_probes = probe_signs.shape[0] * outer
    sub = lax.axis_index("sub")
    blk = lax.axis_index("blk")
    peers = outer * subs
    place = jnp.stack([blk, sub, lax.axis_index("probe") * subs + sub]).astype(jnp.int32)
    noise = noise_var.reshape(1, width)
    sds = jax.ShapeDtypeStruct

    lists = jnp.concatenate([tile_rows.reshape(-1), tile_cols.reshape(-1), tile_count.reshape(-1)])

    def list_from(back, flip):
        pairs = []
        for s in range(slabs):
            for h in range(subs):
                source = ((s - back) % slabs) * subs + (h + flip) % subs
                pairs.append((source, s * subs + h))
        return lax.ppermute(lists, ("blk", "sub"), pairs)

    own1 = list_from(0, 1)
    low0 = list_from(1, 0)
    low1 = list_from(1, 1)

    signs = lax.dynamic_slice_in_dim(probe_signs, sub * probes, probes, axis=0)
    mine = jnp.concatenate([signs.astype(F32), coords], axis=0)
    above = shifted(mine, "blk", slabs, -1)
    below = shifted(mine, "blk", slabs, 1)

    own_slots = subs * cap + GROUP
    halo_slots = 2 * subs * cap + GROUP
    slots = KEPT
    ext = width + LANES
    ints = jnp.int32
    blocks_f32 = sds((blocks, probes, BLK), F32)
    tile_shape = pltpu.VMEM((slots, 2 * BLK, BLK), BF16)
    acc_shape = ((blocks + 1, probes, BLK), F32)

    rows, cols, src, dst, counts, tiles, z, left_own, right = call(
        "first_inner",
        functools.partial(first_inner_kernel, blocks, cap),
        (
            (
                sds((own_slots,), ints), sds((own_slots,), ints), sds((own_slots,), ints), sds((own_slots,), ints),
                sds((2,), ints), tile_shape, blocks_f32,
                sds((blocks + 1, BLK, FEATS), BF16), sds((blocks + 1, FEATS, BLK), BF16),
            ),
            5,
        ),
        ((lists, own1, mine), 2),
        [acc_shape, ((blocks + 1, probes, 2 * BLK), BF16)],
        (WORK_FIRST, WORK_BYTES),
    )
    src, dst, counts, tiles, w, left_halo = call(
        "first_outer",
        functools.partial(first_outer_kernel, blocks, cap),
        (
            (
                sds((halo_slots,), ints), sds((halo_slots,), ints), sds((2,), ints), tile_shape,
                sds((probes, ext), F32), sds((2 * blocks, BLK, FEATS), BF16),
            ),
            3,
        ),
        ((low0, low1, src, dst, counts, held(tiles), mine, above, below, noise, z, right), 5),
        [acc_shape, ((2 * blocks, probes, 2 * BLK), BF16)],
        (WORK_FIRST, WORK_BYTES),
        {5: 3},
    )

    def exchange(w):
        up = shifted(w, "blk", slabs, -1)
        down = shifted(w, "blk", slabs, 1)
        stats = w[:, width:]
        if slabs == 4:
            far = shifted(stats, "blk", slabs, 2)
            rows = jnp.stack([stats, up[:, width:], far, down[:, width:]])
        else:
            rows = lax.all_gather(stats, "blk", axis=0)
            rows = jnp.roll(rows, -blk, axis=0)
        return up, down, rows

    q = (mine, above, below)
    ab = []
    for step in range(ITERS - 1):
        up, down, stats = exchange(w)
        (z_raw,) = call(
            "inner",
            functools.partial(inner_kernel, blocks),
            ((blocks_f32,), 0),
            ((rows, cols, counts, w, held(tiles), left_own, right), 3),
            [acc_shape, ((blocks + 1, 2 * probes, 2 * BLK), BF16)],
            (WORK_NEXT, WORK_BYTES),
        )
        w, q0, q1, q2, z, next_ab = call(
            "outer",
            functools.partial(outer_kernel, blocks, slabs, points, step),
            (
                (sds((probes, ext), F32), blocks_f32, blocks_f32, blocks_f32, blocks_f32, sds((probes, LANES), F32)),
                0,
            ),
            ((place, src, dst, counts, w, up, down, stats, *q, z_raw, z, noise, held(tiles), left_halo, right, *ab), 4),
            [acc_shape, ((2 * blocks, 2 * probes, 2 * BLK), BF16)],
            (WORK_NEXT, WORK_BYTES),
        )
        q = (q0, q1, q2)
        ab = [next_ab]

    up, down, stats = exchange(w)
    (slopes,) = call(
        "slopes",
        slope_kernel,
        ((pltpu.VMEM((slots, BLK, BLK), F32),), 0),
        ((rows, cols, src, dst, counts, left_own, left_halo, right, w), 5),
        [],
        (WORK_FIRST, WORK_BYTES),
    )
    basis, grad = call(
        "last",
        functools.partial(last_kernel, blocks, slabs, points, all_probes),
        ((sds((probes, ext), F32), sds((3, width), F32)), 0),
        (
            (
                place, rows, cols, src, dst, counts, w, up, down, stats, *q, mine, above, below, *ab, held(slopes), left_own, left_halo, right,
            ),
            6,
        ),
        [
            ((blocks + 1, 16, BLK), F32),
            ((blocks + 1, BLK, 4 * probes), BF16),
            ((2 * blocks, BLK, 4 * probes), BF16),
            ((blocks + 1, 4 * probes, BLK), BF16),
            ((blocks + 1, 16, 2 * BLK), BF16),
            ((2 * blocks, 16, 2 * BLK), BF16),
        ],
        (WORK_FIRST, WORK_BYTES),
    )

    other = shifted(basis, "sub", subs, 1)
    parts = [grad]
    for r in range(1, peers):
        parts.append(shifted(grad, ("probe", "sub"), peers, -r))
    last_basis, alphas, betas, coord_grad = call(
        "close",
        functools.partial(close_kernel, peers),
        (
            (
                sds((subs * probes, width), F32), sds((ITERS, subs * probes), F32), sds((ITERS, subs * probes), F32),
                sds((3, width), F32),
            ),
            0,
        ),
        ((place, basis, other, jnp.stack(parts)), 1),
        [],
        (1000000, 1000000),
    )
    return alphas, betas, last_basis, coord_grad


def solution(mesh):
    return jax.shard_map(
        body,
        mesh=mesh,
        in_specs=(
            P(None, ("groups", "blk")),
            P(("groups", "blk")),
            P("probe", ("groups", "blk")),
            P(("groups", "blk"), "sub", None),
            P(("groups", "blk"), "sub", None),
            P(("groups", "blk"), "sub"),
        ),
        out_specs=(
            P(None, ("groups", "probe")),
            P(None, ("groups", "probe")),
            P("probe", ("groups", "blk")),
            P(None, ("groups", "blk")),
        ),
        check_vma=False,
    )
```

```python
import functools
import math

import jax
import jax.numpy as jnp
from jax import lax
from jax.experimental import pallas as pl
from jax.experimental.pallas import tpu as pltpu
from jax.sharding import PartitionSpec as P

ITERS = 3
SIGNAL_VAR = 0.1
LENGTH_SQ = 2.0
TAPER_SQ = 16.0
WARP_GAIN = 0.4
EPSILON = 1e-06

BLK = 128
LANES = 128
FEATS = 32
GROUP = 16
TAIL = 4
LIST_ROWS = 8
LIMIT_MIB = 16
KEPT = 256
WORK_FIRST = 300000000
WORK_NEXT = 100000000
WORK_BYTES = 4000000

S_OF_D = -math.log2(math.e) / (2.0 * LENGTH_SQ)
D_OF_S = 1.0 / S_OF_D
ROOT_VAR = math.sqrt(SIGNAL_VAR)
TAPER_STEP = 4.0 * LENGTH_SQ / TAPER_SQ * ROOT_VAR
T_SLOPE = -ROOT_VAR * D_OF_S / TAPER_SQ

F32 = jnp.float32
BF16 = jnp.bfloat16


def split_two(x):
    high = x.astype(BF16)
    low = (x - high.astype(F32)).astype(BF16)
    return high, low


def split_three(x):
    one = x.astype(BF16).astype(F32)
    rest = x - one
    two = rest.astype(BF16).astype(F32)
    three = (rest - two).astype(BF16).astype(F32)
    return one, two, three


def warp(x):
    return x + WARP_GAIN * jnp.tanh(x)


def mxu(a, b):
    return lax.dot_general(a, b, (((1,), (0,)), ((), ())), preferred_element_type=F32)


def features(x):
    scale = -2.0 * S_OF_D
    y = x * scale
    norm = S_OF_D * jnp.sum(x * x, axis=0, keepdims=True)
    x1, x2, x3 = split_three(x)
    y1, y2, y3 = split_three(y)
    n1, n2, n3 = split_three(norm)
    one = jnp.ones_like(norm)
    pad = jnp.zeros((FEATS - 24, x.shape[1]), F32)
    left = jnp.concatenate([x1, x1, x2, x2, x1, x3, n1, n2, n3, one, one, one, pad], axis=0)
    right = jnp.concatenate([y1, y2, y1, y2, y3, y1, one, one, one, n1, n2, n3, pad], axis=0)
    return left, right


def tile_terms(left, right):
    s = mxu(left, right)
    e = jnp.exp2(s)
    t = jnp.maximum(T_SLOPE * s + ROOT_VAR, 0.0)
    return e, t


def put_stats(ref, base, w_of, q_of, qq, qw, blocks):
    alpha_s = qw / jnp.maximum(qq, 1e-30)
    acc = jnp.zeros((qq.shape[0], LANES), F32)
    for b in range(blocks):
        r = w_of(b) - alpha_s * q_of(b)
        acc = acc + r * r
    res = jnp.sum(acc, axis=1, keepdims=True)
    lane = lax.broadcasted_iota(jnp.int32, (qq.shape[0], LANES), 1)
    out = jnp.where(lane == 0, qw, jnp.where(lane == 1, qq, jnp.where(lane == 2, res, 0.0)))
    ref[:, base : base + LANES] = out


def mxu_turned(a, b):
    return lax.dot_general(a, b, (((1,), (1,)), ((), ())), preferred_element_type=F32)


def fold(out, probes):
    if out.shape[0] > probes:
        return out[:probes] + out[probes:]
    return out


def fold_turned(out, probes):
    total = out[:probes, :BLK] + out[:probes, BLK:]
    if out.shape[0] > probes:
        total = total + out[probes:, :BLK]
    return total


def stack_vec(q, exact):
    if exact:
        high = q.astype(BF16)
        return jnp.concatenate([high, high], axis=1)
    high, low = split_two(q)
    return jnp.concatenate(
        [jnp.concatenate([high, high], axis=1), jnp.concatenate([low, jnp.zeros_like(low)], axis=1)], axis=0
    )


def stack_tile(tile):
    return jnp.concatenate(split_two(tile), axis=0)


def ranges(first, last, body):
    long = (last - first) // GROUP
    middle = first + long * GROUP

    def big(g, carry):
        body(first + g * GROUP, GROUP)
        return carry

    def small(g, carry):
        body(middle + g * TAIL, TAIL)
        return carry

    lax.fori_loop(0, long, big, 0)
    lax.fori_loop(0, (last - middle) // TAIL, small, 0)


def kept_and_made(total, room, body, kept, made):
    first = jnp.minimum(total, room)
    ranges(0, first, functools.partial(body, kept))
    many = (total - first) // TAIL

    def rest(g, carry):
        body(made, first + g * TAIL, TAIL)
        return carry

    lax.fori_loop(0, many, rest, 0)


def inner_edges(acc, vecs, rows, cols, counts, kept, made):
    acc[...] = jnp.zeros_like(acc)
    size = acc.shape[1]

    def group(tile_of, start, many):
        outs = []
        for u in range(many):
            slot = start + u
            a = rows[slot]
            c = cols[slot]
            tile = tile_of(slot, a, c)
            outs.append((c, fold(mxu(vecs[a], tile), size)))
            outs.append((a, fold_turned(mxu_turned(vecs[c][:, :BLK], tile), size)))
        for c, out in outs:
            acc[c] = acc[c] + out

    kept_and_made(counts[0], KEPT, group, kept, made)


def outer_edges(acc, vecs, src, dst, counts, kept, made):
    size = acc.shape[1]
    base = counts[0]

    def group(tile_of, start, many):
        outs = []
        for u in range(many):
            at = start + u
            a = src[at]
            c = dst[at]
            outs.append((c, fold(mxu(vecs[a], tile_of(base + at, a, c)), size)))
        for c, out in outs:
            acc[c] = acc[c] + out

    kept_and_made(counts[1], jnp.maximum(KEPT - base, 0), group, kept, made)


def maker(tiles, left, right):
    def make(slot, a, c):
        e, t = tile_terms(left[a], right[c])
        tile = stack_tile(e * t * t)
        if tiles is not None:
            tiles[slot] = tile
        return tile

    return make


def keeper(tiles):
    return lambda slot, a, c: tiles[slot]


def whole(n):
    return (n + TAIL - 1) // TAIL * TAIL


def pack_kernel(probes, place, tile_rows, tile_cols, tile_count, signs, coords, lists, mine):
    first = pl.multiple_of(place[1] * probes, probes)
    mine[:probes] = signs[pl.ds(first, probes), :].astype(F32)
    mine[probes : probes + 3] = coords[...]
    lists[...] = jnp.zeros(lists.shape, jnp.int32)
    lists[0:1, : tile_rows.shape[1]] = tile_rows[...]
    lists[1:2, : tile_cols.shape[1]] = tile_cols[...]
    lists[2:3, 0:1] = tile_count[...]


def first_inner_kernel(
    blocks, own0, own1, mine,
    rows, cols, src, dst, counts, tiles, z_ref, left, right, acc, vecs,
):
    probes = mine.shape[0] - 3

    def own(lst):
        def step(t, carry):
            n, m = carry
            a = lst[0, t]
            c = lst[1, t]
            inside = (c < blocks).astype(jnp.int32)
            rows[n] = a
            cols[n] = c
            src[m] = c - blocks
            dst[m] = a
            return n + inside, m + 1 - inside

        return step

    n, m = lax.fori_loop(0, own0[2, 0], own(own0), (0, 0))
    n, m = lax.fori_loop(0, own1[2, 0], own(own1), (n, m))
    for u in range(TAIL):
        rows[n + u] = blocks
        cols[n + u] = blocks
    counts[0] = whole(n)
    counts[1] = m

    for b in range(blocks):
        part = slice(b * BLK, (b + 1) * BLK)
        vecs[b] = stack_vec(mine[:probes, part], True)
        lf, rt = features(warp(mine[probes : probes + 3, part]))
        left[b] = lf.T.astype(BF16)
        right[b] = rt.astype(BF16)
    left[blocks] = jnp.zeros((BLK, FEATS), BF16)
    right[blocks] = jnp.zeros((FEATS, BLK), BF16)
    vecs[blocks] = jnp.zeros((probes, 2 * BLK), BF16)
    inner_edges(acc, vecs, rows, cols, counts, maker(tiles, left, right), maker(None, left, right))
    z_ref[...] = acc[:blocks]


def finish_apply(blocks, acc, z_of, w_ref, q_of, prev_of, beta, noise_ref):
    probes = acc.shape[1]
    qq = jnp.zeros((probes, LANES), F32)
    qw = jnp.zeros((probes, LANES), F32)
    for b in range(blocks):
        q = q_of(b)
        part = slice(b * BLK, (b + 1) * BLK)
        w = acc[b] + z_of(b) + noise_ref[:, part] * q
        if prev_of is not None:
            w = w - beta * prev_of(b)
        w_ref[:, part] = w
        qq = qq + q * q
        qw = qw + q * w
    put_stats(
        w_ref,
        blocks * BLK,
        lambda b: w_ref[:, b * BLK : (b + 1) * BLK],
        q_of,
        jnp.sum(qq, axis=1, keepdims=True),
        jnp.sum(qw, axis=1, keepdims=True),
        blocks,
    )


def first_outer_kernel(
    blocks, low, old_src, old_dst, old_counts, old_tiles, mine, above, below, noise_ref, z_ref, right,
    src, dst, counts, tiles, w_ref, left, acc, vecs,
):
    probes = mine.shape[0] - 3
    del old_tiles

    def keep(t, carry):
        src[t] = old_src[t]
        dst[t] = old_dst[t]
        return carry

    def lower(row):
        def step(t, m):
            c = low[row + 1, t]
            src[m] = blocks + low[row, t]
            dst[m] = c - blocks
            return m + (c >= blocks).astype(jnp.int32)

        return step

    lax.fori_loop(0, old_counts[1], keep, 0)
    m = lax.fori_loop(0, low[2, 0], lower(0), old_counts[1])
    m = lax.fori_loop(0, low[LIST_ROWS + 2, 0], lower(LIST_ROWS), m)
    for u in range(TAIL):
        src[m + u] = 0
        dst[m + u] = blocks
    counts[0] = old_counts[0]
    counts[1] = whole(m)

    for part, ref in enumerate((above, below)):
        for b in range(blocks):
            at = part * blocks + b
            cols = slice(b * BLK, (b + 1) * BLK)
            vecs[at] = stack_vec(ref[:probes, cols], True)
            lf, _ = features(warp(ref[probes : probes + 3, cols]))
            left[at] = lf.T.astype(BF16)
    acc[...] = jnp.zeros_like(acc)
    outer_edges(acc, vecs, src, dst, counts, maker(tiles, left, right), maker(None, left, right))
    finish_apply(
        blocks, acc, lambda b: z_ref[b], w_ref, lambda b: mine[:probes, b * BLK : (b + 1) * BLK], None, None, noise_ref
    )


def inner_kernel(blocks, rows, cols, counts, w_ref, tiles, left, right, z_ref, acc, vecs):
    for b in range(blocks):
        vecs[b] = stack_vec(w_ref[:, b * BLK : (b + 1) * BLK], False)
    vecs[blocks] = jnp.zeros(vecs.shape[1:], BF16)
    inner_edges(acc, vecs, rows, cols, counts, keeper(tiles), maker(None, left, right))
    z_ref[...] = acc[:blocks]


def alpha_beta(stats, points):
    qw = [s[:, 0:1] for s in stats]
    qq = [s[:, 1:2] for s in stats]
    res = [s[:, 2:3] for s in stats]
    alpha = functools.reduce(jnp.add, qw) / points
    total = jnp.zeros_like(alpha)
    for w, q, r in zip(qw, qq, res):
        gap = alpha - w / jnp.maximum(q, 1e-30)
        total = total + (r + gap * gap * q)
    return alpha, jnp.sqrt(total / points + EPSILON)


def global_alpha_beta(slabs, points, place, stats_ref):
    order = [stats_ref[lax.rem(slab - place[0] + slabs, slabs)] for slab in range(slabs)]
    return alpha_beta(order, points)


def add_ab(ref, base, old_ab, step, alpha, beta):
    shape = (alpha.shape[0], LANES)
    lane = lax.broadcasted_iota(jnp.int32, shape, 1)
    out = jnp.zeros(shape, F32) if old_ab is None else old_ab[...]
    out = jnp.where(lane == step, alpha, out)
    ref[:, base : base + LANES] = jnp.where(lane == ITERS + step, beta, out)


def block_of(ref, rows, b):
    if len(ref.shape) == 3:
        return ref[b]
    return ref[:rows, b * BLK : (b + 1) * BLK]


def outer_kernel(
    blocks, slabs, points, step, place, src, dst, counts, mine, above, below, stats_ref,
    q_own, q_above, q_below, z_raw, z_old, noise_ref, tiles, left, right, *rest,
):
    probes = mine.shape[0]
    old_ab = None
    if step > 0:
        old_ab = rest[0]
        rest = rest[1:]
    w_ref, own_ref, above_ref, below_ref, z_ref, ab_ref, acc, vecs = rest
    alpha, beta = global_alpha_beta(slabs, points, place, stats_ref)
    scale = 1.0 / beta
    add_ab(ab_ref, 0, old_ab, step, alpha, beta)
    halves = ((mine, q_own, own_ref), (above, q_above, above_ref), (below, q_below, below_ref))
    for part, (w, old, new) in enumerate(halves):
        for b in range(blocks):
            q = (w[:, b * BLK : (b + 1) * BLK] - alpha * block_of(old, probes, b)) * scale
            new[b] = q
            if part > 0:
                vecs[(part - 1) * blocks + b] = stack_vec(q, False)
            else:
                z_ref[b] = (z_raw[b] - alpha * z_old[b]) * scale
    acc[...] = jnp.zeros_like(acc)
    outer_edges(acc, vecs, src, dst, counts, keeper(tiles), maker(None, left, right))
    finish_apply(
        blocks, acc, lambda b: z_ref[b], w_ref, lambda b: own_ref[b], lambda b: block_of(q_own, probes, b), beta, noise_ref
    )


def slope_of(left, right):
    e, t = tile_terms(left, right)
    return (e * t) * (t + TAPER_STEP)


def slope_kernel(rows, cols, src, dst, counts, left_own, left_halo, right, after, slopes):
    del after
    base = counts[0]

    def inner(start, many):
        for u in range(many):
            slot = start + u
            slopes[slot] = slope_of(left_own[rows[slot]], right[cols[slot]])

    def outer(start, many):
        for u in range(many):
            at = start + u
            slopes[base + at] = slope_of(left_halo[src[at]], right[dst[at]])

    ranges(0, jnp.minimum(counts[0], KEPT), inner)
    ranges(0, jnp.minimum(counts[1], jnp.maximum(KEPT - base, 0)), outer)


def last_kernel(
    blocks, slabs, points, all_probes, place, rows, cols, src, dst, counts, mine, above, below, stats_ref,
    q_own, q_above, q_below, pts, pts_above, pts_below, old_ab, slopes, left_own, left_out, right,
    basis_ref, grad_ref, acc, form_left, halo_left, form_right, pnts, halo_pnts,
):
    probes = pts.shape[0] - 3
    alpha, beta = global_alpha_beta(slabs, points, place, stats_ref)
    scale = 1.0 / beta
    add_ab(basis_ref, blocks * BLK, old_ab, ITERS - 1, alpha, beta)
    for part, (w, old, ref) in enumerate(((mine, q_own, pts), (above, q_above, pts_above), (below, q_below, pts_below))):
        for b in range(blocks):
            part_cols = slice(b * BLK, (b + 1) * BLK)
            u = (w[:, part_cols] - alpha * block_of(old, probes, b)) * scale
            v = ref[:probes, part_cols]
            high = u.astype(BF16).astype(F32)
            low = u - high
            turned = jnp.concatenate([high, low, v, v], axis=0).T.astype(BF16)
            x = warp(ref[probes : probes + 3, part_cols])
            x1, x2, x3 = split_three(x)
            y = jnp.concatenate([x1, x2, x3, jnp.ones((1, BLK), F32), jnp.zeros((6, BLK), F32)], axis=0).astype(BF16)
            y = jnp.concatenate([y, y], axis=1)
            if part == 0:
                basis_ref[:, part_cols] = u
                form_left[b] = turned
                form_right[b] = jnp.concatenate([v, v, high, low], axis=0).astype(BF16)
                pnts[b] = y
            else:
                halo_left[(part - 1) * blocks + b] = turned
                halo_pnts[(part - 1) * blocks + b] = y
    form_left[blocks] = jnp.zeros((BLK, 4 * probes), BF16)
    form_right[blocks] = jnp.zeros((4 * probes, BLK), BF16)
    pnts[blocks] = jnp.zeros((16, 2 * BLK), BF16)

    def pull(side):
        return lambda slot, a, c: stack_tile(mxu(side[a], form_right[c]) * slopes[slot])

    def pull_made(side, left):
        return lambda slot, a, c: stack_tile(mxu(side[a], form_right[c]) * slope_of(left[a], right[c]))

    inner_edges(acc, pnts, rows, cols, counts, pull(form_left), pull_made(form_left, left_own))
    outer_edges(acc, halo_pnts, src, dst, counts, pull(halo_left), pull_made(halo_left, left_out))
    for b in range(blocks):
        part_cols = slice(b * BLK, (b + 1) * BLK)
        raw = pts[probes : probes + 3, part_cols]
        bent = jnp.tanh(raw)
        x = raw + WARP_GAIN * bent
        sums = acc[b]
        moved = sums[0:3] + sums[3:6] + sums[6:9] - x * sums[9:10]
        chain = 1.0 + WARP_GAIN * (1.0 - bent * bent)
        grad_ref[:, part_cols] = moved * chain * (1.0 / (LENGTH_SQ * all_probes))


def close_kernel(peers, place, own, other, grads, basis_ref, alpha_ref, beta_ref, grad_ref):
    probes = own.shape[0]
    width = basis_ref.shape[1]
    lower = place[1] == 0
    mine = own[...]
    theirs = other[...]
    first = jnp.where(lower, mine, theirs)
    second = jnp.where(lower, theirs, mine)
    basis_ref[:probes] = first[:, :width]
    basis_ref[probes:] = second[:, :width]
    ab = jnp.concatenate([first[:, width:], second[:, width:]], axis=0)
    turned = jnp.concatenate([ab, jnp.zeros((LANES - 2 * probes, LANES), F32)], axis=0).T
    alpha_ref[...] = turned[:ITERS, : 2 * probes]
    beta_ref[...] = turned[ITERS : 2 * ITERS, : 2 * probes]
    total = grads[lax.rem(peers - place[2], peers)]
    for k in range(1, peers):
        total = total + grads[lax.rem(k - place[2] + peers, peers)]
    grad_ref[...] = total


def vmem(count):
    return [pl.BlockSpec(memory_space=pltpu.VMEM)] * count


def smem(count):
    return [pl.BlockSpec(memory_space=pltpu.SMEM)] * count


def held(array):
    return pltpu.with_memory_space_constraint(array, pltpu.VMEM)


def call(name, kernel, outs, ins, scratch, work, aliases=None):
    out_shapes, out_scalars = outs
    arrays, scalars = ins
    flops, moved = work
    return pl.pallas_call(
        kernel,
        out_shape=tuple(out_shapes),
        in_specs=smem(scalars) + vmem(len(arrays) - scalars),
        out_specs=tuple(smem(out_scalars) + vmem(len(out_shapes) - out_scalars)),
        scratch_shapes=[pltpu.VMEM(shape, dtype) for shape, dtype in scratch],
        compiler_params=pltpu.CompilerParams(vmem_limit_bytes=LIMIT_MIB * 1024 * 1024),
        cost_estimate=pl.CostEstimate(flops=flops, bytes_accessed=moved, transcendentals=0),
        input_output_aliases=aliases or {},
        name=name,
    )(*arrays)


def shifted(value, axes, count, steps):
    return lax.ppermute(value, axes, [(source, (source + steps) % count) for source in range(count)])


def body(coords, noise_var, probe_signs, tile_rows, tile_cols, tile_count):
    slabs = lax.axis_size("blk")
    subs = lax.axis_size("sub")
    outer = lax.axis_size("probe")
    probes = probe_signs.shape[0] // subs
    width = coords.shape[1]
    blocks = width // BLK
    cap = tile_rows.shape[-1]
    points = float(width * slabs)
    all_probes = probe_signs.shape[0] * outer
    sub = lax.axis_index("sub")
    blk = lax.axis_index("blk")
    peers = outer * subs
    place = jnp.stack([blk, sub, lax.axis_index("probe") * subs + sub]).astype(jnp.int32)
    noise = noise_var.reshape(1, width)
    sds = jax.ShapeDtypeStruct

    lists, mine = call(
        "pack",
        functools.partial(pack_kernel, probes),
        ((sds((LIST_ROWS, LANES), jnp.int32), sds((probes + 3, width), F32)), 0),
        (
            (
                place, tile_rows.reshape(1, cap), tile_cols.reshape(1, cap), tile_count.reshape(1, 1),
                probe_signs, coords,
            ),
            1,
        ),
        [],
        (1000000, 1000000),
    )
    sibling = shifted(lists, "sub", subs, 1)
    above = shifted(mine, "blk", slabs, -1)
    below = shifted(mine, "blk", slabs, 1)
    low = shifted(jnp.concatenate([lists, sibling], axis=0), "blk", slabs, 1)

    own_slots = subs * cap + TAIL
    halo_slots = 2 * subs * cap + TAIL
    slots = KEPT
    ext = width + LANES
    ints = jnp.int32
    blocks_f32 = sds((blocks, probes, BLK), F32)
    tile_shape = pltpu.VMEM((slots, 2 * BLK, BLK), BF16)
    acc_shape = ((blocks + 1, probes, BLK), F32)

    rows, cols, src, dst, counts, tiles, z, left_own, right = call(
        "first_inner",
        functools.partial(first_inner_kernel, blocks),
        (
            (
                sds((own_slots,), ints), sds((own_slots,), ints), sds((own_slots,), ints), sds((own_slots,), ints),
                sds((2,), ints), tile_shape, blocks_f32,
                sds((blocks + 1, BLK, FEATS), BF16), sds((blocks + 1, FEATS, BLK), BF16),
            ),
            5,
        ),
        ((lists, sibling, mine), 2),
        [acc_shape, ((blocks + 1, probes, 2 * BLK), BF16)],
        (WORK_FIRST, WORK_BYTES),
    )
    src, dst, counts, tiles, w, left_halo = call(
        "first_outer",
        functools.partial(first_outer_kernel, blocks),
        (
            (
                sds((halo_slots,), ints), sds((halo_slots,), ints), sds((2,), ints), tile_shape,
                sds((probes, ext), F32), sds((2 * blocks, BLK, FEATS), BF16),
            ),
            3,
        ),
        ((low, src, dst, counts, held(tiles), mine, above, below, noise, z, right), 4),
        [acc_shape, ((2 * blocks, probes, 2 * BLK), BF16)],
        (WORK_FIRST, WORK_BYTES),
        {4: 3},
    )

    def exchange(w):
        up = shifted(w, "blk", slabs, -1)
        down = shifted(w, "blk", slabs, 1)
        stats = w[:, width:]
        if slabs == 4:
            far = shifted(stats, "blk", slabs, 2)
            rows = jnp.stack([stats, up[:, width:], far, down[:, width:]])
        else:
            rows = lax.all_gather(stats, "blk", axis=0)
            rows = jnp.roll(rows, -blk, axis=0)
        return up, down, rows

    q = (mine, above, below)
    ab = []
    for step in range(ITERS - 1):
        up, down, stats = exchange(w)
        (z_raw,) = call(
            "inner",
            functools.partial(inner_kernel, blocks),
            ((blocks_f32,), 0),
            ((rows, cols, counts, w, held(tiles), left_own, right), 3),
            [acc_shape, ((blocks + 1, 2 * probes, 2 * BLK), BF16)],
            (WORK_NEXT, WORK_BYTES),
        )
        w, q0, q1, q2, z, next_ab = call(
            "outer",
            functools.partial(outer_kernel, blocks, slabs, points, step),
            (
                (sds((probes, ext), F32), blocks_f32, blocks_f32, blocks_f32, blocks_f32, sds((probes, LANES), F32)),
                0,
            ),
            ((place, src, dst, counts, w, up, down, stats, *q, z_raw, z, noise, held(tiles), left_halo, right, *ab), 4),
            [acc_shape, ((2 * blocks, 2 * probes, 2 * BLK), BF16)],
            (WORK_NEXT, WORK_BYTES),
        )
        q = (q0, q1, q2)
        ab = [next_ab]

    up, down, stats = exchange(w)
    (slopes,) = call(
        "slopes",
        slope_kernel,
        ((pltpu.VMEM((slots, BLK, BLK), F32),), 0),
        ((rows, cols, src, dst, counts, left_own, left_halo, right, w), 5),
        [],
        (WORK_FIRST, WORK_BYTES),
    )
    basis, grad = call(
        "last",
        functools.partial(last_kernel, blocks, slabs, points, all_probes),
        ((sds((probes, ext), F32), sds((3, width), F32)), 0),
        (
            (
                place, rows, cols, src, dst, counts, w, up, down, stats, *q, mine, above, below, *ab, held(slopes), left_own, left_halo, right,
            ),
            6,
        ),
        [
            ((blocks + 1, 16, BLK), F32),
            ((blocks + 1, BLK, 4 * probes), BF16),
            ((2 * blocks, BLK, 4 * probes), BF16),
            ((blocks + 1, 4 * probes, BLK), BF16),
            ((blocks + 1, 16, 2 * BLK), BF16),
            ((2 * blocks, 16, 2 * BLK), BF16),
        ],
        (WORK_FIRST, WORK_BYTES),
    )

    other = shifted(basis, "sub", subs, 1)
    parts = [grad]
    for r in range(1, peers):
        parts.append(shifted(grad, ("probe", "sub"), peers, -r))
    last_basis, alphas, betas, coord_grad = call(
        "close",
        functools.partial(close_kernel, peers),
        (
            (
                sds((subs * probes, width), F32), sds((ITERS, subs * probes), F32), sds((ITERS, subs * probes), F32),
                sds((3, width), F32),
            ),
            0,
        ),
        ((place, basis, other, jnp.stack(parts)), 1),
        [],
        (1000000, 1000000),
    )
    return alphas, betas, last_basis, coord_grad


def solution(mesh):
    return jax.shard_map(
        body,
        mesh=mesh,
        in_specs=(
            P(None, ("groups", "blk")),
            P(("groups", "blk")),
            P("probe", ("groups", "blk")),
            P(("groups", "blk"), "sub", None),
            P(("groups", "blk"), "sub", None),
            P(("groups", "blk"), "sub"),
        ),
        out_specs=(
            P(None, ("groups", "probe")),
            P(None, ("groups", "probe")),
            P("probe", ("groups", "blk")),
            P(None, ("groups", "blk")),
        ),
        check_vma=False,
    )
```

```python
import functools
import math

import jax
import jax.numpy as jnp
from jax import lax
from jax.experimental import pallas as pl
from jax.experimental.pallas import tpu as pltpu
from jax.sharding import PartitionSpec as P

ITERS = 3
SIGNAL_VAR = 0.1
LENGTH_SQ = 2.0
TAPER_SQ = 16.0
WARP_GAIN = 0.4
EPSILON = 1e-06

BLK = 128
LANES = 128
FEATS = 32
GROUP = 16
TAIL = 4
LIST_ROWS = 8
OWN_ROWS = 4
LIMIT_MIB = 16
KEPT = 256
WORK_FIRST = 300000000
WORK_NEXT = 100000000
WORK_BYTES = 4000000

S_OF_D = -math.log2(math.e) / (2.0 * LENGTH_SQ)
D_OF_S = 1.0 / S_OF_D
ROOT_VAR = math.sqrt(SIGNAL_VAR)
TAPER_STEP = 4.0 * LENGTH_SQ / TAPER_SQ * ROOT_VAR
T_SLOPE = -ROOT_VAR * D_OF_S / TAPER_SQ

F32 = jnp.float32
BF16 = jnp.bfloat16


def split_two(x):
    high = x.astype(BF16)
    low = (x - high.astype(F32)).astype(BF16)
    return high, low


def split_three(x):
    one = x.astype(BF16).astype(F32)
    rest = x - one
    two = rest.astype(BF16).astype(F32)
    three = (rest - two).astype(BF16).astype(F32)
    return one, two, three


def warp(x):
    return x + WARP_GAIN * jnp.tanh(x)


def mxu(a, b):
    return lax.dot_general(a, b, (((1,), (0,)), ((), ())), preferred_element_type=F32)


def features(x):
    scale = -2.0 * S_OF_D
    y = x * scale
    norm = S_OF_D * jnp.sum(x * x, axis=0, keepdims=True)
    x1, x2, x3 = split_three(x)
    y1, y2, y3 = split_three(y)
    n1, n2, n3 = split_three(norm)
    one = jnp.ones_like(norm)
    pad = jnp.zeros((FEATS - 24, x.shape[1]), F32)
    left = jnp.concatenate([x1, x1, x2, x2, x1, x3, n1, n2, n3, one, one, one, pad], axis=0)
    right = jnp.concatenate([y1, y2, y1, y2, y3, y1, one, one, one, n1, n2, n3, pad], axis=0)
    return left, right


def tile_terms(left, right):
    s = mxu(left, right)
    e = jnp.exp2(s)
    t = jnp.maximum(T_SLOPE * s + ROOT_VAR, 0.0)
    return e, t


def put_stats(ref, base, w_of, q_of, qq, qw, blocks):
    alpha_s = qw / jnp.maximum(qq, 1e-30)
    acc = jnp.zeros((qq.shape[0], LANES), F32)
    for b in range(blocks):
        r = w_of(b) - alpha_s * q_of(b)
        acc = acc + r * r
    res = jnp.sum(acc, axis=1, keepdims=True)
    lane = lax.broadcasted_iota(jnp.int32, (qq.shape[0], LANES), 1)
    out = jnp.where(lane == 0, qw, jnp.where(lane == 1, qq, jnp.where(lane == 2, res, 0.0)))
    ref[:, base : base + LANES] = out


def mxu_turned(a, b):
    return lax.dot_general(a, b, (((1,), (1,)), ((), ())), preferred_element_type=F32)


def fold(out, probes):
    if out.shape[0] > probes:
        return out[:probes] + out[probes:]
    return out


def fold_turned(out, probes):
    total = out[:probes, :BLK] + out[:probes, BLK:]
    if out.shape[0] > probes:
        total = total + out[probes:, :BLK]
    return total


def stack_vec(q, exact):
    if exact:
        high = q.astype(BF16)
        return jnp.concatenate([high, high], axis=1)
    high, low = split_two(q)
    return jnp.concatenate(
        [jnp.concatenate([high, high], axis=1), jnp.concatenate([low, jnp.zeros_like(low)], axis=1)], axis=0
    )


def stack_tile(tile):
    return jnp.concatenate(split_two(tile), axis=0)


def ranges(first, last, body):
    long = (last - first) // GROUP
    middle = first + long * GROUP

    def big(g, carry):
        body(first + g * GROUP, GROUP)
        return carry

    def small(g, carry):
        body(middle + g * TAIL, TAIL)
        return carry

    lax.fori_loop(0, long, big, 0)
    lax.fori_loop(0, (last - middle) // TAIL, small, 0)


def kept_and_made(total, room, body, kept, made):
    first = jnp.minimum(total, room)
    ranges(0, first, functools.partial(body, kept))
    many = (total - first) // TAIL

    def rest(g, carry):
        body(made, first + g * TAIL, TAIL)
        return carry

    lax.fori_loop(0, many, rest, 0)


def inner_edges(acc, vecs, rows, cols, counts, kept, made):
    acc[...] = jnp.zeros_like(acc)
    size = acc.shape[1]

    def group(tile_of, start, many):
        outs = []
        for u in range(many):
            slot = start + u
            a = rows[slot]
            c = cols[slot]
            tile = tile_of(slot, a, c)
            outs.append((c, fold(mxu(vecs[a], tile), size)))
            outs.append((a, fold_turned(mxu_turned(vecs[c][:, :BLK], tile), size)))
        for c, out in outs:
            acc[c] = acc[c] + out

    kept_and_made(counts[0], KEPT, group, kept, made)


def outer_edges(acc, vecs, src, dst, counts, kept, made):
    size = acc.shape[1]
    base = counts[0]

    def group(tile_of, start, many):
        outs = []
        for u in range(many):
            at = start + u
            a = src[at]
            c = dst[at]
            outs.append((c, fold(mxu(vecs[a], tile_of(base + at, a, c)), size)))
        for c, out in outs:
            acc[c] = acc[c] + out

    kept_and_made(counts[1], jnp.maximum(KEPT - base, 0), group, kept, made)


def maker(left, right):
    def make(slot, a, c):
        e, t = tile_terms(left[a], right[c])
        return stack_tile(e * t * t)

    return make


def fill(into, base, total, first_index, second_index, make):
    def body(start, many):
        for u in range(many):
            at = start + u
            into[base + at] = make(base + at, first_index[at], second_index[at])

    ranges(0, jnp.minimum(total, jnp.maximum(KEPT - base, 0)), body)


def keeper(tiles):
    return lambda slot, a, c: tiles[slot]


def whole(n):
    return (n + TAIL - 1) // TAIL * TAIL


def pack_kernel(
    blocks, place, tile_rows, tile_cols, tile_count, signs, coords, noise,
    lists, mine, left, right, got_signs, got_coords, got_noise, got_rows, got_cols, sems,
):
    probes = mine.shape[0] - OWN_ROWS
    first = pl.multiple_of(place[1] * probes, probes)
    moves = [
        pltpu.make_async_copy(coords, got_coords, sems.at[0]),
        pltpu.make_async_copy(signs.at[pl.ds(first, probes), :], got_signs, sems.at[1]),
        pltpu.make_async_copy(noise, got_noise, sems.at[2]),
        pltpu.make_async_copy(tile_rows, got_rows, sems.at[3]),
        pltpu.make_async_copy(tile_cols, got_cols, sems.at[4]),
    ]
    for move in moves:
        move.start()
    lists[...] = jnp.zeros(lists.shape, jnp.int32)
    lists[2:3, :] = jnp.full((1, LANES), tile_count[0], jnp.int32)
    moves[0].wait()
    mine[probes : probes + 3] = got_coords[...]
    for b in range(blocks):
        lf, rt = features(warp(got_coords[:, b * BLK : (b + 1) * BLK]))
        left[b] = lf.T.astype(BF16)
        right[b] = rt.astype(BF16)
    left[blocks] = jnp.zeros((BLK, FEATS), BF16)
    right[blocks] = jnp.zeros((FEATS, BLK), BF16)
    for move in moves[1:]:
        move.wait()
    mine[:probes] = got_signs[...].astype(F32)
    mine[probes + 3 : probes + OWN_ROWS] = got_noise[...]
    lists[0:1, : tile_rows.shape[1]] = got_rows[...]
    lists[1:2, : tile_cols.shape[1]] = got_cols[...]


def first_inner_kernel(
    blocks, own0, own1, mine, left, right,
    rows, cols, src, dst, counts, tiles, z_ref, acc, vecs,
):
    probes = mine.shape[0] - OWN_ROWS

    def own(lst):
        def step(t, carry):
            n, m = carry
            a = lst[0, t]
            c = lst[1, t]
            inside = (c < blocks).astype(jnp.int32)
            rows[n] = a
            cols[n] = c
            src[m] = c - blocks
            dst[m] = a
            return n + inside, m + 1 - inside

        return step

    n, m = lax.fori_loop(0, own0[2, 0], own(own0), (0, 0))
    n, m = lax.fori_loop(0, own1[2, 0], own(own1), (n, m))
    for u in range(TAIL):
        rows[n + u] = blocks
        cols[n + u] = blocks
    counts[0] = whole(n)
    counts[1] = m

    for b in range(blocks):
        part = slice(b * BLK, (b + 1) * BLK)
        vecs[b] = stack_vec(mine[:probes, part], True)
    vecs[blocks] = jnp.zeros((probes, 2 * BLK), BF16)
    make = maker(left, right)
    fill(tiles, 0, counts[0], rows, cols, make)
    inner_edges(acc, vecs, rows, cols, counts, keeper(tiles), make)
    z_ref[...] = acc[:blocks]


def finish_apply(blocks, acc, z_of, w_ref, q_of, prev_of, beta, pts):
    probes = acc.shape[1]
    qq = jnp.zeros((probes, LANES), F32)
    qw = jnp.zeros((probes, LANES), F32)
    for b in range(blocks):
        q = q_of(b)
        part = slice(b * BLK, (b + 1) * BLK)
        w = acc[b] + z_of(b) + pts[probes + 3 : probes + OWN_ROWS, part] * q
        if prev_of is not None:
            w = w - beta * prev_of(b)
        w_ref[:, part] = w
        qq = qq + q * q
        qw = qw + q * w
    put_stats(
        w_ref,
        blocks * BLK,
        lambda b: w_ref[:, b * BLK : (b + 1) * BLK],
        q_of,
        jnp.sum(qq, axis=1, keepdims=True),
        jnp.sum(qw, axis=1, keepdims=True),
        blocks,
    )


def first_outer_kernel(
    blocks, low, old_src, old_dst, old_counts, old_tiles, mine, above, below, z_ref, right,
    src, dst, counts, tiles, w_ref, left, acc, vecs,
):
    probes = mine.shape[0] - OWN_ROWS
    del old_tiles

    def keep(t, carry):
        src[t] = old_src[t]
        dst[t] = old_dst[t]
        return carry

    def lower(row):
        def step(t, m):
            c = low[row + 1, t]
            src[m] = blocks + low[row, t]
            dst[m] = c - blocks
            return m + (c >= blocks).astype(jnp.int32)

        return step

    lax.fori_loop(0, old_counts[1], keep, 0)
    m = lax.fori_loop(0, low[2, 0], lower(0), old_counts[1])
    m = lax.fori_loop(0, low[LIST_ROWS + 2, 0], lower(LIST_ROWS), m)
    for u in range(TAIL):
        src[m + u] = 0
        dst[m + u] = blocks
    counts[0] = old_counts[0]
    counts[1] = whole(m)

    for part, ref in enumerate((above, below)):
        for b in range(blocks):
            at = part * blocks + b
            cols = slice(b * BLK, (b + 1) * BLK)
            vecs[at] = stack_vec(ref[:probes, cols], True)
            lf, _ = features(warp(ref[probes : probes + 3, cols]))
            left[at] = lf.T.astype(BF16)
    acc[...] = jnp.zeros_like(acc)
    make = maker(left, right)
    fill(tiles, counts[0], counts[1], src, dst, make)
    outer_edges(acc, vecs, src, dst, counts, keeper(tiles), make)
    finish_apply(
        blocks, acc, lambda b: z_ref[b], w_ref, lambda b: mine[:probes, b * BLK : (b + 1) * BLK], None, None, mine
    )


def inner_kernel(blocks, rows, cols, counts, w_ref, tiles, left, right, z_ref, acc, vecs):
    for b in range(blocks):
        vecs[b] = stack_vec(w_ref[:, b * BLK : (b + 1) * BLK], False)
    vecs[blocks] = jnp.zeros(vecs.shape[1:], BF16)
    inner_edges(acc, vecs, rows, cols, counts, keeper(tiles), maker(left, right))
    z_ref[...] = acc[:blocks]


def alpha_beta(stats, points):
    qw = [s[:, 0:1] for s in stats]
    qq = [s[:, 1:2] for s in stats]
    res = [s[:, 2:3] for s in stats]
    alpha = functools.reduce(jnp.add, qw) / points
    total = jnp.zeros_like(alpha)
    for w, q, r in zip(qw, qq, res):
        gap = alpha - w / jnp.maximum(q, 1e-30)
        total = total + (r + gap * gap * q)
    return alpha, jnp.sqrt(total / points + EPSILON)


def global_alpha_beta(slabs, points, place, stats_ref):
    order = [stats_ref[lax.rem(slab - place[0] + slabs, slabs)] for slab in range(slabs)]
    return alpha_beta(order, points)


def add_ab(ref, base, old_ab, step, alpha, beta):
    shape = (alpha.shape[0], LANES)
    lane = lax.broadcasted_iota(jnp.int32, shape, 1)
    out = jnp.zeros(shape, F32) if old_ab is None else old_ab[...]
    out = jnp.where(lane == step, alpha, out)
    ref[:, base : base + LANES] = jnp.where(lane == ITERS + step, beta, out)


def block_of(ref, rows, b):
    if len(ref.shape) == 3:
        return ref[b]
    return ref[:rows, b * BLK : (b + 1) * BLK]


def outer_kernel(
    blocks, slabs, points, step, place, src, dst, counts, mine, above, below, stats_ref,
    q_own, q_above, q_below, z_raw, z_old, pts, tiles, left, right, *rest,
):
    probes = mine.shape[0]
    old_ab = None
    if step > 0:
        old_ab = rest[0]
        rest = rest[1:]
    w_ref, own_ref, above_ref, below_ref, z_ref, ab_ref, acc, vecs = rest
    alpha, beta = global_alpha_beta(slabs, points, place, stats_ref)
    scale = 1.0 / beta
    add_ab(ab_ref, 0, old_ab, step, alpha, beta)
    halves = ((mine, q_own, own_ref), (above, q_above, above_ref), (below, q_below, below_ref))
    for part, (w, old, new) in enumerate(halves):
        for b in range(blocks):
            q = (w[:, b * BLK : (b + 1) * BLK] - alpha * block_of(old, probes, b)) * scale
            new[b] = q
            if part > 0:
                vecs[(part - 1) * blocks + b] = stack_vec(q, False)
            else:
                z_ref[b] = (z_raw[b] - alpha * z_old[b]) * scale
    acc[...] = jnp.zeros_like(acc)
    outer_edges(acc, vecs, src, dst, counts, keeper(tiles), maker(left, right))
    finish_apply(
        blocks, acc, lambda b: z_ref[b], w_ref, lambda b: own_ref[b], lambda b: block_of(q_own, probes, b), beta, pts
    )


def slope_of(left, right):
    e, t = tile_terms(left, right)
    return (e * t) * (t + TAPER_STEP)


def slope_kernel(rows, cols, src, dst, counts, left_own, left_halo, right, after, slopes):
    del after
    fill(slopes, 0, counts[0], rows, cols, lambda slot, a, c: slope_of(left_own[a], right[c]))
    fill(slopes, counts[0], counts[1], src, dst, lambda slot, a, c: slope_of(left_halo[a], right[c]))


def last_kernel(
    blocks, slabs, points, all_probes, place, rows, cols, src, dst, counts, mine, above, below, stats_ref,
    q_own, q_above, q_below, pts, pts_above, pts_below, old_ab, slopes, left_own, left_out, right,
    basis_ref, grad_ref, acc, form_left, halo_left, form_right, pnts, halo_pnts, pulls,
):
    probes = pts.shape[0] - OWN_ROWS
    alpha, beta = global_alpha_beta(slabs, points, place, stats_ref)
    scale = 1.0 / beta
    add_ab(basis_ref, blocks * BLK, old_ab, ITERS - 1, alpha, beta)
    for part, (w, old, ref) in enumerate(((mine, q_own, pts), (above, q_above, pts_above), (below, q_below, pts_below))):
        for b in range(blocks):
            part_cols = slice(b * BLK, (b + 1) * BLK)
            u = (w[:, part_cols] - alpha * block_of(old, probes, b)) * scale
            v = ref[:probes, part_cols]
            high = u.astype(BF16).astype(F32)
            low = u - high
            turned = jnp.concatenate([high, low, v, v], axis=0).T.astype(BF16)
            x = warp(ref[probes : probes + 3, part_cols])
            x1, x2, x3 = split_three(x)
            y = jnp.concatenate([x1, x2, x3, jnp.ones((1, BLK), F32), jnp.zeros((6, BLK), F32)], axis=0).astype(BF16)
            y = jnp.concatenate([y, y], axis=1)
            if part == 0:
                basis_ref[:, part_cols] = u
                form_left[b] = turned
                form_right[b] = jnp.concatenate([v, v, high, low], axis=0).astype(BF16)
                pnts[b] = y
            else:
                halo_left[(part - 1) * blocks + b] = turned
                halo_pnts[(part - 1) * blocks + b] = y
    form_left[blocks] = jnp.zeros((BLK, 4 * probes), BF16)
    form_right[blocks] = jnp.zeros((4 * probes, BLK), BF16)
    pnts[blocks] = jnp.zeros((16, 2 * BLK), BF16)

    def pull(side):
        return lambda slot, a, c: stack_tile(mxu(side[a], form_right[c]) * slopes[slot])

    def pull_made(side, left):
        return lambda slot, a, c: stack_tile(mxu(side[a], form_right[c]) * slope_of(left[a], right[c]))

    fill(pulls, 0, counts[0], rows, cols, pull(form_left))
    fill(pulls, counts[0], counts[1], src, dst, pull(halo_left))
    inner_edges(acc, pnts, rows, cols, counts, keeper(pulls), pull_made(form_left, left_own))
    outer_edges(acc, halo_pnts, src, dst, counts, keeper(pulls), pull_made(halo_left, left_out))
    for b in range(blocks):
        part_cols = slice(b * BLK, (b + 1) * BLK)
        raw = pts[probes : probes + 3, part_cols]
        bent = jnp.tanh(raw)
        x = raw + WARP_GAIN * bent
        sums = acc[b]
        moved = sums[0:3] + sums[3:6] + sums[6:9] - x * sums[9:10]
        chain = 1.0 + WARP_GAIN * (1.0 - bent * bent)
        grad_ref[:, part_cols] = moved * chain * (1.0 / (LENGTH_SQ * all_probes))


def close_kernel(peers, place, own, other, grads, basis_ref, alpha_ref, beta_ref, grad_ref):
    probes = own.shape[0]
    width = basis_ref.shape[1]
    lower = place[1] == 0
    mine = own[...]
    theirs = other[...]
    first = jnp.where(lower, mine, theirs)
    second = jnp.where(lower, theirs, mine)
    basis_ref[:probes] = first[:, :width]
    basis_ref[probes:] = second[:, :width]
    ab = jnp.concatenate([first[:, width:], second[:, width:]], axis=0)
    turned = jnp.concatenate([ab, jnp.zeros((LANES - 2 * probes, LANES), F32)], axis=0).T
    alpha_ref[...] = turned[:ITERS, : 2 * probes]
    beta_ref[...] = turned[ITERS : 2 * ITERS, : 2 * probes]
    total = grads[lax.rem(peers - place[2], peers)]
    for k in range(1, peers):
        total = total + grads[lax.rem(k - place[2] + peers, peers)]
    grad_ref[...] = total


def vmem(count):
    return [pl.BlockSpec(memory_space=pltpu.VMEM)] * count


def smem(count):
    return [pl.BlockSpec(memory_space=pltpu.SMEM)] * count


def held(array):
    return pltpu.with_memory_space_constraint(array, pltpu.VMEM)


def stays(array):
    return pltpu.with_memory_space_constraint(array, pltpu.HBM)


def in_hbm(count):
    return [pl.BlockSpec(memory_space=pltpu.HBM)] * count


def call(name, kernel, outs, ins, scratch, work, aliases=None, limit=LIMIT_MIB):
    out_shapes, out_scalars = outs
    arrays, scalars = ins
    flops, moved = work
    return pl.pallas_call(
        kernel,
        out_shape=tuple(out_shapes),
        in_specs=smem(scalars) + vmem(len(arrays) - scalars),
        out_specs=tuple(smem(out_scalars) + vmem(len(out_shapes) - out_scalars)),
        scratch_shapes=[pltpu.VMEM(shape, dtype) for shape, dtype in scratch],
        compiler_params=pltpu.CompilerParams(vmem_limit_bytes=limit * 1024 * 1024),
        cost_estimate=pl.CostEstimate(flops=flops, bytes_accessed=moved, transcendentals=0),
        input_output_aliases=aliases or {},
        name=name,
    )(*arrays)


def shifted(value, axes, count, steps):
    return lax.ppermute(value, axes, [(source, (source + steps) % count) for source in range(count)])


def body(coords, noise_var, probe_signs, tile_rows, tile_cols, tile_count):
    slabs = lax.axis_size("blk")
    subs = lax.axis_size("sub")
    outer = lax.axis_size("probe")
    probes = probe_signs.shape[0] // subs
    width = coords.shape[1]
    blocks = width // BLK
    cap = tile_rows.shape[-1]
    points = float(width * slabs)
    all_probes = probe_signs.shape[0] * outer
    sub = lax.axis_index("sub")
    blk = lax.axis_index("blk")
    peers = outer * subs
    place = jnp.stack([blk, sub, lax.axis_index("probe") * subs + sub]).astype(jnp.int32)
    sds = jax.ShapeDtypeStruct

    left_shape = sds((blocks + 1, BLK, FEATS), BF16)
    right_shape = sds((blocks + 1, FEATS, BLK), BF16)
    lists, mine, left_own, right = pl.pallas_call(
        functools.partial(pack_kernel, blocks),
        out_shape=(sds((LIST_ROWS, LANES), jnp.int32), sds((probes + OWN_ROWS, width), F32), left_shape, right_shape),
        in_specs=smem(1) + in_hbm(2) + smem(1) + in_hbm(3),
        out_specs=tuple(vmem(4)),
        scratch_shapes=[
            pltpu.VMEM((probes, width), jnp.int32),
            pltpu.VMEM((3, width), F32),
            pltpu.VMEM((1, width), F32),
            pltpu.VMEM((1, cap), jnp.int32),
            pltpu.VMEM((1, cap), jnp.int32),
            pltpu.SemaphoreType.DMA((5,)),
        ],
        compiler_params=pltpu.CompilerParams(vmem_limit_bytes=LIMIT_MIB * 1024 * 1024),
        name="pack",
    )(
        place, stays(tile_rows.reshape(1, cap)), stays(tile_cols.reshape(1, cap)), tile_count.reshape(1),
        stays(probe_signs), stays(coords), stays(noise_var.reshape(1, width)),
    )
    sibling = shifted(lists, "sub", subs, 1)
    above = shifted(mine, "blk", slabs, -1)
    below = shifted(mine, "blk", slabs, 1)
    low = shifted(jnp.concatenate([lists, sibling], axis=0), "blk", slabs, 1)

    own_slots = subs * cap + TAIL
    halo_slots = 2 * subs * cap + TAIL
    slots = KEPT
    ext = width + LANES
    ints = jnp.int32
    blocks_f32 = sds((blocks, probes, BLK), F32)
    tile_shape = pltpu.VMEM((slots, 2 * BLK, BLK), BF16)
    acc_shape = ((blocks + 1, probes, BLK), F32)

    rows, cols, src, dst, counts, tiles, z = call(
        "first_inner",
        functools.partial(first_inner_kernel, blocks),
        (
            (
                sds((own_slots,), ints), sds((own_slots,), ints), sds((own_slots,), ints), sds((own_slots,), ints),
                sds((2,), ints), tile_shape, blocks_f32,
            ),
            5,
        ),
        ((lists, sibling, mine, left_own, right), 2),
        [acc_shape, ((blocks + 1, probes, 2 * BLK), BF16)],
        (WORK_FIRST, WORK_BYTES),
    )
    src, dst, counts, tiles, w, left_halo = call(
        "first_outer",
        functools.partial(first_outer_kernel, blocks),
        (
            (
                sds((halo_slots,), ints), sds((halo_slots,), ints), sds((2,), ints), tile_shape,
                sds((probes, ext), F32), sds((2 * blocks, BLK, FEATS), BF16),
            ),
            3,
        ),
        ((low, src, dst, counts, held(tiles), mine, above, below, z, right), 4),
        [acc_shape, ((2 * blocks, probes, 2 * BLK), BF16)],
        (WORK_FIRST, WORK_BYTES),
        {4: 3},
    )

    def exchange(w):
        up = shifted(w, "blk", slabs, -1)
        down = shifted(w, "blk", slabs, 1)
        stats = w[:, width:]
        if slabs == 4:
            far = shifted(stats, "blk", slabs, 2)
            rows = jnp.stack([stats, up[:, width:], far, down[:, width:]])
        else:
            rows = lax.all_gather(stats, "blk", axis=0)
            rows = jnp.roll(rows, -blk, axis=0)
        return up, down, rows

    q = (mine, above, below)
    ab = []
    for step in range(ITERS - 1):
        up, down, stats = exchange(w)
        (z_raw,) = call(
            "inner",
            functools.partial(inner_kernel, blocks),
            ((blocks_f32,), 0),
            ((rows, cols, counts, w, held(tiles), left_own, right), 3),
            [acc_shape, ((blocks + 1, 2 * probes, 2 * BLK), BF16)],
            (WORK_NEXT, WORK_BYTES),
        )
        w, q0, q1, q2, z, next_ab = call(
            "outer",
            functools.partial(outer_kernel, blocks, slabs, points, step),
            (
                (sds((probes, ext), F32), blocks_f32, blocks_f32, blocks_f32, blocks_f32, sds((probes, LANES), F32)),
                0,
            ),
            ((place, src, dst, counts, w, up, down, stats, *q, z_raw, z, mine, held(tiles), left_halo, right, *ab), 4),
            [acc_shape, ((2 * blocks, 2 * probes, 2 * BLK), BF16)],
            (WORK_NEXT, WORK_BYTES),
        )
        q = (q0, q1, q2)
        ab = [next_ab]

    up, down, stats = exchange(w)
    (slopes,) = call(
        "slopes",
        slope_kernel,
        ((pltpu.VMEM((slots, BLK, BLK), F32),), 0),
        ((rows, cols, src, dst, counts, left_own, left_halo, right, w), 5),
        [],
        (WORK_FIRST, WORK_BYTES),
    )
    basis, grad = call(
        "last",
        functools.partial(last_kernel, blocks, slabs, points, all_probes),
        ((sds((probes, ext), F32), sds((3, width), F32)), 0),
        (
            (
                place, rows, cols, src, dst, counts, w, up, down, stats, *q, mine, above, below, *ab, held(slopes), left_own, left_halo, right,
            ),
            6,
        ),
        [
            ((blocks + 1, 16, BLK), F32),
            ((blocks + 1, BLK, 4 * probes), BF16),
            ((2 * blocks, BLK, 4 * probes), BF16),
            ((blocks + 1, 4 * probes, BLK), BF16),
            ((blocks + 1, 16, 2 * BLK), BF16),
            ((2 * blocks, 16, 2 * BLK), BF16),
            ((slots, 2 * BLK, BLK), BF16),
        ],
        (WORK_FIRST, WORK_BYTES),
        limit=2 * LIMIT_MIB,
    )

    other = shifted(basis, "sub", subs, 1)
    parts = [grad]
    for r in range(1, peers):
        parts.append(shifted(grad, ("probe", "sub"), peers, -r))
    last_basis, alphas, betas, coord_grad = call(
        "close",
        functools.partial(close_kernel, peers),
        (
            (
                sds((subs * probes, width), F32), sds((ITERS, subs * probes), F32), sds((ITERS, subs * probes), F32),
                sds((3, width), F32),
            ),
            0,
        ),
        ((place, basis, other, jnp.stack(parts)), 1),
        [],
        (1000000, 1000000),
    )
    return alphas, betas, last_basis, coord_grad


def solution(mesh):
    return jax.shard_map(
        body,
        mesh=mesh,
        in_specs=(
            P(None, ("groups", "blk")),
            P(("groups", "blk")),
            P("probe", ("groups", "blk")),
            P(("groups", "blk"), "sub", None),
            P(("groups", "blk"), "sub", None),
            P(("groups", "blk"), "sub"),
        ),
        out_specs=(
            P(None, ("groups", "probe")),
            P(None, ("groups", "probe")),
            P("probe", ("groups", "blk")),
            P(None, ("groups", "blk")),
        ),
        check_vma=False,
    )
```

```python
import functools
import math

import jax
import jax.numpy as jnp
from jax import lax
from jax.experimental import pallas as pl
from jax.experimental.pallas import tpu as pltpu
from jax.sharding import PartitionSpec as P

ITERS = 3
SIGNAL_VAR = 0.1
LENGTH_SQ = 2.0
TAPER_SQ = 16.0
WARP_GAIN = 0.4
EPSILON = 1e-06

BLK = 128
LANES = 128
FEATS = 32
GROUP = 16
TAIL = 4
LIST_ROWS = 8
OWN_ROWS = 4
LIMIT_MIB = 16
KEPT = 256
WORK_FIRST = 300000000
WORK_NEXT = 100000000
WORK_BYTES = 4000000

S_OF_D = -math.log2(math.e) / (2.0 * LENGTH_SQ)
D_OF_S = 1.0 / S_OF_D
ROOT_VAR = math.sqrt(SIGNAL_VAR)
TAPER_STEP = 4.0 * LENGTH_SQ / TAPER_SQ * ROOT_VAR
T_SLOPE = -ROOT_VAR * D_OF_S / TAPER_SQ

F32 = jnp.float32
BF16 = jnp.bfloat16


def split_two(x):
    high = x.astype(BF16)
    low = (x - high.astype(F32)).astype(BF16)
    return high, low


def split_three(x):
    one = x.astype(BF16).astype(F32)
    rest = x - one
    two = rest.astype(BF16).astype(F32)
    three = (rest - two).astype(BF16).astype(F32)
    return one, two, three


def warp(x):
    return x + WARP_GAIN * jnp.tanh(x)


def mxu(a, b):
    return lax.dot_general(a, b, (((1,), (0,)), ((), ())), preferred_element_type=F32)


def features(x):
    scale = -2.0 * S_OF_D
    y = x * scale
    norm = S_OF_D * jnp.sum(x * x, axis=0, keepdims=True)
    x1, x2, x3 = split_three(x)
    y1, y2, y3 = split_three(y)
    n1, n2, n3 = split_three(norm)
    one = jnp.ones_like(norm)
    pad = jnp.zeros((FEATS - 24, x.shape[1]), F32)
    left = jnp.concatenate([x1, x1, x2, x2, x1, x3, n1, n2, n3, one, one, one, pad], axis=0)
    right = jnp.concatenate([y1, y2, y1, y2, y3, y1, one, one, one, n1, n2, n3, pad], axis=0)
    return left, right


def tile_terms(left, right):
    s = mxu(left, right)
    e = jnp.exp2(s)
    t = jnp.maximum(T_SLOPE * s + ROOT_VAR, 0.0)
    return e, t


def put_stats(ref, base, w_of, q_of, qq, qw, blocks):
    alpha_s = qw / jnp.maximum(qq, 1e-30)
    acc = jnp.zeros((qq.shape[0], LANES), F32)
    for b in range(blocks):
        r = w_of(b) - alpha_s * q_of(b)
        acc = acc + r * r
    res = jnp.sum(acc, axis=1, keepdims=True)
    lane = lax.broadcasted_iota(jnp.int32, (qq.shape[0], LANES), 1)
    out = jnp.where(lane == 0, qw, jnp.where(lane == 1, qq, jnp.where(lane == 2, res, 0.0)))
    ref[:, base : base + LANES] = out


def mxu_turned(a, b):
    return lax.dot_general(a, b, (((1,), (1,)), ((), ())), preferred_element_type=F32)


def fold(out, probes):
    if out.shape[0] > probes:
        return out[:probes] + out[probes:]
    return out


def fold_turned(out, probes):
    total = out[:probes, :BLK] + out[:probes, BLK:]
    if out.shape[0] > probes:
        total = total + out[probes:, :BLK]
    return total


def stack_vec(q, exact):
    if exact:
        high = q.astype(BF16)
        return jnp.concatenate([high, high], axis=1)
    high, low = split_two(q)
    return jnp.concatenate(
        [jnp.concatenate([high, high], axis=1), jnp.concatenate([low, jnp.zeros_like(low)], axis=1)], axis=0
    )


def stack_tile(tile):
    return jnp.concatenate(split_two(tile), axis=0)


def ranges(first, last, body):
    long = (last - first) // GROUP
    middle = first + long * GROUP

    def big(g, carry):
        body(first + g * GROUP, GROUP)
        return carry

    def small(g, carry):
        body(middle + g * TAIL, TAIL)
        return carry

    lax.fori_loop(0, long, big, 0)
    lax.fori_loop(0, (last - middle) // TAIL, small, 0)


def kept_and_made(total, room, body, kept, made):
    first = jnp.minimum(total, room)
    ranges(0, first, functools.partial(body, kept))
    many = (total - first) // TAIL

    def rest(g, carry):
        body(made, first + g * TAIL, TAIL)
        return carry

    lax.fori_loop(0, many, rest, 0)


def inner_edges(acc, vecs, rows, cols, counts, kept, made):
    acc[...] = jnp.zeros_like(acc)
    size = acc.shape[1]

    def group(tile_of, start, many):
        outs = []
        for u in range(many):
            slot = start + u
            a = rows[slot]
            c = cols[slot]
            tile = tile_of(slot, a, c)
            outs.append((c, fold(mxu(vecs[a], tile), size)))
            outs.append((a, fold_turned(mxu_turned(vecs[c][:, :BLK], tile), size)))
        for c, out in outs:
            acc[c] = acc[c] + out

    kept_and_made(counts[0], KEPT, group, kept, made)


def outer_edges(acc, vecs, src, dst, counts, kept, made):
    size = acc.shape[1]
    base = counts[0]

    def group(tile_of, start, many):
        outs = []
        for u in range(many):
            at = start + u
            a = src[at]
            c = dst[at]
            outs.append((c, fold(mxu(vecs[a], tile_of(base + at, a, c)), size)))
        for c, out in outs:
            acc[c] = acc[c] + out

    kept_and_made(counts[1], jnp.maximum(KEPT - base, 0), group, kept, made)


def maker(left, right):
    def make(slot, a, c):
        e, t = tile_terms(left[a], right[c])
        return stack_tile(e * t * t)

    return make


def fill(into, base, total, first_index, second_index, make):
    def body(start, many):
        for u in range(many):
            at = start + u
            into[base + at] = make(base + at, first_index[at], second_index[at])

    ranges(0, jnp.minimum(total, jnp.maximum(KEPT - base, 0)), body)


def keeper(tiles):
    return lambda slot, a, c: tiles[slot]


def whole(n):
    return (n + TAIL - 1) // TAIL * TAIL


def pack_kernel(
    blocks, place, tile_rows, tile_cols, tile_count, signs, coords, noise,
    lists, mine, left, right, got_signs, got_coords, got_noise, got_rows, got_cols, sems,
):
    probes = mine.shape[0] - OWN_ROWS
    first = pl.multiple_of(place[1] * probes, probes)
    moves = [
        pltpu.make_async_copy(coords, got_coords, sems.at[0]),
        pltpu.make_async_copy(signs.at[pl.ds(first, probes), :], got_signs, sems.at[1]),
        pltpu.make_async_copy(noise, got_noise, sems.at[2]),
        pltpu.make_async_copy(tile_rows, got_rows, sems.at[3]),
        pltpu.make_async_copy(tile_cols, got_cols, sems.at[4]),
    ]
    for move in moves:
        move.start()
    lists[...] = jnp.zeros(lists.shape, jnp.int32)
    lists[2:3, :] = jnp.full((1, LANES), tile_count[0], jnp.int32)
    moves[0].wait()
    mine[probes : probes + 3] = got_coords[...]
    for b in range(blocks):
        lf, rt = features(warp(got_coords[:, b * BLK : (b + 1) * BLK]))
        left[b] = lf.T.astype(BF16)
        right[b] = rt.astype(BF16)
    left[blocks] = jnp.zeros((BLK, FEATS), BF16)
    right[blocks] = jnp.zeros((FEATS, BLK), BF16)
    for move in moves[1:]:
        move.wait()
    mine[:probes] = got_signs[...].astype(F32)
    mine[probes + 3 : probes + OWN_ROWS] = got_noise[...]
    lists[0:1, : tile_rows.shape[1]] = got_rows[...]
    lists[1:2, : tile_cols.shape[1]] = got_cols[...]


def first_inner_kernel(
    blocks, own0, own1, mine, left, right,
    rows, cols, src, dst, counts, tiles, z_ref, acc, vecs,
):
    probes = mine.shape[0] - OWN_ROWS

    def own(lst):
        def step(t, carry):
            n, m = carry
            a = lst[0, t]
            c = lst[1, t]
            inside = (c < blocks).astype(jnp.int32)
            rows[n] = a
            cols[n] = c
            src[m] = c - blocks
            dst[m] = a
            return n + inside, m + 1 - inside

        return step

    n, m = lax.fori_loop(0, own0[2, 0], own(own0), (0, 0))
    n, m = lax.fori_loop(0, own1[2, 0], own(own1), (n, m))
    for u in range(TAIL):
        rows[n + u] = blocks
        cols[n + u] = blocks
    counts[0] = whole(n)
    counts[1] = m

    for b in range(blocks):
        part = slice(b * BLK, (b + 1) * BLK)
        vecs[b] = stack_vec(mine[:probes, part], True)
    vecs[blocks] = jnp.zeros((probes, 2 * BLK), BF16)
    make = maker(left, right)
    fill(tiles, 0, counts[0], rows, cols, make)
    inner_edges(acc, vecs, rows, cols, counts, keeper(tiles), make)
    z_ref[...] = acc[:blocks]


def finish_apply(blocks, acc, z_of, w_ref, q_of, prev_of, beta, pts):
    probes = acc.shape[1]
    qq = jnp.zeros((probes, LANES), F32)
    qw = jnp.zeros((probes, LANES), F32)
    for b in range(blocks):
        q = q_of(b)
        part = slice(b * BLK, (b + 1) * BLK)
        w = acc[b] + z_of(b) + pts[probes + 3 : probes + OWN_ROWS, part] * q
        if prev_of is not None:
            w = w - beta * prev_of(b)
        w_ref[:, part] = w
        qq = qq + q * q
        qw = qw + q * w
    put_stats(
        w_ref,
        blocks * BLK,
        lambda b: w_ref[:, b * BLK : (b + 1) * BLK],
        q_of,
        jnp.sum(qq, axis=1, keepdims=True),
        jnp.sum(qw, axis=1, keepdims=True),
        blocks,
    )


def first_outer_kernel(
    blocks, low, old_src, old_dst, old_counts, old_tiles, mine, above, below, z_ref, right,
    src, dst, counts, tiles, w_ref, left, acc, vecs,
):
    probes = mine.shape[0] - OWN_ROWS
    del old_tiles

    def keep(t, carry):
        src[t] = old_src[t]
        dst[t] = old_dst[t]
        return carry

    def lower(row):
        def step(t, m):
            c = low[row + 1, t]
            src[m] = blocks + low[row, t]
            dst[m] = c - blocks
            return m + (c >= blocks).astype(jnp.int32)

        return step

    lax.fori_loop(0, old_counts[1], keep, 0)
    m = lax.fori_loop(0, low[2, 0], lower(0), old_counts[1])
    m = lax.fori_loop(0, low[LIST_ROWS + 2, 0], lower(LIST_ROWS), m)
    for u in range(TAIL):
        src[m + u] = 0
        dst[m + u] = blocks
    counts[0] = old_counts[0]
    counts[1] = whole(m)

    for part, ref in enumerate((above, below)):
        for b in range(blocks):
            at = part * blocks + b
            cols = slice(b * BLK, (b + 1) * BLK)
            vecs[at] = stack_vec(ref[:probes, cols], True)
            lf, _ = features(warp(ref[probes : probes + 3, cols]))
            left[at] = lf.T.astype(BF16)
    acc[...] = jnp.zeros_like(acc)
    make = maker(left, right)
    fill(tiles, counts[0], counts[1], src, dst, make)
    outer_edges(acc, vecs, src, dst, counts, keeper(tiles), make)
    finish_apply(
        blocks, acc, lambda b: z_ref[b], w_ref, lambda b: mine[:probes, b * BLK : (b + 1) * BLK], None, None, mine
    )


def inner_kernel(blocks, rows, cols, counts, w_ref, tiles, left, right, z_ref, acc, vecs):
    for b in range(blocks):
        vecs[b] = stack_vec(w_ref[:, b * BLK : (b + 1) * BLK], False)
    vecs[blocks] = jnp.zeros(vecs.shape[1:], BF16)
    inner_edges(acc, vecs, rows, cols, counts, keeper(tiles), maker(left, right))
    z_ref[...] = acc[:blocks]


def alpha_beta(stats, points):
    qw = [s[:, 0:1] for s in stats]
    qq = [s[:, 1:2] for s in stats]
    res = [s[:, 2:3] for s in stats]
    alpha = functools.reduce(jnp.add, qw) / points
    total = jnp.zeros_like(alpha)
    for w, q, r in zip(qw, qq, res):
        gap = alpha - w / jnp.maximum(q, 1e-30)
        total = total + (r + gap * gap * q)
    return alpha, jnp.sqrt(total / points + EPSILON)


def global_alpha_beta(slabs, points, place, stats_ref):
    return alpha_beta([stats_ref[slab][...] for slab in range(slabs)], points)


def gathered(slabs, width, place, every):
    above = every.at[lax.rem(place[0] + 1, slabs)]
    below = every.at[lax.rem(place[0] + slabs - 1, slabs)]
    return above, below, [every.at[slab, :, width : width + LANES] for slab in range(slabs)]


def add_ab(ref, base, old_ab, step, alpha, beta):
    shape = (alpha.shape[0], LANES)
    lane = lax.broadcasted_iota(jnp.int32, shape, 1)
    out = jnp.zeros(shape, F32) if old_ab is None else old_ab[...]
    out = jnp.where(lane == step, alpha, out)
    ref[:, base : base + LANES] = jnp.where(lane == ITERS + step, beta, out)


def block_of(ref, rows, b):
    if len(ref.shape) == 3:
        return ref[b]
    return ref[:rows, b * BLK : (b + 1) * BLK]


def outer_kernel(
    blocks, slabs, points, step, place, src, dst, counts, mine, every,
    q_own, q_above, q_below, z_raw, z_old, pts, tiles, left, right, *rest,
):
    probes = mine.shape[0]
    old_ab = None
    if step > 0:
        old_ab = rest[0]
        rest = rest[1:]
    w_ref, own_ref, above_ref, below_ref, z_ref, ab_ref, acc, vecs = rest
    above, below, stats_ref = gathered(slabs, blocks * BLK, place, every)
    alpha, beta = global_alpha_beta(slabs, points, place, stats_ref)
    scale = 1.0 / beta
    add_ab(ab_ref, 0, old_ab, step, alpha, beta)
    halves = ((mine, q_own, own_ref), (above, q_above, above_ref), (below, q_below, below_ref))
    for part, (w, old, new) in enumerate(halves):
        for b in range(blocks):
            q = (w[:, b * BLK : (b + 1) * BLK] - alpha * block_of(old, probes, b)) * scale
            new[b] = q
            if part > 0:
                vecs[(part - 1) * blocks + b] = stack_vec(q, False)
            else:
                z_ref[b] = (z_raw[b] - alpha * z_old[b]) * scale
    acc[...] = jnp.zeros_like(acc)
    outer_edges(acc, vecs, src, dst, counts, keeper(tiles), maker(left, right))
    finish_apply(
        blocks, acc, lambda b: z_ref[b], w_ref, lambda b: own_ref[b], lambda b: block_of(q_own, probes, b), beta, pts
    )


def slope_of(left, right):
    e, t = tile_terms(left, right)
    return (e * t) * (t + TAPER_STEP)


def slope_kernel(rows, cols, src, dst, counts, left_own, left_halo, right, after, slopes):
    del after
    fill(slopes, 0, counts[0], rows, cols, lambda slot, a, c: slope_of(left_own[a], right[c]))
    fill(slopes, counts[0], counts[1], src, dst, lambda slot, a, c: slope_of(left_halo[a], right[c]))


def last_kernel(
    blocks, slabs, points, all_probes, place, rows, cols, src, dst, counts, mine, every,
    q_own, q_above, q_below, pts, pts_above, pts_below, old_ab, slopes, left_own, left_out, right,
    basis_ref, grad_ref, acc, form_left, halo_left, form_right, pnts, halo_pnts, pulls,
):
    probes = pts.shape[0] - OWN_ROWS
    above, below, stats_ref = gathered(slabs, blocks * BLK, place, every)
    alpha, beta = global_alpha_beta(slabs, points, place, stats_ref)
    scale = 1.0 / beta
    add_ab(basis_ref, blocks * BLK, old_ab, ITERS - 1, alpha, beta)
    for part, (w, old, ref) in enumerate(((mine, q_own, pts), (above, q_above, pts_above), (below, q_below, pts_below))):
        for b in range(blocks):
            part_cols = slice(b * BLK, (b + 1) * BLK)
            u = (w[:, part_cols] - alpha * block_of(old, probes, b)) * scale
            v = ref[:probes, part_cols]
            high = u.astype(BF16).astype(F32)
            low = u - high
            turned = jnp.concatenate([high, low, v, v], axis=0).T.astype(BF16)
            x = warp(ref[probes : probes + 3, part_cols])
            x1, x2, x3 = split_three(x)
            y = jnp.concatenate([x1, x2, x3, jnp.ones((1, BLK), F32), jnp.zeros((6, BLK), F32)], axis=0).astype(BF16)
            y = jnp.concatenate([y, y], axis=1)
            if part == 0:
                basis_ref[:, part_cols] = u
                form_left[b] = turned
                form_right[b] = jnp.concatenate([v, v, high, low], axis=0).astype(BF16)
                pnts[b] = y
            else:
                halo_left[(part - 1) * blocks + b] = turned
                halo_pnts[(part - 1) * blocks + b] = y
    form_left[blocks] = jnp.zeros((BLK, 4 * probes), BF16)
    form_right[blocks] = jnp.zeros((4 * probes, BLK), BF16)
    pnts[blocks] = jnp.zeros((16, 2 * BLK), BF16)

    def pull(side):
        return lambda slot, a, c: stack_tile(mxu(side[a], form_right[c]) * slopes[slot])

    def pull_made(side, left):
        return lambda slot, a, c: stack_tile(mxu(side[a], form_right[c]) * slope_of(left[a], right[c]))

    fill(pulls, 0, counts[0], rows, cols, pull(form_left))
    fill(pulls, counts[0], counts[1], src, dst, pull(halo_left))
    inner_edges(acc, pnts, rows, cols, counts, keeper(pulls), pull_made(form_left, left_own))
    outer_edges(acc, halo_pnts, src, dst, counts, keeper(pulls), pull_made(halo_left, left_out))
    for b in range(blocks):
        part_cols = slice(b * BLK, (b + 1) * BLK)
        raw = pts[probes : probes + 3, part_cols]
        bent = jnp.tanh(raw)
        x = raw + WARP_GAIN * bent
        sums = acc[b]
        moved = sums[0:3] + sums[3:6] + sums[6:9] - x * sums[9:10]
        chain = 1.0 + WARP_GAIN * (1.0 - bent * bent)
        grad_ref[:, part_cols] = moved * chain * (1.0 / (LENGTH_SQ * all_probes))


def close_kernel(peers, place, own, other, grads, basis_ref, alpha_ref, beta_ref, grad_ref):
    probes = own.shape[0]
    width = basis_ref.shape[1]
    lower = place[1] == 0
    mine = own[...]
    theirs = other[...]
    first = jnp.where(lower, mine, theirs)
    second = jnp.where(lower, theirs, mine)
    basis_ref[:probes] = first[:, :width]
    basis_ref[probes:] = second[:, :width]
    ab = jnp.concatenate([first[:, width:], second[:, width:]], axis=0)
    turned = jnp.concatenate([ab, jnp.zeros((LANES - 2 * probes, LANES), F32)], axis=0).T
    alpha_ref[...] = turned[:ITERS, : 2 * probes]
    beta_ref[...] = turned[ITERS : 2 * ITERS, : 2 * probes]
    total = grads[lax.rem(peers - place[2], peers)]
    for k in range(1, peers):
        total = total + grads[lax.rem(k - place[2] + peers, peers)]
    grad_ref[...] = total


def vmem(count):
    return [pl.BlockSpec(memory_space=pltpu.VMEM)] * count


def smem(count):
    return [pl.BlockSpec(memory_space=pltpu.SMEM)] * count


def held(array):
    return pltpu.with_memory_space_constraint(array, pltpu.VMEM)


def stays(array):
    return pltpu.with_memory_space_constraint(array, pltpu.HBM)


def in_hbm(count):
    return [pl.BlockSpec(memory_space=pltpu.HBM)] * count


def call(name, kernel, outs, ins, scratch, work, aliases=None, limit=LIMIT_MIB):
    out_shapes, out_scalars = outs
    arrays, scalars = ins
    flops, moved = work
    return pl.pallas_call(
        kernel,
        out_shape=tuple(out_shapes),
        in_specs=smem(scalars) + vmem(len(arrays) - scalars),
        out_specs=tuple(smem(out_scalars) + vmem(len(out_shapes) - out_scalars)),
        scratch_shapes=[pltpu.VMEM(shape, dtype) for shape, dtype in scratch],
        compiler_params=pltpu.CompilerParams(vmem_limit_bytes=limit * 1024 * 1024),
        cost_estimate=pl.CostEstimate(flops=flops, bytes_accessed=moved, transcendentals=0),
        input_output_aliases=aliases or {},
        name=name,
    )(*arrays)


def shifted(value, axes, count, steps):
    return lax.ppermute(value, axes, [(source, (source + steps) % count) for source in range(count)])


def body(coords, noise_var, probe_signs, tile_rows, tile_cols, tile_count):
    slabs = lax.axis_size("blk")
    subs = lax.axis_size("sub")
    outer = lax.axis_size("probe")
    probes = probe_signs.shape[0] // subs
    width = coords.shape[1]
    blocks = width // BLK
    cap = tile_rows.shape[-1]
    points = float(width * slabs)
    all_probes = probe_signs.shape[0] * outer
    sub = lax.axis_index("sub")
    blk = lax.axis_index("blk")
    peers = outer * subs
    place = jnp.stack([blk, sub, lax.axis_index("probe") * subs + sub]).astype(jnp.int32)
    sds = jax.ShapeDtypeStruct

    left_shape = sds((blocks + 1, BLK, FEATS), BF16)
    right_shape = sds((blocks + 1, FEATS, BLK), BF16)
    lists, mine, left_own, right = pl.pallas_call(
        functools.partial(pack_kernel, blocks),
        out_shape=(sds((LIST_ROWS, LANES), jnp.int32), sds((probes + OWN_ROWS, width), F32), left_shape, right_shape),
        in_specs=smem(1) + in_hbm(2) + smem(1) + in_hbm(3),
        out_specs=tuple(vmem(4)),
        scratch_shapes=[
            pltpu.VMEM((probes, width), jnp.int32),
            pltpu.VMEM((3, width), F32),
            pltpu.VMEM((1, width), F32),
            pltpu.VMEM((1, cap), jnp.int32),
            pltpu.VMEM((1, cap), jnp.int32),
            pltpu.SemaphoreType.DMA((5,)),
        ],
        compiler_params=pltpu.CompilerParams(vmem_limit_bytes=LIMIT_MIB * 1024 * 1024),
        name="pack",
    )(
        place, stays(tile_rows.reshape(1, cap)), stays(tile_cols.reshape(1, cap)), tile_count.reshape(1),
        stays(probe_signs), stays(coords), stays(noise_var.reshape(1, width)),
    )
    sibling = shifted(lists, "sub", subs, 1)
    above = shifted(mine, "blk", slabs, -1)
    below = shifted(mine, "blk", slabs, 1)
    low = shifted(jnp.concatenate([lists, sibling], axis=0), "blk", slabs, 1)

    own_slots = subs * cap + TAIL
    halo_slots = 2 * subs * cap + TAIL
    slots = KEPT
    ext = width + LANES
    ints = jnp.int32
    blocks_f32 = sds((blocks, probes, BLK), F32)
    tile_shape = pltpu.VMEM((slots, 2 * BLK, BLK), BF16)
    acc_shape = ((blocks + 1, probes, BLK), F32)

    rows, cols, src, dst, counts, tiles, z = call(
        "first_inner",
        functools.partial(first_inner_kernel, blocks),
        (
            (
                sds((own_slots,), ints), sds((own_slots,), ints), sds((own_slots,), ints), sds((own_slots,), ints),
                sds((2,), ints), tile_shape, blocks_f32,
            ),
            5,
        ),
        ((lists, sibling, mine, left_own, right), 2),
        [acc_shape, ((blocks + 1, probes, 2 * BLK), BF16)],
        (WORK_FIRST, WORK_BYTES),
    )
    src, dst, counts, tiles, w, left_halo = call(
        "first_outer",
        functools.partial(first_outer_kernel, blocks),
        (
            (
                sds((halo_slots,), ints), sds((halo_slots,), ints), sds((2,), ints), tile_shape,
                sds((probes, ext), F32), sds((2 * blocks, BLK, FEATS), BF16),
            ),
            3,
        ),
        ((low, src, dst, counts, held(tiles), mine, above, below, z, right), 4),
        [acc_shape, ((2 * blocks, probes, 2 * BLK), BF16)],
        (WORK_FIRST, WORK_BYTES),
        {4: 3},
    )

    q = (mine, above, below)
    ab = []
    for step in range(ITERS - 1):
        every = lax.all_gather(w, "blk", axis=0)
        (z_raw,) = call(
            "inner",
            functools.partial(inner_kernel, blocks),
            ((blocks_f32,), 0),
            ((rows, cols, counts, w, held(tiles), left_own, right), 3),
            [acc_shape, ((blocks + 1, 2 * probes, 2 * BLK), BF16)],
            (WORK_NEXT, WORK_BYTES),
        )
        w, q0, q1, q2, z, next_ab = call(
            "outer",
            functools.partial(outer_kernel, blocks, slabs, points, step),
            (
                (sds((probes, ext), F32), blocks_f32, blocks_f32, blocks_f32, blocks_f32, sds((probes, LANES), F32)),
                0,
            ),
            ((place, src, dst, counts, w, every, *q, z_raw, z, mine, held(tiles), left_halo, right, *ab), 4),
            [acc_shape, ((2 * blocks, 2 * probes, 2 * BLK), BF16)],
            (WORK_NEXT, WORK_BYTES),
        )
        q = (q0, q1, q2)
        ab = [next_ab]

    every = lax.all_gather(w, "blk", axis=0)
    (slopes,) = call(
        "slopes",
        slope_kernel,
        ((pltpu.VMEM((slots, BLK, BLK), F32),), 0),
        ((rows, cols, src, dst, counts, left_own, left_halo, right, w), 5),
        [],
        (WORK_FIRST, WORK_BYTES),
    )
    basis, grad = call(
        "last",
        functools.partial(last_kernel, blocks, slabs, points, all_probes),
        ((sds((probes, ext), F32), sds((3, width), F32)), 0),
        (
            (
                place, rows, cols, src, dst, counts, w, every, *q, mine, above, below, *ab, held(slopes), left_own, left_halo, right,
            ),
            6,
        ),
        [
            ((blocks + 1, 16, BLK), F32),
            ((blocks + 1, BLK, 4 * probes), BF16),
            ((2 * blocks, BLK, 4 * probes), BF16),
            ((blocks + 1, 4 * probes, BLK), BF16),
            ((blocks + 1, 16, 2 * BLK), BF16),
            ((2 * blocks, 16, 2 * BLK), BF16),
            ((slots, 2 * BLK, BLK), BF16),
        ],
        (WORK_FIRST, WORK_BYTES),
        limit=2 * LIMIT_MIB,
    )

    other = shifted(basis, "sub", subs, 1)
    parts = [grad]
    for r in range(1, peers):
        parts.append(shifted(grad, ("probe", "sub"), peers, -r))
    last_basis, alphas, betas, coord_grad = call(
        "close",
        functools.partial(close_kernel, peers),
        (
            (
                sds((subs * probes, width), F32), sds((ITERS, subs * probes), F32), sds((ITERS, subs * probes), F32),
                sds((3, width), F32),
            ),
            0,
        ),
        ((place, basis, other, jnp.stack(parts)), 1),
        [],
        (1000000, 1000000),
    )
    return alphas, betas, last_basis, coord_grad


def solution(mesh):
    return jax.shard_map(
        body,
        mesh=mesh,
        in_specs=(
            P(None, ("groups", "blk")),
            P(("groups", "blk")),
            P("probe", ("groups", "blk")),
            P(("groups", "blk"), "sub", None),
            P(("groups", "blk"), "sub", None),
            P(("groups", "blk"), "sub"),
        ),
        out_specs=(
            P(None, ("groups", "probe")),
            P(None, ("groups", "probe")),
            P("probe", ("groups", "blk")),
            P(None, ("groups", "blk")),
        ),
        check_vma=False,
    )
```

```python
import functools
import math

import jax
import jax.numpy as jnp
from jax import lax
from jax.experimental import pallas as pl
from jax.experimental.pallas import tpu as pltpu
from jax.sharding import PartitionSpec as P

ITERS = 3
SIGNAL_VAR = 0.1
LENGTH_SQ = 2.0
TAPER_SQ = 16.0
WARP_GAIN = 0.4
EPSILON = 1e-06

BLK = 128
LANES = 128
FEATS = 32
GROUP = 16
TAIL = 4
LIST_ROWS = 8
OWN_ROWS = 4
LIMIT_MIB = 16
KEPT = 256
WORK_FIRST = 300000000
WORK_NEXT = 100000000
WORK_BYTES = 4000000

S_OF_D = -math.log2(math.e) / (2.0 * LENGTH_SQ)
D_OF_S = 1.0 / S_OF_D
ROOT_VAR = math.sqrt(SIGNAL_VAR)
TAPER_STEP = 4.0 * LENGTH_SQ / TAPER_SQ * ROOT_VAR
T_SLOPE = -ROOT_VAR * D_OF_S / TAPER_SQ

F32 = jnp.float32
BF16 = jnp.bfloat16


def split_two(x):
    high = x.astype(BF16)
    low = (x - high.astype(F32)).astype(BF16)
    return high, low


def split_three(x):
    one = x.astype(BF16).astype(F32)
    rest = x - one
    two = rest.astype(BF16).astype(F32)
    three = (rest - two).astype(BF16).astype(F32)
    return one, two, three


def warp(x):
    return x + WARP_GAIN * jnp.tanh(x)


def mxu(a, b):
    return lax.dot_general(a, b, (((1,), (0,)), ((), ())), preferred_element_type=F32)


def features(x):
    scale = -2.0 * S_OF_D
    y = x * scale
    norm = S_OF_D * jnp.sum(x * x, axis=0, keepdims=True)
    x1, x2, x3 = split_three(x)
    y1, y2, y3 = split_three(y)
    n1, n2, n3 = split_three(norm)
    one = jnp.ones_like(norm)
    pad = jnp.zeros((FEATS - 24, x.shape[1]), F32)
    left = jnp.concatenate([x1, x1, x2, x2, x1, x3, n1, n2, n3, one, one, one, pad], axis=0)
    right = jnp.concatenate([y1, y2, y1, y2, y3, y1, one, one, one, n1, n2, n3, pad], axis=0)
    return left, right


def tile_terms(left, right):
    s = mxu(left, right)
    e = jnp.exp2(s)
    t = jnp.maximum(T_SLOPE * s + ROOT_VAR, 0.0)
    return e, t


def put_stats(ref, base, w_of, q_of, qq, qw, blocks):
    alpha_s = qw / jnp.maximum(qq, 1e-30)
    acc = jnp.zeros((qq.shape[0], LANES), F32)
    for b in range(blocks):
        r = w_of(b) - alpha_s * q_of(b)
        acc = acc + r * r
    res = jnp.sum(acc, axis=1, keepdims=True)
    lane = lax.broadcasted_iota(jnp.int32, (qq.shape[0], LANES), 1)
    out = jnp.where(lane == 0, qw, jnp.where(lane == 1, qq, jnp.where(lane == 2, res, 0.0)))
    ref[:, base : base + LANES] = out


def mxu_turned(a, b):
    return lax.dot_general(a, b, (((1,), (1,)), ((), ())), preferred_element_type=F32)


def fold(out, probes):
    if out.shape[0] > probes:
        return out[:probes] + out[probes:]
    return out


def fold_turned(out, probes):
    total = out[:probes, :BLK] + out[:probes, BLK:]
    if out.shape[0] > probes:
        total = total + out[probes:, :BLK]
    return total


def stack_vec(q, exact):
    if exact:
        high = q.astype(BF16)
        return jnp.concatenate([high, high], axis=1)
    high, low = split_two(q)
    return jnp.concatenate(
        [jnp.concatenate([high, high], axis=1), jnp.concatenate([low, jnp.zeros_like(low)], axis=1)], axis=0
    )


def stack_tile(tile):
    return jnp.concatenate(split_two(tile), axis=0)


def ranges(first, last, body):
    long = (last - first) // GROUP
    middle = first + long * GROUP

    def big(g, carry):
        body(first + g * GROUP, GROUP)
        return carry

    def small(g, carry):
        body(middle + g * TAIL, TAIL)
        return carry

    lax.fori_loop(0, long, big, 0)
    lax.fori_loop(0, (last - middle) // TAIL, small, 0)


def kept_and_made(total, room, body, kept, made):
    first = jnp.minimum(total, room)
    ranges(0, first, functools.partial(body, kept))
    many = (total - first) // TAIL

    def rest(g, carry):
        body(made, first + g * TAIL, TAIL)
        return carry

    lax.fori_loop(0, many, rest, 0)


def inner_edges(acc, vecs, plan, kept, made):
    acc[...] = jnp.zeros_like(acc)
    size = acc.shape[1]

    def group(tile_of, start, many):
        outs = []
        for u in range(many):
            slot = start + u
            a = plan[0, slot]
            c = plan[1, slot]
            times = plan[2, slot].astype(F32)
            tile = tile_of(slot, a, c)
            outs.append((c, fold(mxu(vecs[a], tile), size) * times))
            outs.append((a, fold_turned(mxu_turned(vecs[c][:, :BLK], tile), size) * times))
        for c, out in outs:
            acc[c] = acc[c] + out

    kept_and_made(plan[3, 0], KEPT, group, kept, made)


def outer_edges(acc, vecs, plan, base, kept, made):
    size = acc.shape[1]

    def group(tile_of, start, many):
        outs = []
        for u in range(many):
            at = start + u
            a = plan[0, at]
            c = plan[1, at]
            times = plan[2, at].astype(F32)
            outs.append((c, fold(mxu(vecs[a], tile_of(base + at, a, c)), size) * times))
        for c, out in outs:
            acc[c] = acc[c] + out

    kept_and_made(plan[3, 0], jnp.maximum(KEPT - base, 0), group, kept, made)


def maker(left, right):
    def make(slot, a, c):
        e, t = tile_terms(left[a], right[c])
        return stack_tile(e * t * t)

    return make


def fill(into, base, plan, make):
    def body(start, many):
        for u in range(many):
            at = start + u
            into[base + at] = make(base + at, plan[0, at], plan[1, at])

    ranges(0, jnp.minimum(plan[3, 0], jnp.maximum(KEPT - base, 0)), body)


def keeper(tiles):
    return lambda slot, a, c: tiles[slot]


def whole(n):
    return jnp.floor((n + (TAIL - 1)) * (1.0 / TAIL)) * TAIL


def keys(lists, blocks, cross):
    out = []
    for lst in lists:
        a = lst[0:1, :]
        c = lst[1:2, :]
        live = lax.broadcasted_iota(jnp.int32, a.shape, 1) < lst[2:3, :]
        if cross:
            out.append(jnp.where(live & (c >= blocks), a * blocks + c - blocks, -1))
        else:
            out.append(jnp.where(live & (c < blocks), a * blocks + c, -1))
    return jnp.concatenate(out, axis=1)


def compact(key, blocks, slots, first):
    size = blocks * blocks
    hot = jnp.where(lax.broadcasted_iota(jnp.int32, (size, key.shape[1]), 0) == key, 1.0, 0.0).astype(BF16)
    counts = mxu(hot, jnp.ones((key.shape[1], LANES), BF16))
    flags = jnp.minimum(counts, 1.0)
    shape = (size, size)
    ahead = lax.broadcasted_iota(jnp.int32, shape, 0) > lax.broadcasted_iota(jnp.int32, shape, 1)
    place = mxu(jnp.where(ahead, 1.0, 0.0).astype(BF16), flags.astype(BF16)) + first
    index = lax.broadcasted_iota(jnp.int32, (16, size), 1).astype(F32)
    row = jnp.floor((index + 0.5) * (1.0 / blocks))
    line = lax.broadcasted_iota(jnp.int32, (16, size), 0)
    names = jnp.where(line == 0, row, jnp.where(line == 1, index - row * blocks, 1.0)).astype(BF16)
    found = []
    times = []
    for part in range(slots // LANES):
        lane = (lax.broadcasted_iota(jnp.int32, (size, LANES), 1) + part * LANES).astype(F32)
        here = (place == lane) & (flags > 0.5)
        found.append(mxu(names, jnp.where(here, 1.0, 0.0).astype(BF16)))
        times.append(mxu(names, jnp.where(here, counts, 0.0).astype(BF16))[2:3])
    found = jnp.concatenate(found, axis=1)
    end = place[size - 1 :] + flags[size - 1 :]
    return found[0:1], found[1:2], found[2:3], jnp.concatenate(times, axis=1), end


def put_plan(ref, rows):
    ref[...] = jnp.zeros(ref.shape, ref.dtype)
    for at, row in enumerate(rows):
        ref[at : at + 1, :] = row.astype(ref.dtype)


def spread(row, width):
    return jnp.concatenate([row] * (width // LANES), axis=1)


def side_features(blocks, coords_of, left, right):
    for g in range(0, blocks, 4):
        stack = []
        for b in range(g, g + 4):
            lf, rt = features(warp(coords_of(slice(b * BLK, (b + 1) * BLK))))
            stack.append(lf)
            if right is not None:
                right[b] = rt.astype(BF16)
        turned = jnp.concatenate(stack, axis=0).T.astype(BF16)
        for b in range(4):
            left[g + b] = turned[:, b * FEATS : (b + 1) * FEATS]


def pack_kernel(
    blocks, place, tile_rows, tile_cols, tile_count, signs, coords, noise,
    lists, mine, left, right, got_signs, got_coords, got_noise, got_rows, got_cols, sems,
):
    probes = mine.shape[0] - OWN_ROWS
    first = pl.multiple_of(place[1] * probes, probes)
    moves = [
        pltpu.make_async_copy(coords, got_coords, sems.at[0]),
        pltpu.make_async_copy(signs.at[pl.ds(first, probes), :], got_signs, sems.at[1]),
        pltpu.make_async_copy(noise, got_noise, sems.at[2]),
        pltpu.make_async_copy(tile_rows, got_rows, sems.at[3]),
        pltpu.make_async_copy(tile_cols, got_cols, sems.at[4]),
    ]
    for move in moves:
        move.start()
    lists[...] = jnp.zeros(lists.shape, jnp.int32)
    lists[2:3, :] = jnp.full((1, LANES), tile_count[0], jnp.int32)
    moves[0].wait()
    mine[probes : probes + 3] = got_coords[...]
    side_features(blocks, lambda cols: got_coords[:, cols], left, right)
    left[blocks] = jnp.zeros((BLK, FEATS), BF16)
    right[blocks] = jnp.zeros((FEATS, BLK), BF16)
    for move in moves[1:]:
        move.wait()
    mine[:probes] = got_signs[...].astype(F32)
    mine[probes + 3 : probes + OWN_ROWS] = got_noise[...]
    lists[0:1, : tile_rows.shape[1]] = got_rows[...]
    lists[1:2, : tile_cols.shape[1]] = got_cols[...]


def first_inner_kernel(
    blocks, own0, own1, mine, left, right,
    plan, tiles, z_ref, cross, acc, vecs, held_plan, sem,
):
    probes = mine.shape[0] - OWN_ROWS
    lists = (own0, own1)
    row, col, _, times, end = compact(keys(lists, blocks, False), blocks, held_plan.shape[1], 0.0)
    put_plan(held_plan, (row, col, times, spread(whole(end), held_plan.shape[1])))
    move = pltpu.make_async_copy(held_plan, plan, sem)
    move.start()
    row, col, _, times, end = compact(keys(lists, blocks, True), blocks, cross.shape[1], 0.0)
    put_plan(cross, (col, row, times, spread(end, cross.shape[1])))
    for b in range(blocks):
        vecs[b] = stack_vec(mine[:probes, b * BLK : (b + 1) * BLK], True)
    move.wait()
    make = maker(left, right)
    fill(tiles, 0, plan, make)
    inner_edges(acc, vecs, plan, keeper(tiles), make)
    z_ref[...] = acc[:blocks]


def finish_apply(blocks, acc, z_of, w_ref, q_of, prev_of, beta, pts):
    probes = acc.shape[1]
    qq = jnp.zeros((probes, LANES), F32)
    qw = jnp.zeros((probes, LANES), F32)
    for b in range(blocks):
        q = q_of(b)
        part = slice(b * BLK, (b + 1) * BLK)
        w = acc[b] + z_of(b) + pts[probes + 3 : probes + OWN_ROWS, part] * q
        if prev_of is not None:
            w = w - beta * prev_of(b)
        w_ref[:, part] = w
        qq = qq + q * q
        qw = qw + q * w
    put_stats(
        w_ref,
        blocks * BLK,
        lambda b: w_ref[:, b * BLK : (b + 1) * BLK],
        q_of,
        jnp.sum(qq, axis=1, keepdims=True),
        jnp.sum(qw, axis=1, keepdims=True),
        blocks,
    )


def first_outer_kernel(
    blocks, inner_plan, low, old_tiles, mine, above, below, z_ref, right, cross,
    plan, tiles, w_ref, left, acc, vecs, held_plan, sem,
):
    probes = mine.shape[0] - OWN_ROWS
    del old_tiles
    slots = held_plan.shape[1]
    row, col, one, times, end = compact(keys((low[:LIST_ROWS], low[LIST_ROWS:]), blocks, True), blocks, slots, cross[3:4, :LANES])
    put_plan(
        held_plan,
        (cross[0:1] + row + blocks * one, cross[1:2] + col, cross[2:3] + times, spread(whole(end), slots)),
    )
    move = pltpu.make_async_copy(held_plan, plan, sem)
    move.start()
    for part, ref in enumerate((above, below)):
        side_features(
            blocks,
            lambda cols, ref=ref: ref[probes : probes + 3, cols],
            left.at[part * blocks : (part + 1) * blocks],
            None,
        )
        for b in range(blocks):
            vecs[part * blocks + b] = stack_vec(ref[:probes, b * BLK : (b + 1) * BLK], True)
    acc[...] = jnp.zeros_like(acc)
    move.wait()
    make = maker(left, right)
    base = inner_plan[3, 0]
    fill(tiles, base, plan, make)
    outer_edges(acc, vecs, plan, base, keeper(tiles), make)
    finish_apply(
        blocks, acc, lambda b: z_ref[b], w_ref, lambda b: mine[:probes, b * BLK : (b + 1) * BLK], None, None, mine
    )


def inner_kernel(blocks, plan, w_ref, tiles, left, right, z_ref, acc, vecs):
    for b in range(blocks):
        vecs[b] = stack_vec(w_ref[:, b * BLK : (b + 1) * BLK], False)
    inner_edges(acc, vecs, plan, keeper(tiles), maker(left, right))
    z_ref[...] = acc[:blocks]


def alpha_beta(stats, points):
    qw = [s[:, 0:1] for s in stats]
    qq = [s[:, 1:2] for s in stats]
    res = [s[:, 2:3] for s in stats]
    alpha = functools.reduce(jnp.add, qw) / points
    total = jnp.zeros_like(alpha)
    for w, q, r in zip(qw, qq, res):
        gap = alpha - w / jnp.maximum(q, 1e-30)
        total = total + (r + gap * gap * q)
    return alpha, jnp.sqrt(total / points + EPSILON)


def global_alpha_beta(slabs, points, place, stats_ref):
    order = [stats_ref[lax.rem(slab - place[0] + slabs, slabs)] for slab in range(slabs)]
    return alpha_beta(order, points)


def add_ab(ref, base, old_ab, step, alpha, beta):
    shape = (alpha.shape[0], LANES)
    lane = lax.broadcasted_iota(jnp.int32, shape, 1)
    out = jnp.zeros(shape, F32) if old_ab is None else old_ab[...]
    out = jnp.where(lane == step, alpha, out)
    ref[:, base : base + LANES] = jnp.where(lane == ITERS + step, beta, out)


def block_of(ref, rows, b):
    if len(ref.shape) == 3:
        return ref[b]
    return ref[:rows, b * BLK : (b + 1) * BLK]


def outer_kernel(
    blocks, slabs, points, step, place, inner_plan, plan, mine, above, below, stats_ref,
    q_own, q_above, q_below, z_raw, z_old, pts, tiles, left, right, *rest,
):
    probes = mine.shape[0]
    old_ab = None
    if step > 0:
        old_ab = rest[0]
        rest = rest[1:]
    w_ref, own_ref, above_ref, below_ref, z_ref, ab_ref, acc, vecs = rest
    alpha, beta = global_alpha_beta(slabs, points, place, stats_ref)
    scale = 1.0 / beta
    add_ab(ab_ref, 0, old_ab, step, alpha, beta)
    halves = ((mine, q_own, own_ref), (above, q_above, above_ref), (below, q_below, below_ref))
    for part, (w, old, new) in enumerate(halves):
        for b in range(blocks):
            q = (w[:, b * BLK : (b + 1) * BLK] - alpha * block_of(old, probes, b)) * scale
            new[b] = q
            if part > 0:
                vecs[(part - 1) * blocks + b] = stack_vec(q, False)
            else:
                z_ref[b] = (z_raw[b] - alpha * z_old[b]) * scale
    acc[...] = jnp.zeros_like(acc)
    outer_edges(acc, vecs, plan, inner_plan[3, 0], keeper(tiles), maker(left, right))
    finish_apply(
        blocks, acc, lambda b: z_ref[b], w_ref, lambda b: own_ref[b], lambda b: block_of(q_own, probes, b), beta, pts
    )


def slope_of(left, right):
    e, t = tile_terms(left, right)
    return (e * t) * (t + TAPER_STEP)


def slope_kernel(inner_plan, plan, left_own, left_halo, right, after, slopes):
    del after
    fill(slopes, 0, inner_plan, lambda slot, a, c: slope_of(left_own[a], right[c]))
    fill(slopes, inner_plan[3, 0], plan, lambda slot, a, c: slope_of(left_halo[a], right[c]))


def last_kernel(
    blocks, slabs, points, all_probes, place, inner_plan, plan, mine, above, below, stats_ref,
    q_own, q_above, q_below, pts, pts_above, pts_below, old_ab, slopes, left_own, left_out, right,
    basis_ref, grad_ref, acc, form_left, halo_left, form_right, pnts, halo_pnts, pulls,
):
    probes = pts.shape[0] - OWN_ROWS
    alpha, beta = global_alpha_beta(slabs, points, place, stats_ref)
    scale = 1.0 / beta
    add_ab(basis_ref, blocks * BLK, old_ab, ITERS - 1, alpha, beta)
    for part, (w, old, ref) in enumerate(((mine, q_own, pts), (above, q_above, pts_above), (below, q_below, pts_below))):
        for b in range(blocks):
            part_cols = slice(b * BLK, (b + 1) * BLK)
            u = (w[:, part_cols] - alpha * block_of(old, probes, b)) * scale
            v = ref[:probes, part_cols]
            high = u.astype(BF16).astype(F32)
            low = u - high
            turned = jnp.concatenate([high, low, v, v], axis=0).T.astype(BF16)
            x = warp(ref[probes : probes + 3, part_cols])
            x1, x2, x3 = split_three(x)
            y = jnp.concatenate([x1, x2, x3, jnp.ones((1, BLK), F32), jnp.zeros((6, BLK), F32)], axis=0).astype(BF16)
            y = jnp.concatenate([y, y], axis=1)
            if part == 0:
                basis_ref[:, part_cols] = u
                form_left[b] = turned
                form_right[b] = jnp.concatenate([v, v, high, low], axis=0).astype(BF16)
                pnts[b] = y
            else:
                halo_left[(part - 1) * blocks + b] = turned
                halo_pnts[(part - 1) * blocks + b] = y
    form_left[blocks] = jnp.zeros((BLK, 4 * probes), BF16)
    form_right[blocks] = jnp.zeros((4 * probes, BLK), BF16)
    pnts[blocks] = jnp.zeros((16, 2 * BLK), BF16)

    def pull(side):
        return lambda slot, a, c: stack_tile(mxu(side[a], form_right[c]) * slopes[slot])

    def pull_made(side, left):
        return lambda slot, a, c: stack_tile(mxu(side[a], form_right[c]) * slope_of(left[a], right[c]))

    base = inner_plan[3, 0]
    fill(pulls, 0, inner_plan, pull(form_left))
    fill(pulls, base, plan, pull(halo_left))
    inner_edges(acc, pnts, inner_plan, keeper(pulls), pull_made(form_left, left_own))
    outer_edges(acc, halo_pnts, plan, base, keeper(pulls), pull_made(halo_left, left_out))
    for b in range(blocks):
        part_cols = slice(b * BLK, (b + 1) * BLK)
        raw = pts[probes : probes + 3, part_cols]
        bent = jnp.tanh(raw)
        x = raw + WARP_GAIN * bent
        sums = acc[b]
        moved = sums[0:3] + sums[3:6] + sums[6:9] - x * sums[9:10]
        chain = 1.0 + WARP_GAIN * (1.0 - bent * bent)
        grad_ref[:, part_cols] = moved * chain * (1.0 / (LENGTH_SQ * all_probes))


def close_kernel(peers, place, own, other, grads, basis_ref, alpha_ref, beta_ref, grad_ref):
    probes = own.shape[0]
    width = basis_ref.shape[1]
    lower = place[1] == 0
    mine = own[...]
    theirs = other[...]
    first = jnp.where(lower, mine, theirs)
    second = jnp.where(lower, theirs, mine)
    basis_ref[:probes] = first[:, :width]
    basis_ref[probes:] = second[:, :width]
    ab = jnp.concatenate([first[:, width:], second[:, width:]], axis=0)
    turned = jnp.concatenate([ab, jnp.zeros((LANES - 2 * probes, LANES), F32)], axis=0).T
    alpha_ref[...] = turned[:ITERS, : 2 * probes]
    beta_ref[...] = turned[ITERS : 2 * ITERS, : 2 * probes]
    total = grads[lax.rem(peers - place[2], peers)]
    for k in range(1, peers):
        total = total + grads[lax.rem(k - place[2] + peers, peers)]
    grad_ref[...] = total


def vmem(count):
    return [pl.BlockSpec(memory_space=pltpu.VMEM)] * count


def smem(count):
    return [pl.BlockSpec(memory_space=pltpu.SMEM)] * count


def held(array):
    return pltpu.with_memory_space_constraint(array, pltpu.VMEM)


def stays(array):
    return pltpu.with_memory_space_constraint(array, pltpu.HBM)


def in_hbm(count):
    return [pl.BlockSpec(memory_space=pltpu.HBM)] * count


def call(name, kernel, outs, ins, scratch, work, aliases=None, limit=LIMIT_MIB):
    out_shapes, out_scalars = outs
    arrays, scalars = ins
    flops, moved = work
    return pl.pallas_call(
        kernel,
        out_shape=tuple(out_shapes),
        in_specs=smem(scalars) + vmem(len(arrays) - scalars),
        out_specs=tuple(smem(out_scalars) + vmem(len(out_shapes) - out_scalars)),
        scratch_shapes=[pltpu.VMEM(*entry) if isinstance(entry, tuple) else entry for entry in scratch],
        compiler_params=pltpu.CompilerParams(vmem_limit_bytes=limit * 1024 * 1024),
        cost_estimate=pl.CostEstimate(flops=flops, bytes_accessed=moved, transcendentals=0),
        input_output_aliases=aliases or {},
        name=name,
    )(*arrays)


def shifted(value, axes, count, steps):
    return lax.ppermute(value, axes, [(source, (source + steps) % count) for source in range(count)])


def body(coords, noise_var, probe_signs, tile_rows, tile_cols, tile_count):
    slabs = lax.axis_size("blk")
    subs = lax.axis_size("sub")
    outer = lax.axis_size("probe")
    probes = probe_signs.shape[0] // subs
    width = coords.shape[1]
    blocks = width // BLK
    cap = tile_rows.shape[-1]
    points = float(width * slabs)
    all_probes = probe_signs.shape[0] * outer
    sub = lax.axis_index("sub")
    blk = lax.axis_index("blk")
    peers = outer * subs
    place = jnp.stack([blk, sub, lax.axis_index("probe") * subs + sub]).astype(jnp.int32)
    sds = jax.ShapeDtypeStruct

    left_shape = sds((blocks + 1, BLK, FEATS), BF16)
    right_shape = sds((blocks + 1, FEATS, BLK), BF16)
    lists, mine, left_own, right = pl.pallas_call(
        functools.partial(pack_kernel, blocks),
        out_shape=(sds((LIST_ROWS, LANES), jnp.int32), sds((probes + OWN_ROWS, width), F32), left_shape, right_shape),
        in_specs=smem(1) + in_hbm(2) + smem(1) + in_hbm(3),
        out_specs=tuple(vmem(4)),
        scratch_shapes=[
            pltpu.VMEM((probes, width), jnp.int32),
            pltpu.VMEM((3, width), F32),
            pltpu.VMEM((1, width), F32),
            pltpu.VMEM((1, cap), jnp.int32),
            pltpu.VMEM((1, cap), jnp.int32),
            pltpu.SemaphoreType.DMA((5,)),
        ],
        compiler_params=pltpu.CompilerParams(vmem_limit_bytes=LIMIT_MIB * 1024 * 1024),
        name="pack",
    )(
        place, stays(tile_rows.reshape(1, cap)), stays(tile_cols.reshape(1, cap)), tile_count.reshape(1),
        stays(probe_signs), stays(coords), stays(noise_var.reshape(1, width)),
    )
    sibling = shifted(lists, "sub", subs, 1)
    above = shifted(mine, "blk", slabs, -1)
    below = shifted(mine, "blk", slabs, 1)
    low = shifted(jnp.concatenate([lists, sibling], axis=0), "blk", slabs, 1)

    ints = jnp.int32
    inner_slots = (blocks * (blocks + 1) // 2 + TAIL + LANES - 1) // LANES * LANES
    outer_slots = (blocks * (blocks + 1) + TAIL + LANES - 1) // LANES * LANES
    plan_shape = sds((LIST_ROWS, inner_slots), ints)
    outer_plan_shape = sds((LIST_ROWS, outer_slots), ints)
    slots = KEPT
    ext = width + LANES
    blocks_f32 = sds((blocks, probes, BLK), F32)
    tile_shape = pltpu.VMEM((slots, 2 * BLK, BLK), BF16)
    acc_shape = ((blocks + 1, probes, BLK), F32)

    inner_plan, tiles, z, cross = call(
        "first_inner",
        functools.partial(first_inner_kernel, blocks),
        ((plan_shape, tile_shape, blocks_f32, sds((LIST_ROWS, outer_slots), F32)), 1),
        ((lists, sibling, mine, left_own, right), 0),
        [
            acc_shape, ((blocks + 1, probes, 2 * BLK), BF16), ((LIST_ROWS, inner_slots), ints),
            pltpu.SemaphoreType.DMA,
        ],
        (WORK_FIRST, WORK_BYTES),
    )
    outer_plan, tiles, w, left_halo = call(
        "first_outer",
        functools.partial(first_outer_kernel, blocks),
        ((outer_plan_shape, tile_shape, sds((probes, ext), F32), sds((2 * blocks, BLK, FEATS), BF16)), 1),
        ((inner_plan, low, held(tiles), mine, above, below, z, right, cross), 1),
        [
            acc_shape, ((2 * blocks, probes, 2 * BLK), BF16), ((LIST_ROWS, outer_slots), ints),
            pltpu.SemaphoreType.DMA,
        ],
        (WORK_FIRST, WORK_BYTES),
        {2: 1},
    )

    def exchange(w):
        up = shifted(w, "blk", slabs, -1)
        down = shifted(w, "blk", slabs, 1)
        stats = w[:, width:]
        if slabs == 4:
            far = shifted(stats, "blk", slabs, 2)
            rows = jnp.stack([stats, up[:, width:], far, down[:, width:]])
        else:
            rows = lax.all_gather(stats, "blk", axis=0)
            rows = jnp.roll(rows, -blk, axis=0)
        return up, down, rows

    q = (mine, above, below)
    ab = []
    for step in range(ITERS - 1):
        up, down, stats = exchange(w)
        (z_raw,) = call(
            "inner",
            functools.partial(inner_kernel, blocks),
            ((blocks_f32,), 0),
            ((inner_plan, w, held(tiles), left_own, right), 1),
            [acc_shape, ((blocks + 1, 2 * probes, 2 * BLK), BF16)],
            (WORK_NEXT, WORK_BYTES),
        )
        w, q0, q1, q2, z, next_ab = call(
            "outer",
            functools.partial(outer_kernel, blocks, slabs, points, step),
            (
                (sds((probes, ext), F32), blocks_f32, blocks_f32, blocks_f32, blocks_f32, sds((probes, LANES), F32)),
                0,
            ),
            ((place, inner_plan, outer_plan, w, up, down, stats, *q, z_raw, z, mine, held(tiles), left_halo, right, *ab), 3),
            [acc_shape, ((2 * blocks, 2 * probes, 2 * BLK), BF16)],
            (WORK_NEXT, WORK_BYTES),
        )
        q = (q0, q1, q2)
        ab = [next_ab]

    up, down, stats = exchange(w)
    (slopes,) = call(
        "slopes",
        slope_kernel,
        ((pltpu.VMEM((slots, BLK, BLK), F32),), 0),
        ((inner_plan, outer_plan, left_own, left_halo, right, w), 2),
        [],
        (WORK_FIRST, WORK_BYTES),
    )
    basis, grad = call(
        "last",
        functools.partial(last_kernel, blocks, slabs, points, all_probes),
        ((sds((probes, ext), F32), sds((3, width), F32)), 0),
        (
            (
                place, inner_plan, outer_plan, w, up, down, stats, *q, mine, above, below, *ab, held(slopes), left_own, left_halo, right,
            ),
            3,
        ),
        [
            ((blocks + 1, 16, BLK), F32),
            ((blocks + 1, BLK, 4 * probes), BF16),
            ((2 * blocks, BLK, 4 * probes), BF16),
            ((blocks + 1, 4 * probes, BLK), BF16),
            ((blocks + 1, 16, 2 * BLK), BF16),
            ((2 * blocks, 16, 2 * BLK), BF16),
            ((slots, 2 * BLK, BLK), BF16),
        ],
        (WORK_FIRST, WORK_BYTES),
        limit=2 * LIMIT_MIB,
    )

    other = shifted(basis, "sub", subs, 1)
    parts = [grad]
    for r in range(1, peers):
        parts.append(shifted(grad, ("probe", "sub"), peers, -r))
    last_basis, alphas, betas, coord_grad = call(
        "close",
        functools.partial(close_kernel, peers),
        (
            (
                sds((subs * probes, width), F32), sds((ITERS, subs * probes), F32), sds((ITERS, subs * probes), F32),
                sds((3, width), F32),
            ),
            0,
        ),
        ((place, basis, other, jnp.stack(parts)), 1),
        [],
        (1000000, 1000000),
    )
    return alphas, betas, last_basis, coord_grad


def solution(mesh):
    return jax.shard_map(
        body,
        mesh=mesh,
        in_specs=(
            P(None, ("groups", "blk")),
            P(("groups", "blk")),
            P("probe", ("groups", "blk")),
            P(("groups", "blk"), "sub", None),
            P(("groups", "blk"), "sub", None),
            P(("groups", "blk"), "sub"),
        ),
        out_specs=(
            P(None, ("groups", "probe")),
            P(None, ("groups", "probe")),
            P("probe", ("groups", "blk")),
            P(None, ("groups", "blk")),
        ),
        check_vma=False,
    )
```

```python
import functools
import math

import jax
import jax.numpy as jnp
from jax import lax
from jax.experimental import pallas as pl
from jax.experimental.pallas import tpu as pltpu
from jax.sharding import PartitionSpec as P

ITERS = 3
SIGNAL_VAR = 0.1
LENGTH_SQ = 2.0
TAPER_SQ = 16.0
WARP_GAIN = 0.4
EPSILON = 1e-06

BLK = 128
LANES = 128
FEATS = 32
GROUP = 16
TAIL = 4
LIST_ROWS = 8
LIMIT_MIB = 16
KEPT = 256
WORK_FIRST = 300000000
WORK_NEXT = 100000000
WORK_BYTES = 4000000

S_OF_D = -math.log2(math.e) / (2.0 * LENGTH_SQ)
D_OF_S = 1.0 / S_OF_D
ROOT_VAR = math.sqrt(SIGNAL_VAR)
TAPER_STEP = 4.0 * LENGTH_SQ / TAPER_SQ * ROOT_VAR
T_SLOPE = -ROOT_VAR * D_OF_S / TAPER_SQ

F32 = jnp.float32
BF16 = jnp.bfloat16


def split_two(x):
    high = x.astype(BF16)
    low = (x - high.astype(F32)).astype(BF16)
    return high, low


def split_three(x):
    one = x.astype(BF16).astype(F32)
    rest = x - one
    two = rest.astype(BF16).astype(F32)
    three = (rest - two).astype(BF16).astype(F32)
    return one, two, three


def warp(x):
    return x + WARP_GAIN * jnp.tanh(x)


def mxu(a, b):
    return lax.dot_general(a, b, (((1,), (0,)), ((), ())), preferred_element_type=F32)


def tile_terms(left, right):
    s = mxu(left, right)
    e = jnp.exp2(s)
    t = jnp.maximum(T_SLOPE * s + ROOT_VAR, 0.0)
    return e, t


def put_stats(ref, base, w_of, q_of, qq, qw, blocks):
    alpha_s = qw / jnp.maximum(qq, 1e-30)
    acc = jnp.zeros((qq.shape[0], LANES), F32)
    for b in range(blocks):
        r = w_of(b) - alpha_s * q_of(b)
        acc = acc + r * r
    res = jnp.sum(acc, axis=1, keepdims=True)
    lane = lax.broadcasted_iota(jnp.int32, (qq.shape[0], LANES), 1)
    out = jnp.where(lane == 0, qw, jnp.where(lane == 1, qq, jnp.where(lane == 2, res, 0.0)))
    ref[:, base : base + LANES] = out


def mxu_turned(a, b):
    return lax.dot_general(a, b, (((1,), (1,)), ((), ())), preferred_element_type=F32)


def fold(out, probes):
    if out.shape[0] > probes:
        return out[:probes] + out[probes:]
    return out


def fold_turned(out, probes):
    total = out[:probes, :BLK] + out[:probes, BLK:]
    if out.shape[0] > probes:
        total = total + out[probes:, :BLK]
    return total


def stack_vec(q, exact):
    if exact:
        high = q.astype(BF16)
        return jnp.concatenate([high, high], axis=1)
    high, low = split_two(q)
    return jnp.concatenate(
        [jnp.concatenate([high, high], axis=1), jnp.concatenate([low, jnp.zeros_like(low)], axis=1)], axis=0
    )


def stack_tile(tile):
    return jnp.concatenate(split_two(tile), axis=0)


def ranges(first, last, body):
    long = (last - first) // GROUP
    middle = first + long * GROUP

    def big(g, carry):
        body(first + g * GROUP, GROUP)
        return carry

    def small(g, carry):
        body(middle + g * TAIL, TAIL)
        return carry

    lax.fori_loop(0, long, big, 0)
    lax.fori_loop(0, (last - middle) // TAIL, small, 0)


def kept_and_made(total, room, body, kept, made):
    first = jnp.minimum(total, room)
    ranges(0, first, functools.partial(body, kept))
    many = (total - first) // TAIL

    def rest(g, carry):
        body(made, first + g * TAIL, TAIL)
        return carry

    lax.fori_loop(0, many, rest, 0)


def inner_edges(acc, vecs, plan, kept, made):
    acc[...] = jnp.zeros_like(acc)
    size = acc.shape[1]

    def group(tile_of, start, many):
        outs = []
        for u in range(many):
            slot = start + u
            a = plan[0, slot]
            c = plan[1, slot]
            times = plan[2, slot].astype(F32)
            tile = tile_of(slot, a, c)
            outs.append((c, fold(mxu(vecs[a], tile), size) * times))
            outs.append((a, fold_turned(mxu_turned(vecs[c][:, :BLK], tile), size) * times))
        for c, out in outs:
            acc[c] = acc[c] + out

    kept_and_made(plan[3, 0], KEPT, group, kept, made)


def outer_edges(acc, vecs, plan, base, kept, made):
    size = acc.shape[1]

    def group(tile_of, start, many):
        outs = []
        for u in range(many):
            at = start + u
            a = plan[0, at]
            c = plan[1, at]
            times = plan[2, at].astype(F32)
            outs.append((c, fold(mxu(vecs[a], tile_of(base + at, a, c)), size) * times))
        for c, out in outs:
            acc[c] = acc[c] + out

    kept_and_made(plan[3, 0], jnp.maximum(KEPT - base, 0), group, kept, made)


def maker(left, right):
    def make(slot, a, c):
        e, t = tile_terms(left[a], right[c])
        return stack_tile(e * t * t)

    return make


def fill(into, base, plan, make):
    def body(start, many):
        for u in range(many):
            at = start + u
            into[base + at] = make(base + at, plan[0, at], plan[1, at])

    ranges(0, jnp.minimum(plan[3, 0], jnp.maximum(KEPT - base, 0)), body)


def keeper(tiles):
    return lambda slot, a, c: tiles[slot]


def whole(n):
    return jnp.floor((n + (TAIL - 1)) * (1.0 / TAIL)) * TAIL


def keys(lists, blocks, cross):
    out = []
    whole_lists = lists.astype(jnp.int32)
    for at in (0, 3):
        a = whole_lists[at : at + 1]
        c = whole_lists[at + 1 : at + 2]
        live = lax.broadcasted_iota(jnp.int32, a.shape, 1) < whole_lists[at + 2 : at + 3]
        if cross:
            out.append(jnp.where(live & (c >= blocks), a * blocks + c - blocks, -1))
        else:
            out.append(jnp.where(live & (c < blocks), a * blocks + c, -1))
    return jnp.concatenate(out, axis=1)


def compact(key, blocks, slots, first):
    size = blocks * blocks
    hot = jnp.where(lax.broadcasted_iota(jnp.int32, (size, key.shape[1]), 0) == key, 1.0, 0.0).astype(BF16)
    counts = mxu(hot, jnp.ones((key.shape[1], LANES), BF16))
    flags = jnp.minimum(counts, 1.0)
    shape = (size, size)
    ahead = lax.broadcasted_iota(jnp.int32, shape, 0) > lax.broadcasted_iota(jnp.int32, shape, 1)
    place = mxu(jnp.where(ahead, 1.0, 0.0).astype(BF16), flags.astype(BF16)) + first
    index = lax.broadcasted_iota(jnp.int32, (16, size), 1).astype(F32)
    row = jnp.floor((index + 0.5) * (1.0 / blocks))
    line = lax.broadcasted_iota(jnp.int32, (16, size), 0)
    names = jnp.where(line == 0, row, jnp.where(line == 1, index - row * blocks, 1.0)).astype(BF16)
    found = []
    times = []
    for part in range(slots // LANES):
        lane = (lax.broadcasted_iota(jnp.int32, (size, LANES), 1) + part * LANES).astype(F32)
        here = (place == lane) & (flags > 0.5)
        found.append(mxu(names, jnp.where(here, 1.0, 0.0).astype(BF16)))
        times.append(mxu(names, jnp.where(here, counts, 0.0).astype(BF16))[2:3])
    found = jnp.concatenate(found, axis=1)
    end = place[size - 1 :] + flags[size - 1 :]
    return found[0:1], found[1:2], found[2:3], jnp.concatenate(times, axis=1), end


def put_plan(ref, rows):
    ref[...] = jnp.zeros(ref.shape, ref.dtype)
    for at, row in enumerate(rows):
        ref[at : at + 1, :] = row.astype(ref.dtype)


def spread(row, width):
    return jnp.concatenate([row] * (width // LANES), axis=1)


def side_features(blocks, coords, kinds, left, right):
    x = warp(coords)
    scale = -2.0 * S_OF_D
    square = x * x
    norm = S_OF_D * (square[:blocks] + square[blocks : 2 * blocks] + square[2 * blocks :])
    x1, x2, x3 = split_three(x)
    n1, n2, n3 = split_three(norm)
    one = jnp.ones_like(norm)
    pad = jnp.zeros(((FEATS - 24) * blocks, BLK), F32)
    kinds[...] = jnp.concatenate([x1, x1, x2, x2, x1, x3, n1, n2, n3, one, one, one, pad], axis=0)
    for g in range(0, blocks, 4):
        stack = [kinds[pl.ds(b, FEATS, stride=blocks), :] for b in range(g, g + 4)]
        turned = jnp.concatenate(stack, axis=0).T.astype(BF16)
        for b in range(4):
            left[g + b] = turned[:, b * FEATS : (b + 1) * FEATS]
    if right is not None:
        y1, y2, y3 = split_three(x * scale)
        kinds[...] = jnp.concatenate([y1, y2, y1, y2, y3, y1, one, one, one, n1, n2, n3, pad], axis=0)
        for b in range(blocks):
            right[b] = kinds[pl.ds(b, FEATS, stride=blocks), :].astype(BF16)


def rows_of(packed, blocks):
    lists = packed.shape[0] - LIST_ROWS
    coords = lists - 3 * blocks
    return coords // blocks, coords, lists


def pack_kernel(
    blocks, place, tile_rows, tile_cols, tile_count, signs, coords, noise,
    lists, mine, left, right, noise_here, got_signs, got_coords, got_rows, got_cols, kinds, sems,
):
    probes, coord_row, list_row = rows_of(mine, blocks)
    first = pl.multiple_of(place[1] * probes, probes)
    moves = [
        pltpu.make_async_copy(coords, got_coords, sems.at[0]),
        pltpu.make_async_copy(signs.at[pl.ds(first, probes), :], got_signs, sems.at[1]),
        pltpu.make_async_copy(tile_rows, got_rows, sems.at[2]),
        pltpu.make_async_copy(tile_cols, got_cols, sems.at[3]),
        pltpu.make_async_copy(noise, noise_here, sems.at[4]),
    ]
    for move in moves:
        move.start()
    lists[...] = jnp.zeros(lists.shape, F32)
    lists[2:3, :] = jnp.full((1, LANES), tile_count[0], jnp.int32).astype(F32)
    for move in moves[2:4]:
        move.wait()
    lists[0:1, : tile_rows.shape[1]] = got_rows[...].astype(F32)
    lists[1:2, : tile_cols.shape[1]] = got_cols[...].astype(F32)
    mine[list_row:] = lists[...]
    moves[0].wait()
    for c in range(3):
        for b in range(blocks):
            at = coord_row + c * blocks + b
            mine[at : at + 1] = got_coords[c : c + 1, b * BLK : (b + 1) * BLK]
    side_features(blocks, mine[coord_row:list_row], kinds, left, right)
    moves[1].wait()
    for b in range(blocks):
        mine[b * probes : (b + 1) * probes] = got_signs[:, b * BLK : (b + 1) * BLK].astype(F32)
    moves[4].wait()


def join_kernel(sibling, old, mine):
    del old
    at = mine.shape[0] - LIST_ROWS + 3
    mine[at : at + 3] = sibling[0:3]


def first_inner_kernel(
    blocks, mine, left, right,
    plan, tiles, z_ref, cross, acc, vecs, held_plan, sem,
):
    probes, _, list_row = rows_of(mine, blocks)
    lists = mine[list_row:]
    row, col, _, times, end = compact(keys(lists, blocks, False), blocks, held_plan.shape[1], 0.0)
    put_plan(held_plan, (row, col, times, spread(whole(end), held_plan.shape[1])))
    move = pltpu.make_async_copy(held_plan, plan, sem)
    move.start()
    row, col, _, times, end = compact(keys(lists, blocks, True), blocks, cross.shape[1], 0.0)
    put_plan(cross, (col, row, times, spread(end, cross.shape[1])))
    for b in range(blocks):
        vecs[b] = stack_vec(mine[b * probes : (b + 1) * probes], True)
    move.wait()
    make = maker(left, right)
    fill(tiles, 0, plan, make)
    inner_edges(acc, vecs, plan, keeper(tiles), make)
    z_ref[...] = acc[:blocks]


def finish_apply(blocks, acc, z_of, w_ref, q_of, prev_of, beta, noise):
    probes = acc.shape[1]
    qq = jnp.zeros((probes, LANES), F32)
    qw = jnp.zeros((probes, LANES), F32)
    for b in range(blocks):
        q = q_of(b)
        part = slice(b * BLK, (b + 1) * BLK)
        w = acc[b] + z_of(b) + noise[b : b + 1] * q
        if prev_of is not None:
            w = w - beta * prev_of(b)
        w_ref[:, part] = w
        qq = qq + q * q
        qw = qw + q * w
    put_stats(
        w_ref,
        blocks * BLK,
        lambda b: w_ref[:, b * BLK : (b + 1) * BLK],
        q_of,
        jnp.sum(qq, axis=1, keepdims=True),
        jnp.sum(qw, axis=1, keepdims=True),
        blocks,
    )


def first_outer_kernel(
    blocks, inner_plan, old_tiles, mine, above, below, noise, z_ref, right, cross,
    plan, tiles, w_ref, left, acc, vecs, held_plan, kinds, sem,
):
    probes, coord_row, list_row = rows_of(mine, blocks)
    del old_tiles
    slots = held_plan.shape[1]
    row, col, one, times, end = compact(keys(below[list_row:], blocks, True), blocks, slots, cross[3:4, :LANES])
    put_plan(
        held_plan,
        (cross[0:1] + row + blocks * one, cross[1:2] + col, cross[2:3] + times, spread(whole(end), slots)),
    )
    move = pltpu.make_async_copy(held_plan, plan, sem)
    move.start()
    for part, ref in enumerate((above, below)):
        side_features(blocks, ref[coord_row:list_row], kinds, left.at[part * blocks : (part + 1) * blocks], None)
        for b in range(blocks):
            vecs[part * blocks + b] = stack_vec(ref[b * probes : (b + 1) * probes], True)
    acc[...] = jnp.zeros_like(acc)
    move.wait()
    make = maker(left, right)
    base = inner_plan[3, 0]
    fill(tiles, base, plan, make)
    outer_edges(acc, vecs, plan, base, keeper(tiles), make)
    finish_apply(
        blocks, acc, lambda b: z_ref[b], w_ref, lambda b: mine[b * probes : (b + 1) * probes], None, None, noise
    )


def slab_alpha(w_ref, blocks):
    sums = w_ref[:, blocks * BLK : (blocks + 1) * BLK]
    return sums[:, 0:1] / jnp.maximum(sums[:, 1:2], 1e-30)


def inner_kernel(blocks, plan, w_ref, q_own, tiles, left, right, z_ref, acc, vecs):
    alpha = slab_alpha(w_ref, blocks)
    probes = w_ref.shape[0]
    for b in range(blocks):
        vecs[b] = stack_vec(w_ref[:, b * BLK : (b + 1) * BLK] - alpha * block_of(q_own, probes, b), False)
    inner_edges(acc, vecs, plan, keeper(tiles), maker(left, right))
    z_ref[...] = acc[:blocks]


def alpha_beta(stats, points):
    qw = [s[:, 0:1] for s in stats]
    qq = [s[:, 1:2] for s in stats]
    res = [s[:, 2:3] for s in stats]
    alpha = functools.reduce(jnp.add, qw) / points
    total = jnp.zeros_like(alpha)
    for w, q, r in zip(qw, qq, res):
        gap = alpha - w / jnp.maximum(q, 1e-30)
        total = total + (r + gap * gap * q)
    return alpha, jnp.sqrt(total / points + EPSILON)


def global_alpha_beta(slabs, points, place, stats_ref):
    order = [stats_ref[lax.rem(slab - place[0] + slabs, slabs)] for slab in range(slabs)]
    return alpha_beta(order, points)


def add_ab(ref, base, old_ab, step, alpha, beta):
    shape = (alpha.shape[0], LANES)
    lane = lax.broadcasted_iota(jnp.int32, shape, 1)
    out = jnp.zeros(shape, F32) if old_ab is None else old_ab[...]
    out = jnp.where(lane == step, alpha, out)
    ref[:, base : base + LANES] = jnp.where(lane == ITERS + step, beta, out)


def block_of(ref, rows, b):
    if len(ref.shape) == 3:
        return ref[b]
    return ref[b * rows : (b + 1) * rows]


def outer_kernel(
    blocks, slabs, points, step, place, inner_plan, plan, mine, above, below, stats_ref,
    q_own, q_above, q_below, z_raw, z_old, noise, tiles, left, right, *rest,
):
    probes = mine.shape[0]
    old_ab = None
    if step > 0:
        old_ab = rest[0]
        rest = rest[1:]
    w_ref, own_ref, above_ref, below_ref, z_ref, ab_ref, acc, vecs = rest
    alpha, beta = global_alpha_beta(slabs, points, place, stats_ref)
    scale = 1.0 / beta
    apart = alpha - slab_alpha(mine, blocks)
    add_ab(ab_ref, 0, old_ab, step, alpha, beta)
    halves = ((mine, q_own, own_ref), (above, q_above, above_ref), (below, q_below, below_ref))
    for part, (w, old, new) in enumerate(halves):
        for b in range(blocks):
            q = (w[:, b * BLK : (b + 1) * BLK] - alpha * block_of(old, probes, b)) * scale
            new[b] = q
            if part > 0:
                vecs[(part - 1) * blocks + b] = stack_vec(q, False)
            else:
                z_ref[b] = (z_raw[b] - apart * z_old[b]) * scale
    acc[...] = jnp.zeros_like(acc)
    outer_edges(acc, vecs, plan, inner_plan[3, 0], keeper(tiles), maker(left, right))
    finish_apply(
        blocks, acc, lambda b: z_ref[b], w_ref, lambda b: own_ref[b], lambda b: block_of(q_own, probes, b), beta, noise
    )


def slope_of(left, right):
    e, t = tile_terms(left, right)
    return (e * t) * (t + TAPER_STEP)


def slope_kernel(inner_plan, plan, left_own, left_halo, right, after, slopes):
    del after
    fill(slopes, 0, inner_plan, lambda slot, a, c: slope_of(left_own[a], right[c]))
    fill(slopes, inner_plan[3, 0], plan, lambda slot, a, c: slope_of(left_halo[a], right[c]))


def last_kernel(
    blocks, slabs, points, all_probes, place, inner_plan, plan, mine, above, below, stats_ref,
    q_own, q_above, q_below, pts, pts_above, pts_below, old_ab, slopes, left_own, left_out, right,
    basis_ref, grad_ref, acc, form_left, halo_left, form_right, pnts, halo_pnts, kinds, slack, pulls,
):
    probes, coord_row, list_row = rows_of(pts, blocks)
    alpha, beta = global_alpha_beta(slabs, points, place, stats_ref)
    scale = 1.0 / beta
    add_ab(basis_ref, blocks * BLK, old_ab, ITERS - 1, alpha, beta)
    for part, (w, old, ref) in enumerate(((mine, q_own, pts), (above, q_above, pts_above), (below, q_below, pts_below))):
        raw = ref[coord_row:list_row]
        bent = jnp.tanh(raw)
        x = raw + WARP_GAIN * bent
        x1, x2, x3 = split_three(x)
        one = jnp.ones((blocks, BLK), F32)
        kinds[...] = jnp.concatenate([x1, x2, x3, one, jnp.zeros((6 * blocks, BLK), F32)], axis=0)
        if part == 0:
            slack[...] = jnp.concatenate([x, 1.0 + WARP_GAIN * (1.0 - bent * bent)], axis=0)
        for b in range(blocks):
            part_cols = slice(b * BLK, (b + 1) * BLK)
            u = (w[:, part_cols] - alpha * block_of(old, probes, b)) * scale
            v = ref[b * probes : (b + 1) * probes]
            high = u.astype(BF16).astype(F32)
            low = u - high
            turned = jnp.concatenate([high, low, v, v], axis=0).T.astype(BF16)
            y = kinds[pl.ds(b, 16, stride=blocks), :].astype(BF16)
            y = jnp.concatenate([y, y], axis=1)
            if part == 0:
                basis_ref[:, part_cols] = u
                form_left[b] = turned
                form_right[b] = jnp.concatenate([v, v, high, low], axis=0).astype(BF16)
                pnts[b] = y
            else:
                halo_left[(part - 1) * blocks + b] = turned
                halo_pnts[(part - 1) * blocks + b] = y

    def pull(side):
        return lambda slot, a, c: stack_tile(mxu(side[a], form_right[c]) * slopes[slot])

    def pull_made(side, left):
        return lambda slot, a, c: stack_tile(mxu(side[a], form_right[c]) * slope_of(left[a], right[c]))

    base = inner_plan[3, 0]
    fill(pulls, 0, inner_plan, pull(form_left))
    fill(pulls, base, plan, pull(halo_left))
    inner_edges(acc, pnts, inner_plan, keeper(pulls), pull_made(form_left, left_own))
    outer_edges(acc, halo_pnts, plan, base, keeper(pulls), pull_made(halo_left, left_out))
    for b in range(blocks):
        part_cols = slice(b * BLK, (b + 1) * BLK)
        x = slack[pl.ds(b, 3, stride=blocks), :]
        chain = slack[pl.ds(3 * blocks + b, 3, stride=blocks), :]
        sums = acc[b]
        moved = sums[0:3] + sums[3:6] + sums[6:9] - x * sums[9:10]
        grad_ref[:, part_cols] = moved * chain * (1.0 / (LENGTH_SQ * all_probes))


def close_kernel(peers, place, own, other, grads, basis_ref, alpha_ref, beta_ref, grad_ref):
    probes = own.shape[0]
    width = basis_ref.shape[1]
    lower = place[1] == 0
    mine = own[...]
    theirs = other[...]
    first = jnp.where(lower, mine, theirs)
    second = jnp.where(lower, theirs, mine)
    basis_ref[:probes] = first[:, :width]
    basis_ref[probes:] = second[:, :width]
    ab = jnp.concatenate([first[:, width:], second[:, width:]], axis=0)
    turned = jnp.concatenate([ab, jnp.zeros((LANES - 2 * probes, LANES), F32)], axis=0).T
    alpha_ref[...] = turned[:ITERS, : 2 * probes]
    beta_ref[...] = turned[ITERS : 2 * ITERS, : 2 * probes]
    total = grads[lax.rem(peers - place[2], peers)]
    for k in range(1, peers):
        total = total + grads[lax.rem(k - place[2] + peers, peers)]
    grad_ref[...] = total


def vmem(count):
    return [pl.BlockSpec(memory_space=pltpu.VMEM)] * count


def smem(count):
    return [pl.BlockSpec(memory_space=pltpu.SMEM)] * count


def held(array):
    return pltpu.with_memory_space_constraint(array, pltpu.VMEM)


def stays(array):
    return pltpu.with_memory_space_constraint(array, pltpu.HBM)


def in_hbm(count):
    return [pl.BlockSpec(memory_space=pltpu.HBM)] * count


def call(name, kernel, outs, ins, scratch, work, aliases=None, limit=LIMIT_MIB):
    out_shapes, out_scalars = outs
    arrays, scalars = ins
    flops, moved = work
    return pl.pallas_call(
        kernel,
        out_shape=tuple(out_shapes),
        in_specs=smem(scalars) + vmem(len(arrays) - scalars),
        out_specs=tuple(smem(out_scalars) + vmem(len(out_shapes) - out_scalars)),
        scratch_shapes=[pltpu.VMEM(*entry) if isinstance(entry, tuple) else entry for entry in scratch],
        compiler_params=pltpu.CompilerParams(vmem_limit_bytes=limit * 1024 * 1024),
        cost_estimate=pl.CostEstimate(flops=flops, bytes_accessed=moved, transcendentals=0),
        input_output_aliases=aliases or {},
        name=name,
    )(*arrays)


def shifted(value, axes, count, steps):
    return lax.ppermute(value, axes, [(source, (source + steps) % count) for source in range(count)])


def body(coords, noise_var, probe_signs, tile_rows, tile_cols, tile_count):
    slabs = lax.axis_size("blk")
    subs = lax.axis_size("sub")
    outer = lax.axis_size("probe")
    probes = probe_signs.shape[0] // subs
    width = coords.shape[1]
    blocks = width // BLK
    cap = tile_rows.shape[-1]
    points = float(width * slabs)
    all_probes = probe_signs.shape[0] * outer
    sub = lax.axis_index("sub")
    blk = lax.axis_index("blk")
    peers = outer * subs
    place = jnp.stack([blk, sub, lax.axis_index("probe") * subs + sub]).astype(jnp.int32)
    sds = jax.ShapeDtypeStruct

    left_shape = sds((blocks, BLK, FEATS), BF16)
    right_shape = sds((blocks, FEATS, BLK), BF16)
    packed = sds((blocks * (probes + 3) + LIST_ROWS, BLK), F32)
    kinds = ((blocks * FEATS, BLK), F32)
    lists, own, left_own, right, noise = pl.pallas_call(
        functools.partial(pack_kernel, blocks),
        out_shape=(sds((LIST_ROWS, LANES), F32), packed, left_shape, right_shape, sds((blocks, BLK), F32)),
        in_specs=smem(1) + in_hbm(2) + smem(1) + in_hbm(3),
        out_specs=tuple(vmem(5)),
        scratch_shapes=[
            pltpu.VMEM((probes, width), jnp.int32),
            pltpu.VMEM((3, width), F32),
            pltpu.VMEM((1, cap), jnp.int32),
            pltpu.VMEM((1, cap), jnp.int32),
            pltpu.VMEM(*kinds),
            pltpu.SemaphoreType.DMA((5,)),
        ],
        compiler_params=pltpu.CompilerParams(vmem_limit_bytes=LIMIT_MIB * 1024 * 1024),
        name="pack",
    )(
        place, stays(tile_rows.reshape(1, cap)), stays(tile_cols.reshape(1, cap)), tile_count.reshape(1),
        stays(probe_signs), stays(coords), stays(noise_var.reshape(blocks, BLK)),
    )
    sibling = shifted(lists, "sub", subs, 1)
    (mine,) = call("join", join_kernel, ((packed,), 0), ((sibling, own), 0), [], (1000, 1000), {1: 0})
    above = shifted(mine, "blk", slabs, -1)
    below = shifted(mine, "blk", slabs, 1)

    ints = jnp.int32
    inner_slots = (blocks * (blocks + 1) // 2 + TAIL + LANES - 1) // LANES * LANES
    outer_slots = (blocks * (blocks + 1) + TAIL + LANES - 1) // LANES * LANES
    plan_shape = sds((LIST_ROWS, inner_slots), ints)
    outer_plan_shape = sds((LIST_ROWS, outer_slots), ints)
    slots = KEPT
    ext = width + LANES
    blocks_f32 = sds((blocks, probes, BLK), F32)
    tile_shape = pltpu.VMEM((slots, 2 * BLK, BLK), BF16)
    acc_shape = ((blocks, probes, BLK), F32)

    inner_plan, tiles, z, cross = call(
        "first_inner",
        functools.partial(first_inner_kernel, blocks),
        ((plan_shape, tile_shape, blocks_f32, sds((LIST_ROWS, outer_slots), F32)), 1),
        ((mine, left_own, right), 0),
        [
            acc_shape, ((blocks, probes, 2 * BLK), BF16), ((LIST_ROWS, inner_slots), ints),
            pltpu.SemaphoreType.DMA,
        ],
        (WORK_FIRST, WORK_BYTES),
    )
    outer_plan, tiles, w, left_halo = call(
        "first_outer",
        functools.partial(first_outer_kernel, blocks),
        ((outer_plan_shape, tile_shape, sds((probes, ext), F32), sds((2 * blocks, BLK, FEATS), BF16)), 1),
        ((inner_plan, held(tiles), mine, above, below, noise, z, right, cross), 1),
        [
            acc_shape, ((2 * blocks, probes, 2 * BLK), BF16), ((LIST_ROWS, outer_slots), ints), kinds,
            pltpu.SemaphoreType.DMA,
        ],
        (WORK_FIRST, WORK_BYTES),
        {1: 1},
    )

    def exchange(w):
        up = shifted(w, "blk", slabs, -1)
        down = shifted(w, "blk", slabs, 1)
        stats = w[:, width:]
        if slabs == 4:
            far = shifted(stats, "blk", slabs, 2)
            rows = jnp.stack([stats, up[:, width:], far, down[:, width:]])
        else:
            rows = lax.all_gather(stats, "blk", axis=0)
            rows = jnp.roll(rows, -blk, axis=0)
        return up, down, rows

    q = (mine, above, below)
    ab = []
    for step in range(ITERS - 1):
        up, down, stats = exchange(w)
        (z_raw,) = call(
            "inner",
            functools.partial(inner_kernel, blocks),
            ((blocks_f32,), 0),
            ((inner_plan, w, q[0], held(tiles), left_own, right), 1),
            [acc_shape, ((blocks, 2 * probes, 2 * BLK), BF16)],
            (WORK_NEXT, WORK_BYTES),
        )
        w, q0, q1, q2, z, next_ab = call(
            "outer",
            functools.partial(outer_kernel, blocks, slabs, points, step),
            (
                (sds((probes, ext), F32), blocks_f32, blocks_f32, blocks_f32, blocks_f32, sds((probes, LANES), F32)),
                0,
            ),
            ((place, inner_plan, outer_plan, w, up, down, stats, *q, z_raw, z, noise, held(tiles), left_halo, right, *ab), 3),
            [acc_shape, ((2 * blocks, 2 * probes, 2 * BLK), BF16)],
            (WORK_NEXT, WORK_BYTES),
        )
        q = (q0, q1, q2)
        ab = [next_ab]

    up, down, stats = exchange(w)
    (slopes,) = call(
        "slopes",
        slope_kernel,
        ((pltpu.VMEM((slots, BLK, BLK), F32),), 0),
        ((inner_plan, outer_plan, left_own, left_halo, right, w), 2),
        [],
        (WORK_FIRST, WORK_BYTES),
    )
    basis, grad = call(
        "last",
        functools.partial(last_kernel, blocks, slabs, points, all_probes),
        ((sds((probes, ext), F32), sds((3, width), F32)), 0),
        (
            (
                place, inner_plan, outer_plan, w, up, down, stats, *q, mine, above, below, *ab, held(slopes), left_own, left_halo, right,
            ),
            3,
        ),
        [
            ((blocks, 16, BLK), F32),
            ((blocks, BLK, 4 * probes), BF16),
            ((2 * blocks, BLK, 4 * probes), BF16),
            ((blocks, 4 * probes, BLK), BF16),
            ((blocks, 16, 2 * BLK), BF16),
            ((2 * blocks, 16, 2 * BLK), BF16),
            ((blocks * 16, BLK), F32),
            ((blocks * 6, BLK), F32),
            ((slots, 2 * BLK, BLK), BF16),
        ],
        (WORK_FIRST, WORK_BYTES),
        limit=2 * LIMIT_MIB,
    )

    other = shifted(basis, "sub", subs, 1)
    parts = [grad]
    for r in range(1, peers):
        parts.append(shifted(grad, ("probe", "sub"), peers, -r))
    last_basis, alphas, betas, coord_grad = call(
        "close",
        functools.partial(close_kernel, peers),
        (
            (
                sds((subs * probes, width), F32), sds((ITERS, subs * probes), F32), sds((ITERS, subs * probes), F32),
                sds((3, width), F32),
            ),
            0,
        ),
        ((place, basis, other, jnp.stack(parts)), 1),
        [],
        (1000000, 1000000),
    )
    return alphas, betas, last_basis, coord_grad


def solution(mesh):
    return jax.shard_map(
        body,
        mesh=mesh,
        in_specs=(
            P(None, ("groups", "blk")),
            P(("groups", "blk")),
            P("probe", ("groups", "blk")),
            P(("groups", "blk"), "sub", None),
            P(("groups", "blk"), "sub", None),
            P(("groups", "blk"), "sub"),
        ),
        out_specs=(
            P(None, ("groups", "probe")),
            P(None, ("groups", "probe")),
            P("probe", ("groups", "blk")),
            P(None, ("groups", "blk")),
        ),
        check_vma=False,
    )
```

```python
import functools
import math

import jax
import jax.numpy as jnp
from jax import lax
from jax.experimental import pallas as pl
from jax.experimental.pallas import tpu as pltpu
from jax.sharding import PartitionSpec as P

ITERS = 3
SIGNAL_VAR = 0.1
LENGTH_SQ = 2.0
TAPER_SQ = 16.0
WARP_GAIN = 0.4
EPSILON = 1e-06

BLK = 128
LANES = 128
FEATS = 32
GROUP = 16
TAIL = 4
LIST_ROWS = 8
LIMIT_MIB = 16
KEPT = 224
WORK_FIRST = 300000000
WORK_NEXT = 100000000
WORK_BYTES = 4000000

S_OF_D = -math.log2(math.e) / (2.0 * LENGTH_SQ)
D_OF_S = 1.0 / S_OF_D
ROOT_VAR = math.sqrt(SIGNAL_VAR)
TAPER_STEP = 4.0 * LENGTH_SQ / TAPER_SQ * ROOT_VAR
T_SLOPE = -ROOT_VAR * D_OF_S / TAPER_SQ

F32 = jnp.float32
BF16 = jnp.bfloat16


def split_two(x):
    high = x.astype(BF16)
    low = (x - high.astype(F32)).astype(BF16)
    return high, low


def split_three(x):
    one = x.astype(BF16).astype(F32)
    rest = x - one
    two = rest.astype(BF16).astype(F32)
    three = (rest - two).astype(BF16).astype(F32)
    return one, two, three


def warp(x):
    return x + WARP_GAIN * jnp.tanh(x)


def mxu(a, b):
    return lax.dot_general(a, b, (((1,), (0,)), ((), ())), preferred_element_type=F32)


def terms(s):
    e = jnp.exp2(s)
    t = jnp.maximum(T_SLOPE * s + ROOT_VAR, 0.0)
    return e, t


def put_stats(ref, base, w_of, q_of, qq, qw, blocks):
    alpha_s = qw / jnp.maximum(qq, 1e-30)
    acc = jnp.zeros((qq.shape[0], LANES), F32)
    for b in range(blocks):
        r = w_of(b) - alpha_s * q_of(b)
        acc = acc + r * r
    res = jnp.sum(acc, axis=1, keepdims=True)
    lane = lax.broadcasted_iota(jnp.int32, (qq.shape[0], LANES), 1)
    out = jnp.where(lane == 0, qw, jnp.where(lane == 1, qq, jnp.where(lane == 2, res, 0.0)))
    ref[:, base : base + LANES] = out


def mxu_turned(a, b):
    return lax.dot_general(a, b, (((1,), (1,)), ((), ())), preferred_element_type=F32)


def fold(out, probes):
    if out.shape[0] > probes:
        return out[:probes] + out[probes:]
    return out


def fold_turned(out, probes):
    total = out[:probes, :BLK] + out[:probes, BLK:]
    if out.shape[0] > probes:
        total = total + out[probes:, :BLK]
    return total


def stack_vec(q, exact):
    if exact:
        high = q.astype(BF16)
        return jnp.concatenate([high, high], axis=1)
    high, low = split_two(q)
    return jnp.concatenate(
        [jnp.concatenate([high, high], axis=1), jnp.concatenate([low, jnp.zeros_like(low)], axis=1)], axis=0
    )


def stack_tile(tile):
    return jnp.concatenate(split_two(tile), axis=0)


def ranges(first, last, body):
    long = (last - first) // GROUP
    middle = first + long * GROUP

    def big(g, carry):
        body(first + g * GROUP, GROUP)
        return carry

    def small(g, carry):
        body(middle + g * TAIL, TAIL)
        return carry

    lax.fori_loop(0, long, big, 0)
    lax.fori_loop(0, (last - middle) // TAIL, small, 0)


def kept_and_made(total, room, body, kept, made):
    first = jnp.minimum(total, room)
    ranges(0, first, functools.partial(body, kept))
    many = (total - first) // TAIL

    def rest(g, carry):
        body(made, first + g * TAIL, TAIL)
        return carry

    lax.fori_loop(0, many, rest, 0)


def inner_edges(acc, vecs, plan, kept, made):
    acc[...] = jnp.zeros_like(acc)
    size = acc.shape[1]

    def group(tile_of, start, many):
        outs = []
        for u in range(many):
            slot = start + u
            a = plan[0, slot]
            c = plan[1, slot]
            times = plan[2, slot].astype(F32)
            tile = tile_of(slot, a, c)
            outs.append((c, fold(mxu(vecs[a], tile), size) * times))
            outs.append((a, fold_turned(mxu_turned(vecs[c][:, :BLK], tile), size) * times))
        for c, out in outs:
            acc[c] = acc[c] + out

    kept_and_made(plan[3, 0], KEPT, group, kept, made)


def outer_edges(acc, vecs, plan, base, kept, made):
    size = acc.shape[1]

    def group(tile_of, start, many):
        outs = []
        for u in range(many):
            at = start + u
            a = plan[0, at]
            c = plan[1, at]
            times = plan[2, at].astype(F32)
            outs.append((c, fold(mxu(vecs[a], tile_of(base + at, a, c)), size) * times))
        for c, out in outs:
            acc[c] = acc[c] + out

    kept_and_made(plan[3, 0], jnp.maximum(KEPT - base, 0), group, kept, made)


def beside(first, second):
    empty = jnp.zeros_like(first)
    return jnp.concatenate(
        [jnp.concatenate([first, empty], axis=1), jnp.concatenate([empty, second], axis=1)], axis=0
    )


def both_sides(left, right, pair):
    (a, c), (b, d) = pair
    return mxu(left[0, a] + left[1, b], beside(right[c], right[d]))


def one_side(left, right, a, c):
    return mxu(left[0, a], jnp.concatenate([right[c], jnp.zeros_like(right[c])], axis=0))


def kernel_value(s):
    e, t = terms(s)
    return e * t * t


def slope_value(s):
    e, t = terms(s)
    return (e * t) * (t + TAPER_STEP)


def fill(into, base, plan, make):
    def body(start, many):
        for u in range(0, many, 2):
            at = start + u
            pair = ((plan[0, at], plan[1, at]), (plan[0, at + 1], plan[1, at + 1]))
            first, second = make(base + at, pair)
            into[base + at] = first
            into[base + at + 1] = second

    ranges(0, jnp.minimum(plan[3, 0], jnp.maximum(KEPT - base, 0)), body)


def halves(x):
    return x[:, :BLK], x[:, BLK:]


def tile_maker(left, right):
    def make(slot, pair):
        return [stack_tile(x) for x in halves(kernel_value(both_sides(left, right, pair)))]

    return make


def maker(left, right):
    return lambda slot, a, c: stack_tile(kernel_value(one_side(left, right, a, c)))


def keeper(tiles):
    return lambda slot, a, c: tiles[slot]


def whole(n):
    return jnp.floor((n + (TAIL - 1)) * (1.0 / TAIL)) * TAIL


def keys(lists, blocks, cross):
    out = []
    whole_lists = lists.astype(jnp.int32)
    for at in (0, 3):
        a = whole_lists[at : at + 1]
        c = whole_lists[at + 1 : at + 2]
        live = lax.broadcasted_iota(jnp.int32, a.shape, 1) < whole_lists[at + 2 : at + 3]
        if cross:
            out.append(jnp.where(live & (c >= blocks), a * blocks + c - blocks, -1))
        else:
            out.append(jnp.where(live & (c < blocks), a * blocks + c, -1))
    return jnp.concatenate(out, axis=1)


def compact(key, blocks, slots, first):
    size = blocks * blocks
    hot = jnp.where(lax.broadcasted_iota(jnp.int32, (size, key.shape[1]), 0) == key, 1.0, 0.0).astype(BF16)
    counts = mxu(hot, jnp.ones((key.shape[1], LANES), BF16))
    flags = jnp.minimum(counts, 1.0)
    shape = (size, size)
    ahead = lax.broadcasted_iota(jnp.int32, shape, 0) > lax.broadcasted_iota(jnp.int32, shape, 1)
    place = mxu(jnp.where(ahead, 1.0, 0.0).astype(BF16), flags.astype(BF16)) + first
    index = lax.broadcasted_iota(jnp.int32, (16, size), 1).astype(F32)
    row = jnp.floor((index + 0.5) * (1.0 / blocks))
    line = lax.broadcasted_iota(jnp.int32, (16, size), 0)
    names = jnp.where(line == 0, row, jnp.where(line == 1, index - row * blocks, 1.0)).astype(BF16)
    found = []
    times = []
    for part in range(slots // LANES):
        lane = (lax.broadcasted_iota(jnp.int32, (size, LANES), 1) + part * LANES).astype(F32)
        here = (place == lane) & (flags > 0.5)
        found.append(mxu(names, jnp.where(here, 1.0, 0.0).astype(BF16)))
        times.append(mxu(names, jnp.where(here, counts, 0.0).astype(BF16))[2:3])
    found = jnp.concatenate(found, axis=1)
    end = place[size - 1 :] + flags[size - 1 :]
    return found[0:1], found[1:2], found[2:3], jnp.concatenate(times, axis=1), end


def put_plan(ref, rows):
    ref[...] = jnp.zeros(ref.shape, ref.dtype)
    for at, row in enumerate(rows):
        ref[at : at + 1, :] = row.astype(ref.dtype)


def spread(row, width):
    return jnp.concatenate([row] * (width // LANES), axis=1)


def side_features(blocks, coords, kinds, left, right):
    x = warp(coords)
    scale = -2.0 * S_OF_D
    square = x * x
    norm = S_OF_D * (square[:blocks] + square[blocks : 2 * blocks] + square[2 * blocks :])
    x1, x2, x3 = split_three(x)
    n1, n2, n3 = split_three(norm)
    one = jnp.ones_like(norm)
    pad = jnp.zeros(((FEATS - 24) * blocks, BLK), F32)
    kinds[...] = jnp.concatenate([x1, x1, x2, x2, x1, x3, n1, n2, n3, one, one, one, pad], axis=0)
    for g in range(0, blocks, 4):
        stack = [kinds[pl.ds(b, FEATS, stride=blocks), :] for b in range(g, g + 4)]
        turned = jnp.concatenate(stack, axis=0).T.astype(BF16)
        for b in range(4):
            piece = turned[:, b * FEATS : (b + 1) * FEATS]
            left[0, g + b] = jnp.concatenate([piece, jnp.zeros_like(piece)], axis=1)
            left[1, g + b] = jnp.concatenate([jnp.zeros_like(piece), piece], axis=1)
    if right is not None:
        y1, y2, y3 = split_three(x * scale)
        kinds[...] = jnp.concatenate([y1, y2, y1, y2, y3, y1, one, one, one, n1, n2, n3, pad], axis=0)
        for b in range(blocks):
            right[b] = kinds[pl.ds(b, FEATS, stride=blocks), :].astype(BF16)


def rows_of(packed, blocks):
    lists = packed.shape[0] - LIST_ROWS
    coords = lists - 3 * blocks
    return coords // blocks, coords, lists


def pack_kernel(
    blocks, place, tile_rows, tile_cols, tile_count, signs, coords, noise,
    lists, mine, noise_here, got_signs, got_coords, got_rows, got_cols, sems,
):
    probes, coord_row, list_row = rows_of(mine, blocks)
    first = pl.multiple_of(place[1] * probes, probes)
    moves = [
        pltpu.make_async_copy(coords, got_coords, sems.at[0]),
        pltpu.make_async_copy(signs.at[pl.ds(first, probes), :], got_signs, sems.at[1]),
        pltpu.make_async_copy(tile_rows, got_rows, sems.at[2]),
        pltpu.make_async_copy(tile_cols, got_cols, sems.at[3]),
        pltpu.make_async_copy(noise, noise_here, sems.at[4]),
    ]
    for move in moves:
        move.start()
    lists[...] = jnp.zeros(lists.shape, F32)
    lists[2:3, :] = jnp.full((1, LANES), tile_count[0], jnp.int32).astype(F32)
    for move in moves[2:4]:
        move.wait()
    lists[0:1, : tile_rows.shape[1]] = got_rows[...].astype(F32)
    lists[1:2, : tile_cols.shape[1]] = got_cols[...].astype(F32)
    mine[list_row:] = lists[...]
    moves[0].wait()
    for c in range(3):
        for b in range(blocks):
            at = coord_row + c * blocks + b
            mine[at : at + 1] = got_coords[c : c + 1, b * BLK : (b + 1) * BLK]
    moves[1].wait()
    for b in range(blocks):
        mine[b * probes : (b + 1) * probes] = got_signs[:, b * BLK : (b + 1) * BLK].astype(F32)
    moves[4].wait()


def join_kernel(sibling, old, mine):
    del old
    at = mine.shape[0] - LIST_ROWS + 3
    mine[at : at + 3] = sibling[0:3]


def first_inner_kernel(
    blocks, mine,
    plan, tiles, z_ref, cross, left, right, acc, vecs, held_plan, kinds, sem,
):
    probes, coord_row, list_row = rows_of(mine, blocks)
    lists = mine[list_row:]
    row, col, _, times, end = compact(keys(lists, blocks, False), blocks, held_plan.shape[1], 0.0)
    put_plan(held_plan, (row, col, times, spread(whole(end), held_plan.shape[1])))
    move = pltpu.make_async_copy(held_plan, plan, sem)
    move.start()
    row, col, _, times, end = compact(keys(lists, blocks, True), blocks, cross.shape[1], 0.0)
    put_plan(cross, (col, row, times, spread(end, cross.shape[1])))
    for b in range(blocks):
        vecs[b] = stack_vec(mine[b * probes : (b + 1) * probes], True)
    side_features(blocks, mine[coord_row:list_row], kinds, left, right)
    move.wait()
    fill(tiles, 0, plan, tile_maker(left, right))
    inner_edges(acc, vecs, plan, keeper(tiles), maker(left, right))
    z_ref[...] = acc[:blocks]


def finish_apply(blocks, acc, z_of, w_ref, q_of, prev_of, beta, noise):
    probes = acc.shape[1]
    qq = jnp.zeros((probes, LANES), F32)
    qw = jnp.zeros((probes, LANES), F32)
    for b in range(blocks):
        q = q_of(b)
        part = slice(b * BLK, (b + 1) * BLK)
        w = acc[b] + z_of(b) + noise[b : b + 1] * q
        if prev_of is not None:
            w = w - beta * prev_of(b)
        w_ref[:, part] = w
        qq = qq + q * q
        qw = qw + q * w
    put_stats(
        w_ref,
        blocks * BLK,
        lambda b: w_ref[:, b * BLK : (b + 1) * BLK],
        q_of,
        jnp.sum(qq, axis=1, keepdims=True),
        jnp.sum(qw, axis=1, keepdims=True),
        blocks,
    )


def first_outer_kernel(
    blocks, inner_plan, old_tiles, mine, above, below, noise, z_ref, right, cross,
    plan, tiles, w_ref, left, acc, vecs, held_plan, kinds, sem,
):
    probes, coord_row, list_row = rows_of(mine, blocks)
    del old_tiles
    slots = held_plan.shape[1]
    row, col, one, times, end = compact(keys(below[list_row:], blocks, True), blocks, slots, cross[3:4, :LANES])
    put_plan(
        held_plan,
        (cross[0:1] + row + blocks * one, cross[1:2] + col, cross[2:3] + times, spread(whole(end), slots)),
    )
    move = pltpu.make_async_copy(held_plan, plan, sem)
    move.start()
    for part, ref in enumerate((above, below)):
        side_features(blocks, ref[coord_row:list_row], kinds, left.at[:, part * blocks : (part + 1) * blocks], None)
        for b in range(blocks):
            vecs[part * blocks + b] = stack_vec(ref[b * probes : (b + 1) * probes], True)
    acc[...] = jnp.zeros_like(acc)
    move.wait()
    base = inner_plan[3, 0]
    fill(tiles, base, plan, tile_maker(left, right))
    outer_edges(acc, vecs, plan, base, keeper(tiles), maker(left, right))
    finish_apply(
        blocks, acc, lambda b: z_ref[b], w_ref, lambda b: mine[b * probes : (b + 1) * probes], None, None, noise
    )


def slab_alpha(w_ref, blocks):
    sums = w_ref[:, blocks * BLK : (blocks + 1) * BLK]
    return sums[:, 0:1] / jnp.maximum(sums[:, 1:2], 1e-30)


def inner_kernel(blocks, plan, w_ref, q_own, tiles, left, right, z_ref, acc, vecs):
    alpha = slab_alpha(w_ref, blocks)
    probes = w_ref.shape[0]
    for b in range(blocks):
        vecs[b] = stack_vec(w_ref[:, b * BLK : (b + 1) * BLK] - alpha * block_of(q_own, probes, b), False)
    inner_edges(acc, vecs, plan, keeper(tiles), maker(left, right))
    z_ref[...] = acc[:blocks]


def alpha_beta(stats, points):
    qw = [s[:, 0:1] for s in stats]
    qq = [s[:, 1:2] for s in stats]
    res = [s[:, 2:3] for s in stats]
    alpha = functools.reduce(jnp.add, qw) / points
    total = jnp.zeros_like(alpha)
    for w, q, r in zip(qw, qq, res):
        gap = alpha - w / jnp.maximum(q, 1e-30)
        total = total + (r + gap * gap * q)
    return alpha, jnp.sqrt(total / points + EPSILON)


def global_alpha_beta(slabs, points, place, stats_ref):
    order = [stats_ref[lax.rem(slab - place[0] + slabs, slabs)] for slab in range(slabs)]
    return alpha_beta(order, points)


def add_ab(ref, base, old_ab, step, alpha, beta):
    shape = (alpha.shape[0], LANES)
    lane = lax.broadcasted_iota(jnp.int32, shape, 1)
    out = jnp.zeros(shape, F32) if old_ab is None else old_ab[...]
    out = jnp.where(lane == step, alpha, out)
    ref[:, base : base + LANES] = jnp.where(lane == ITERS + step, beta, out)


def block_of(ref, rows, b):
    if len(ref.shape) == 3:
        return ref[b]
    return ref[b * rows : (b + 1) * rows]


def outer_kernel(
    blocks, slabs, points, step, place, inner_plan, plan, mine, above, below, stats_ref,
    q_own, q_above, q_below, z_raw, z_old, noise, tiles, left, right, *rest,
):
    probes = mine.shape[0]
    old_ab = None
    if step > 0:
        old_ab = rest[0]
        rest = rest[1:]
    w_ref, own_ref, above_ref, below_ref, z_ref, ab_ref, acc, vecs = rest
    alpha, beta = global_alpha_beta(slabs, points, place, stats_ref)
    scale = 1.0 / beta
    apart = alpha - slab_alpha(mine, blocks)
    add_ab(ab_ref, 0, old_ab, step, alpha, beta)
    halves = ((mine, q_own, own_ref), (above, q_above, above_ref), (below, q_below, below_ref))
    for part, (w, old, new) in enumerate(halves):
        for b in range(blocks):
            q = (w[:, b * BLK : (b + 1) * BLK] - alpha * block_of(old, probes, b)) * scale
            new[b] = q
            if part > 0:
                vecs[(part - 1) * blocks + b] = stack_vec(q, False)
            else:
                z_ref[b] = (z_raw[b] - apart * z_old[b]) * scale
    acc[...] = jnp.zeros_like(acc)
    outer_edges(acc, vecs, plan, inner_plan[3, 0], keeper(tiles), maker(left, right))
    finish_apply(
        blocks, acc, lambda b: z_ref[b], w_ref, lambda b: own_ref[b], lambda b: block_of(q_own, probes, b), beta, noise
    )


def slope_kernel(inner_plan, plan, left_own, left_halo, right, after, slopes):
    del after

    def make(left):
        return lambda slot, pair: halves(slope_value(both_sides(left, right, pair)))

    fill(slopes, 0, inner_plan, make(left_own))
    fill(slopes, inner_plan[3, 0], plan, make(left_halo))


def points_kernel(blocks, pts, pts_above, pts_below, after, pnts, halo_pnts, slack, kinds):
    del after
    _, coord_row, list_row = rows_of(pts, blocks)
    for part, ref in enumerate((pts, pts_above, pts_below)):
        raw = ref[coord_row:list_row]
        bent = jnp.tanh(raw)
        x = raw + WARP_GAIN * bent
        x1, x2, x3 = split_three(x)
        one = jnp.ones((blocks, BLK), F32)
        kinds[...] = jnp.concatenate([x1, x2, x3, one, jnp.zeros((6 * blocks, BLK), F32)], axis=0)
        if part == 0:
            slack[...] = jnp.concatenate([x, 1.0 + WARP_GAIN * (1.0 - bent * bent)], axis=0)
        for b in range(blocks):
            y = kinds[pl.ds(b, 16, stride=blocks), :].astype(BF16)
            y = jnp.concatenate([y, y], axis=1)
            if part == 0:
                pnts[b] = y
            else:
                halo_pnts[(part - 1) * blocks + b] = y


def last_kernel(
    blocks, slabs, points, all_probes, place, inner_plan, plan, mine, above, below, stats_ref,
    q_own, q_above, q_below, pts, pts_above, pts_below, old_ab, slopes, left_own, left_out, right, pnts, halo_pnts, slack,
    out_ref, acc, form_left, halo_left, form_right, pulls,
):
    probes, _, _ = rows_of(pts, blocks)
    alpha, beta = global_alpha_beta(slabs, points, place, stats_ref)
    scale = 1.0 / beta
    out_ref[probes:, blocks * BLK :] = jnp.zeros((3, LANES), F32)
    add_ab(out_ref.at[:probes], blocks * BLK, old_ab, ITERS - 1, alpha, beta)
    for part, (w, old, ref) in enumerate(((mine, q_own, pts), (above, q_above, pts_above), (below, q_below, pts_below))):
        for b in range(blocks):
            part_cols = slice(b * BLK, (b + 1) * BLK)
            u = (w[:, part_cols] - alpha * block_of(old, probes, b)) * scale
            v = ref[b * probes : (b + 1) * probes]
            high = u.astype(BF16).astype(F32)
            low = u - high
            turned = jnp.concatenate([high, low, v, v], axis=0).T.astype(BF16)
            first = jnp.concatenate([turned, jnp.zeros_like(turned)], axis=1)
            second = jnp.concatenate([jnp.zeros_like(turned), turned], axis=1)
            if part == 0:
                out_ref[:probes, part_cols] = u
                form_left[0, b] = first
                form_left[1, b] = second
                form_right[b] = jnp.concatenate([v, v, high, low], axis=0).astype(BF16)
            else:
                halo_left[0, (part - 1) * blocks + b] = first
                halo_left[1, (part - 1) * blocks + b] = second

    def pull(side):
        def make(slot, pair):
            first, second = halves(both_sides(side, form_right, pair))
            return stack_tile(first * slopes[slot]), stack_tile(second * slopes[slot + 1])

        return make

    def pull_made(side, left):
        return lambda slot, a, c: stack_tile(
            one_side(side, form_right, a, c) * slope_value(one_side(left, right, a, c))
        )

    base = inner_plan[3, 0]
    fill(pulls, 0, inner_plan, pull(form_left))
    fill(pulls, base, plan, pull(halo_left))
    inner_edges(acc, pnts, inner_plan, keeper(pulls), pull_made(form_left, left_own))
    outer_edges(acc, halo_pnts, plan, base, keeper(pulls), pull_made(halo_left, left_out))
    for b in range(blocks):
        part_cols = slice(b * BLK, (b + 1) * BLK)
        x = slack[pl.ds(b, 3, stride=blocks), :]
        chain = slack[pl.ds(3 * blocks + b, 3, stride=blocks), :]
        sums = acc[b]
        moved = sums[0:3] + sums[3:6] + sums[6:9] - x * sums[9:10]
        out_ref[probes:, part_cols] = moved * chain * (1.0 / (LENGTH_SQ * all_probes))


def pair_kernel(own, other, grad_ref):
    probes = own.shape[0] - 3
    width = grad_ref.shape[1]
    grad_ref[...] = own[probes:, :width] + other[probes:, :width]


def close_kernel(place, own, other, basis_ref, alpha_ref, beta_ref):
    probes = own.shape[0] - 3
    width = basis_ref.shape[1]
    lower = place[1] == 0
    mine = own[:probes]
    theirs = other[:probes]
    first = jnp.where(lower, mine, theirs)
    second = jnp.where(lower, theirs, mine)
    basis_ref[:probes] = first[:, :width]
    basis_ref[probes:] = second[:, :width]
    ab = jnp.concatenate([first[:, width:], second[:, width:]], axis=0)
    turned = jnp.concatenate([ab, jnp.zeros((LANES - 2 * probes, LANES), F32)], axis=0).T
    alpha_ref[...] = turned[:ITERS, : 2 * probes]
    beta_ref[...] = turned[ITERS : 2 * ITERS, : 2 * probes]


def vmem(count):
    return [pl.BlockSpec(memory_space=pltpu.VMEM)] * count


def smem(count):
    return [pl.BlockSpec(memory_space=pltpu.SMEM)] * count


def held(array):
    return pltpu.with_memory_space_constraint(array, pltpu.VMEM)


def stays(array):
    return pltpu.with_memory_space_constraint(array, pltpu.HBM)


def in_hbm(count):
    return [pl.BlockSpec(memory_space=pltpu.HBM)] * count


def call(name, kernel, outs, ins, scratch, work, aliases=None, limit=LIMIT_MIB):
    out_shapes, out_scalars = outs
    arrays, scalars = ins
    flops, moved = work
    return pl.pallas_call(
        kernel,
        out_shape=tuple(out_shapes),
        in_specs=smem(scalars) + vmem(len(arrays) - scalars),
        out_specs=tuple(smem(out_scalars) + vmem(len(out_shapes) - out_scalars)),
        scratch_shapes=[pltpu.VMEM(*entry) if isinstance(entry, tuple) else entry for entry in scratch],
        compiler_params=pltpu.CompilerParams(vmem_limit_bytes=limit * 1024 * 1024),
        cost_estimate=pl.CostEstimate(flops=flops, bytes_accessed=moved, transcendentals=0),
        input_output_aliases=aliases or {},
        name=name,
    )(*arrays)


def shifted(value, axes, count, steps):
    return lax.ppermute(value, axes, [(source, (source + steps) % count) for source in range(count)])


def body(coords, noise_var, probe_signs, tile_rows, tile_cols, tile_count):
    slabs = lax.axis_size("blk")
    subs = lax.axis_size("sub")
    outer = lax.axis_size("probe")
    probes = probe_signs.shape[0] // subs
    width = coords.shape[1]
    blocks = width // BLK
    cap = tile_rows.shape[-1]
    points = float(width * slabs)
    all_probes = probe_signs.shape[0] * outer
    sub = lax.axis_index("sub")
    blk = lax.axis_index("blk")
    place = jnp.stack([blk, sub]).astype(jnp.int32)
    sds = jax.ShapeDtypeStruct

    left_shape = sds((2, blocks, BLK, 2 * FEATS), BF16)
    right_shape = sds((blocks, FEATS, BLK), BF16)
    packed = sds((blocks * (probes + 3) + LIST_ROWS, BLK), F32)
    kinds = ((blocks * FEATS, BLK), F32)
    lists, own, noise = pl.pallas_call(
        functools.partial(pack_kernel, blocks),
        out_shape=(sds((LIST_ROWS, LANES), F32), packed, sds((blocks, BLK), F32)),
        in_specs=smem(1) + in_hbm(2) + smem(1) + in_hbm(3),
        out_specs=tuple(vmem(3)),
        scratch_shapes=[
            pltpu.VMEM((probes, width), jnp.int32),
            pltpu.VMEM((3, width), F32),
            pltpu.VMEM((1, cap), jnp.int32),
            pltpu.VMEM((1, cap), jnp.int32),
            pltpu.SemaphoreType.DMA((5,)),
        ],
        compiler_params=pltpu.CompilerParams(vmem_limit_bytes=LIMIT_MIB * 1024 * 1024),
        name="pack",
    )(
        place, stays(tile_rows.reshape(1, cap)), stays(tile_cols.reshape(1, cap)), tile_count.reshape(1),
        stays(probe_signs), stays(coords), stays(noise_var.reshape(blocks, BLK)),
    )
    sibling = shifted(lists, "sub", subs, 1)
    (mine,) = call("join", join_kernel, ((packed,), 0), ((sibling, own), 0), [], (1000, 1000), {1: 0})
    above = shifted(mine, "blk", slabs, -1)
    below = shifted(mine, "blk", slabs, 1)

    ints = jnp.int32
    inner_slots = (blocks * (blocks + 1) // 2 + TAIL + LANES - 1) // LANES * LANES
    outer_slots = (blocks * (blocks + 1) + TAIL + LANES - 1) // LANES * LANES
    plan_shape = sds((LIST_ROWS, inner_slots), ints)
    outer_plan_shape = sds((LIST_ROWS, outer_slots), ints)
    slots = KEPT
    ext = width + LANES
    blocks_f32 = sds((blocks, probes, BLK), F32)
    tile_shape = pltpu.VMEM((slots, 2 * BLK, BLK), BF16)
    acc_shape = ((blocks, probes, BLK), F32)

    inner_plan, tiles, z, cross, left_own, right = call(
        "first_inner",
        functools.partial(first_inner_kernel, blocks),
        ((plan_shape, tile_shape, blocks_f32, sds((LIST_ROWS, outer_slots), F32), left_shape, right_shape), 1),
        ((mine,), 0),
        [
            acc_shape, ((blocks, probes, 2 * BLK), BF16), ((LIST_ROWS, inner_slots), ints), kinds,
            pltpu.SemaphoreType.DMA,
        ],
        (WORK_FIRST, WORK_BYTES),
    )
    outer_plan, tiles, w, left_halo = call(
        "first_outer",
        functools.partial(first_outer_kernel, blocks),
        ((outer_plan_shape, tile_shape, sds((probes, ext), F32), sds((2, 2 * blocks, BLK, 2 * FEATS), BF16)), 1),
        ((inner_plan, held(tiles), mine, above, below, noise, z, right, cross), 1),
        [
            acc_shape, ((2 * blocks, probes, 2 * BLK), BF16), ((LIST_ROWS, outer_slots), ints), kinds,
            pltpu.SemaphoreType.DMA,
        ],
        (WORK_FIRST, WORK_BYTES),
        {1: 1},
    )

    def exchange(w):
        up = shifted(w, "blk", slabs, -1)
        down = shifted(w, "blk", slabs, 1)
        stats = w[:, width:]
        if slabs == 4:
            far = shifted(stats, "blk", slabs, 2)
            rows = jnp.stack([stats, up[:, width:], far, down[:, width:]])
        else:
            rows = lax.all_gather(stats, "blk", axis=0)
            rows = jnp.roll(rows, -blk, axis=0)
        return up, down, rows

    q = (mine, above, below)
    ab = []
    for step in range(ITERS - 1):
        up, down, stats = exchange(w)
        (z_raw,) = call(
            "inner",
            functools.partial(inner_kernel, blocks),
            ((blocks_f32,), 0),
            ((inner_plan, w, q[0], held(tiles), left_own, right), 1),
            [acc_shape, ((blocks, 2 * probes, 2 * BLK), BF16)],
            (WORK_NEXT, WORK_BYTES),
        )
        w, q0, q1, q2, z, next_ab = call(
            "outer",
            functools.partial(outer_kernel, blocks, slabs, points, step),
            (
                (sds((probes, ext), F32), blocks_f32, blocks_f32, blocks_f32, blocks_f32, sds((probes, LANES), F32)),
                0,
            ),
            ((place, inner_plan, outer_plan, w, up, down, stats, *q, z_raw, z, noise, held(tiles), left_halo, right, *ab), 3),
            [acc_shape, ((2 * blocks, 2 * probes, 2 * BLK), BF16)],
            (WORK_NEXT, WORK_BYTES),
        )
        q = (q0, q1, q2)
        ab = [next_ab]

    up, down, stats = exchange(w)
    (slopes,) = call(
        "slopes",
        slope_kernel,
        ((pltpu.VMEM((slots, BLK, BLK), F32),), 0),
        ((inner_plan, outer_plan, left_own, left_halo, right, w), 2),
        [],
        (WORK_FIRST, WORK_BYTES),
    )
    pnts, halo_pnts, slack = call(
        "points",
        functools.partial(points_kernel, blocks),
        (
            (
                sds((blocks, 16, 2 * BLK), BF16), sds((2 * blocks, 16, 2 * BLK), BF16), sds((6 * blocks, BLK), F32),
            ),
            0,
        ),
        ((mine, above, below, w), 0),
        [((blocks * 16, BLK), F32)],
        (WORK_NEXT, WORK_BYTES),
    )
    (result,) = call(
        "last",
        functools.partial(last_kernel, blocks, slabs, points, all_probes),
        ((sds((probes + 3, ext), F32),), 0),
        (
            (
                place, inner_plan, outer_plan, w, up, down, stats, *q, mine, above, below, *ab, held(slopes), left_own, left_halo,
                right, pnts, halo_pnts, slack,
            ),
            3,
        ),
        [
            ((blocks, 16, BLK), F32),
            ((2, blocks, BLK, 8 * probes), BF16),
            ((2, 2 * blocks, BLK, 8 * probes), BF16),
            ((blocks, 4 * probes, BLK), BF16),
            ((slots, 2 * BLK, BLK), BF16),
        ],
        (WORK_FIRST, WORK_BYTES),
        limit=LIMIT_MIB * 3 // 2,
    )

    other = shifted(result, "sub", subs, 1)
    (grad,) = call("pair", pair_kernel, ((sds((3, width), F32),), 0), ((result, other), 0), [], (1000, 1000))
    if outer == 2:
        coord_grad = grad + shifted(grad, "probe", outer, 1)
    else:
        coord_grad = lax.psum(grad, "probe")
    last_basis, alphas, betas = call(
        "close",
        close_kernel,
        (
            (
                sds((subs * probes, width), F32), sds((ITERS, subs * probes), F32), sds((ITERS, subs * probes), F32),
            ),
            0,
        ),
        ((place, result, other), 1),
        [],
        (1000000, 1000000),
    )
    return alphas, betas, last_basis, coord_grad


def solution(mesh):
    return jax.shard_map(
        body,
        mesh=mesh,
        in_specs=(
            P(None, ("groups", "blk")),
            P(("groups", "blk")),
            P("probe", ("groups", "blk")),
            P(("groups", "blk"), "sub", None),
            P(("groups", "blk"), "sub", None),
            P(("groups", "blk"), "sub"),
        ),
        out_specs=(
            P(None, ("groups", "probe")),
            P(None, ("groups", "probe")),
            P("probe", ("groups", "blk")),
            P(None, ("groups", "blk")),
        ),
        check_vma=False,
    )
```

```python
import functools
import math

import jax
import jax.numpy as jnp
from jax import lax
from jax.experimental import pallas as pl
from jax.experimental.pallas import tpu as pltpu
from jax.sharding import PartitionSpec as P

ITERS = 3
SIGNAL_VAR = 0.1
LENGTH_SQ = 2.0
TAPER_SQ = 16.0
WARP_GAIN = 0.4
EPSILON = 1e-06

BLK = 128
LANES = 128
FEATS = 32
GROUP = 16
TAIL = 8
LIST_ROWS = 8
LIMIT_MIB = 16
KEPT = 256
WORK_FIRST = 300000000
WORK_NEXT = 100000000
WORK_BYTES = 4000000

DECAY = TAPER_SQ / (2.0 * LENGTH_SQ)
Z_TOP = math.sqrt(SIGNAL_VAR * math.exp(-DECAY))
Z_RATE = DECAY / Z_TOP
Z_OF_D = -Z_TOP / TAPER_SQ
Z_STEP = 4.0 * LENGTH_SQ / TAPER_SQ * Z_TOP

F32 = jnp.float32
BF16 = jnp.bfloat16


def split_two(x):
    high = x.astype(BF16)
    low = (x - high.astype(F32)).astype(BF16)
    return high, low


def split_three(x):
    one = x.astype(BF16).astype(F32)
    rest = x - one
    two = rest.astype(BF16).astype(F32)
    three = (rest - two).astype(BF16).astype(F32)
    return one, two, three


def warp(x):
    return x + WARP_GAIN * jnp.tanh(x)


def mxu(a, b):
    return lax.dot_general(a, b, (((1,), (0,)), ((), ())), preferred_element_type=F32)


def put_stats(ref, base, w_of, q_of, qq, qw, blocks):
    alpha_s = qw / jnp.maximum(qq, 1e-30)
    acc = jnp.zeros((qq.shape[0], LANES), F32)
    for b in range(blocks):
        r = w_of(b) - alpha_s * q_of(b)
        acc = acc + r * r
    res = jnp.sum(acc, axis=1, keepdims=True)
    lane = lax.broadcasted_iota(jnp.int32, (qq.shape[0], LANES), 1)
    out = jnp.where(lane == 0, qw, jnp.where(lane == 1, qq, jnp.where(lane == 2, res, 0.0)))
    ref[:, base : base + LANES] = out


def mxu_turned(a, b):
    return lax.dot_general(a, b, (((1,), (1,)), ((), ())), preferred_element_type=F32)


def fold(out, probes):
    if out.shape[0] > probes:
        return out[:probes] + out[probes:]
    return out


def fold_turned(out, probes):
    total = out[:probes, :BLK] + out[:probes, BLK:]
    if out.shape[0] > probes:
        total = total + out[probes:, :BLK]
    return total


def stack_vec(q, exact):
    if exact:
        high = q.astype(BF16)
        return jnp.concatenate([high, high], axis=1)
    high, low = split_two(q)
    return jnp.concatenate(
        [jnp.concatenate([high, high], axis=1), jnp.concatenate([low, jnp.zeros_like(low)], axis=1)], axis=0
    )


def stack_tile(tile):
    return jnp.concatenate(split_two(tile), axis=0)


def ranges(first, last, body):
    long = (last - first) // GROUP
    middle = first + long * GROUP

    def big(g, carry):
        body(first + g * GROUP, GROUP)
        return carry

    def small(g, carry):
        body(middle + g * TAIL, TAIL)
        return carry

    lax.fori_loop(0, long, big, 0)
    lax.fori_loop(0, (last - middle) // TAIL, small, 0)


def kept_and_made(total, room, body, kept, made):
    first = jnp.minimum(total, room)
    ranges(0, first, functools.partial(body, kept))
    many = (total - first) // TAIL

    def rest(g, carry):
        body(made, first + g * TAIL, TAIL)
        return carry

    lax.fori_loop(0, many, rest, 0)


def inner_edges(acc, vecs, plan, kept, made):
    acc[...] = jnp.zeros_like(acc)
    size = acc.shape[1]

    def group(tile_of, start, many):
        outs = []
        for u in range(many):
            slot = start + u
            a = plan[0, slot]
            c = plan[1, slot]
            times = plan[2, slot].astype(F32)
            tile = tile_of(slot, a, c)
            outs.append((c, fold(mxu(vecs[a], tile), size) * times))
            outs.append((a, fold_turned(mxu_turned(vecs[c][:, :BLK], tile), size) * times))
        for c, out in outs:
            acc[c] = acc[c] + out

    kept_and_made(plan[3, 0], KEPT, group, kept, made)


def outer_edges(acc, vecs, plan, base, kept, made):
    size = acc.shape[1]

    def group(tile_of, start, many):
        outs = []
        for u in range(many):
            at = start + u
            a = plan[0, at]
            c = plan[1, at]
            times = plan[2, at].astype(F32)
            outs.append((c, fold(mxu(vecs[a], tile_of(base + at, a, c)), size) * times))
        for c, out in outs:
            acc[c] = acc[c] + out

    kept_and_made(plan[3, 0], jnp.maximum(KEPT - base, 0), group, kept, made)


def tile_value(z):
    z = jnp.maximum(z, 0.0)
    return jnp.exp(z * Z_RATE) * (z * z)


def slope_value(z):
    z = jnp.maximum(z, 0.0)
    return (jnp.exp(z * Z_RATE) * z) * (z + Z_STEP)


def fill(into, base, plan, make):
    def body(start, many):
        for u in range(many):
            at = start + u
            into[base + at] = make(base + at, plan[0, at], plan[1, at])

    ranges(0, jnp.minimum(plan[3, 0], jnp.maximum(KEPT - base, 0)), body)


def maker(left, right):
    return lambda slot, a, c: stack_tile(tile_value(mxu(left[a], right[c])))


def keeper(tiles):
    return lambda slot, a, c: tiles[slot]


def whole(n):
    return jnp.floor((n + (TAIL - 1)) * (1.0 / TAIL)) * TAIL


def keys(lists, blocks, cross):
    out = []
    whole_lists = lists.astype(jnp.int32)
    for at in (0, 3):
        a = whole_lists[at : at + 1]
        c = whole_lists[at + 1 : at + 2]
        live = lax.broadcasted_iota(jnp.int32, a.shape, 1) < whole_lists[at + 2 : at + 3]
        if cross:
            out.append(jnp.where(live & (c >= blocks), a * blocks + c - blocks, -1))
        else:
            out.append(jnp.where(live & (c < blocks), a * blocks + c, -1))
    return jnp.concatenate(out, axis=1)


def compact(key, blocks, slots, first):
    size = blocks * blocks
    hot = jnp.where(lax.broadcasted_iota(jnp.int32, (size, key.shape[1]), 0) == key, 1.0, 0.0).astype(BF16)
    counts = mxu(hot, jnp.ones((key.shape[1], LANES), BF16))
    flags = jnp.minimum(counts, 1.0)
    shape = (size, size)
    ahead = lax.broadcasted_iota(jnp.int32, shape, 0) > lax.broadcasted_iota(jnp.int32, shape, 1)
    place = mxu(jnp.where(ahead, 1.0, 0.0).astype(BF16), flags.astype(BF16)) + first
    index = lax.broadcasted_iota(jnp.int32, (16, size), 1).astype(F32)
    row = jnp.floor((index + 0.5) * (1.0 / blocks))
    line = lax.broadcasted_iota(jnp.int32, (16, size), 0)
    names = jnp.where(line == 0, row, jnp.where(line == 1, index - row * blocks, 1.0)).astype(BF16)
    found = []
    times = []
    for part in range(slots // LANES):
        lane = (lax.broadcasted_iota(jnp.int32, (size, LANES), 1) + part * LANES).astype(F32)
        here = (place == lane) & (flags > 0.5)
        found.append(mxu(names, jnp.where(here, 1.0, 0.0).astype(BF16)))
        times.append(mxu(names, jnp.where(here, counts, 0.0).astype(BF16))[2:3])
    found = jnp.concatenate(found, axis=1)
    end = place[size - 1 :] + flags[size - 1 :]
    return found[0:1], found[1:2], found[2:3], jnp.concatenate(times, axis=1), end


def put_plan(ref, rows):
    ref[...] = jnp.zeros(ref.shape, ref.dtype)
    for at, row in enumerate(rows):
        ref[at : at + 1, :] = row.astype(ref.dtype)


def spread(row, width):
    return jnp.concatenate([row] * (width // LANES), axis=1)


def side_features(blocks, coords, kinds, left, right):
    x = warp(coords)
    scale = -2.0 * Z_OF_D
    square = x * x
    norm = Z_OF_D * (square[:blocks] + square[blocks : 2 * blocks] + square[2 * blocks :])
    x1, x2, x3 = split_three(x)
    n1, n2, n3 = split_three(norm)
    m1, m2, m3 = split_three(norm + Z_TOP)
    one = jnp.ones_like(norm)
    pad = jnp.zeros(((FEATS - 24) * blocks, BLK), F32)
    kinds[...] = jnp.concatenate([x1, x1, x2, x2, x1, x3, n1, n2, n3, one, one, one, pad], axis=0)
    for g in range(0, blocks, 4):
        stack = [kinds[pl.ds(b, FEATS, stride=blocks), :] for b in range(g, g + 4)]
        turned = jnp.concatenate(stack, axis=0).T.astype(BF16)
        for b in range(4):
            left[g + b] = turned[:, b * FEATS : (b + 1) * FEATS]
    if right is not None:
        y1, y2, y3 = split_three(x * scale)
        kinds[...] = jnp.concatenate([y1, y2, y1, y2, y3, y1, one, one, one, m1, m2, m3, pad], axis=0)
        for b in range(blocks):
            right[b] = kinds[pl.ds(b, FEATS, stride=blocks), :].astype(BF16)


def rows_of(packed, blocks):
    lists = packed.shape[0] - LIST_ROWS
    coords = lists - 3 * blocks
    return coords // blocks, coords, lists


def pack_kernel(
    blocks, place, tile_rows, tile_cols, tile_count, signs, coords, noise,
    lists, mine, noise_here, got_signs, got_coords, got_rows, got_cols, sems,
):
    probes, coord_row, list_row = rows_of(mine, blocks)
    first = pl.multiple_of(place[1] * probes, probes)
    moves = [
        pltpu.make_async_copy(coords, got_coords, sems.at[0]),
        pltpu.make_async_copy(signs.at[pl.ds(first, probes), :], got_signs, sems.at[1]),
        pltpu.make_async_copy(tile_rows, got_rows, sems.at[2]),
        pltpu.make_async_copy(tile_cols, got_cols, sems.at[3]),
        pltpu.make_async_copy(noise, noise_here, sems.at[4]),
    ]
    for move in moves:
        move.start()
    lists[...] = jnp.zeros(lists.shape, F32)
    lists[2:3, :] = jnp.full((1, LANES), tile_count[0], jnp.int32).astype(F32)
    for move in moves[2:4]:
        move.wait()
    lists[0:1, : tile_rows.shape[1]] = got_rows[...].astype(F32)
    lists[1:2, : tile_cols.shape[1]] = got_cols[...].astype(F32)
    mine[list_row:] = lists[...]
    moves[0].wait()
    for c in range(3):
        for b in range(blocks):
            at = coord_row + c * blocks + b
            mine[at : at + 1] = got_coords[c : c + 1, b * BLK : (b + 1) * BLK]
    moves[1].wait()
    for b in range(blocks):
        mine[b * probes : (b + 1) * probes] = got_signs[:, b * BLK : (b + 1) * BLK].astype(F32)
    moves[4].wait()


def join_kernel(sibling, old, mine):
    del old
    at = mine.shape[0] - LIST_ROWS + 3
    mine[at : at + 3] = sibling[0:3]


def first_inner_kernel(
    blocks, mine,
    plan, tiles, z_ref, cross, left, right, acc, vecs, held_plan, kinds, sem,
):
    probes, coord_row, list_row = rows_of(mine, blocks)
    lists = mine[list_row:]
    row, col, _, times, end = compact(keys(lists, blocks, False), blocks, held_plan.shape[1], 0.0)
    put_plan(held_plan, (row, col, times, spread(whole(end), held_plan.shape[1])))
    move = pltpu.make_async_copy(held_plan, plan, sem)
    move.start()
    row, col, _, times, end = compact(keys(lists, blocks, True), blocks, cross.shape[1], 0.0)
    put_plan(cross, (col, row, times, spread(end, cross.shape[1])))
    for b in range(blocks):
        vecs[b] = stack_vec(mine[b * probes : (b + 1) * probes], True)
    side_features(blocks, mine[coord_row:list_row], kinds, left, right)
    move.wait()
    fill(tiles, 0, plan, maker(left, right))
    inner_edges(acc, vecs, plan, keeper(tiles), maker(left, right))
    z_ref[...] = acc[:blocks]


def finish_apply(blocks, acc, z_of, w_ref, q_of, prev_of, beta, noise):
    probes = acc.shape[1]
    qq = jnp.zeros((probes, LANES), F32)
    qw = jnp.zeros((probes, LANES), F32)
    for b in range(blocks):
        q = q_of(b)
        part = slice(b * BLK, (b + 1) * BLK)
        w = acc[b] + z_of(b) + noise[b : b + 1] * q
        if prev_of is not None:
            w = w - beta * prev_of(b)
        w_ref[:, part] = w
        qq = qq + q * q
        qw = qw + q * w
    put_stats(
        w_ref,
        blocks * BLK,
        lambda b: w_ref[:, b * BLK : (b + 1) * BLK],
        q_of,
        jnp.sum(qq, axis=1, keepdims=True),
        jnp.sum(qw, axis=1, keepdims=True),
        blocks,
    )


def first_outer_kernel(
    blocks, inner_plan, old_tiles, mine, above, below, noise, z_ref, right, cross,
    plan, tiles, w_ref, left, acc, vecs, held_plan, kinds, sem,
):
    probes, coord_row, list_row = rows_of(mine, blocks)
    del old_tiles
    slots = held_plan.shape[1]
    row, col, one, times, end = compact(keys(below[list_row:], blocks, True), blocks, slots, cross[3:4, :LANES])
    put_plan(
        held_plan,
        (cross[0:1] + row + blocks * one, cross[1:2] + col, cross[2:3] + times, spread(whole(end), slots)),
    )
    move = pltpu.make_async_copy(held_plan, plan, sem)
    move.start()
    for part, ref in enumerate((above, below)):
        side_features(blocks, ref[coord_row:list_row], kinds, left.at[part * blocks : (part + 1) * blocks], None)
        for b in range(blocks):
            vecs[part * blocks + b] = stack_vec(ref[b * probes : (b + 1) * probes], True)
    acc[...] = jnp.zeros_like(acc)
    move.wait()
    base = inner_plan[3, 0]
    fill(tiles, base, plan, maker(left, right))
    outer_edges(acc, vecs, plan, base, keeper(tiles), maker(left, right))
    finish_apply(
        blocks, acc, lambda b: z_ref[b], w_ref, lambda b: mine[b * probes : (b + 1) * probes], None, None, noise
    )


def slab_alpha(w_ref, blocks):
    sums = w_ref[:, blocks * BLK : (blocks + 1) * BLK]
    return sums[:, 0:1] / jnp.maximum(sums[:, 1:2], 1e-30)


def inner_kernel(blocks, plan, w_ref, q_own, tiles, left, right, z_ref, acc, vecs):
    alpha = slab_alpha(w_ref, blocks)
    probes = w_ref.shape[0]
    for b in range(blocks):
        vecs[b] = stack_vec(w_ref[:, b * BLK : (b + 1) * BLK] - alpha * block_of(q_own, probes, b), False)
    inner_edges(acc, vecs, plan, keeper(tiles), maker(left, right))
    z_ref[...] = acc[:blocks]


def alpha_beta(stats, points):
    qw = [s[:, 0:1] for s in stats]
    qq = [s[:, 1:2] for s in stats]
    res = [s[:, 2:3] for s in stats]
    alpha = functools.reduce(jnp.add, qw) / points
    total = jnp.zeros_like(alpha)
    for w, q, r in zip(qw, qq, res):
        gap = alpha - w / jnp.maximum(q, 1e-30)
        total = total + (r + gap * gap * q)
    return alpha, jnp.sqrt(total / points + EPSILON)


def global_alpha_beta(slabs, points, place, stats_ref):
    order = [stats_ref[lax.rem(slab - place[0] + slabs, slabs)] for slab in range(slabs)]
    return alpha_beta(order, points)


def add_ab(ref, base, old_ab, step, alpha, beta):
    shape = (alpha.shape[0], LANES)
    lane = lax.broadcasted_iota(jnp.int32, shape, 1)
    out = jnp.zeros(shape, F32) if old_ab is None else old_ab[...]
    out = jnp.where(lane == step, alpha, out)
    ref[:, base : base + LANES] = jnp.where(lane == ITERS + step, beta, out)


def block_of(ref, rows, b):
    if len(ref.shape) == 3:
        return ref[b]
    return ref[b * rows : (b + 1) * rows]


def outer_kernel(
    blocks, slabs, points, step, place, inner_plan, plan, mine, above, below, stats_ref,
    q_own, q_above, q_below, z_raw, z_old, noise, tiles, left, right, *rest,
):
    probes = mine.shape[0]
    old_ab = None
    if step > 0:
        old_ab = rest[0]
        rest = rest[1:]
    w_ref, own_ref, above_ref, below_ref, ab_ref, *z_ref, acc, vecs, held_z = rest
    alpha, beta = global_alpha_beta(slabs, points, place, stats_ref)
    scale = 1.0 / beta
    apart = alpha - slab_alpha(mine, blocks)
    add_ab(ab_ref, 0, old_ab, step, alpha, beta)
    halves = ((mine, q_own, own_ref), (above, q_above, above_ref), (below, q_below, below_ref))
    for part, (w, old, new) in enumerate(halves):
        for b in range(blocks):
            q = (w[:, b * BLK : (b + 1) * BLK] - alpha * block_of(old, probes, b)) * scale
            new[b] = q
            if part > 0:
                vecs[(part - 1) * blocks + b] = stack_vec(q, False)
            else:
                z = (z_raw[b] - apart * z_old[b]) * scale
                held_z[b] = z
                for ref in z_ref:
                    ref[b] = z
    acc[...] = jnp.zeros_like(acc)
    outer_edges(acc, vecs, plan, inner_plan[3, 0], keeper(tiles), maker(left, right))
    finish_apply(
        blocks, acc, lambda b: held_z[b], w_ref, lambda b: own_ref[b], lambda b: block_of(q_own, probes, b), beta, noise
    )


def slope_kernel(inner_plan, plan, left_own, left_halo, right, after, slopes):
    del after

    def make(left):
        return lambda slot, a, c: slope_value(mxu(left[a], right[c]))

    fill(slopes, 0, inner_plan, make(left_own))
    fill(slopes, inner_plan[3, 0], plan, make(left_halo))


def points_kernel(blocks, pts, pts_above, pts_below, after, pnts, halo_pnts, slack, kinds):
    del after
    _, coord_row, list_row = rows_of(pts, blocks)
    for part, ref in enumerate((pts, pts_above, pts_below)):
        raw = ref[coord_row:list_row]
        bent = jnp.tanh(raw)
        x = raw + WARP_GAIN * bent
        x1, x2, x3 = split_three(x)
        one = jnp.ones((blocks, BLK), F32)
        kinds[...] = jnp.concatenate([x1, x2, x3, one, jnp.zeros((6 * blocks, BLK), F32)], axis=0)
        if part == 0:
            slack[...] = jnp.concatenate([x, 1.0 + WARP_GAIN * (1.0 - bent * bent)], axis=0)
        for b in range(blocks):
            y = kinds[pl.ds(b, 16, stride=blocks), :].astype(BF16)
            y = jnp.concatenate([y, y], axis=1)
            if part == 0:
                pnts[b] = y
            else:
                halo_pnts[(part - 1) * blocks + b] = y


def last_kernel(
    blocks, slabs, points, all_probes, place, inner_plan, plan, mine, above, below, stats_ref,
    q_own, q_above, q_below, pts, pts_above, pts_below, old_ab, slopes, left_own, left_out, right, pnts, halo_pnts, slack,
    out_ref, acc, form_left, halo_left, form_right, pulls,
):
    probes, _, _ = rows_of(pts, blocks)
    alpha, beta = global_alpha_beta(slabs, points, place, stats_ref)
    scale = 1.0 / beta
    out_ref[probes:, blocks * BLK :] = jnp.zeros((3, LANES), F32)
    add_ab(out_ref.at[:probes], blocks * BLK, old_ab, ITERS - 1, alpha, beta)
    for part, (w, old, ref) in enumerate(((mine, q_own, pts), (above, q_above, pts_above), (below, q_below, pts_below))):
        for b in range(blocks):
            part_cols = slice(b * BLK, (b + 1) * BLK)
            u = (w[:, part_cols] - alpha * block_of(old, probes, b)) * scale
            v = ref[b * probes : (b + 1) * probes]
            high = u.astype(BF16).astype(F32)
            low = u - high
            turned = jnp.concatenate([high, low, v, v], axis=0).T.astype(BF16)
            if part == 0:
                out_ref[:probes, part_cols] = u
                form_left[b] = turned
                form_right[b] = jnp.concatenate([v, v, high, low], axis=0).astype(BF16)
            else:
                halo_left[(part - 1) * blocks + b] = turned

    def pull(side):
        return lambda slot, a, c: stack_tile(mxu(side[a], form_right[c]) * slopes[slot])

    def pull_made(side, left):
        return lambda slot, a, c: stack_tile(mxu(side[a], form_right[c]) * slope_value(mxu(left[a], right[c])))

    base = inner_plan[3, 0]
    fill(pulls, 0, inner_plan, pull(form_left))
    fill(pulls, base, plan, pull(halo_left))
    inner_edges(acc, pnts, inner_plan, keeper(pulls), pull_made(form_left, left_own))
    outer_edges(acc, halo_pnts, plan, base, keeper(pulls), pull_made(halo_left, left_out))
    for b in range(blocks):
        part_cols = slice(b * BLK, (b + 1) * BLK)
        x = slack[pl.ds(b, 3, stride=blocks), :]
        chain = slack[pl.ds(3 * blocks + b, 3, stride=blocks), :]
        sums = acc[b]
        moved = sums[0:3] + sums[3:6] + sums[6:9] - x * sums[9:10]
        out_ref[probes:, part_cols] = moved * chain * (1.0 / (LENGTH_SQ * all_probes))


def pair_kernel(own, other, grad_ref):
    probes = own.shape[0] - 3
    width = grad_ref.shape[1]
    grad_ref[...] = own[probes:, :width] + other[probes:, :width]


def close_kernel(place, own, other, basis_ref, alpha_ref, beta_ref):
    probes = own.shape[0] - 3
    width = basis_ref.shape[1]
    lower = place[1] == 0
    mine = own[:probes]
    theirs = other[:probes]
    first = jnp.where(lower, mine, theirs)
    second = jnp.where(lower, theirs, mine)
    basis_ref[:probes] = first[:, :width]
    basis_ref[probes:] = second[:, :width]
    ab = jnp.concatenate([first[:, width:], second[:, width:]], axis=0)
    turned = jnp.concatenate([ab, jnp.zeros((LANES - 2 * probes, LANES), F32)], axis=0).T
    alpha_ref[...] = turned[:ITERS, : 2 * probes]
    beta_ref[...] = turned[ITERS : 2 * ITERS, : 2 * probes]


def vmem(count):
    return [pl.BlockSpec(memory_space=pltpu.VMEM)] * count


def smem(count):
    return [pl.BlockSpec(memory_space=pltpu.SMEM)] * count


def held(array):
    return pltpu.with_memory_space_constraint(array, pltpu.VMEM)


def stays(array):
    return pltpu.with_memory_space_constraint(array, pltpu.HBM)


def in_hbm(count):
    return [pl.BlockSpec(memory_space=pltpu.HBM)] * count


def call(name, kernel, outs, ins, scratch, work, aliases=None, limit=LIMIT_MIB):
    out_shapes, out_scalars = outs
    arrays, scalars = ins
    flops, moved = work
    return pl.pallas_call(
        kernel,
        out_shape=tuple(out_shapes),
        in_specs=smem(scalars) + vmem(len(arrays) - scalars),
        out_specs=tuple(smem(out_scalars) + vmem(len(out_shapes) - out_scalars)),
        scratch_shapes=[pltpu.VMEM(*entry) if isinstance(entry, tuple) else entry for entry in scratch],
        compiler_params=pltpu.CompilerParams(vmem_limit_bytes=limit * 1024 * 1024),
        cost_estimate=pl.CostEstimate(flops=flops, bytes_accessed=moved, transcendentals=0),
        input_output_aliases=aliases or {},
        name=name,
    )(*arrays)


def shifted(value, axes, count, steps):
    return lax.ppermute(value, axes, [(source, (source + steps) % count) for source in range(count)])


def body(coords, noise_var, probe_signs, tile_rows, tile_cols, tile_count):
    slabs = lax.axis_size("blk")
    subs = lax.axis_size("sub")
    outer = lax.axis_size("probe")
    probes = probe_signs.shape[0] // subs
    width = coords.shape[1]
    blocks = width // BLK
    cap = tile_rows.shape[-1]
    points = float(width * slabs)
    all_probes = probe_signs.shape[0] * outer
    sub = lax.axis_index("sub")
    blk = lax.axis_index("blk")
    place = jnp.stack([blk, sub]).astype(jnp.int32)
    sds = jax.ShapeDtypeStruct

    left_shape = sds((blocks, BLK, FEATS), BF16)
    right_shape = sds((blocks, FEATS, BLK), BF16)
    packed = sds((blocks * (probes + 3) + LIST_ROWS, BLK), F32)
    kinds = ((blocks * FEATS, BLK), F32)
    lists, own, noise = pl.pallas_call(
        functools.partial(pack_kernel, blocks),
        out_shape=(sds((LIST_ROWS, LANES), F32), packed, sds((blocks, BLK), F32)),
        in_specs=smem(1) + in_hbm(2) + smem(1) + in_hbm(3),
        out_specs=tuple(vmem(3)),
        scratch_shapes=[
            pltpu.VMEM((probes, width), jnp.int32),
            pltpu.VMEM((3, width), F32),
            pltpu.VMEM((1, cap), jnp.int32),
            pltpu.VMEM((1, cap), jnp.int32),
            pltpu.SemaphoreType.DMA((5,)),
        ],
        compiler_params=pltpu.CompilerParams(vmem_limit_bytes=LIMIT_MIB * 1024 * 1024),
        name="pack",
    )(
        place, stays(tile_rows.reshape(1, cap)), stays(tile_cols.reshape(1, cap)), tile_count.reshape(1),
        stays(probe_signs), stays(coords), stays(noise_var.reshape(blocks, BLK)),
    )
    sibling = shifted(lists, "sub", subs, 1)
    (mine,) = call("join", join_kernel, ((packed,), 0), ((sibling, own), 0), [], (1000, 1000), {1: 0})
    above = shifted(mine, "blk", slabs, -1)
    below = shifted(mine, "blk", slabs, 1)

    ints = jnp.int32
    inner_slots = (blocks * (blocks + 1) // 2 + TAIL + LANES - 1) // LANES * LANES
    outer_slots = (blocks * (blocks + 1) + TAIL + LANES - 1) // LANES * LANES
    plan_shape = sds((LIST_ROWS, inner_slots), ints)
    outer_plan_shape = sds((LIST_ROWS, outer_slots), ints)
    slots = KEPT
    ext = width + LANES
    blocks_f32 = sds((blocks, probes, BLK), F32)
    tile_shape = pltpu.VMEM((slots, 2 * BLK, BLK), BF16)
    acc_shape = ((blocks, probes, BLK), F32)

    inner_plan, tiles, z, cross, left_own, right = call(
        "first_inner",
        functools.partial(first_inner_kernel, blocks),
        ((plan_shape, tile_shape, blocks_f32, sds((LIST_ROWS, outer_slots), F32), left_shape, right_shape), 1),
        ((mine,), 0),
        [
            acc_shape, ((blocks, probes, 2 * BLK), BF16), ((LIST_ROWS, inner_slots), ints), kinds,
            pltpu.SemaphoreType.DMA,
        ],
        (WORK_FIRST, WORK_BYTES),
    )
    outer_plan, tiles, w, left_halo = call(
        "first_outer",
        functools.partial(first_outer_kernel, blocks),
        ((outer_plan_shape, tile_shape, sds((probes, ext), F32), sds((2 * blocks, BLK, FEATS), BF16)), 1),
        ((inner_plan, held(tiles), mine, above, below, noise, z, right, cross), 1),
        [
            acc_shape, ((2 * blocks, probes, 2 * BLK), BF16), ((LIST_ROWS, outer_slots), ints), kinds,
            pltpu.SemaphoreType.DMA,
        ],
        (WORK_FIRST, WORK_BYTES),
        {1: 1},
    )

    def exchange(w):
        stats = w[:, width:]
        if slabs == 4:
            far = shifted(stats, "blk", slabs, 2)
        up = shifted(w, "blk", slabs, -1)
        down = shifted(w, "blk", slabs, 1)
        if slabs == 4:
            rows = jnp.stack([stats, up[:, width:], far, down[:, width:]])
        else:
            rows = lax.all_gather(stats, "blk", axis=0)
            rows = jnp.roll(rows, -blk, axis=0)
        return up, down, rows

    q = (mine, above, below)
    ab = []
    z_old = z
    for step in range(ITERS - 1):
        up, down, stats = exchange(w)
        (z_raw,) = call(
            "inner",
            functools.partial(inner_kernel, blocks),
            ((blocks_f32,), 0),
            ((inner_plan, w, q[0], held(tiles), left_own, right), 1),
            [acc_shape, ((blocks, 2 * probes, 2 * BLK), BF16)],
            (WORK_NEXT, WORK_BYTES),
        )
        w, q0, q1, q2, next_ab, *z = call(
            "outer",
            functools.partial(outer_kernel, blocks, slabs, points, step),
            (
                (
                    sds((probes, ext), F32), blocks_f32, blocks_f32, blocks_f32, sds((probes, LANES), F32),
                    *([blocks_f32] if step < ITERS - 2 else []),
                ),
                0,
            ),
            ((place, inner_plan, outer_plan, w, up, down, stats, *q, z_raw, z_old, noise, held(tiles), left_halo, right, *ab), 3),
            [acc_shape, ((2 * blocks, 2 * probes, 2 * BLK), BF16), ((blocks, probes, BLK), F32)],
            (WORK_NEXT, WORK_BYTES),
        )
        q = (q0, q1, q2)
        ab = [next_ab]
        z_old = z[0] if z else None

    up, down, stats = exchange(w)
    (slopes,) = call(
        "slopes",
        slope_kernel,
        ((pltpu.VMEM((slots, BLK, BLK), F32),), 0),
        ((inner_plan, outer_plan, left_own, left_halo, right, w), 2),
        [],
        (WORK_FIRST, WORK_BYTES),
    )
    pnts, halo_pnts, slack = call(
        "points",
        functools.partial(points_kernel, blocks),
        (
            (
                sds((blocks, 16, 2 * BLK), BF16), sds((2 * blocks, 16, 2 * BLK), BF16), sds((6 * blocks, BLK), F32),
            ),
            0,
        ),
        ((mine, above, below, w), 0),
        [((blocks * 16, BLK), F32)],
        (WORK_NEXT, WORK_BYTES),
    )
    (result,) = call(
        "last",
        functools.partial(last_kernel, blocks, slabs, points, all_probes),
        ((sds((probes + 3, ext), F32),), 0),
        (
            (
                place, inner_plan, outer_plan, w, up, down, stats, *q, mine, above, below, *ab, held(slopes), left_own, left_halo,
                right, pnts, halo_pnts, slack,
            ),
            3,
        ),
        [
            ((blocks, 16, BLK), F32),
            ((blocks, BLK, 4 * probes), BF16),
            ((2 * blocks, BLK, 4 * probes), BF16),
            ((blocks, 4 * probes, BLK), BF16),
            ((slots, 2 * BLK, BLK), BF16),
        ],
        (WORK_FIRST, WORK_BYTES),
        limit=LIMIT_MIB * 3 // 2,
    )

    other = shifted(result, "sub", subs, 1)
    (grad,) = call("pair", pair_kernel, ((sds((3, width), F32),), 0), ((result, other), 0), [], (1000, 1000))
    if outer == 2:
        coord_grad = grad + shifted(grad, "probe", outer, 1)
    else:
        coord_grad = lax.psum(grad, "probe")
    last_basis, alphas, betas = call(
        "close",
        close_kernel,
        (
            (
                sds((subs * probes, width), F32), sds((ITERS, subs * probes), F32), sds((ITERS, subs * probes), F32),
            ),
            0,
        ),
        ((place, result, other), 1),
        [],
        (1000000, 1000000),
    )
    return alphas, betas, last_basis, coord_grad


def solution(mesh):
    return jax.shard_map(
        body,
        mesh=mesh,
        in_specs=(
            P(None, ("groups", "blk")),
            P(("groups", "blk")),
            P("probe", ("groups", "blk")),
            P(("groups", "blk"), "sub", None),
            P(("groups", "blk"), "sub", None),
            P(("groups", "blk"), "sub"),
        ),
        out_specs=(
            P(None, ("groups", "probe")),
            P(None, ("groups", "probe")),
            P("probe", ("groups", "blk")),
            P(None, ("groups", "blk")),
        ),
        check_vma=False,
    )
```

```python
import functools
import math

import jax
import jax.numpy as jnp
from jax import lax
from jax.experimental import pallas as pl
from jax.experimental.pallas import tpu as pltpu
from jax.sharding import PartitionSpec as P

ITERS = 3
SIGNAL_VAR = 0.1
LENGTH_SQ = 2.0
TAPER_SQ = 16.0
WARP_GAIN = 0.4
EPSILON = 1e-06

BLK = 128
LANES = 128
FEATS = 32
GROUP = 16
TAIL = 8
LIST_ROWS = 8
LIMIT_MIB = 16
KEPT = 256
WORK_FIRST = 300000000
WORK_NEXT = 100000000
WORK_BYTES = 4000000

DECAY = TAPER_SQ / (2.0 * LENGTH_SQ)
Z_TOP = math.sqrt(SIGNAL_VAR * math.exp(-DECAY))
Z_RATE = DECAY / Z_TOP
Z_OF_D = -Z_TOP / TAPER_SQ
Z_STEP = 4.0 * LENGTH_SQ / TAPER_SQ * Z_TOP

F32 = jnp.float32
BF16 = jnp.bfloat16


def split_two(x):
    high = x.astype(BF16)
    low = (x - high.astype(F32)).astype(BF16)
    return high, low


def split_three(x):
    one = x.astype(BF16).astype(F32)
    rest = x - one
    two = rest.astype(BF16).astype(F32)
    three = (rest - two).astype(BF16).astype(F32)
    return one, two, three


def warp(x):
    return x + WARP_GAIN * jnp.tanh(x)


def mxu(a, b):
    return lax.dot_general(a, b, (((1,), (0,)), ((), ())), preferred_element_type=F32)


def put_stats(ref, base, w_of, q_of, qq, qw, blocks):
    alpha_s = qw / jnp.maximum(qq, 1e-30)
    acc = jnp.zeros((qq.shape[0], LANES), F32)
    for b in range(blocks):
        r = w_of(b) - alpha_s * q_of(b)
        acc = acc + r * r
    res = jnp.sum(acc, axis=1, keepdims=True)
    lane = lax.broadcasted_iota(jnp.int32, (qq.shape[0], LANES), 1)
    out = jnp.where(lane == 0, qw, jnp.where(lane == 1, qq, jnp.where(lane == 2, res, 0.0)))
    ref[:, base : base + LANES] = out


def mxu_turned(a, b):
    return lax.dot_general(a, b, (((1,), (1,)), ((), ())), preferred_element_type=F32)


def fold(out, probes):
    if out.shape[0] > probes:
        return out[:probes] + out[probes:]
    return out


def fold_turned(out, probes):
    total = out[:probes, :BLK] + out[:probes, BLK:]
    if out.shape[0] > probes:
        total = total + out[probes:, :BLK]
    return total


def stack_vec(q, exact):
    if exact:
        high = q.astype(BF16)
        return jnp.concatenate([high, high], axis=1)
    high, low = split_two(q)
    return jnp.concatenate(
        [jnp.concatenate([high, high], axis=1), jnp.concatenate([low, jnp.zeros_like(low)], axis=1)], axis=0
    )


def stack_tile(tile):
    return jnp.concatenate(split_two(tile), axis=0)


def ranges(first, last, body):
    long = (last - first) // GROUP
    middle = first + long * GROUP

    def big(g, carry):
        body(first + g * GROUP, GROUP)
        return carry

    def small(g, carry):
        body(middle + g * TAIL, TAIL)
        return carry

    lax.fori_loop(0, long, big, 0)
    lax.fori_loop(0, (last - middle) // TAIL, small, 0)


def kept_and_made(total, room, body, kept, made):
    first = jnp.minimum(total, room)
    ranges(0, first, functools.partial(body, kept))
    many = (total - first) // TAIL

    def rest(g, carry):
        body(made, first + g * TAIL, TAIL)
        return carry

    lax.fori_loop(0, many, rest, 0)


def inner_edges(acc, vecs, plan, kept, made):
    acc[...] = jnp.zeros_like(acc)
    size = acc.shape[1]

    def group(tile_of, start, many):
        outs = []
        for u in range(many):
            slot = start + u
            a = plan[0, slot]
            c = plan[1, slot]
            times = plan[2, slot].astype(F32)
            tile = tile_of(slot, a, c)
            outs.append((c, fold(mxu(vecs[a], tile), size) * times))
            outs.append((a, fold_turned(mxu_turned(vecs[c][:, :BLK], tile), size) * times))
        for c, out in outs:
            acc[c] = acc[c] + out

    kept_and_made(plan[3, 0], KEPT, group, kept, made)


def outer_edges(acc, vecs, plan, base, kept, made):
    size = acc.shape[1]

    def group(tile_of, start, many):
        outs = []
        for u in range(many):
            at = start + u
            a = plan[0, at]
            c = plan[1, at]
            times = plan[2, at].astype(F32)
            outs.append((c, fold(mxu(vecs[a], tile_of(base + at, a, c)), size) * times))
        for c, out in outs:
            acc[c] = acc[c] + out

    kept_and_made(plan[3, 0], jnp.maximum(KEPT - base, 0), group, kept, made)


def tile_value(z):
    z = jnp.maximum(z, 0.0)
    return jnp.exp(z * Z_RATE) * (z * z)


def slope_value(z):
    z = jnp.maximum(z, 0.0)
    return (jnp.exp(z * Z_RATE) * z) * (z + Z_STEP)


def fill(into, base, plan, make):
    def body(start, many):
        for u in range(many):
            at = start + u
            into[base + at] = make(base + at, plan[0, at], plan[1, at])

    ranges(0, jnp.minimum(plan[3, 0], jnp.maximum(KEPT - base, 0)), body)


def maker(left, right):
    return lambda slot, a, c: stack_tile(tile_value(mxu(left[a], right[c])))


def keeper(tiles):
    return lambda slot, a, c: tiles[slot]


def whole(n):
    return jnp.floor((n + (TAIL - 1)) * (1.0 / TAIL)) * TAIL


def keys(lists, blocks, cross):
    out = []
    whole_lists = lists.astype(jnp.int32)
    for at in (0, 3):
        a = whole_lists[at : at + 1]
        c = whole_lists[at + 1 : at + 2]
        live = lax.broadcasted_iota(jnp.int32, a.shape, 1) < whole_lists[at + 2 : at + 3]
        if cross:
            out.append(jnp.where(live & (c >= blocks), a * blocks + c - blocks, -1))
        else:
            out.append(jnp.where(live & (c < blocks), a * blocks + c, -1))
    return jnp.concatenate(out, axis=1)


def compact(key, blocks, slots, first):
    size = blocks * blocks
    hot = jnp.where(lax.broadcasted_iota(jnp.int32, (size, key.shape[1]), 0) == key, 1.0, 0.0).astype(BF16)
    counts = mxu(hot, jnp.ones((key.shape[1], LANES), BF16))
    flags = jnp.minimum(counts, 1.0)
    shape = (size, size)
    ahead = lax.broadcasted_iota(jnp.int32, shape, 0) > lax.broadcasted_iota(jnp.int32, shape, 1)
    place = mxu(jnp.where(ahead, 1.0, 0.0).astype(BF16), flags.astype(BF16)) + first
    index = lax.broadcasted_iota(jnp.int32, (16, size), 1).astype(F32)
    row = jnp.floor((index + 0.5) * (1.0 / blocks))
    line = lax.broadcasted_iota(jnp.int32, (16, size), 0)
    names = jnp.where(line == 0, row, jnp.where(line == 1, index - row * blocks, 1.0)).astype(BF16)
    found = []
    times = []
    for part in range(slots // LANES):
        lane = (lax.broadcasted_iota(jnp.int32, (size, LANES), 1) + part * LANES).astype(F32)
        here = (place == lane) & (flags > 0.5)
        found.append(mxu(names, jnp.where(here, 1.0, 0.0).astype(BF16)))
        times.append(mxu(names, jnp.where(here, counts, 0.0).astype(BF16))[2:3])
    found = jnp.concatenate(found, axis=1)
    end = place[size - 1 :] + flags[size - 1 :]
    return found[0:1], found[1:2], found[2:3], jnp.concatenate(times, axis=1), end


def put_plan(ref, rows):
    ref[...] = jnp.zeros(ref.shape, ref.dtype)
    for at, row in enumerate(rows):
        ref[at : at + 1, :] = row.astype(ref.dtype)


def to_smem(pairs, sems):
    moves = [pltpu.make_async_copy(source, target, sems.at[at]) for at, (source, target) in enumerate(pairs)]
    for move in moves:
        move.start()
    return moves


def spread(row, width):
    return jnp.concatenate([row] * (width // LANES), axis=1)


def side_features(blocks, coords, kinds, left, right):
    x = warp(coords)
    scale = -2.0 * Z_OF_D
    square = x * x
    norm = Z_OF_D * (square[:blocks] + square[blocks : 2 * blocks] + square[2 * blocks :])
    x1, x2, x3 = split_three(x)
    n1, n2, n3 = split_three(norm)
    m1, m2, m3 = split_three(norm + Z_TOP)
    one = jnp.ones_like(norm)
    pad = jnp.zeros(((FEATS - 24) * blocks, BLK), F32)
    kinds[...] = jnp.concatenate([x1, x1, x2, x2, x1, x3, n1, n2, n3, one, one, one, pad], axis=0)
    for g in range(0, blocks, 4):
        stack = [kinds[pl.ds(b, FEATS, stride=blocks), :] for b in range(g, g + 4)]
        turned = jnp.concatenate(stack, axis=0).T.astype(BF16)
        for b in range(4):
            left[g + b] = turned[:, b * FEATS : (b + 1) * FEATS]
    if right is not None:
        y1, y2, y3 = split_three(x * scale)
        kinds[...] = jnp.concatenate([y1, y2, y1, y2, y3, y1, one, one, one, m1, m2, m3, pad], axis=0)
        for b in range(blocks):
            right[b] = kinds[pl.ds(b, FEATS, stride=blocks), :].astype(BF16)


def rows_of(packed, blocks):
    lists = packed.shape[0] - LIST_ROWS
    coords = lists - 3 * blocks
    return coords // blocks, coords, lists


def pack_kernel(
    blocks, place, tile_rows, tile_cols, tile_count, signs, coords, noise,
    lists, mine, noise_here, got_signs, got_coords, got_rows, got_cols, sems,
):
    probes, coord_row, list_row = rows_of(mine, blocks)
    first = pl.multiple_of(place[1] * probes, probes)
    moves = [
        pltpu.make_async_copy(coords, got_coords, sems.at[0]),
        pltpu.make_async_copy(signs.at[pl.ds(first, probes), :], got_signs, sems.at[1]),
        pltpu.make_async_copy(tile_rows, got_rows, sems.at[2]),
        pltpu.make_async_copy(tile_cols, got_cols, sems.at[3]),
        pltpu.make_async_copy(noise, noise_here, sems.at[4]),
    ]
    for move in moves:
        move.start()
    lists[...] = jnp.zeros(lists.shape, F32)
    lists[2:3, :] = jnp.full((1, LANES), tile_count[0], jnp.int32).astype(F32)
    for move in moves[2:4]:
        move.wait()
    lists[0:1, : tile_rows.shape[1]] = got_rows[...].astype(F32)
    lists[1:2, : tile_cols.shape[1]] = got_cols[...].astype(F32)
    mine[list_row:] = lists[...]
    moves[0].wait()
    for c in range(3):
        for b in range(blocks):
            at = coord_row + c * blocks + b
            mine[at : at + 1] = got_coords[c : c + 1, b * BLK : (b + 1) * BLK]
    moves[1].wait()
    for b in range(blocks):
        mine[b * probes : (b + 1) * probes] = got_signs[:, b * BLK : (b + 1) * BLK].astype(F32)
    moves[4].wait()


def join_kernel(sibling, old, mine):
    del old
    at = mine.shape[0] - LIST_ROWS + 3
    mine[at : at + 3] = sibling[0:3]


def first_inner_kernel(
    blocks, mine,
    held_plan, tiles, z_ref, cross, left, right, acc, vecs, plan, kinds, sem,
):
    probes, coord_row, list_row = rows_of(mine, blocks)
    lists = mine[list_row:]
    row, col, _, times, end = compact(keys(lists, blocks, False), blocks, held_plan.shape[1], 0.0)
    put_plan(held_plan, (row, col, times, spread(whole(end), held_plan.shape[1])))
    move = pltpu.make_async_copy(held_plan, plan, sem)
    move.start()
    row, col, _, times, end = compact(keys(lists, blocks, True), blocks, cross.shape[1], 0.0)
    put_plan(cross, (col, row, times, spread(end, cross.shape[1])))
    for b in range(blocks):
        vecs[b] = stack_vec(mine[b * probes : (b + 1) * probes], True)
    side_features(blocks, mine[coord_row:list_row], kinds, left, right)
    move.wait()
    fill(tiles, 0, plan, maker(left, right))
    inner_edges(acc, vecs, plan, keeper(tiles), maker(left, right))
    z_ref[...] = acc[:blocks]


def finish_apply(blocks, acc, z_of, w_ref, q_of, prev_of, beta, noise):
    probes = acc.shape[1]
    qq = jnp.zeros((probes, LANES), F32)
    qw = jnp.zeros((probes, LANES), F32)
    for b in range(blocks):
        q = q_of(b)
        part = slice(b * BLK, (b + 1) * BLK)
        w = acc[b] + z_of(b) + noise[b : b + 1] * q
        if prev_of is not None:
            w = w - beta * prev_of(b)
        w_ref[:, part] = w
        qq = qq + q * q
        qw = qw + q * w
    put_stats(
        w_ref,
        blocks * BLK,
        lambda b: w_ref[:, b * BLK : (b + 1) * BLK],
        q_of,
        jnp.sum(qq, axis=1, keepdims=True),
        jnp.sum(qw, axis=1, keepdims=True),
        blocks,
    )


def first_outer_kernel(
    blocks, inner_plan, old_tiles, mine, above, below, noise, z_ref, right, cross,
    held_plan, tiles, w_ref, left, acc, vecs, inner_smem, plan, kinds, sems,
):
    probes, coord_row, list_row = rows_of(mine, blocks)
    del old_tiles
    slots = held_plan.shape[1]
    row, col, one, times, end = compact(keys(below[list_row:], blocks, True), blocks, slots, cross[3:4, :LANES])
    put_plan(
        held_plan,
        (cross[0:1] + row + blocks * one, cross[1:2] + col, cross[2:3] + times, spread(whole(end), slots)),
    )
    moves = to_smem(((inner_plan, inner_smem), (held_plan, plan)), sems)
    for part, ref in enumerate((above, below)):
        side_features(blocks, ref[coord_row:list_row], kinds, left.at[part * blocks : (part + 1) * blocks], None)
        for b in range(blocks):
            vecs[part * blocks + b] = stack_vec(ref[b * probes : (b + 1) * probes], True)
    acc[...] = jnp.zeros_like(acc)
    for move in moves:
        move.wait()
    base = inner_smem[3, 0]
    fill(tiles, base, plan, maker(left, right))
    outer_edges(acc, vecs, plan, base, keeper(tiles), maker(left, right))
    finish_apply(
        blocks, acc, lambda b: z_ref[b], w_ref, lambda b: mine[b * probes : (b + 1) * probes], None, None, noise
    )


def slab_alpha(w_ref, blocks):
    sums = w_ref[:, blocks * BLK : (blocks + 1) * BLK]
    return sums[:, 0:1] / jnp.maximum(sums[:, 1:2], 1e-30)


def inner_kernel(blocks, plan, w_ref, q_own, tiles, left, right, z_ref, acc, vecs):
    alpha = slab_alpha(w_ref, blocks)
    probes = w_ref.shape[0]
    for b in range(blocks):
        vecs[b] = stack_vec(w_ref[:, b * BLK : (b + 1) * BLK] - alpha * block_of(q_own, probes, b), False)
    inner_edges(acc, vecs, plan, keeper(tiles), maker(left, right))
    z_ref[...] = acc[:blocks]


def alpha_beta(stats, points):
    qw = [s[:, 0:1] for s in stats]
    qq = [s[:, 1:2] for s in stats]
    res = [s[:, 2:3] for s in stats]
    alpha = functools.reduce(jnp.add, qw) / points
    total = jnp.zeros_like(alpha)
    for w, q, r in zip(qw, qq, res):
        gap = alpha - w / jnp.maximum(q, 1e-30)
        total = total + (r + gap * gap * q)
    return alpha, jnp.sqrt(total / points + EPSILON)


def global_alpha_beta(slabs, points, place, stats_ref):
    order = [stats_ref[lax.rem(slab - place[0] + slabs, slabs)] for slab in range(slabs)]
    return alpha_beta(order, points)


def add_ab(ref, base, old_ab, step, alpha, beta):
    shape = (alpha.shape[0], LANES)
    lane = lax.broadcasted_iota(jnp.int32, shape, 1)
    out = jnp.zeros(shape, F32) if old_ab is None else old_ab[...]
    out = jnp.where(lane == step, alpha, out)
    ref[:, base : base + LANES] = jnp.where(lane == ITERS + step, beta, out)


def block_of(ref, rows, b):
    if len(ref.shape) == 3:
        return ref[b]
    return ref[b * rows : (b + 1) * rows]


def outer_kernel(
    blocks, slabs, points, step, place, held_inner, held_outer, mine, above, below, stats_ref,
    q_own, q_above, q_below, z_raw, z_old, noise, tiles, left, right, *rest,
):
    probes = mine.shape[0]
    old_ab = None
    if step > 0:
        old_ab = rest[0]
        rest = rest[1:]
    w_ref, own_ref, above_ref, below_ref, ab_ref, *z_ref, acc, vecs, held_z, inner_plan, plan, sems = rest
    moves = to_smem(((held_inner, inner_plan), (held_outer, plan)), sems)
    alpha, beta = global_alpha_beta(slabs, points, place, stats_ref)
    scale = 1.0 / beta
    apart = alpha - slab_alpha(mine, blocks)
    add_ab(ab_ref, 0, old_ab, step, alpha, beta)
    halves = ((mine, q_own, own_ref), (above, q_above, above_ref), (below, q_below, below_ref))
    for part, (w, old, new) in enumerate(halves):
        for b in range(blocks):
            q = (w[:, b * BLK : (b + 1) * BLK] - alpha * block_of(old, probes, b)) * scale
            new[b] = q
            if part > 0:
                vecs[(part - 1) * blocks + b] = stack_vec(q, False)
            else:
                z = (z_raw[b] - apart * z_old[b]) * scale
                held_z[b] = z
                for ref in z_ref:
                    ref[b] = z
    acc[...] = jnp.zeros_like(acc)
    for move in moves:
        move.wait()
    outer_edges(acc, vecs, plan, inner_plan[3, 0], keeper(tiles), maker(left, right))
    finish_apply(
        blocks, acc, lambda b: held_z[b], w_ref, lambda b: own_ref[b], lambda b: block_of(q_own, probes, b), beta, noise
    )


def slope_kernel(inner_plan, plan, left_own, left_halo, right, after, slopes):
    del after

    def make(left):
        return lambda slot, a, c: slope_value(mxu(left[a], right[c]))

    fill(slopes, 0, inner_plan, make(left_own))
    fill(slopes, inner_plan[3, 0], plan, make(left_halo))


def points_kernel(blocks, pts, pts_above, pts_below, after, pnts, halo_pnts, slack, kinds):
    del after
    _, coord_row, list_row = rows_of(pts, blocks)
    for part, ref in enumerate((pts, pts_above, pts_below)):
        raw = ref[coord_row:list_row]
        bent = jnp.tanh(raw)
        x = raw + WARP_GAIN * bent
        x1, x2, x3 = split_three(x)
        one = jnp.ones((blocks, BLK), F32)
        kinds[...] = jnp.concatenate([x1, x2, x3, one, jnp.zeros((6 * blocks, BLK), F32)], axis=0)
        if part == 0:
            slack[...] = jnp.concatenate([x, 1.0 + WARP_GAIN * (1.0 - bent * bent)], axis=0)
        for b in range(blocks):
            y = kinds[pl.ds(b, 16, stride=blocks), :].astype(BF16)
            y = jnp.concatenate([y, y], axis=1)
            if part == 0:
                pnts[b] = y
            else:
                halo_pnts[(part - 1) * blocks + b] = y


def last_kernel(
    blocks, slabs, points, all_probes, place, held_inner, held_outer, mine, above, below, stats_ref,
    q_own, q_above, q_below, pts, pts_above, pts_below, old_ab, slopes, left_own, left_out, right, pnts, halo_pnts, slack,
    basis_ref, grad_ref, acc, form_left, halo_left, form_right, pulls, inner_plan, plan, sems,
):
    probes, _, _ = rows_of(pts, blocks)
    moves = to_smem(((held_inner, inner_plan), (held_outer, plan)), sems)
    alpha, beta = global_alpha_beta(slabs, points, place, stats_ref)
    scale = 1.0 / beta
    add_ab(basis_ref, blocks * BLK, old_ab, ITERS - 1, alpha, beta)
    for part, (w, old, ref) in enumerate(((mine, q_own, pts), (above, q_above, pts_above), (below, q_below, pts_below))):
        for b in range(blocks):
            part_cols = slice(b * BLK, (b + 1) * BLK)
            u = (w[:, part_cols] - alpha * block_of(old, probes, b)) * scale
            v = ref[b * probes : (b + 1) * probes]
            high = u.astype(BF16).astype(F32)
            low = u - high
            turned = jnp.concatenate([high, low, v, v], axis=0).T.astype(BF16)
            if part == 0:
                basis_ref[:, part_cols] = u
                form_left[b] = turned
                form_right[b] = jnp.concatenate([v, v, high, low], axis=0).astype(BF16)
            else:
                halo_left[(part - 1) * blocks + b] = turned

    def pull(side):
        return lambda slot, a, c: stack_tile(mxu(side[a], form_right[c]) * slopes[slot])

    def pull_made(side, left):
        return lambda slot, a, c: stack_tile(mxu(side[a], form_right[c]) * slope_value(mxu(left[a], right[c])))

    for move in moves:
        move.wait()
    base = inner_plan[3, 0]
    fill(pulls, 0, inner_plan, pull(form_left))
    fill(pulls, base, plan, pull(halo_left))
    inner_edges(acc, pnts, inner_plan, keeper(pulls), pull_made(form_left, left_own))
    outer_edges(acc, halo_pnts, plan, base, keeper(pulls), pull_made(halo_left, left_out))
    for b in range(blocks):
        part_cols = slice(b * BLK, (b + 1) * BLK)
        x = slack[pl.ds(b, 3, stride=blocks), :]
        chain = slack[pl.ds(3 * blocks + b, 3, stride=blocks), :]
        sums = acc[b]
        moved = sums[0:3] + sums[3:6] + sums[6:9] - x * sums[9:10]
        grad_ref[:, part_cols] = moved * chain * (1.0 / (LENGTH_SQ * all_probes))


def pair_kernel(one, two, after, out):
    del after
    out[...] = one[...] + two[...]


def close_kernel(place, own, other, basis_ref, alpha_ref, beta_ref):
    probes = own.shape[0]
    width = basis_ref.shape[1]
    lower = place[1] == 0
    mine = own[...]
    theirs = other[...]
    first = jnp.where(lower, mine, theirs)
    second = jnp.where(lower, theirs, mine)
    basis_ref[:probes] = first[:, :width]
    basis_ref[probes:] = second[:, :width]
    ab = jnp.concatenate([first[:, width:], second[:, width:]], axis=0)
    turned = jnp.concatenate([ab, jnp.zeros((LANES - 2 * probes, LANES), F32)], axis=0).T
    alpha_ref[...] = turned[:ITERS, : 2 * probes]
    beta_ref[...] = turned[ITERS : 2 * ITERS, : 2 * probes]


def vmem(count):
    return [pl.BlockSpec(memory_space=pltpu.VMEM)] * count


def smem(count):
    return [pl.BlockSpec(memory_space=pltpu.SMEM)] * count


def held(array):
    return pltpu.with_memory_space_constraint(array, pltpu.VMEM)


def stays(array):
    return pltpu.with_memory_space_constraint(array, pltpu.HBM)


def in_hbm(count):
    return [pl.BlockSpec(memory_space=pltpu.HBM)] * count


def call(name, kernel, outs, ins, scratch, work, aliases=None, limit=LIMIT_MIB):
    out_shapes, out_scalars = outs
    arrays, scalars = ins
    flops, moved = work
    return pl.pallas_call(
        kernel,
        out_shape=tuple(out_shapes),
        in_specs=smem(scalars) + vmem(len(arrays) - scalars),
        out_specs=tuple(smem(out_scalars) + vmem(len(out_shapes) - out_scalars)),
        scratch_shapes=[pltpu.VMEM(*entry) if isinstance(entry, tuple) else entry for entry in scratch],
        compiler_params=pltpu.CompilerParams(vmem_limit_bytes=limit * 1024 * 1024),
        cost_estimate=pl.CostEstimate(flops=flops, bytes_accessed=moved, transcendentals=0),
        input_output_aliases=aliases or {},
        name=name,
    )(*arrays)


def shifted(value, axes, count, steps):
    return lax.ppermute(value, axes, [(source, (source + steps) % count) for source in range(count)])


def body(coords, noise_var, probe_signs, tile_rows, tile_cols, tile_count):
    slabs = lax.axis_size("blk")
    subs = lax.axis_size("sub")
    outer = lax.axis_size("probe")
    probes = probe_signs.shape[0] // subs
    width = coords.shape[1]
    blocks = width // BLK
    cap = tile_rows.shape[-1]
    points = float(width * slabs)
    all_probes = probe_signs.shape[0] * outer
    sub = lax.axis_index("sub")
    blk = lax.axis_index("blk")
    place = jnp.stack([blk, sub]).astype(jnp.int32)
    sds = jax.ShapeDtypeStruct

    left_shape = sds((blocks, BLK, FEATS), BF16)
    right_shape = sds((blocks, FEATS, BLK), BF16)
    packed = sds((blocks * (probes + 3) + LIST_ROWS, BLK), F32)
    kinds = ((blocks * FEATS, BLK), F32)
    lists, own, noise = pl.pallas_call(
        functools.partial(pack_kernel, blocks),
        out_shape=(sds((LIST_ROWS, LANES), F32), packed, sds((blocks, BLK), F32)),
        in_specs=smem(1) + in_hbm(2) + smem(1) + in_hbm(3),
        out_specs=tuple(vmem(3)),
        scratch_shapes=[
            pltpu.VMEM((probes, width), jnp.int32),
            pltpu.VMEM((3, width), F32),
            pltpu.VMEM((1, cap), jnp.int32),
            pltpu.VMEM((1, cap), jnp.int32),
            pltpu.SemaphoreType.DMA((5,)),
        ],
        compiler_params=pltpu.CompilerParams(vmem_limit_bytes=LIMIT_MIB * 1024 * 1024),
        name="pack",
    )(
        place, stays(tile_rows.reshape(1, cap)), stays(tile_cols.reshape(1, cap)), tile_count.reshape(1),
        stays(probe_signs), stays(coords), stays(noise_var.reshape(blocks, BLK)),
    )
    sibling = shifted(lists, "sub", subs, 1)
    (mine,) = call("join", join_kernel, ((packed,), 0), ((sibling, own), 0), [], (1000, 1000), {1: 0})
    above = shifted(mine, "blk", slabs, -1)
    below = shifted(mine, "blk", slabs, 1)

    ints = jnp.int32
    inner_slots = (blocks * (blocks + 1) // 2 + TAIL + LANES - 1) // LANES * LANES
    outer_slots = (blocks * (blocks + 1) + TAIL + LANES - 1) // LANES * LANES
    plan_shape = sds((LIST_ROWS, inner_slots), ints)
    outer_plan_shape = sds((LIST_ROWS, outer_slots), ints)
    inner_smem = pltpu.SMEM((LIST_ROWS, inner_slots), ints)
    outer_smem = pltpu.SMEM((LIST_ROWS, outer_slots), ints)
    slots = KEPT
    ext = width + LANES
    blocks_f32 = sds((blocks, probes, BLK), F32)
    tile_shape = pltpu.VMEM((slots, 2 * BLK, BLK), BF16)
    acc_shape = ((blocks, probes, BLK), F32)

    inner_plan, tiles, z, cross, left_own, right = call(
        "first_inner",
        functools.partial(first_inner_kernel, blocks),
        ((plan_shape, tile_shape, blocks_f32, sds((LIST_ROWS, outer_slots), F32), left_shape, right_shape), 0),
        ((mine,), 0),
        [
            acc_shape, ((blocks, probes, 2 * BLK), BF16), inner_smem, kinds,
            pltpu.SemaphoreType.DMA,
        ],
        (WORK_FIRST, WORK_BYTES),
    )
    outer_plan, tiles, w, left_halo = call(
        "first_outer",
        functools.partial(first_outer_kernel, blocks),
        ((outer_plan_shape, tile_shape, sds((probes, ext), F32), sds((2 * blocks, BLK, FEATS), BF16)), 0),
        ((inner_plan, held(tiles), mine, above, below, noise, z, right, cross), 0),
        [
            acc_shape, ((2 * blocks, probes, 2 * BLK), BF16), inner_smem, outer_smem, kinds,
            pltpu.SemaphoreType.DMA((2,)),
        ],
        (WORK_FIRST, WORK_BYTES),
        {1: 1},
    )

    def exchange(w):
        stats = w[:, width:]
        if slabs == 4:
            far = shifted(stats, "blk", slabs, 2)
        up = shifted(w, "blk", slabs, -1)
        down = shifted(w, "blk", slabs, 1)
        if slabs == 4:
            rows = jnp.stack([stats, up[:, width:], far, down[:, width:]])
        else:
            rows = lax.all_gather(stats, "blk", axis=0)
            rows = jnp.roll(rows, -blk, axis=0)
        return up, down, rows

    q = (mine, above, below)
    ab = []
    z_old = z
    for step in range(ITERS - 1):
        up, down, stats = exchange(w)
        (z_raw,) = call(
            "inner",
            functools.partial(inner_kernel, blocks),
            ((blocks_f32,), 0),
            ((inner_plan, w, q[0], held(tiles), left_own, right), 1),
            [acc_shape, ((blocks, 2 * probes, 2 * BLK), BF16)],
            (WORK_NEXT, WORK_BYTES),
        )
        w, q0, q1, q2, next_ab, *z = call(
            "outer",
            functools.partial(outer_kernel, blocks, slabs, points, step),
            (
                (
                    sds((probes, ext), F32), blocks_f32, blocks_f32, blocks_f32, sds((probes, LANES), F32),
                    *([blocks_f32] if step < ITERS - 2 else []),
                ),
                0,
            ),
            ((place, inner_plan, outer_plan, w, up, down, stats, *q, z_raw, z_old, noise, held(tiles), left_halo, right, *ab), 1),
            [
                acc_shape, ((2 * blocks, 2 * probes, 2 * BLK), BF16), ((blocks, probes, BLK), F32), inner_smem, outer_smem,
                pltpu.SemaphoreType.DMA((2,)),
            ],
            (WORK_NEXT, WORK_BYTES),
        )
        q = (q0, q1, q2)
        ab = [next_ab]
        z_old = z[0] if z else None

    up, down, stats = exchange(w)
    (slopes,) = call(
        "slopes",
        slope_kernel,
        ((pltpu.VMEM((slots, BLK, BLK), F32),), 0),
        ((inner_plan, outer_plan, left_own, left_halo, right, w), 2),
        [],
        (WORK_FIRST, WORK_BYTES),
    )
    pnts, halo_pnts, slack = call(
        "points",
        functools.partial(points_kernel, blocks),
        (
            (
                sds((blocks, 16, 2 * BLK), BF16), sds((2 * blocks, 16, 2 * BLK), BF16), sds((6 * blocks, BLK), F32),
            ),
            0,
        ),
        ((mine, above, below, w), 0),
        [((blocks * 16, BLK), F32)],
        (WORK_NEXT, WORK_BYTES),
    )
    basis, grad = call(
        "last",
        functools.partial(last_kernel, blocks, slabs, points, all_probes),
        ((sds((probes, ext), F32), sds((3, width), F32)), 0),
        (
            (
                place, inner_plan, outer_plan, w, up, down, stats, *q, mine, above, below, *ab, held(slopes), left_own, left_halo,
                right, pnts, halo_pnts, slack,
            ),
            1,
        ),
        [
            ((blocks, 16, BLK), F32),
            ((blocks, BLK, 4 * probes), BF16),
            ((2 * blocks, BLK, 4 * probes), BF16),
            ((blocks, 4 * probes, BLK), BF16),
            ((slots, 2 * BLK, BLK), BF16),
            inner_smem,
            outer_smem,
            pltpu.SemaphoreType.DMA((2,)),
        ],
        (WORK_FIRST, WORK_BYTES),
        limit=LIMIT_MIB * 3 // 2,
    )

    other = shifted(basis, "sub", subs, 1)
    if outer == 2:
        across = shifted(grad, "probe", outer, 1)
        (grad,) = call("pair", pair_kernel, ((sds((3, width), F32),), 0), ((grad, across, other), 0), [], (1000, 1000))
    else:
        grad = lax.psum(grad, "probe")
    coord_grad = grad + shifted(grad, "sub", subs, 1)
    last_basis, alphas, betas = call(
        "close",
        close_kernel,
        (
            (
                sds((subs * probes, width), F32), sds((ITERS, subs * probes), F32), sds((ITERS, subs * probes), F32),
            ),
            0,
        ),
        ((place, basis, other), 1),
        [],
        (1000000, 1000000),
    )
    return alphas, betas, last_basis, coord_grad


def solution(mesh):
    return jax.shard_map(
        body,
        mesh=mesh,
        in_specs=(
            P(None, ("groups", "blk")),
            P(("groups", "blk")),
            P("probe", ("groups", "blk")),
            P(("groups", "blk"), "sub", None),
            P(("groups", "blk"), "sub", None),
            P(("groups", "blk"), "sub"),
        ),
        out_specs=(
            P(None, ("groups", "probe")),
            P(None, ("groups", "probe")),
            P("probe", ("groups", "blk")),
            P(None, ("groups", "blk")),
        ),
        check_vma=False,
    )
```

```python
import functools
import math

import jax
import jax.numpy as jnp
from jax import lax
from jax.experimental import pallas as pl
from jax.experimental.pallas import tpu as pltpu
from jax.sharding import PartitionSpec as P

ITERS = 3
SIGNAL_VAR = 0.1
LENGTH_SQ = 2.0
TAPER_SQ = 16.0
WARP_GAIN = 0.4
EPSILON = 1e-06

BLK = 128
LANES = 128
FEATS = 32
GROUP = 16
TAIL = 8
LIST_ROWS = 8
LIMIT_MIB = 16
KEPT = 256
WORK_FIRST = 300000000
WORK_NEXT = 100000000
WORK_BYTES = 4000000

DECAY = TAPER_SQ / (2.0 * LENGTH_SQ)
Z_TOP = math.sqrt(SIGNAL_VAR * math.exp(-DECAY))
Z_RATE = DECAY / Z_TOP
Z_OF_D = -Z_TOP / TAPER_SQ
Z_STEP = 4.0 * LENGTH_SQ / TAPER_SQ * Z_TOP

F32 = jnp.float32
BF16 = jnp.bfloat16


def split_two(x):
    high = x.astype(BF16)
    low = (x - high.astype(F32)).astype(BF16)
    return high, low


def split_three(x):
    one = x.astype(BF16).astype(F32)
    rest = x - one
    two = rest.astype(BF16).astype(F32)
    three = (rest - two).astype(BF16).astype(F32)
    return one, two, three


def warp(x):
    return x + WARP_GAIN * jnp.tanh(x)


def mxu(a, b):
    return lax.dot_general(a, b, (((1,), (0,)), ((), ())), preferred_element_type=F32)


def put_stats(ref, base, w_of, q_of, qq, qw, blocks):
    alpha_s = qw / jnp.maximum(qq, 1e-30)
    acc = jnp.zeros((qq.shape[0], LANES), F32)
    for b in range(blocks):
        r = w_of(b) - alpha_s * q_of(b)
        acc = acc + r * r
    res = jnp.sum(acc, axis=1, keepdims=True)
    lane = lax.broadcasted_iota(jnp.int32, (qq.shape[0], LANES), 1)
    out = jnp.where(lane == 0, qw, jnp.where(lane == 1, qq, jnp.where(lane == 2, res, 0.0)))
    ref[:, base : base + LANES] = out


def mxu_turned(a, b):
    return lax.dot_general(a, b, (((1,), (1,)), ((), ())), preferred_element_type=F32)


def fold(out, probes):
    if out.shape[0] > probes:
        return out[:probes] + out[probes:]
    return out


def fold_turned(out, probes):
    total = out[:probes, :BLK] + out[:probes, BLK:]
    if out.shape[0] > probes:
        total = total + out[probes:, :BLK]
    return total


def stack_vec(q, exact):
    if exact:
        high = q.astype(BF16)
        return jnp.concatenate([high, high], axis=1)
    high, low = split_two(q)
    return jnp.concatenate(
        [jnp.concatenate([high, high], axis=1), jnp.concatenate([low, jnp.zeros_like(low)], axis=1)], axis=0
    )


def stack_tile(tile):
    return jnp.concatenate(split_two(tile), axis=0)


def ranges(first, last, body):
    long = (last - first) // GROUP
    middle = first + long * GROUP

    def big(g, carry):
        body(first + g * GROUP, GROUP)
        return carry

    def small(g, carry):
        body(middle + g * TAIL, TAIL)
        return carry

    lax.fori_loop(0, long, big, 0)
    lax.fori_loop(0, (last - middle) // TAIL, small, 0)


def kept_and_made(total, room, body, kept, made):
    first = jnp.minimum(total, room)
    ranges(0, first, functools.partial(body, kept))
    many = (total - first) // TAIL

    def rest(g, carry):
        body(made, first + g * TAIL, TAIL)
        return carry

    lax.fori_loop(0, many, rest, 0)


def inner_edges(acc, vecs, plan, kept, made):
    acc[...] = jnp.zeros_like(acc)
    size = acc.shape[1]

    def group(tile_of, start, many):
        outs = []
        for u in range(many):
            slot = start + u
            a = plan[0, slot]
            c = plan[1, slot]
            times = plan[2, slot].astype(F32)
            tile = tile_of(slot, a, c)
            outs.append((c, fold(mxu(vecs[a], tile), size) * times))
            outs.append((a, fold_turned(mxu_turned(vecs[c][:, :BLK], tile), size) * times))
        for c, out in outs:
            acc[c] = acc[c] + out

    kept_and_made(plan[3, 0], KEPT, group, kept, made)


def outer_edges(acc, vecs, plan, base, kept, made):
    size = acc.shape[1]

    def group(tile_of, start, many):
        outs = []
        for u in range(many):
            at = start + u
            a = plan[0, at]
            c = plan[1, at]
            times = plan[2, at].astype(F32)
            outs.append((c, fold(mxu(vecs[a], tile_of(base + at, a, c)), size) * times))
        for c, out in outs:
            acc[c] = acc[c] + out

    kept_and_made(plan[3, 0], jnp.maximum(KEPT - base, 0), group, kept, made)


def tile_value(z):
    z = jnp.maximum(z, 0.0)
    return jnp.exp(z * Z_RATE) * (z * z)


def slope_value(z):
    z = jnp.maximum(z, 0.0)
    return (jnp.exp(z * Z_RATE) * z) * (z + Z_STEP)


def fill(into, base, plan, make):
    def body(start, many):
        for u in range(many):
            at = start + u
            into[base + at] = make(base + at, plan[0, at], plan[1, at])

    ranges(0, jnp.minimum(plan[3, 0], jnp.maximum(KEPT - base, 0)), body)


def maker(left, right):
    return lambda slot, a, c: stack_tile(tile_value(mxu(left[a], right[c])))


def keeper(tiles):
    return lambda slot, a, c: tiles[slot]


def whole(n):
    return jnp.floor((n + (TAIL - 1)) * (1.0 / TAIL)) * TAIL


def keys(lists, blocks, cross):
    out = []
    whole_lists = lists.astype(jnp.int32)
    for at in (0, 3):
        a = whole_lists[at : at + 1]
        c = whole_lists[at + 1 : at + 2]
        live = lax.broadcasted_iota(jnp.int32, a.shape, 1) < whole_lists[at + 2 : at + 3]
        if cross:
            out.append(jnp.where(live & (c >= blocks), a * blocks + c - blocks, -1))
        else:
            out.append(jnp.where(live & (c < blocks), a * blocks + c, -1))
    return jnp.concatenate(out, axis=1)


def compact(key, blocks, slots, first):
    size = blocks * blocks
    hot = jnp.where(lax.broadcasted_iota(jnp.int32, (size, key.shape[1]), 0) == key, 1.0, 0.0).astype(BF16)
    counts = mxu(hot, jnp.ones((key.shape[1], LANES), BF16))
    flags = jnp.minimum(counts, 1.0)
    shape = (size, size)
    ahead = lax.broadcasted_iota(jnp.int32, shape, 0) > lax.broadcasted_iota(jnp.int32, shape, 1)
    place = mxu(jnp.where(ahead, 1.0, 0.0).astype(BF16), flags.astype(BF16)) + first
    index = lax.broadcasted_iota(jnp.int32, (16, size), 1).astype(F32)
    row = jnp.floor((index + 0.5) * (1.0 / blocks))
    line = lax.broadcasted_iota(jnp.int32, (16, size), 0)
    names = jnp.where(line == 0, row, jnp.where(line == 1, index - row * blocks, 1.0)).astype(BF16)
    found = []
    times = []
    for part in range(slots // LANES):
        lane = (lax.broadcasted_iota(jnp.int32, (size, LANES), 1) + part * LANES).astype(F32)
        here = (place == lane) & (flags > 0.5)
        found.append(mxu(names, jnp.where(here, 1.0, 0.0).astype(BF16)))
        times.append(mxu(names, jnp.where(here, counts, 0.0).astype(BF16))[2:3])
    found = jnp.concatenate(found, axis=1)
    end = place[size - 1 :] + flags[size - 1 :]
    return found[0:1], found[1:2], found[2:3], jnp.concatenate(times, axis=1), end


def put_plan(ref, rows):
    ref[...] = jnp.zeros(ref.shape, ref.dtype)
    for at, row in enumerate(rows):
        ref[at : at + 1, :] = row.astype(ref.dtype)


def spread(row, width):
    return jnp.concatenate([row] * (width // LANES), axis=1)


def side_features(blocks, coords, kinds, left, right):
    x = warp(coords)
    scale = -2.0 * Z_OF_D
    square = x * x
    norm = Z_OF_D * (square[:blocks] + square[blocks : 2 * blocks] + square[2 * blocks :])
    x1, x2, x3 = split_three(x)
    n1, n2, n3 = split_three(norm)
    m1, m2, m3 = split_three(norm + Z_TOP)
    one = jnp.ones_like(norm)
    pad = jnp.zeros(((FEATS - 24) * blocks, BLK), F32)
    kinds[...] = jnp.concatenate([x1, x1, x2, x2, x1, x3, n1, n2, n3, one, one, one, pad], axis=0)
    for g in range(0, blocks, 4):
        stack = [kinds[pl.ds(b, FEATS, stride=blocks), :] for b in range(g, g + 4)]
        turned = jnp.concatenate(stack, axis=0).T.astype(BF16)
        for b in range(4):
            left[g + b] = turned[:, b * FEATS : (b + 1) * FEATS]
    if right is not None:
        y1, y2, y3 = split_three(x * scale)
        kinds[...] = jnp.concatenate([y1, y2, y1, y2, y3, y1, one, one, one, m1, m2, m3, pad], axis=0)
        for b in range(blocks):
            right[b] = kinds[pl.ds(b, FEATS, stride=blocks), :].astype(BF16)


def rows_of(packed, blocks):
    lists = packed.shape[0] - LIST_ROWS
    coords = lists - 3 * blocks
    return coords // blocks, coords, lists


def pack_kernel(
    blocks, place, tile_rows, tile_cols, tile_count, signs, coords, noise,
    lists, mine, noise_here, got_signs, got_coords, got_rows, got_cols, sems,
):
    probes, coord_row, list_row = rows_of(mine, blocks)
    first = pl.multiple_of(place[1] * probes, probes)
    moves = [
        pltpu.make_async_copy(coords, got_coords, sems.at[0]),
        pltpu.make_async_copy(signs.at[pl.ds(first, probes), :], got_signs, sems.at[1]),
        pltpu.make_async_copy(tile_rows, got_rows, sems.at[2]),
        pltpu.make_async_copy(tile_cols, got_cols, sems.at[3]),
        pltpu.make_async_copy(noise, noise_here, sems.at[4]),
    ]
    for move in moves:
        move.start()
    lists[...] = jnp.zeros(lists.shape, F32)
    lists[2:3, :] = jnp.full((1, LANES), tile_count[0], jnp.int32).astype(F32)
    for move in moves[2:4]:
        move.wait()
    lists[0:1, : tile_rows.shape[1]] = got_rows[...].astype(F32)
    lists[1:2, : tile_cols.shape[1]] = got_cols[...].astype(F32)
    mine[list_row:] = lists[...]
    moves[0].wait()
    for c in range(3):
        for b in range(blocks):
            at = coord_row + c * blocks + b
            mine[at : at + 1] = got_coords[c : c + 1, b * BLK : (b + 1) * BLK]
    moves[1].wait()
    for b in range(blocks):
        mine[b * probes : (b + 1) * probes] = got_signs[:, b * BLK : (b + 1) * BLK].astype(F32)
    moves[4].wait()


def join_kernel(sibling, old, mine):
    del old
    at = mine.shape[0] - LIST_ROWS + 3
    mine[at : at + 3] = sibling[0:3]


def first_inner_kernel(
    blocks, mine,
    held_plan, tiles, z_ref, cross, left, right, acc, vecs, plan, kinds, sem,
):
    probes, coord_row, list_row = rows_of(mine, blocks)
    lists = mine[list_row:]
    row, col, _, times, end = compact(keys(lists, blocks, False), blocks, held_plan.shape[1], 0.0)
    put_plan(held_plan, (row, col, times, spread(whole(end), held_plan.shape[1])))
    move = pltpu.make_async_copy(held_plan, plan, sem)
    move.start()
    row, col, _, times, end = compact(keys(lists, blocks, True), blocks, cross.shape[1], 0.0)
    put_plan(cross, (col, row, times, spread(end, cross.shape[1])))
    for b in range(blocks):
        vecs[b] = stack_vec(mine[b * probes : (b + 1) * probes], True)
    side_features(blocks, mine[coord_row:list_row], kinds, left, right)
    move.wait()
    fill(tiles, 0, plan, maker(left, right))
    inner_edges(acc, vecs, plan, keeper(tiles), maker(left, right))
    z_ref[...] = acc[:blocks]


def finish_apply(blocks, acc, z_of, w_ref, q_of, prev_of, beta, noise):
    probes = acc.shape[1]
    qq = jnp.zeros((probes, LANES), F32)
    qw = jnp.zeros((probes, LANES), F32)
    for b in range(blocks):
        q = q_of(b)
        part = slice(b * BLK, (b + 1) * BLK)
        w = acc[b] + z_of(b) + noise[b : b + 1] * q
        if prev_of is not None:
            w = w - beta * prev_of(b)
        w_ref[:, part] = w
        qq = qq + q * q
        qw = qw + q * w
    put_stats(
        w_ref,
        blocks * BLK,
        lambda b: w_ref[:, b * BLK : (b + 1) * BLK],
        q_of,
        jnp.sum(qq, axis=1, keepdims=True),
        jnp.sum(qw, axis=1, keepdims=True),
        blocks,
    )


def first_outer_kernel(
    blocks, inner_plan, old_tiles, mine, above, below, noise, z_ref, right, cross,
    held_plan, tiles, w_ref, left, acc, vecs, plan, kinds, sem,
):
    probes, coord_row, list_row = rows_of(mine, blocks)
    del old_tiles
    slots = held_plan.shape[1]
    row, col, one, times, end = compact(keys(below[list_row:], blocks, True), blocks, slots, cross[3:4, :LANES])
    put_plan(
        held_plan,
        (cross[0:1] + row + blocks * one, cross[1:2] + col, cross[2:3] + times, spread(whole(end), slots)),
    )
    move = pltpu.make_async_copy(held_plan, plan, sem)
    move.start()
    for part, ref in enumerate((above, below)):
        side_features(blocks, ref[coord_row:list_row], kinds, left.at[part * blocks : (part + 1) * blocks], None)
        for b in range(blocks):
            vecs[part * blocks + b] = stack_vec(ref[b * probes : (b + 1) * probes], True)
    acc[...] = jnp.zeros_like(acc)
    move.wait()
    base = inner_plan[3, 0]
    fill(tiles, base, plan, maker(left, right))
    outer_edges(acc, vecs, plan, base, keeper(tiles), maker(left, right))
    finish_apply(
        blocks, acc, lambda b: z_ref[b], w_ref, lambda b: mine[b * probes : (b + 1) * probes], None, None, noise
    )


def slab_alpha(w_ref, blocks):
    sums = w_ref[:, blocks * BLK : (blocks + 1) * BLK]
    return sums[:, 0:1] / jnp.maximum(sums[:, 1:2], 1e-30)


def inner_kernel(blocks, plan, w_ref, q_own, tiles, left, right, z_ref, acc, vecs):
    alpha = slab_alpha(w_ref, blocks)
    probes = w_ref.shape[0]
    for b in range(blocks):
        vecs[b] = stack_vec(w_ref[:, b * BLK : (b + 1) * BLK] - alpha * block_of(q_own, probes, b), False)
    inner_edges(acc, vecs, plan, keeper(tiles), maker(left, right))
    z_ref[...] = acc[:blocks]


def alpha_beta(stats, points):
    qw = [s[:, 0:1] for s in stats]
    qq = [s[:, 1:2] for s in stats]
    res = [s[:, 2:3] for s in stats]
    alpha = functools.reduce(jnp.add, qw) / points
    total = jnp.zeros_like(alpha)
    for w, q, r in zip(qw, qq, res):
        gap = alpha - w / jnp.maximum(q, 1e-30)
        total = total + (r + gap * gap * q)
    return alpha, jnp.sqrt(total / points + EPSILON)


def global_alpha_beta(slabs, points, place, stats_ref):
    order = [stats_ref[lax.rem(slab - place[0] + slabs, slabs)] for slab in range(slabs)]
    return alpha_beta(order, points)


def add_ab(ref, base, old_ab, step, alpha, beta):
    shape = (alpha.shape[0], LANES)
    lane = lax.broadcasted_iota(jnp.int32, shape, 1)
    out = jnp.zeros(shape, F32) if old_ab is None else old_ab[...]
    out = jnp.where(lane == step, alpha, out)
    ref[:, base : base + LANES] = jnp.where(lane == ITERS + step, beta, out)


def block_of(ref, rows, b):
    if len(ref.shape) == 3:
        return ref[b]
    return ref[b * rows : (b + 1) * rows]


def outer_kernel(
    blocks, slabs, points, step, place, inner_plan, plan, mine, above, below, stats_ref,
    q_own, q_above, q_below, z_raw, z_old, noise, tiles, left, right, *rest,
):
    probes = mine.shape[0]
    old_ab = None
    if step > 0:
        old_ab = rest[0]
        rest = rest[1:]
    w_ref, own_ref, above_ref, below_ref, ab_ref, *z_ref, acc, vecs, held_z = rest
    alpha, beta = global_alpha_beta(slabs, points, place, stats_ref)
    scale = 1.0 / beta
    apart = alpha - slab_alpha(mine, blocks)
    add_ab(ab_ref, 0, old_ab, step, alpha, beta)
    halves = ((mine, q_own, own_ref), (above, q_above, above_ref), (below, q_below, below_ref))
    for part, (w, old, new) in enumerate(halves):
        for b in range(blocks):
            q = (w[:, b * BLK : (b + 1) * BLK] - alpha * block_of(old, probes, b)) * scale
            new[b] = q
            if part > 0:
                vecs[(part - 1) * blocks + b] = stack_vec(q, False)
            else:
                z = (z_raw[b] - apart * z_old[b]) * scale
                held_z[b] = z
                for ref in z_ref:
                    ref[b] = z
    acc[...] = jnp.zeros_like(acc)
    outer_edges(acc, vecs, plan, inner_plan[3, 0], keeper(tiles), maker(left, right))
    finish_apply(
        blocks, acc, lambda b: held_z[b], w_ref, lambda b: own_ref[b], lambda b: block_of(q_own, probes, b), beta, noise
    )


def slope_kernel(inner_plan, plan, left_own, left_halo, right, after, slopes):
    del after

    def make(left):
        return lambda slot, a, c: slope_value(mxu(left[a], right[c]))

    fill(slopes, 0, inner_plan, make(left_own))
    fill(slopes, inner_plan[3, 0], plan, make(left_halo))


def points_kernel(blocks, pts, pts_above, pts_below, after, pnts, halo_pnts, slack, kinds):
    del after
    _, coord_row, list_row = rows_of(pts, blocks)
    for part, ref in enumerate((pts, pts_above, pts_below)):
        raw = ref[coord_row:list_row]
        bent = jnp.tanh(raw)
        x = raw + WARP_GAIN * bent
        x1, x2, x3 = split_three(x)
        one = jnp.ones((blocks, BLK), F32)
        kinds[...] = jnp.concatenate([x1, x2, x3, one, jnp.zeros((6 * blocks, BLK), F32)], axis=0)
        if part == 0:
            slack[...] = jnp.concatenate([x, 1.0 + WARP_GAIN * (1.0 - bent * bent)], axis=0)
        for b in range(blocks):
            y = kinds[pl.ds(b, 16, stride=blocks), :].astype(BF16)
            y = jnp.concatenate([y, y], axis=1)
            if part == 0:
                pnts[b] = y
            else:
                halo_pnts[(part - 1) * blocks + b] = y


def last_kernel(
    blocks, slabs, points, all_probes, place, inner_plan, plan, mine, above, below, stats_ref,
    q_own, q_above, q_below, pts, pts_above, pts_below, old_ab, slopes, left_own, left_out, right, pnts, halo_pnts, slack,
    basis_ref, grad_ref, acc, form_left, halo_left, form_right, pulls,
):
    probes, _, _ = rows_of(pts, blocks)
    alpha, beta = global_alpha_beta(slabs, points, place, stats_ref)
    scale = 1.0 / beta
    add_ab(basis_ref, blocks * BLK, old_ab, ITERS - 1, alpha, beta)
    for part, (w, old, ref) in enumerate(((mine, q_own, pts), (above, q_above, pts_above), (below, q_below, pts_below))):
        for b in range(blocks):
            part_cols = slice(b * BLK, (b + 1) * BLK)
            u = (w[:, part_cols] - alpha * block_of(old, probes, b)) * scale
            v = ref[b * probes : (b + 1) * probes]
            high = u.astype(BF16).astype(F32)
            low = u - high
            turned = jnp.concatenate([high, low, v, v], axis=0).T.astype(BF16)
            if part == 0:
                basis_ref[:, part_cols] = u
                form_left[b] = turned
                form_right[b] = jnp.concatenate([v, v, high, low], axis=0).astype(BF16)
            else:
                halo_left[(part - 1) * blocks + b] = turned

    def pull(side):
        return lambda slot, a, c: stack_tile(mxu(side[a], form_right[c]) * slopes[slot])

    def pull_made(side, left):
        return lambda slot, a, c: stack_tile(mxu(side[a], form_right[c]) * slope_value(mxu(left[a], right[c])))

    base = inner_plan[3, 0]
    fill(pulls, 0, inner_plan, pull(form_left))
    fill(pulls, base, plan, pull(halo_left))
    inner_edges(acc, pnts, inner_plan, keeper(pulls), pull_made(form_left, left_own))
    outer_edges(acc, halo_pnts, plan, base, keeper(pulls), pull_made(halo_left, left_out))
    for b in range(blocks):
        part_cols = slice(b * BLK, (b + 1) * BLK)
        x = slack[pl.ds(b, 3, stride=blocks), :]
        chain = slack[pl.ds(3 * blocks + b, 3, stride=blocks), :]
        sums = acc[b]
        moved = sums[0:3] + sums[3:6] + sums[6:9] - x * sums[9:10]
        grad_ref[:, part_cols] = moved * chain * (1.0 / (LENGTH_SQ * all_probes))


def sum_kernel(place, *refs):
    *parts, _, out, held = refs
    peers = len(parts)
    for r, part in enumerate(parts):
        held[r] = part[...]
    total = held[lax.rem(peers - place[2], peers)]
    for k in range(1, peers):
        total = total + held[lax.rem(k - place[2] + peers, peers)]
    out[...] = total


def close_kernel(place, own, other, basis_ref, alpha_ref, beta_ref, mark):
    mark[...] = jnp.zeros(mark.shape, F32)
    probes = own.shape[0]
    width = basis_ref.shape[1]
    lower = place[1] == 0
    mine = own[...]
    theirs = other[...]
    first = jnp.where(lower, mine, theirs)
    second = jnp.where(lower, theirs, mine)
    basis_ref[:probes] = first[:, :width]
    basis_ref[probes:] = second[:, :width]
    ab = jnp.concatenate([first[:, width:], second[:, width:]], axis=0)
    turned = jnp.concatenate([ab, jnp.zeros((LANES - 2 * probes, LANES), F32)], axis=0).T
    alpha_ref[...] = turned[:ITERS, : 2 * probes]
    beta_ref[...] = turned[ITERS : 2 * ITERS, : 2 * probes]


def vmem(count):
    return [pl.BlockSpec(memory_space=pltpu.VMEM)] * count


def smem(count):
    return [pl.BlockSpec(memory_space=pltpu.SMEM)] * count


def held(array):
    return pltpu.with_memory_space_constraint(array, pltpu.VMEM)


def stays(array):
    return pltpu.with_memory_space_constraint(array, pltpu.HBM)


def in_hbm(count):
    return [pl.BlockSpec(memory_space=pltpu.HBM)] * count


def call(name, kernel, outs, ins, scratch, work, aliases=None, limit=LIMIT_MIB):
    out_shapes, out_scalars = outs
    arrays, scalars = ins
    flops, moved = work
    return pl.pallas_call(
        kernel,
        out_shape=tuple(out_shapes),
        in_specs=smem(scalars) + vmem(len(arrays) - scalars),
        out_specs=tuple(smem(out_scalars) + vmem(len(out_shapes) - out_scalars)),
        scratch_shapes=[pltpu.VMEM(*entry) if isinstance(entry, tuple) else entry for entry in scratch],
        compiler_params=pltpu.CompilerParams(vmem_limit_bytes=limit * 1024 * 1024),
        cost_estimate=pl.CostEstimate(flops=flops, bytes_accessed=moved, transcendentals=0),
        input_output_aliases=aliases or {},
        name=name,
    )(*arrays)


def shifted(value, axes, count, steps):
    return lax.ppermute(value, axes, [(source, (source + steps) % count) for source in range(count)])


def body(coords, noise_var, probe_signs, tile_rows, tile_cols, tile_count):
    slabs = lax.axis_size("blk")
    subs = lax.axis_size("sub")
    outer = lax.axis_size("probe")
    probes = probe_signs.shape[0] // subs
    width = coords.shape[1]
    blocks = width // BLK
    cap = tile_rows.shape[-1]
    points = float(width * slabs)
    all_probes = probe_signs.shape[0] * outer
    sub = lax.axis_index("sub")
    blk = lax.axis_index("blk")
    place = jnp.stack([blk, sub, lax.axis_index("probe") * subs + sub]).astype(jnp.int32)
    sds = jax.ShapeDtypeStruct

    left_shape = sds((blocks, BLK, FEATS), BF16)
    right_shape = sds((blocks, FEATS, BLK), BF16)
    packed = sds((blocks * (probes + 3) + LIST_ROWS, BLK), F32)
    kinds = ((blocks * FEATS, BLK), F32)
    lists, own, noise = pl.pallas_call(
        functools.partial(pack_kernel, blocks),
        out_shape=(sds((LIST_ROWS, LANES), F32), packed, sds((blocks, BLK), F32)),
        in_specs=smem(1) + in_hbm(2) + smem(1) + in_hbm(3),
        out_specs=tuple(vmem(3)),
        scratch_shapes=[
            pltpu.VMEM((probes, width), jnp.int32),
            pltpu.VMEM((3, width), F32),
            pltpu.VMEM((1, cap), jnp.int32),
            pltpu.VMEM((1, cap), jnp.int32),
            pltpu.SemaphoreType.DMA((5,)),
        ],
        compiler_params=pltpu.CompilerParams(vmem_limit_bytes=LIMIT_MIB * 1024 * 1024),
        name="pack",
    )(
        place, stays(tile_rows.reshape(1, cap)), stays(tile_cols.reshape(1, cap)), tile_count.reshape(1),
        stays(probe_signs), stays(coords), stays(noise_var.reshape(blocks, BLK)),
    )
    sibling = shifted(lists, "sub", subs, 1)
    (mine,) = call("join", join_kernel, ((packed,), 0), ((sibling, own), 0), [], (1000, 1000), {1: 0})
    above = shifted(mine, "blk", slabs, -1)
    below = shifted(mine, "blk", slabs, 1)

    ints = jnp.int32
    inner_slots = (blocks * (blocks + 1) // 2 + TAIL + LANES - 1) // LANES * LANES
    outer_slots = (blocks * (blocks + 1) + TAIL + LANES - 1) // LANES * LANES
    plan_shape = sds((LIST_ROWS, inner_slots), ints)
    outer_plan_shape = sds((LIST_ROWS, outer_slots), ints)
    inner_smem = pltpu.SMEM((LIST_ROWS, inner_slots), ints)
    outer_smem = pltpu.SMEM((LIST_ROWS, outer_slots), ints)
    slots = KEPT
    ext = width + LANES
    blocks_f32 = sds((blocks, probes, BLK), F32)
    tile_shape = pltpu.VMEM((slots, 2 * BLK, BLK), BF16)
    acc_shape = ((blocks, probes, BLK), F32)

    inner_plan, tiles, z, cross, left_own, right = call(
        "first_inner",
        functools.partial(first_inner_kernel, blocks),
        ((plan_shape, tile_shape, blocks_f32, sds((LIST_ROWS, outer_slots), F32), left_shape, right_shape), 0),
        ((mine,), 0),
        [
            acc_shape, ((blocks, probes, 2 * BLK), BF16), inner_smem, kinds,
            pltpu.SemaphoreType.DMA,
        ],
        (WORK_FIRST, WORK_BYTES),
    )
    outer_plan, tiles, w, left_halo = call(
        "first_outer",
        functools.partial(first_outer_kernel, blocks),
        ((outer_plan_shape, tile_shape, sds((probes, ext), F32), sds((2 * blocks, BLK, FEATS), BF16)), 0),
        ((inner_plan, held(tiles), mine, above, below, noise, z, right, cross), 1),
        [
            acc_shape, ((2 * blocks, probes, 2 * BLK), BF16), outer_smem, kinds,
            pltpu.SemaphoreType.DMA,
        ],
        (WORK_FIRST, WORK_BYTES),
        {1: 1},
    )

    def exchange(w):
        stats = w[:, width:]
        if slabs == 4:
            far = shifted(stats, "blk", slabs, 2)
        up = shifted(w, "blk", slabs, -1)
        down = shifted(w, "blk", slabs, 1)
        if slabs == 4:
            rows = jnp.stack([stats, up[:, width:], far, down[:, width:]])
        else:
            rows = lax.all_gather(stats, "blk", axis=0)
            rows = jnp.roll(rows, -blk, axis=0)
        return up, down, rows

    q = (mine, above, below)
    ab = []
    z_old = z
    for step in range(ITERS - 1):
        up, down, stats = exchange(w)
        (z_raw,) = call(
            "inner",
            functools.partial(inner_kernel, blocks),
            ((blocks_f32,), 0),
            ((inner_plan, w, q[0], held(tiles), left_own, right), 1),
            [acc_shape, ((blocks, 2 * probes, 2 * BLK), BF16)],
            (WORK_NEXT, WORK_BYTES),
        )
        w, q0, q1, q2, next_ab, *z = call(
            "outer",
            functools.partial(outer_kernel, blocks, slabs, points, step),
            (
                (
                    sds((probes, ext), F32), blocks_f32, blocks_f32, blocks_f32, sds((probes, LANES), F32),
                    *([blocks_f32] if step < ITERS - 2 else []),
                ),
                0,
            ),
            ((place, inner_plan, outer_plan, w, up, down, stats, *q, z_raw, z_old, noise, held(tiles), left_halo, right, *ab), 3),
            [acc_shape, ((2 * blocks, 2 * probes, 2 * BLK), BF16), ((blocks, probes, BLK), F32)],
            (WORK_NEXT, WORK_BYTES),
        )
        q = (q0, q1, q2)
        ab = [next_ab]
        z_old = z[0] if z else None

    up, down, stats = exchange(w)
    (slopes,) = call(
        "slopes",
        slope_kernel,
        ((pltpu.VMEM((slots, BLK, BLK), F32),), 0),
        ((inner_plan, outer_plan, left_own, left_halo, right, w), 2),
        [],
        (WORK_FIRST, WORK_BYTES),
    )
    pnts, halo_pnts, slack = call(
        "points",
        functools.partial(points_kernel, blocks),
        (
            (
                sds((blocks, 16, 2 * BLK), BF16), sds((2 * blocks, 16, 2 * BLK), BF16), sds((6 * blocks, BLK), F32),
            ),
            0,
        ),
        ((mine, above, below, w), 0),
        [((blocks * 16, BLK), F32)],
        (WORK_NEXT, WORK_BYTES),
    )
    basis, grad = call(
        "last",
        functools.partial(last_kernel, blocks, slabs, points, all_probes),
        ((sds((probes, ext), F32), sds((3, width), F32)), 0),
        (
            (
                place, inner_plan, outer_plan, w, up, down, stats, *q, mine, above, below, *ab, held(slopes), left_own, left_halo,
                right, pnts, halo_pnts, slack,
            ),
            3,
        ),
        [
            ((blocks, 16, BLK), F32),
            ((blocks, BLK, 4 * probes), BF16),
            ((2 * blocks, BLK, 4 * probes), BF16),
            ((blocks, 4 * probes, BLK), BF16),
            ((slots, 2 * BLK, BLK), BF16),
        ],
        (WORK_FIRST, WORK_BYTES),
        limit=LIMIT_MIB * 3 // 2,
    )

    peers = outer * subs
    parts = [grad]
    for r in range(1, peers):
        parts.append(shifted(grad, ("probe", "sub"), peers, -r))
    other = shifted(basis, "sub", subs, 1)
    last_basis, alphas, betas, mark = call(
        "close",
        close_kernel,
        (
            (
                sds((subs * probes, width), F32), sds((ITERS, subs * probes), F32), sds((ITERS, subs * probes), F32),
                sds((8, LANES), F32),
            ),
            0,
        ),
        ((place, basis, other), 1),
        [],
        (1000000, 1000000),
    )
    (coord_grad,) = call(
        "sum",
        sum_kernel,
        ((sds((3, width), F32),), 0),
        ((place, *parts, mark), 1),
        [((peers, 3, width), F32)],
        (1000, 1000),
    )
    return alphas, betas, last_basis, coord_grad


def solution(mesh):
    return jax.shard_map(
        body,
        mesh=mesh,
        in_specs=(
            P(None, ("groups", "blk")),
            P(("groups", "blk")),
            P("probe", ("groups", "blk")),
            P(("groups", "blk"), "sub", None),
            P(("groups", "blk"), "sub", None),
            P(("groups", "blk"), "sub"),
        ),
        out_specs=(
            P(None, ("groups", "probe")),
            P(None, ("groups", "probe")),
            P("probe", ("groups", "blk")),
            P(None, ("groups", "blk")),
        ),
        check_vma=False,
    )
```

```python
import functools
import math

import jax
import jax.numpy as jnp
from jax import lax
from jax.experimental import pallas as pl
from jax.experimental.pallas import tpu as pltpu
from jax.sharding import PartitionSpec as P

ITERS = 3
SIGNAL_VAR = 0.1
LENGTH_SQ = 2.0
TAPER_SQ = 16.0
WARP_GAIN = 0.4
EPSILON = 1e-06

BLK = 128
LANES = 128
FEATS = 32
GROUP = 16
TAIL = 8
LIST_ROWS = 8
LIMIT_MIB = 16
KEPT = 256
WORK_FIRST = 300000000
WORK_NEXT = 100000000
WORK_BYTES = 4000000

DECAY = TAPER_SQ / (2.0 * LENGTH_SQ)
Z_TOP = math.sqrt(SIGNAL_VAR * math.exp(-DECAY))
Z_RATE = DECAY / Z_TOP
Z_OF_D = -Z_TOP / TAPER_SQ
Z_STEP = 4.0 * LENGTH_SQ / TAPER_SQ * Z_TOP

F32 = jnp.float32
BF16 = jnp.bfloat16


def split_two(x):
    high = x.astype(BF16)
    low = (x - high.astype(F32)).astype(BF16)
    return high, low


def split_three(x):
    one = x.astype(BF16).astype(F32)
    rest = x - one
    two = rest.astype(BF16).astype(F32)
    three = (rest - two).astype(BF16).astype(F32)
    return one, two, three


def warp(x):
    return x + WARP_GAIN * jnp.tanh(x)


def mxu(a, b):
    return lax.dot_general(a, b, (((1,), (0,)), ((), ())), preferred_element_type=F32)


def put_stats(ref, base, w_of, q_of, qq, qw, blocks):
    alpha_s = qw / jnp.maximum(qq, 1e-30)
    acc = jnp.zeros((qq.shape[0], LANES), F32)
    for b in range(blocks):
        r = w_of(b) - alpha_s * q_of(b)
        acc = acc + r * r
    res = jnp.sum(acc, axis=1, keepdims=True)
    lane = lax.broadcasted_iota(jnp.int32, (qq.shape[0], LANES), 1)
    out = jnp.where(lane == 0, qw, jnp.where(lane == 1, qq, jnp.where(lane == 2, res, 0.0)))
    ref[:, base : base + LANES] = out


def mxu_turned(a, b):
    return lax.dot_general(a, b, (((1,), (1,)), ((), ())), preferred_element_type=F32)


def fold(out, probes):
    if out.shape[0] > probes:
        return out[:probes] + out[probes:]
    return out


def fold_turned(out, probes):
    total = out[:probes, :BLK] + out[:probes, BLK:]
    if out.shape[0] > probes:
        total = total + out[probes:, :BLK]
    return total


def stack_vec(q, exact):
    if exact:
        high = q.astype(BF16)
        return jnp.concatenate([high, high], axis=1)
    high, low = split_two(q)
    return jnp.concatenate(
        [jnp.concatenate([high, high], axis=1), jnp.concatenate([low, jnp.zeros_like(low)], axis=1)], axis=0
    )


def stack_tile(tile):
    return jnp.concatenate(split_two(tile), axis=0)


def ranges(first, last, body):
    long = (last - first) // GROUP
    middle = first + long * GROUP

    def big(g, carry):
        body(first + g * GROUP, GROUP)
        return carry

    def small(g, carry):
        body(middle + g * TAIL, TAIL)
        return carry

    lax.fori_loop(0, long, big, 0)
    lax.fori_loop(0, (last - middle) // TAIL, small, 0)


def kept_and_made(total, room, body, kept, made):
    first = jnp.minimum(total, room)
    ranges(0, first, functools.partial(body, kept))
    many = (total - first) // TAIL

    def rest(g, carry):
        body(made, first + g * TAIL, TAIL)
        return carry

    lax.fori_loop(0, many, rest, 0)


def entry(plan, slot):
    word = plan[0, slot]
    return word & 63, (word >> 6) & 63, (word >> 12).astype(F32)


def total_of(plan):
    return plan[0, plan.shape[1] - 1]


def inner_edges(acc, vecs, plan, kept, made):
    acc[...] = jnp.zeros_like(acc)
    size = acc.shape[1]

    def group(tile_of, start, many):
        outs = []
        for u in range(many):
            slot = start + u
            a, c, times = entry(plan, slot)
            tile = tile_of(slot, a, c)
            outs.append((c, fold(mxu(vecs[a], tile), size) * times))
            outs.append((a, fold_turned(mxu_turned(vecs[c][:, :BLK], tile), size) * times))
        for c, out in outs:
            acc[c] = acc[c] + out

    kept_and_made(total_of(plan), KEPT, group, kept, made)


def outer_edges(acc, vecs, plan, base, kept, made):
    size = acc.shape[1]

    def group(tile_of, start, many):
        outs = []
        for u in range(many):
            at = start + u
            a, c, times = entry(plan, at)
            outs.append((c, fold(mxu(vecs[a], tile_of(base + at, a, c)), size) * times))
        for c, out in outs:
            acc[c] = acc[c] + out

    kept_and_made(total_of(plan), jnp.maximum(KEPT - base, 0), group, kept, made)


def tile_value(z):
    z = jnp.maximum(z, 0.0)
    return jnp.exp(z * Z_RATE) * (z * z)


def slope_value(z):
    z = jnp.maximum(z, 0.0)
    return (jnp.exp(z * Z_RATE) * z) * (z + Z_STEP)


def fill(into, base, plan, make):
    def body(start, many):
        for u in range(many):
            at = start + u
            a, c, _ = entry(plan, at)
            into[base + at] = make(base + at, a, c)

    ranges(0, jnp.minimum(total_of(plan), jnp.maximum(KEPT - base, 0)), body)


def maker(left, right):
    return lambda slot, a, c: stack_tile(tile_value(mxu(left[a], right[c])))


def keeper(tiles):
    return lambda slot, a, c: tiles[slot]


def whole(n):
    return jnp.floor((n + (TAIL - 1)) * (1.0 / TAIL)) * TAIL


def keys(lists, blocks, cross):
    out = []
    whole_lists = lists.astype(jnp.int32)
    for at in (0, 3):
        a = whole_lists[at : at + 1]
        c = whole_lists[at + 1 : at + 2]
        live = lax.broadcasted_iota(jnp.int32, a.shape, 1) < whole_lists[at + 2 : at + 3]
        if cross:
            out.append(jnp.where(live & (c >= blocks), a * blocks + c - blocks, -1))
        else:
            out.append(jnp.where(live & (c < blocks), a * blocks + c, -1))
    return jnp.concatenate(out, axis=1)


def compact(key, blocks, slots, first):
    size = blocks * blocks
    hot = jnp.where(lax.broadcasted_iota(jnp.int32, (size, key.shape[1]), 0) == key, 1.0, 0.0).astype(BF16)
    counts = mxu(hot, jnp.ones((key.shape[1], LANES), BF16))
    flags = jnp.minimum(counts, 1.0)
    shape = (size, size)
    ahead = lax.broadcasted_iota(jnp.int32, shape, 0) > lax.broadcasted_iota(jnp.int32, shape, 1)
    place = mxu(jnp.where(ahead, 1.0, 0.0).astype(BF16), flags.astype(BF16)) + first
    index = lax.broadcasted_iota(jnp.int32, (16, size), 1).astype(F32)
    row = jnp.floor((index + 0.5) * (1.0 / blocks))
    line = lax.broadcasted_iota(jnp.int32, (16, size), 0)
    names = jnp.where(line == 0, row, jnp.where(line == 1, index - row * blocks, 1.0)).astype(BF16)
    found = []
    times = []
    for part in range(slots // LANES):
        lane = (lax.broadcasted_iota(jnp.int32, (size, LANES), 1) + part * LANES).astype(F32)
        here = (place == lane) & (flags > 0.5)
        found.append(mxu(names, jnp.where(here, 1.0, 0.0).astype(BF16)))
        times.append(mxu(names, jnp.where(here, counts, 0.0).astype(BF16))[2:3])
    found = jnp.concatenate(found, axis=1)
    end = place[size - 1 :] + flags[size - 1 :]
    return found[0:1], found[1:2], found[2:3], jnp.concatenate(times, axis=1), end


def put_plan(ref, rows):
    ref[...] = jnp.zeros(ref.shape, ref.dtype)
    for at, row in enumerate(rows):
        ref[at : at + 1, :] = row.astype(ref.dtype)


def put_words(ref, row, col, times, end):
    slots = ref.shape[1]
    last = lax.broadcasted_iota(jnp.int32, ref.shape, 1) == slots - 1
    ref[...] = jnp.where(last, spread(end, slots), row + 64.0 * col + 4096.0 * times).astype(jnp.int32)


def spread(row, width):
    return jnp.concatenate([row] * (width // LANES), axis=1)


def side_features(blocks, coords, kinds, left, right):
    x = warp(coords)
    scale = -2.0 * Z_OF_D
    square = x * x
    norm = Z_OF_D * (square[:blocks] + square[blocks : 2 * blocks] + square[2 * blocks :])
    x1, x2, x3 = split_three(x)
    n1, n2, n3 = split_three(norm)
    m1, m2, m3 = split_three(norm + Z_TOP)
    one = jnp.ones_like(norm)
    pad = jnp.zeros(((FEATS - 24) * blocks, BLK), F32)
    kinds[...] = jnp.concatenate([x1, x1, x2, x2, x1, x3, n1, n2, n3, one, one, one, pad], axis=0)
    for g in range(0, blocks, 4):
        stack = [kinds[pl.ds(b, FEATS, stride=blocks), :] for b in range(g, g + 4)]
        turned = jnp.concatenate(stack, axis=0).T.astype(BF16)
        for b in range(4):
            left[g + b] = turned[:, b * FEATS : (b + 1) * FEATS]
    if right is not None:
        y1, y2, y3 = split_three(x * scale)
        kinds[...] = jnp.concatenate([y1, y2, y1, y2, y3, y1, one, one, one, m1, m2, m3, pad], axis=0)
        for b in range(blocks):
            right[b] = kinds[pl.ds(b, FEATS, stride=blocks), :].astype(BF16)


def rows_of(packed, blocks):
    lists = packed.shape[0] - LIST_ROWS
    coords = lists - 3 * blocks
    return coords // blocks, coords, lists


def pack_kernel(
    blocks, place, tile_rows, tile_cols, tile_count, signs, coords, noise,
    lists, mine, noise_here, got_signs, got_coords, got_rows, got_cols, sems,
):
    probes, coord_row, list_row = rows_of(mine, blocks)
    first = pl.multiple_of(place[1] * probes, probes)
    moves = [
        pltpu.make_async_copy(coords, got_coords, sems.at[0]),
        pltpu.make_async_copy(signs.at[pl.ds(first, probes), :], got_signs, sems.at[1]),
        pltpu.make_async_copy(tile_rows, got_rows, sems.at[2]),
        pltpu.make_async_copy(tile_cols, got_cols, sems.at[3]),
        pltpu.make_async_copy(noise, noise_here, sems.at[4]),
    ]
    for move in moves:
        move.start()
    lists[...] = jnp.zeros(lists.shape, F32)
    lists[2:3, :] = jnp.full((1, LANES), tile_count[0], jnp.int32).astype(F32)
    for move in moves[2:4]:
        move.wait()
    lists[0:1, : tile_rows.shape[1]] = got_rows[...].astype(F32)
    lists[1:2, : tile_cols.shape[1]] = got_cols[...].astype(F32)
    mine[list_row:] = lists[...]
    moves[0].wait()
    for c in range(3):
        for b in range(blocks):
            at = coord_row + c * blocks + b
            mine[at : at + 1] = got_coords[c : c + 1, b * BLK : (b + 1) * BLK]
    moves[1].wait()
    for b in range(blocks):
        mine[b * probes : (b + 1) * probes] = got_signs[:, b * BLK : (b + 1) * BLK].astype(F32)
    moves[4].wait()


def join_kernel(sibling, old, mine):
    del old
    at = mine.shape[0] - LIST_ROWS + 3
    mine[at : at + 3] = sibling[0:3]


def first_inner_kernel(
    blocks, mine,
    held_plan, tiles, z_ref, cross, left, right, acc, vecs, plan, kinds, sem,
):
    probes, coord_row, list_row = rows_of(mine, blocks)
    lists = mine[list_row:]
    row, col, _, times, end = compact(keys(lists, blocks, False), blocks, held_plan.shape[1], 0.0)
    put_words(held_plan, row, col, times, whole(end))
    move = pltpu.make_async_copy(held_plan, plan, sem)
    move.start()
    row, col, _, times, end = compact(keys(lists, blocks, True), blocks, cross.shape[1], 0.0)
    put_plan(cross, (col, row, times, spread(end, cross.shape[1])))
    for b in range(blocks):
        vecs[b] = stack_vec(mine[b * probes : (b + 1) * probes], True)
    side_features(blocks, mine[coord_row:list_row], kinds, left, right)
    move.wait()
    fill(tiles, 0, plan, maker(left, right))
    inner_edges(acc, vecs, plan, keeper(tiles), maker(left, right))
    z_ref[...] = acc[:blocks]


def finish_apply(blocks, acc, z_of, w_ref, q_of, prev_of, beta, noise):
    probes = acc.shape[1]
    qq = jnp.zeros((probes, LANES), F32)
    qw = jnp.zeros((probes, LANES), F32)
    for b in range(blocks):
        q = q_of(b)
        part = slice(b * BLK, (b + 1) * BLK)
        w = acc[b] + z_of(b) + noise[b : b + 1] * q
        if prev_of is not None:
            w = w - beta * prev_of(b)
        w_ref[:, part] = w
        qq = qq + q * q
        qw = qw + q * w
    put_stats(
        w_ref,
        blocks * BLK,
        lambda b: w_ref[:, b * BLK : (b + 1) * BLK],
        q_of,
        jnp.sum(qq, axis=1, keepdims=True),
        jnp.sum(qw, axis=1, keepdims=True),
        blocks,
    )


def first_outer_kernel(
    blocks, inner_plan, old_tiles, mine, above, below, noise, z_ref, right, cross,
    held_plan, tiles, w_ref, left, acc, vecs, plan, kinds, sem,
):
    probes, coord_row, list_row = rows_of(mine, blocks)
    del old_tiles
    slots = held_plan.shape[1]
    row, col, one, times, end = compact(keys(below[list_row:], blocks, True), blocks, slots, cross[3:4, :LANES])
    put_words(held_plan, cross[0:1] + row + blocks * one, cross[1:2] + col, cross[2:3] + times, whole(end))
    move = pltpu.make_async_copy(held_plan, plan, sem)
    move.start()
    for part, ref in enumerate((above, below)):
        side_features(blocks, ref[coord_row:list_row], kinds, left.at[part * blocks : (part + 1) * blocks], None)
        for b in range(blocks):
            vecs[part * blocks + b] = stack_vec(ref[b * probes : (b + 1) * probes], True)
    acc[...] = jnp.zeros_like(acc)
    move.wait()
    base = total_of(inner_plan)
    fill(tiles, base, plan, maker(left, right))
    outer_edges(acc, vecs, plan, base, keeper(tiles), maker(left, right))
    finish_apply(
        blocks, acc, lambda b: z_ref[b], w_ref, lambda b: mine[b * probes : (b + 1) * probes], None, None, noise
    )


def slab_alpha(w_ref, blocks):
    sums = w_ref[:, blocks * BLK : (blocks + 1) * BLK]
    return sums[:, 0:1] / jnp.maximum(sums[:, 1:2], 1e-30)


def inner_kernel(blocks, plan, w_ref, q_own, tiles, left, right, z_ref, acc, vecs):
    alpha = slab_alpha(w_ref, blocks)
    probes = w_ref.shape[0]
    for b in range(blocks):
        vecs[b] = stack_vec(w_ref[:, b * BLK : (b + 1) * BLK] - alpha * block_of(q_own, probes, b), False)
    inner_edges(acc, vecs, plan, keeper(tiles), maker(left, right))
    z_ref[...] = acc[:blocks]


def alpha_beta(stats, points):
    qw = [s[:, 0:1] for s in stats]
    qq = [s[:, 1:2] for s in stats]
    res = [s[:, 2:3] for s in stats]
    alpha = functools.reduce(jnp.add, qw) / points
    total = jnp.zeros_like(alpha)
    for w, q, r in zip(qw, qq, res):
        gap = alpha - w / jnp.maximum(q, 1e-30)
        total = total + (r + gap * gap * q)
    return alpha, jnp.sqrt(total / points + EPSILON)


def global_alpha_beta(slabs, points, place, stats_ref):
    order = [stats_ref[lax.rem(slab - place[0] + slabs, slabs)] for slab in range(slabs)]
    return alpha_beta(order, points)


def add_ab(ref, base, old_ab, step, alpha, beta):
    shape = (alpha.shape[0], LANES)
    lane = lax.broadcasted_iota(jnp.int32, shape, 1)
    out = jnp.zeros(shape, F32) if old_ab is None else old_ab[...]
    out = jnp.where(lane == step, alpha, out)
    ref[:, base : base + LANES] = jnp.where(lane == ITERS + step, beta, out)


def block_of(ref, rows, b):
    if len(ref.shape) == 3:
        return ref[b]
    return ref[b * rows : (b + 1) * rows]


def outer_kernel(
    blocks, slabs, points, step, place, inner_plan, plan, mine, above, below, stats_ref,
    q_own, q_above, q_below, z_raw, z_old, noise, tiles, left, right, *rest,
):
    probes = mine.shape[0]
    old_ab = None
    if step > 0:
        old_ab = rest[0]
        rest = rest[1:]
    w_ref, own_ref, above_ref, below_ref, ab_ref, *z_ref, acc, vecs, held_z = rest
    alpha, beta = global_alpha_beta(slabs, points, place, stats_ref)
    scale = 1.0 / beta
    apart = alpha - slab_alpha(mine, blocks)
    add_ab(ab_ref, 0, old_ab, step, alpha, beta)
    halves = ((mine, q_own, own_ref), (above, q_above, above_ref), (below, q_below, below_ref))
    for part, (w, old, new) in enumerate(halves):
        for b in range(blocks):
            q = (w[:, b * BLK : (b + 1) * BLK] - alpha * block_of(old, probes, b)) * scale
            new[b] = q
            if part > 0:
                vecs[(part - 1) * blocks + b] = stack_vec(q, False)
            else:
                z = (z_raw[b] - apart * z_old[b]) * scale
                held_z[b] = z
                for ref in z_ref:
                    ref[b] = z
    acc[...] = jnp.zeros_like(acc)
    outer_edges(acc, vecs, plan, total_of(inner_plan), keeper(tiles), maker(left, right))
    finish_apply(
        blocks, acc, lambda b: held_z[b], w_ref, lambda b: own_ref[b], lambda b: block_of(q_own, probes, b), beta, noise
    )


def slope_kernel(inner_plan, plan, left_own, left_halo, right, after, slopes):
    del after

    def make(left):
        return lambda slot, a, c: slope_value(mxu(left[a], right[c]))

    fill(slopes, 0, inner_plan, make(left_own))
    fill(slopes, total_of(inner_plan), plan, make(left_halo))


def points_kernel(blocks, pts, pts_above, pts_below, after, pnts, halo_pnts, slack, kinds):
    del after
    _, coord_row, list_row = rows_of(pts, blocks)
    for part, ref in enumerate((pts, pts_above, pts_below)):
        raw = ref[coord_row:list_row]
        bent = jnp.tanh(raw)
        x = raw + WARP_GAIN * bent
        x1, x2, x3 = split_three(x)
        one = jnp.ones((blocks, BLK), F32)
        kinds[...] = jnp.concatenate([x1, x2, x3, one, jnp.zeros((6 * blocks, BLK), F32)], axis=0)
        if part == 0:
            slack[...] = jnp.concatenate([x, 1.0 + WARP_GAIN * (1.0 - bent * bent)], axis=0)
        for b in range(blocks):
            y = kinds[pl.ds(b, 16, stride=blocks), :].astype(BF16)
            y = jnp.concatenate([y, y], axis=1)
            if part == 0:
                pnts[b] = y
            else:
                halo_pnts[(part - 1) * blocks + b] = y


def last_kernel(
    blocks, slabs, points, all_probes, place, inner_plan, plan, mine, above, below, stats_ref,
    q_own, q_above, q_below, pts, pts_above, pts_below, old_ab, slopes, left_own, left_out, right, pnts, halo_pnts, slack,
    basis_ref, grad_ref, acc, form_left, halo_left, form_right, pulls,
):
    probes, _, _ = rows_of(pts, blocks)
    alpha, beta = global_alpha_beta(slabs, points, place, stats_ref)
    scale = 1.0 / beta
    add_ab(basis_ref, blocks * BLK, old_ab, ITERS - 1, alpha, beta)
    for part, (w, old, ref) in enumerate(((mine, q_own, pts), (above, q_above, pts_above), (below, q_below, pts_below))):
        for b in range(blocks):
            part_cols = slice(b * BLK, (b + 1) * BLK)
            u = (w[:, part_cols] - alpha * block_of(old, probes, b)) * scale
            v = ref[b * probes : (b + 1) * probes]
            high = u.astype(BF16).astype(F32)
            low = u - high
            turned = jnp.concatenate([high, low, v, v], axis=0).T.astype(BF16)
            if part == 0:
                basis_ref[:, part_cols] = u
                form_left[b] = turned
                form_right[b] = jnp.concatenate([v, v, high, low], axis=0).astype(BF16)
            else:
                halo_left[(part - 1) * blocks + b] = turned

    def pull(side):
        return lambda slot, a, c: stack_tile(mxu(side[a], form_right[c]) * slopes[slot])

    def pull_made(side, left):
        return lambda slot, a, c: stack_tile(mxu(side[a], form_right[c]) * slope_value(mxu(left[a], right[c])))

    base = total_of(inner_plan)
    fill(pulls, 0, inner_plan, pull(form_left))
    fill(pulls, base, plan, pull(halo_left))
    inner_edges(acc, pnts, inner_plan, keeper(pulls), pull_made(form_left, left_own))
    outer_edges(acc, halo_pnts, plan, base, keeper(pulls), pull_made(halo_left, left_out))
    for b in range(blocks):
        part_cols = slice(b * BLK, (b + 1) * BLK)
        x = slack[pl.ds(b, 3, stride=blocks), :]
        chain = slack[pl.ds(3 * blocks + b, 3, stride=blocks), :]
        sums = acc[b]
        moved = sums[0:3] + sums[3:6] + sums[6:9] - x * sums[9:10]
        grad_ref[:, part_cols] = moved * chain * (1.0 / (LENGTH_SQ * all_probes))


def close_kernel(place, own, other, grad, basis_ref, alpha_ref, beta_ref, same_grad):
    same_grad[...] = grad[...]
    probes = own.shape[0]
    width = basis_ref.shape[1]
    lower = place[1] == 0
    mine = own[...]
    theirs = other[...]
    first = jnp.where(lower, mine, theirs)
    second = jnp.where(lower, theirs, mine)
    basis_ref[:probes] = first[:, :width]
    basis_ref[probes:] = second[:, :width]
    ab = jnp.concatenate([first[:, width:], second[:, width:]], axis=0)
    turned = jnp.concatenate([ab, jnp.zeros((LANES - 2 * probes, LANES), F32)], axis=0).T
    alpha_ref[...] = turned[:ITERS, : 2 * probes]
    beta_ref[...] = turned[ITERS : 2 * ITERS, : 2 * probes]


def vmem(count):
    return [pl.BlockSpec(memory_space=pltpu.VMEM)] * count


def smem(count):
    return [pl.BlockSpec(memory_space=pltpu.SMEM)] * count


def held(array):
    return pltpu.with_memory_space_constraint(array, pltpu.VMEM)


def stays(array):
    return pltpu.with_memory_space_constraint(array, pltpu.HBM)


def in_hbm(count):
    return [pl.BlockSpec(memory_space=pltpu.HBM)] * count


def call(name, kernel, outs, ins, scratch, work, aliases=None, limit=LIMIT_MIB):
    out_shapes, out_scalars = outs
    arrays, scalars = ins
    flops, moved = work
    return pl.pallas_call(
        kernel,
        out_shape=tuple(out_shapes),
        in_specs=smem(scalars) + vmem(len(arrays) - scalars),
        out_specs=tuple(smem(out_scalars) + vmem(len(out_shapes) - out_scalars)),
        scratch_shapes=[pltpu.VMEM(*entry) if isinstance(entry, tuple) else entry for entry in scratch],
        compiler_params=pltpu.CompilerParams(vmem_limit_bytes=limit * 1024 * 1024),
        cost_estimate=pl.CostEstimate(flops=flops, bytes_accessed=moved, transcendentals=0),
        input_output_aliases=aliases or {},
        name=name,
    )(*arrays)


def shifted(value, axes, count, steps):
    return lax.ppermute(value, axes, [(source, (source + steps) % count) for source in range(count)])


def body(coords, noise_var, probe_signs, tile_rows, tile_cols, tile_count):
    slabs = lax.axis_size("blk")
    subs = lax.axis_size("sub")
    outer = lax.axis_size("probe")
    probes = probe_signs.shape[0] // subs
    width = coords.shape[1]
    blocks = width // BLK
    cap = tile_rows.shape[-1]
    points = float(width * slabs)
    all_probes = probe_signs.shape[0] * outer
    sub = lax.axis_index("sub")
    blk = lax.axis_index("blk")
    place = jnp.stack([blk, sub]).astype(jnp.int32)
    sds = jax.ShapeDtypeStruct

    left_shape = sds((blocks, BLK, FEATS), BF16)
    right_shape = sds((blocks, FEATS, BLK), BF16)
    packed = sds((blocks * (probes + 3) + LIST_ROWS, BLK), F32)
    kinds = ((blocks * FEATS, BLK), F32)
    lists, own, noise = pl.pallas_call(
        functools.partial(pack_kernel, blocks),
        out_shape=(sds((LIST_ROWS, LANES), F32), packed, sds((blocks, BLK), F32)),
        in_specs=smem(1) + in_hbm(2) + smem(1) + in_hbm(3),
        out_specs=tuple(vmem(3)),
        scratch_shapes=[
            pltpu.VMEM((probes, width), jnp.int32),
            pltpu.VMEM((3, width), F32),
            pltpu.VMEM((1, cap), jnp.int32),
            pltpu.VMEM((1, cap), jnp.int32),
            pltpu.SemaphoreType.DMA((5,)),
        ],
        compiler_params=pltpu.CompilerParams(vmem_limit_bytes=LIMIT_MIB * 1024 * 1024),
        name="pack",
    )(
        place, stays(tile_rows.reshape(1, cap)), stays(tile_cols.reshape(1, cap)), tile_count.reshape(1),
        stays(probe_signs), stays(coords), stays(noise_var.reshape(blocks, BLK)),
    )
    sibling = shifted(lists, "sub", subs, 1)
    (mine,) = call("join", join_kernel, ((packed,), 0), ((sibling, own), 0), [], (1000, 1000), {1: 0})
    above = shifted(mine, "blk", slabs, -1)
    below = shifted(mine, "blk", slabs, 1)

    ints = jnp.int32
    inner_slots = (blocks * (blocks + 1) // 2 + TAIL + LANES) // LANES * LANES
    outer_slots = (blocks * (blocks + 1) + TAIL + LANES) // LANES * LANES
    plan_shape = sds((1, inner_slots), ints)
    outer_plan_shape = sds((1, outer_slots), ints)
    inner_smem = pltpu.SMEM((1, inner_slots), ints)
    outer_smem = pltpu.SMEM((1, outer_slots), ints)
    slots = KEPT
    ext = width + LANES
    blocks_f32 = sds((blocks, probes, BLK), F32)
    tile_shape = pltpu.VMEM((slots, 2 * BLK, BLK), BF16)
    acc_shape = ((blocks, probes, BLK), F32)

    inner_plan, tiles, z, cross, left_own, right = call(
        "first_inner",
        functools.partial(first_inner_kernel, blocks),
        ((plan_shape, tile_shape, blocks_f32, sds((LIST_ROWS, outer_slots), F32), left_shape, right_shape), 0),
        ((mine,), 0),
        [
            acc_shape, ((blocks, probes, 2 * BLK), BF16), inner_smem, kinds,
            pltpu.SemaphoreType.DMA,
        ],
        (WORK_FIRST, WORK_BYTES),
    )
    outer_plan, tiles, w, left_halo = call(
        "first_outer",
        functools.partial(first_outer_kernel, blocks),
        ((outer_plan_shape, tile_shape, sds((probes, ext), F32), sds((2 * blocks, BLK, FEATS), BF16)), 0),
        ((inner_plan, held(tiles), mine, above, below, noise, z, right, cross), 1),
        [
            acc_shape, ((2 * blocks, probes, 2 * BLK), BF16), outer_smem, kinds,
            pltpu.SemaphoreType.DMA,
        ],
        (WORK_FIRST, WORK_BYTES),
        {1: 1},
    )

    def exchange(w):
        stats = w[:, width:]
        if slabs == 4:
            far = shifted(stats, "blk", slabs, 2)
        up = shifted(w, "blk", slabs, -1)
        down = shifted(w, "blk", slabs, 1)
        if slabs == 4:
            rows = jnp.stack([stats, up[:, width:], far, down[:, width:]])
        else:
            rows = lax.all_gather(stats, "blk", axis=0)
            rows = jnp.roll(rows, -blk, axis=0)
        return up, down, rows

    q = (mine, above, below)
    ab = []
    z_old = z
    for step in range(ITERS - 1):
        up, down, stats = exchange(w)
        (z_raw,) = call(
            "inner",
            functools.partial(inner_kernel, blocks),
            ((blocks_f32,), 0),
            ((inner_plan, w, q[0], held(tiles), left_own, right), 1),
            [acc_shape, ((blocks, 2 * probes, 2 * BLK), BF16)],
            (WORK_NEXT, WORK_BYTES),
        )
        w, q0, q1, q2, next_ab, *z = call(
            "outer",
            functools.partial(outer_kernel, blocks, slabs, points, step),
            (
                (
                    sds((probes, ext), F32), blocks_f32, blocks_f32, blocks_f32, sds((probes, LANES), F32),
                    *([blocks_f32] if step < ITERS - 2 else []),
                ),
                0,
            ),
            ((place, inner_plan, outer_plan, w, up, down, stats, *q, z_raw, z_old, noise, held(tiles), left_halo, right, *ab), 3),
            [acc_shape, ((2 * blocks, 2 * probes, 2 * BLK), BF16), ((blocks, probes, BLK), F32)],
            (WORK_NEXT, WORK_BYTES),
        )
        q = (q0, q1, q2)
        ab = [next_ab]
        z_old = z[0] if z else None

    up, down, stats = exchange(w)
    (slopes,) = call(
        "slopes",
        slope_kernel,
        ((pltpu.VMEM((slots, BLK, BLK), F32),), 0),
        ((inner_plan, outer_plan, left_own, left_halo, right, w), 2),
        [],
        (WORK_FIRST, WORK_BYTES),
    )
    pnts, halo_pnts, slack = call(
        "points",
        functools.partial(points_kernel, blocks),
        (
            (
                sds((blocks, 16, 2 * BLK), BF16), sds((2 * blocks, 16, 2 * BLK), BF16), sds((6 * blocks, BLK), F32),
            ),
            0,
        ),
        ((mine, above, below, w), 0),
        [((blocks * 16, BLK), F32)],
        (WORK_NEXT, WORK_BYTES),
    )
    basis, grad = call(
        "last",
        functools.partial(last_kernel, blocks, slabs, points, all_probes),
        ((sds((probes, ext), F32), sds((3, width), F32)), 0),
        (
            (
                place, inner_plan, outer_plan, w, up, down, stats, *q, mine, above, below, *ab, held(slopes), left_own, left_halo,
                right, pnts, halo_pnts, slack,
            ),
            3,
        ),
        [
            ((blocks, 16, BLK), F32),
            ((blocks, BLK, 4 * probes), BF16),
            ((2 * blocks, BLK, 4 * probes), BF16),
            ((blocks, 4 * probes, BLK), BF16),
            ((slots, 2 * BLK, BLK), BF16),
        ],
        (WORK_FIRST, WORK_BYTES),
        limit=LIMIT_MIB * 3 // 2,
    )

    if outer == 2 and subs == 2:
        axes = ("probe", "sub")
        across, diagonal, beside = (lax.ppermute(grad, axes, [(k, k ^ flip) for k in range(4)]) for flip in (2, 3, 1))
    other = shifted(basis, "sub", subs, 1)
    last_basis, alphas, betas, grad = call(
        "close",
        close_kernel,
        (
            (
                sds((subs * probes, width), F32), sds((ITERS, subs * probes), F32), sds((ITERS, subs * probes), F32),
                sds((3, width), F32),
            ),
            0,
        ),
        ((place, basis, other, grad), 1),
        [],
        (1000000, 1000000),
    )
    if outer == 2 and subs == 2:
        coord_grad = (grad + beside) + (across + diagonal)
    else:
        coord_grad = lax.psum(grad, ("probe", "sub"))
    return alphas, betas, last_basis, coord_grad


def solution(mesh):
    return jax.shard_map(
        body,
        mesh=mesh,
        in_specs=(
            P(None, ("groups", "blk")),
            P(("groups", "blk")),
            P("probe", ("groups", "blk")),
            P(("groups", "blk"), "sub", None),
            P(("groups", "blk"), "sub", None),
            P(("groups", "blk"), "sub"),
        ),
        out_specs=(
            P(None, ("groups", "probe")),
            P(None, ("groups", "probe")),
            P("probe", ("groups", "blk")),
            P(None, ("groups", "blk")),
        ),
        check_vma=False,
    )
```

```python
import functools
import math

import jax
import jax.numpy as jnp
from jax import lax
from jax.experimental import pallas as pl
from jax.experimental.pallas import tpu as pltpu
from jax.sharding import PartitionSpec as P

ITERS = 3
SIGNAL_VAR = 0.1
LENGTH_SQ = 2.0
TAPER_SQ = 16.0
WARP_GAIN = 0.4
EPSILON = 1e-06

BLK = 128
LANES = 128
FEATS = 32
GROUP = 16
TAIL = 8
LIST_ROWS = 8
LIMIT_MIB = 16
KEPT = 256
WORK_FIRST = 300000000
WORK_NEXT = 100000000
WORK_BYTES = 4000000

DECAY = TAPER_SQ / (2.0 * LENGTH_SQ)
Z_TOP = math.sqrt(SIGNAL_VAR * math.exp(-DECAY))
Z_RATE = DECAY / Z_TOP
Z_OF_D = -Z_TOP / TAPER_SQ
Z_STEP = 4.0 * LENGTH_SQ / TAPER_SQ * Z_TOP

F32 = jnp.float32
BF16 = jnp.bfloat16


def split_two(x):
    high = x.astype(BF16)
    low = (x - high.astype(F32)).astype(BF16)
    return high, low


def split_three(x):
    one = x.astype(BF16).astype(F32)
    rest = x - one
    two = rest.astype(BF16).astype(F32)
    three = (rest - two).astype(BF16).astype(F32)
    return one, two, three


def warp(x):
    return x + WARP_GAIN * jnp.tanh(x)


def mxu(a, b):
    return lax.dot_general(a, b, (((1,), (0,)), ((), ())), preferred_element_type=F32)


def put_stats(ref, base, w_of, q_of, qq, qw, blocks):
    alpha_s = qw / jnp.maximum(qq, 1e-30)
    acc = jnp.zeros((qq.shape[0], LANES), F32)
    for b in range(blocks):
        r = w_of(b) - alpha_s * q_of(b)
        acc = acc + r * r
    res = jnp.sum(acc, axis=1, keepdims=True)
    lane = lax.broadcasted_iota(jnp.int32, (qq.shape[0], LANES), 1)
    out = jnp.where(lane == 0, qw, jnp.where(lane == 1, qq, jnp.where(lane == 2, res, 0.0)))
    ref[:, base : base + LANES] = out


def mxu_turned(a, b):
    return lax.dot_general(a, b, (((1,), (1,)), ((), ())), preferred_element_type=F32)


def fold(out, probes):
    if out.shape[0] > probes:
        return out[:probes] + out[probes:]
    return out


def fold_turned(out, probes):
    total = out[:probes, :BLK] + out[:probes, BLK:]
    if out.shape[0] > probes:
        total = total + out[probes:, :BLK]
    return total


def stack_vec(q, exact):
    if exact:
        high = q.astype(BF16)
        return jnp.concatenate([high, high], axis=1)
    high, low = split_two(q)
    return jnp.concatenate(
        [jnp.concatenate([high, high], axis=1), jnp.concatenate([low, jnp.zeros_like(low)], axis=1)], axis=0
    )


def stack_tile(tile):
    return jnp.concatenate(split_two(tile), axis=0)


def ranges(first, last, body):
    long = (last - first) // GROUP
    middle = first + long * GROUP

    def big(g, carry):
        body(first + g * GROUP, GROUP)
        return carry

    def small(g, carry):
        body(middle + g * TAIL, TAIL)
        return carry

    lax.fori_loop(0, long, big, 0)
    lax.fori_loop(0, (last - middle) // TAIL, small, 0)


def kept_and_made(total, room, body, kept, made):
    first = jnp.minimum(total, room)
    ranges(0, first, functools.partial(body, kept))
    many = (total - first) // TAIL

    def rest(g, carry):
        body(made, first + g * TAIL, TAIL)
        return carry

    lax.fori_loop(0, many, rest, 0)


def entry(plan, slot):
    word = plan[0, slot]
    return word & 63, (word >> 6) & 63, (word >> 12).astype(F32)


def total_of(plan):
    return plan[0, plan.shape[1] - 1]


def inner_edges(acc, vecs, plan, kept, made):
    acc[...] = jnp.zeros_like(acc)
    size = acc.shape[1]

    def group(tile_of, start, many):
        outs = []
        for u in range(many):
            slot = start + u
            a, c, times = entry(plan, slot)
            tile = tile_of(slot, a, c)
            outs.append((c, fold(mxu(vecs[a], tile), size) * times))
            outs.append((a, fold_turned(mxu_turned(vecs[c][:, :BLK], tile), size) * times))
        for c, out in outs:
            acc[c] = acc[c] + out

    kept_and_made(total_of(plan), KEPT, group, kept, made)


def outer_edges(acc, vecs, plan, base, kept, made):
    size = acc.shape[1]

    def group(tile_of, start, many):
        outs = []
        for u in range(many):
            at = start + u
            a, c, times = entry(plan, at)
            outs.append((c, fold(mxu(vecs[a], tile_of(base + at, a, c)), size) * times))
        for c, out in outs:
            acc[c] = acc[c] + out

    kept_and_made(total_of(plan), jnp.maximum(KEPT - base, 0), group, kept, made)


def tile_value(z):
    z = jnp.maximum(z, 0.0)
    return jnp.exp(z * Z_RATE) * (z * z)


def slope_value(z):
    z = jnp.maximum(z, 0.0)
    return (jnp.exp(z * Z_RATE) * z) * (z + Z_STEP)


def fill(into, base, plan, make):
    def body(start, many):
        for u in range(many):
            at = start + u
            a, c, _ = entry(plan, at)
            into[base + at] = make(base + at, a, c)

    ranges(0, jnp.minimum(total_of(plan), jnp.maximum(KEPT - base, 0)), body)


def maker(left, right):
    return lambda slot, a, c: stack_tile(tile_value(mxu(left[a], right[c])))


def keeper(tiles):
    return lambda slot, a, c: tiles[slot]


def whole(n):
    return jnp.floor((n + (TAIL - 1)) * (1.0 / TAIL)) * TAIL


def keys(lists, blocks, cross):
    out = []
    whole_lists = lists.astype(jnp.int32)
    for at in (0, 3):
        a = whole_lists[at : at + 1]
        c = whole_lists[at + 1 : at + 2]
        live = lax.broadcasted_iota(jnp.int32, a.shape, 1) < whole_lists[at + 2 : at + 3]
        if cross:
            out.append(jnp.where(live & (c >= blocks), a * blocks + c - blocks, -1))
        else:
            out.append(jnp.where(live & (c < blocks), a * blocks + c, -1))
    return jnp.concatenate(out, axis=1)


def compact(key, blocks, slots, first):
    size = blocks * blocks
    hot = jnp.where(lax.broadcasted_iota(jnp.int32, (size, key.shape[1]), 0) == key, 1.0, 0.0).astype(BF16)
    counts = mxu(hot, jnp.ones((key.shape[1], LANES), BF16))
    flags = jnp.minimum(counts, 1.0)
    shape = (size, size)
    ahead = lax.broadcasted_iota(jnp.int32, shape, 0) > lax.broadcasted_iota(jnp.int32, shape, 1)
    place = mxu(jnp.where(ahead, 1.0, 0.0).astype(BF16), flags.astype(BF16)) + first
    index = lax.broadcasted_iota(jnp.int32, (16, size), 1).astype(F32)
    row = jnp.floor((index + 0.5) * (1.0 / blocks))
    line = lax.broadcasted_iota(jnp.int32, (16, size), 0)
    names = jnp.where(line == 0, row, jnp.where(line == 1, index - row * blocks, 1.0)).astype(BF16)
    found = []
    times = []
    for part in range(slots // LANES):
        lane = (lax.broadcasted_iota(jnp.int32, (size, LANES), 1) + part * LANES).astype(F32)
        here = (place == lane) & (flags > 0.5)
        found.append(mxu(names, jnp.where(here, 1.0, 0.0).astype(BF16)))
        times.append(mxu(names, jnp.where(here, counts, 0.0).astype(BF16))[2:3])
    found = jnp.concatenate(found, axis=1)
    end = place[size - 1 :] + flags[size - 1 :]
    return found[0:1], found[1:2], found[2:3], jnp.concatenate(times, axis=1), end


def put_plan(ref, rows):
    ref[...] = jnp.zeros(ref.shape, ref.dtype)
    for at, row in enumerate(rows):
        ref[at : at + 1, :] = row.astype(ref.dtype)


def put_words(ref, row, col, times, end):
    slots = ref.shape[1]
    last = lax.broadcasted_iota(jnp.int32, ref.shape, 1) == slots - 1
    ref[...] = jnp.where(last, spread(end, slots), row + 64.0 * col + 4096.0 * times).astype(jnp.int32)


def spread(row, width):
    return jnp.concatenate([row] * (width // LANES), axis=1)


def side_features(blocks, coords, kinds, left, right):
    x = warp(coords)
    scale = -2.0 * Z_OF_D
    square = x * x
    norm = Z_OF_D * (square[:blocks] + square[blocks : 2 * blocks] + square[2 * blocks :])
    x1, x2, x3 = split_three(x)
    n1, n2, n3 = split_three(norm)
    m1, m2, m3 = split_three(norm + Z_TOP)
    one = jnp.ones_like(norm)
    pad = jnp.zeros(((FEATS - 24) * blocks, BLK), F32)
    kinds[...] = jnp.concatenate([x1, x1, x2, x2, x1, x3, n1, n2, n3, one, one, one, pad], axis=0)
    for g in range(0, blocks, 4):
        stack = [kinds[pl.ds(b, FEATS, stride=blocks), :] for b in range(g, g + 4)]
        turned = jnp.concatenate(stack, axis=0).T.astype(BF16)
        for b in range(4):
            left[g + b] = turned[:, b * FEATS : (b + 1) * FEATS]
    if right is not None:
        y1, y2, y3 = split_three(x * scale)
        kinds[...] = jnp.concatenate([y1, y2, y1, y2, y3, y1, one, one, one, m1, m2, m3, pad], axis=0)
        for b in range(blocks):
            right[b] = kinds[pl.ds(b, FEATS, stride=blocks), :].astype(BF16)


def rows_of(packed, blocks):
    lists = packed.shape[0] - LIST_ROWS
    coords = lists - 3 * blocks
    return coords // blocks, coords, lists


def pack_kernel(
    blocks, place, tile_rows, tile_cols, tile_count, signs, coords, noise,
    lists, mine, noise_here, got_signs, got_coords, got_rows, got_cols, sems,
):
    probes, coord_row, list_row = rows_of(mine, blocks)
    first = pl.multiple_of(place[1] * probes, probes)
    moves = [
        pltpu.make_async_copy(coords, got_coords, sems.at[0]),
        pltpu.make_async_copy(signs.at[pl.ds(first, probes), :], got_signs, sems.at[1]),
        pltpu.make_async_copy(tile_rows, got_rows, sems.at[2]),
        pltpu.make_async_copy(tile_cols, got_cols, sems.at[3]),
        pltpu.make_async_copy(noise, noise_here, sems.at[4]),
    ]
    for move in moves:
        move.start()
    lists[...] = jnp.zeros(lists.shape, F32)
    lists[2:3, :] = jnp.full((1, LANES), tile_count[0], jnp.int32).astype(F32)
    for move in moves[2:4]:
        move.wait()
    lists[0:1, : tile_rows.shape[1]] = got_rows[...].astype(F32)
    lists[1:2, : tile_cols.shape[1]] = got_cols[...].astype(F32)
    mine[list_row:] = lists[...]
    moves[0].wait()
    for c in range(3):
        for b in range(blocks):
            at = coord_row + c * blocks + b
            mine[at : at + 1] = got_coords[c : c + 1, b * BLK : (b + 1) * BLK]
    moves[1].wait()
    for b in range(blocks):
        mine[b * probes : (b + 1) * probes] = got_signs[:, b * BLK : (b + 1) * BLK].astype(F32)
    moves[4].wait()


def join_kernel(sibling, old, mine):
    del old
    at = mine.shape[0] - LIST_ROWS + 3
    mine[at : at + 3] = sibling[0:3]


def first_inner_kernel(
    blocks, mine,
    held_plan, tiles, z_ref, cross, left, right, acc, vecs, plan, kinds, sem,
):
    probes, coord_row, list_row = rows_of(mine, blocks)
    lists = mine[list_row:]
    row, col, _, times, end = compact(keys(lists, blocks, False), blocks, held_plan.shape[1], 0.0)
    put_words(held_plan, row, col, times, whole(end))
    move = pltpu.make_async_copy(held_plan, plan, sem)
    move.start()
    row, col, _, times, end = compact(keys(lists, blocks, True), blocks, cross.shape[1], 0.0)
    put_plan(cross, (col, row, times, spread(end, cross.shape[1])))
    for b in range(blocks):
        vecs[b] = stack_vec(mine[b * probes : (b + 1) * probes], True)
    side_features(blocks, mine[coord_row:list_row], kinds, left, right)
    move.wait()
    fill(tiles, 0, plan, maker(left, right))
    inner_edges(acc, vecs, plan, keeper(tiles), maker(left, right))
    z_ref[...] = acc[:blocks]


def finish_apply(blocks, acc, z_of, w_ref, q_of, prev_of, beta, noise):
    probes = acc.shape[1]
    qq = jnp.zeros((probes, LANES), F32)
    qw = jnp.zeros((probes, LANES), F32)
    for b in range(blocks):
        q = q_of(b)
        part = slice(b * BLK, (b + 1) * BLK)
        w = acc[b] + z_of(b) + noise[b : b + 1] * q
        if prev_of is not None:
            w = w - beta * prev_of(b)
        w_ref[:, part] = w
        qq = qq + q * q
        qw = qw + q * w
    put_stats(
        w_ref,
        blocks * BLK,
        lambda b: w_ref[:, b * BLK : (b + 1) * BLK],
        q_of,
        jnp.sum(qq, axis=1, keepdims=True),
        jnp.sum(qw, axis=1, keepdims=True),
        blocks,
    )


def first_outer_kernel(
    blocks, inner_plan, old_tiles, mine, above, below, noise, z_ref, right, cross,
    held_plan, tiles, w_ref, left, acc, vecs, plan, kinds, sem,
):
    probes, coord_row, list_row = rows_of(mine, blocks)
    del old_tiles
    slots = held_plan.shape[1]
    row, col, one, times, end = compact(keys(below[list_row:], blocks, True), blocks, slots, cross[3:4, :LANES])
    put_words(held_plan, cross[0:1] + row + blocks * one, cross[1:2] + col, cross[2:3] + times, whole(end))
    move = pltpu.make_async_copy(held_plan, plan, sem)
    move.start()
    for part, ref in enumerate((above, below)):
        side_features(blocks, ref[coord_row:list_row], kinds, left.at[part * blocks : (part + 1) * blocks], None)
        for b in range(blocks):
            vecs[part * blocks + b] = stack_vec(ref[b * probes : (b + 1) * probes], True)
    acc[...] = jnp.zeros_like(acc)
    move.wait()
    base = total_of(inner_plan)
    fill(tiles, base, plan, maker(left, right))
    outer_edges(acc, vecs, plan, base, keeper(tiles), maker(left, right))
    finish_apply(
        blocks, acc, lambda b: z_ref[b], w_ref, lambda b: mine[b * probes : (b + 1) * probes], None, None, noise
    )


def slab_alpha(w_ref, blocks):
    sums = w_ref[:, blocks * BLK : (blocks + 1) * BLK]
    return sums[:, 0:1] / jnp.maximum(sums[:, 1:2], 1e-30)


def inner_kernel(blocks, plan, w_ref, q_own, tiles, left, right, z_ref, acc, vecs):
    alpha = slab_alpha(w_ref, blocks)
    probes = w_ref.shape[0]
    for b in range(blocks):
        vecs[b] = stack_vec(w_ref[:, b * BLK : (b + 1) * BLK] - alpha * block_of(q_own, probes, b), False)
    inner_edges(acc, vecs, plan, keeper(tiles), maker(left, right))
    z_ref[...] = acc[:blocks]


def alpha_beta(stats, points):
    qw = [s[:, 0:1] for s in stats]
    qq = [s[:, 1:2] for s in stats]
    res = [s[:, 2:3] for s in stats]
    alpha = functools.reduce(jnp.add, qw) / points
    total = jnp.zeros_like(alpha)
    for w, q, r in zip(qw, qq, res):
        gap = alpha - w / jnp.maximum(q, 1e-30)
        total = total + (r + gap * gap * q)
    return alpha, jnp.sqrt(total / points + EPSILON)


def global_alpha_beta(slabs, points, place, stats_ref):
    order = [stats_ref[lax.rem(slab - place[0] + slabs, slabs)] for slab in range(slabs)]
    return alpha_beta(order, points)


def add_ab(ref, base, old_ab, step, alpha, beta):
    shape = (alpha.shape[0], LANES)
    lane = lax.broadcasted_iota(jnp.int32, shape, 1)
    out = jnp.zeros(shape, F32) if old_ab is None else old_ab[...]
    out = jnp.where(lane == step, alpha, out)
    ref[:, base : base + LANES] = jnp.where(lane == ITERS + step, beta, out)


def block_of(ref, rows, b):
    if len(ref.shape) == 3:
        return ref[b]
    return ref[b * rows : (b + 1) * rows]


def outer_kernel(
    blocks, slabs, points, step, place, inner_plan, plan, mine, above, below, stats_ref,
    q_own, q_above, q_below, z_raw, z_old, noise, tiles, left, right, *rest,
):
    probes = mine.shape[0]
    old_ab = None
    if step > 0:
        old_ab = rest[0]
        rest = rest[1:]
    w_ref, own_ref, above_ref, below_ref, ab_ref, *z_ref, acc, vecs, held_z = rest
    alpha, beta = global_alpha_beta(slabs, points, place, stats_ref)
    scale = 1.0 / beta
    apart = alpha - slab_alpha(mine, blocks)
    add_ab(ab_ref, 0, old_ab, step, alpha, beta)
    halves = ((mine, q_own, own_ref), (above, q_above, above_ref), (below, q_below, below_ref))
    for part, (w, old, new) in enumerate(halves):
        for b in range(blocks):
            q = (w[:, b * BLK : (b + 1) * BLK] - alpha * block_of(old, probes, b)) * scale
            new[b] = q
            if part > 0:
                vecs[(part - 1) * blocks + b] = stack_vec(q, False)
            else:
                z = (z_raw[b] - apart * z_old[b]) * scale
                held_z[b] = z
                for ref in z_ref:
                    ref[b] = z
    acc[...] = jnp.zeros_like(acc)
    outer_edges(acc, vecs, plan, total_of(inner_plan), keeper(tiles), maker(left, right))
    finish_apply(
        blocks, acc, lambda b: held_z[b], w_ref, lambda b: own_ref[b], lambda b: block_of(q_own, probes, b), beta, noise
    )


def slope_kernel(inner_plan, plan, left_own, left_halo, right, after, slopes):
    del after

    def make(left):
        return lambda slot, a, c: slope_value(mxu(left[a], right[c]))

    fill(slopes, 0, inner_plan, make(left_own))
    fill(slopes, total_of(inner_plan), plan, make(left_halo))


def points_kernel(blocks, pts, pts_above, pts_below, after, pnts, halo_pnts, slack, kinds):
    del after
    _, coord_row, list_row = rows_of(pts, blocks)
    for part, ref in enumerate((pts, pts_above, pts_below)):
        raw = ref[coord_row:list_row]
        bent = jnp.tanh(raw)
        x = raw + WARP_GAIN * bent
        x1, x2, x3 = split_three(x)
        one = jnp.ones((blocks, BLK), F32)
        kinds[...] = jnp.concatenate([x1, x2, x3, one, jnp.zeros((6 * blocks, BLK), F32)], axis=0)
        if part == 0:
            slack[...] = jnp.concatenate([x, 1.0 + WARP_GAIN * (1.0 - bent * bent)], axis=0)
        for b in range(blocks):
            y = kinds[pl.ds(b, 16, stride=blocks), :].astype(BF16)
            y = jnp.concatenate([y, y], axis=1)
            if part == 0:
                pnts[b] = y
            else:
                halo_pnts[(part - 1) * blocks + b] = y


def basis_kernel(blocks, slabs, points, place, mine, stats_ref, q_own, old_ab, after, later, basis_ref):
    del after, later
    probes = mine.shape[0]
    alpha, beta = global_alpha_beta(slabs, points, place, stats_ref)
    scale = 1.0 / beta
    add_ab(basis_ref, blocks * BLK, old_ab, ITERS - 1, alpha, beta)
    for b in range(blocks):
        cols = slice(b * BLK, (b + 1) * BLK)
        basis_ref[:, cols] = (mine[:, cols] - alpha * block_of(q_own, probes, b)) * scale


def last_kernel(
    blocks, slabs, points, all_probes, place, inner_plan, plan, mine, above, below, stats_ref,
    q_own, q_above, q_below, pts, pts_above, pts_below, slopes, left_own, left_out, right, pnts, halo_pnts, slack,
    grad_ref, acc, form_left, halo_left, form_right, pulls,
):
    probes, _, _ = rows_of(pts, blocks)
    alpha, beta = global_alpha_beta(slabs, points, place, stats_ref)
    scale = 1.0 / beta
    for part, (w, old, ref) in enumerate(((mine, q_own, pts), (above, q_above, pts_above), (below, q_below, pts_below))):
        for b in range(blocks):
            part_cols = slice(b * BLK, (b + 1) * BLK)
            u = (w[:, part_cols] - alpha * block_of(old, probes, b)) * scale
            v = ref[b * probes : (b + 1) * probes]
            high = u.astype(BF16).astype(F32)
            low = u - high
            turned = jnp.concatenate([high, low, v, v], axis=0).T.astype(BF16)
            if part == 0:
                form_left[b] = turned
                form_right[b] = jnp.concatenate([v, v, high, low], axis=0).astype(BF16)
            else:
                halo_left[(part - 1) * blocks + b] = turned

    def pull(side):
        return lambda slot, a, c: stack_tile(mxu(side[a], form_right[c]) * slopes[slot])

    def pull_made(side, left):
        return lambda slot, a, c: stack_tile(mxu(side[a], form_right[c]) * slope_value(mxu(left[a], right[c])))

    base = total_of(inner_plan)
    fill(pulls, 0, inner_plan, pull(form_left))
    fill(pulls, base, plan, pull(halo_left))
    inner_edges(acc, pnts, inner_plan, keeper(pulls), pull_made(form_left, left_own))
    outer_edges(acc, halo_pnts, plan, base, keeper(pulls), pull_made(halo_left, left_out))
    for b in range(blocks):
        part_cols = slice(b * BLK, (b + 1) * BLK)
        x = slack[pl.ds(b, 3, stride=blocks), :]
        chain = slack[pl.ds(3 * blocks + b, 3, stride=blocks), :]
        sums = acc[b]
        moved = sums[0:3] + sums[3:6] + sums[6:9] - x * sums[9:10]
        grad_ref[:, part_cols] = moved * chain * (1.0 / (LENGTH_SQ * all_probes))


def pair_kernel(one, two, out):
    out[...] = one[...] + two[...]


def close_kernel(place, own, other, grad, basis_ref, alpha_ref, beta_ref, same_grad):
    same_grad[...] = grad[...]
    probes = own.shape[0]
    width = basis_ref.shape[1]
    lower = place[1] == 0
    mine = own[...]
    theirs = other[...]
    first = jnp.where(lower, mine, theirs)
    second = jnp.where(lower, theirs, mine)
    basis_ref[:probes] = first[:, :width]
    basis_ref[probes:] = second[:, :width]
    ab = jnp.concatenate([first[:, width:], second[:, width:]], axis=0)
    turned = jnp.concatenate([ab, jnp.zeros((LANES - 2 * probes, LANES), F32)], axis=0).T
    alpha_ref[...] = turned[:ITERS, : 2 * probes]
    beta_ref[...] = turned[ITERS : 2 * ITERS, : 2 * probes]


def vmem(count):
    return [pl.BlockSpec(memory_space=pltpu.VMEM)] * count


def smem(count):
    return [pl.BlockSpec(memory_space=pltpu.SMEM)] * count


def held(array):
    return pltpu.with_memory_space_constraint(array, pltpu.VMEM)


def stays(array):
    return pltpu.with_memory_space_constraint(array, pltpu.HBM)


def in_hbm(count):
    return [pl.BlockSpec(memory_space=pltpu.HBM)] * count


def call(name, kernel, outs, ins, scratch, work, aliases=None, limit=LIMIT_MIB):
    out_shapes, out_scalars = outs
    arrays, scalars = ins
    flops, moved = work
    return pl.pallas_call(
        kernel,
        out_shape=tuple(out_shapes),
        in_specs=smem(scalars) + vmem(len(arrays) - scalars),
        out_specs=tuple(smem(out_scalars) + vmem(len(out_shapes) - out_scalars)),
        scratch_shapes=[pltpu.VMEM(*entry) if isinstance(entry, tuple) else entry for entry in scratch],
        compiler_params=pltpu.CompilerParams(vmem_limit_bytes=limit * 1024 * 1024),
        cost_estimate=pl.CostEstimate(flops=flops, bytes_accessed=moved, transcendentals=0),
        input_output_aliases=aliases or {},
        name=name,
    )(*arrays)


def shifted(value, axes, count, steps):
    return lax.ppermute(value, axes, [(source, (source + steps) % count) for source in range(count)])


def body(coords, noise_var, probe_signs, tile_rows, tile_cols, tile_count):
    slabs = lax.axis_size("blk")
    subs = lax.axis_size("sub")
    outer = lax.axis_size("probe")
    probes = probe_signs.shape[0] // subs
    width = coords.shape[1]
    blocks = width // BLK
    cap = tile_rows.shape[-1]
    points = float(width * slabs)
    all_probes = probe_signs.shape[0] * outer
    sub = lax.axis_index("sub")
    blk = lax.axis_index("blk")
    place = jnp.stack([blk, sub]).astype(jnp.int32)
    sds = jax.ShapeDtypeStruct

    left_shape = sds((blocks, BLK, FEATS), BF16)
    right_shape = sds((blocks, FEATS, BLK), BF16)
    packed = sds((blocks * (probes + 3) + LIST_ROWS, BLK), F32)
    kinds = ((blocks * FEATS, BLK), F32)
    lists, own, noise = pl.pallas_call(
        functools.partial(pack_kernel, blocks),
        out_shape=(sds((LIST_ROWS, LANES), F32), packed, sds((blocks, BLK), F32)),
        in_specs=smem(1) + in_hbm(2) + smem(1) + in_hbm(3),
        out_specs=tuple(vmem(3)),
        scratch_shapes=[
            pltpu.VMEM((probes, width), jnp.int32),
            pltpu.VMEM((3, width), F32),
            pltpu.VMEM((1, cap), jnp.int32),
            pltpu.VMEM((1, cap), jnp.int32),
            pltpu.SemaphoreType.DMA((5,)),
        ],
        compiler_params=pltpu.CompilerParams(vmem_limit_bytes=LIMIT_MIB * 1024 * 1024),
        name="pack",
    )(
        place, stays(tile_rows.reshape(1, cap)), stays(tile_cols.reshape(1, cap)), tile_count.reshape(1),
        stays(probe_signs), stays(coords), stays(noise_var.reshape(blocks, BLK)),
    )
    sibling = shifted(lists, "sub", subs, 1)
    (mine,) = call("join", join_kernel, ((packed,), 0), ((sibling, own), 0), [], (1000, 1000), {1: 0})
    above = shifted(mine, "blk", slabs, -1)
    below = shifted(mine, "blk", slabs, 1)

    ints = jnp.int32
    inner_slots = (blocks * (blocks + 1) // 2 + TAIL + LANES) // LANES * LANES
    outer_slots = (blocks * (blocks + 1) + TAIL + LANES) // LANES * LANES
    plan_shape = sds((1, inner_slots), ints)
    outer_plan_shape = sds((1, outer_slots), ints)
    inner_smem = pltpu.SMEM((1, inner_slots), ints)
    outer_smem = pltpu.SMEM((1, outer_slots), ints)
    slots = KEPT
    ext = width + LANES
    blocks_f32 = sds((blocks, probes, BLK), F32)
    tile_shape = pltpu.VMEM((slots, 2 * BLK, BLK), BF16)
    acc_shape = ((blocks, probes, BLK), F32)

    inner_plan, tiles, z, cross, left_own, right = call(
        "first_inner",
        functools.partial(first_inner_kernel, blocks),
        ((plan_shape, tile_shape, blocks_f32, sds((LIST_ROWS, outer_slots), F32), left_shape, right_shape), 0),
        ((mine,), 0),
        [
            acc_shape, ((blocks, probes, 2 * BLK), BF16), inner_smem, kinds,
            pltpu.SemaphoreType.DMA,
        ],
        (WORK_FIRST, WORK_BYTES),
    )
    outer_plan, tiles, w, left_halo = call(
        "first_outer",
        functools.partial(first_outer_kernel, blocks),
        ((outer_plan_shape, tile_shape, sds((probes, ext), F32), sds((2 * blocks, BLK, FEATS), BF16)), 0),
        ((inner_plan, held(tiles), mine, above, below, noise, z, right, cross), 1),
        [
            acc_shape, ((2 * blocks, probes, 2 * BLK), BF16), outer_smem, kinds,
            pltpu.SemaphoreType.DMA,
        ],
        (WORK_FIRST, WORK_BYTES),
        {1: 1},
    )

    def exchange(w):
        stats = w[:, width:]
        if slabs == 4:
            far = shifted(stats, "blk", slabs, 2)
        up = shifted(w, "blk", slabs, -1)
        down = shifted(w, "blk", slabs, 1)
        if slabs == 4:
            rows = jnp.stack([stats, up[:, width:], far, down[:, width:]])
        else:
            rows = lax.all_gather(stats, "blk", axis=0)
            rows = jnp.roll(rows, -blk, axis=0)
        return up, down, rows

    q = (mine, above, below)
    ab = []
    z_old = z
    for step in range(ITERS - 1):
        up, down, stats = exchange(w)
        (z_raw,) = call(
            "inner",
            functools.partial(inner_kernel, blocks),
            ((blocks_f32,), 0),
            ((inner_plan, w, q[0], held(tiles), left_own, right), 1),
            [acc_shape, ((blocks, 2 * probes, 2 * BLK), BF16)],
            (WORK_NEXT, WORK_BYTES),
        )
        w, q0, q1, q2, next_ab, *z = call(
            "outer",
            functools.partial(outer_kernel, blocks, slabs, points, step),
            (
                (
                    sds((probes, ext), F32), blocks_f32, blocks_f32, blocks_f32, sds((probes, LANES), F32),
                    *([blocks_f32] if step < ITERS - 2 else []),
                ),
                0,
            ),
            ((place, inner_plan, outer_plan, w, up, down, stats, *q, z_raw, z_old, noise, held(tiles), left_halo, right, *ab), 3),
            [acc_shape, ((2 * blocks, 2 * probes, 2 * BLK), BF16), ((blocks, probes, BLK), F32)],
            (WORK_NEXT, WORK_BYTES),
        )
        q = (q0, q1, q2)
        ab = [next_ab]
        z_old = z[0] if z else None

    up, down, stats = exchange(w)
    (slopes,) = call(
        "slopes",
        slope_kernel,
        ((pltpu.VMEM((slots, BLK, BLK), F32),), 0),
        ((inner_plan, outer_plan, left_own, left_halo, right, w), 2),
        [],
        (WORK_FIRST, WORK_BYTES),
    )
    pnts, halo_pnts, slack = call(
        "points",
        functools.partial(points_kernel, blocks),
        (
            (
                sds((blocks, 16, 2 * BLK), BF16), sds((2 * blocks, 16, 2 * BLK), BF16), sds((6 * blocks, BLK), F32),
            ),
            0,
        ),
        ((mine, above, below, w), 0),
        [((blocks * 16, BLK), F32)],
        (WORK_NEXT, WORK_BYTES),
    )
    (basis,) = call(
        "basis",
        functools.partial(basis_kernel, blocks, slabs, points),
        ((sds((probes, ext), F32),), 0),
        ((place, w, stats, q[0], *ab, held(slopes), slack), 1),
        [],
        (1000, 1000),
    )
    other = shifted(basis, "sub", subs, 1)
    (grad,) = call(
        "last",
        functools.partial(last_kernel, blocks, slabs, points, all_probes),
        ((sds((3, width), F32),), 0),
        (
            (
                place, inner_plan, outer_plan, w, up, down, stats, *q, mine, above, below, held(slopes), left_own, left_halo,
                right, pnts, halo_pnts, slack,
            ),
            3,
        ),
        [
            ((blocks, 16, BLK), F32),
            ((blocks, BLK, 4 * probes), BF16),
            ((2 * blocks, BLK, 4 * probes), BF16),
            ((blocks, 4 * probes, BLK), BF16),
            ((slots, 2 * BLK, BLK), BF16),
        ],
        (WORK_FIRST, WORK_BYTES),
        limit=LIMIT_MIB * 3 // 2,
    )

    across = shifted(grad, "probe", outer, 1) if outer == 2 else lax.psum(grad, "probe")
    last_basis, alphas, betas, grad = call(
        "close",
        close_kernel,
        (
            (
                sds((subs * probes, width), F32), sds((ITERS, subs * probes), F32), sds((ITERS, subs * probes), F32),
                sds((3, width), F32),
            ),
            0,
        ),
        ((place, basis, other, grad), 1),
        [],
        (1000000, 1000000),
    )
    if outer == 2:
        (grad,) = call("pair", pair_kernel, ((sds((3, width), F32),), 0), ((grad, across), 0), [], (1000, 1000))
    else:
        grad = across
    coord_grad = grad + shifted(grad, "sub", subs, 1)
    return alphas, betas, last_basis, coord_grad


def solution(mesh):
    return jax.shard_map(
        body,
        mesh=mesh,
        in_specs=(
            P(None, ("groups", "blk")),
            P(("groups", "blk")),
            P("probe", ("groups", "blk")),
            P(("groups", "blk"), "sub", None),
            P(("groups", "blk"), "sub", None),
            P(("groups", "blk"), "sub"),
        ),
        out_specs=(
            P(None, ("groups", "probe")),
            P(None, ("groups", "probe")),
            P("probe", ("groups", "blk")),
            P(None, ("groups", "blk")),
        ),
        check_vma=False,
    )
```

```python
import functools
import math

import jax
import jax.numpy as jnp
from jax import lax
from jax.experimental import pallas as pl
from jax.experimental.pallas import tpu as pltpu
from jax.sharding import PartitionSpec as P

ITERS = 3
SIGNAL_VAR = 0.1
LENGTH_SQ = 2.0
TAPER_SQ = 16.0
WARP_GAIN = 0.4
EPSILON = 1e-06

BLK = 128
LANES = 128
FEATS = 32
GROUP = 16
TAIL = 8
LIST_ROWS = 8
LIMIT_MIB = 16
KEPT = 256
WORK_FIRST = 300000000
WORK_NEXT = 100000000
WORK_BYTES = 4000000

DECAY = TAPER_SQ / (2.0 * LENGTH_SQ)
Z_TOP = math.sqrt(SIGNAL_VAR * math.exp(-DECAY))
Z_RATE = DECAY / Z_TOP
Z_OF_D = -Z_TOP / TAPER_SQ
Z_STEP = 4.0 * LENGTH_SQ / TAPER_SQ * Z_TOP

F32 = jnp.float32
BF16 = jnp.bfloat16


def split_two(x):
    high = x.astype(BF16)
    low = (x - high.astype(F32)).astype(BF16)
    return high, low


def split_three(x):
    one = x.astype(BF16).astype(F32)
    rest = x - one
    two = rest.astype(BF16).astype(F32)
    three = (rest - two).astype(BF16).astype(F32)
    return one, two, three


def warp(x):
    return x + WARP_GAIN * jnp.tanh(x)


def mxu(a, b):
    return lax.dot_general(a, b, (((1,), (0,)), ((), ())), preferred_element_type=F32)


def put_stats(ref, base, w_of, q_of, qq, qw, blocks):
    alpha_s = qw / jnp.maximum(qq, 1e-30)
    acc = jnp.zeros((qq.shape[0], LANES), F32)
    for b in range(blocks):
        r = w_of(b) - alpha_s * q_of(b)
        acc = acc + r * r
    res = jnp.sum(acc, axis=1, keepdims=True)
    lane = lax.broadcasted_iota(jnp.int32, (qq.shape[0], LANES), 1)
    out = jnp.where(lane == 0, qw, jnp.where(lane == 1, qq, jnp.where(lane == 2, res, 0.0)))
    ref[:, base : base + LANES] = out


def mxu_turned(a, b):
    return lax.dot_general(a, b, (((1,), (1,)), ((), ())), preferred_element_type=F32)


def fold(out, probes):
    if out.shape[0] > probes:
        return out[:probes] + out[probes:]
    return out


def fold_turned(out, probes):
    total = out[:probes, :BLK] + out[:probes, BLK:]
    if out.shape[0] > probes:
        total = total + out[probes:, :BLK]
    return total


def stack_vec(q, exact):
    if exact:
        high = q.astype(BF16)
        return jnp.concatenate([high, high], axis=1)
    high, low = split_two(q)
    return jnp.concatenate(
        [jnp.concatenate([high, high], axis=1), jnp.concatenate([low, jnp.zeros_like(low)], axis=1)], axis=0
    )


def stack_tile(tile):
    return jnp.concatenate(split_two(tile), axis=0)


def ranges(first, last, body):
    long = (last - first) // GROUP
    middle = first + long * GROUP

    def big(g, carry):
        body(first + g * GROUP, GROUP)
        return carry

    def small(g, carry):
        body(middle + g * TAIL, TAIL)
        return carry

    lax.fori_loop(0, long, big, 0)
    lax.fori_loop(0, (last - middle) // TAIL, small, 0)


def kept_and_made(total, room, body, kept, made):
    first = jnp.minimum(total, room)
    ranges(0, first, functools.partial(body, kept))
    many = (total - first) // TAIL

    def rest(g, carry):
        body(made, first + g * TAIL, TAIL)
        return carry

    lax.fori_loop(0, many, rest, 0)


def entry(plan, slot):
    word = plan[0, slot]
    return word & 63, (word >> 6) & 63, (word >> 12).astype(F32)


def total_of(plan):
    return plan[0, plan.shape[1] - 1]


def inner_edges(acc, vecs, plan, kept, made):
    acc[...] = jnp.zeros_like(acc)
    size = acc.shape[1]

    def group(tile_of, start, many):
        outs = []
        for u in range(many):
            slot = start + u
            a, c, times = entry(plan, slot)
            tile = tile_of(slot, a, c)
            outs.append((c, fold(mxu(vecs[a], tile), size) * times))
            outs.append((a, fold_turned(mxu_turned(vecs[c][:, :BLK], tile), size) * times))
        for c, out in outs:
            acc[c] = acc[c] + out

    kept_and_made(total_of(plan), KEPT, group, kept, made)


def outer_edges(acc, vecs, plan, base, kept, made):
    size = acc.shape[1]

    def group(tile_of, start, many):
        outs = []
        for u in range(many):
            at = start + u
            a, c, times = entry(plan, at)
            outs.append((c, fold(mxu(vecs[a], tile_of(base + at, a, c)), size) * times))
        for c, out in outs:
            acc[c] = acc[c] + out

    kept_and_made(total_of(plan), jnp.maximum(KEPT - base, 0), group, kept, made)


def tile_value(z):
    z = jnp.maximum(z, 0.0)
    return jnp.exp(z * Z_RATE) * (z * z)


def slope_value(z):
    z = jnp.maximum(z, 0.0)
    return (jnp.exp(z * Z_RATE) * z) * (z + Z_STEP)


def fill(into, base, plan, make):
    def body(start, many):
        for u in range(many):
            at = start + u
            a, c, _ = entry(plan, at)
            into[base + at] = make(base + at, a, c)

    ranges(0, jnp.minimum(total_of(plan), jnp.maximum(KEPT - base, 0)), body)


def maker(left, right):
    return lambda slot, a, c: stack_tile(tile_value(mxu(left[a], right[c])))


def keeper(tiles):
    return lambda slot, a, c: tiles[slot]


def whole(n):
    return jnp.floor((n + (TAIL - 1)) * (1.0 / TAIL)) * TAIL


def keys(lists, blocks, cross):
    out = []
    whole_lists = lists.astype(jnp.int32)
    for at in (0, 3):
        a = whole_lists[at : at + 1]
        c = whole_lists[at + 1 : at + 2]
        live = lax.broadcasted_iota(jnp.int32, a.shape, 1) < whole_lists[at + 2 : at + 3]
        if cross:
            out.append(jnp.where(live & (c >= blocks), a * blocks + c - blocks, -1))
        else:
            out.append(jnp.where(live & (c < blocks), a * blocks + c, -1))
    return jnp.concatenate(out, axis=1)


def compact(key, blocks, slots, first):
    size = blocks * blocks
    hot = jnp.where(lax.broadcasted_iota(jnp.int32, (size, key.shape[1]), 0) == key, 1.0, 0.0).astype(BF16)
    counts = mxu(hot, jnp.ones((key.shape[1], LANES), BF16))
    flags = jnp.minimum(counts, 1.0)
    shape = (size, size)
    ahead = lax.broadcasted_iota(jnp.int32, shape, 0) > lax.broadcasted_iota(jnp.int32, shape, 1)
    place = mxu(jnp.where(ahead, 1.0, 0.0).astype(BF16), flags.astype(BF16)) + first
    index = lax.broadcasted_iota(jnp.int32, (16, size), 1).astype(F32)
    row = jnp.floor((index + 0.5) * (1.0 / blocks))
    line = lax.broadcasted_iota(jnp.int32, (16, size), 0)
    names = jnp.where(line == 0, row, jnp.where(line == 1, index - row * blocks, 1.0)).astype(BF16)
    found = []
    times = []
    for part in range(slots // LANES):
        lane = (lax.broadcasted_iota(jnp.int32, (size, LANES), 1) + part * LANES).astype(F32)
        here = (place == lane) & (flags > 0.5)
        found.append(mxu(names, jnp.where(here, 1.0, 0.0).astype(BF16)))
        times.append(mxu(names, jnp.where(here, counts, 0.0).astype(BF16))[2:3])
    found = jnp.concatenate(found, axis=1)
    end = place[size - 1 :] + flags[size - 1 :]
    return found[0:1], found[1:2], found[2:3], jnp.concatenate(times, axis=1), end


def put_plan(ref, rows):
    ref[...] = jnp.zeros(ref.shape, ref.dtype)
    for at, row in enumerate(rows):
        ref[at : at + 1, :] = row.astype(ref.dtype)


def put_words(ref, row, col, times, end):
    slots = ref.shape[1]
    last = lax.broadcasted_iota(jnp.int32, ref.shape, 1) == slots - 1
    ref[...] = jnp.where(last, spread(end, slots), row + 64.0 * col + 4096.0 * times).astype(jnp.int32)


def spread(row, width):
    return jnp.concatenate([row] * (width // LANES), axis=1)


def side_features(blocks, coords, kinds, left, right):
    x = warp(coords)
    scale = -2.0 * Z_OF_D
    square = x * x
    norm = Z_OF_D * (square[:blocks] + square[blocks : 2 * blocks] + square[2 * blocks :])
    x1, x2, x3 = split_three(x)
    n1, n2, n3 = split_three(norm)
    m1, m2, m3 = split_three(norm + Z_TOP)
    one = jnp.ones_like(norm)
    pad = jnp.zeros(((FEATS - 24) * blocks, BLK), F32)
    kinds[...] = jnp.concatenate([x1, x1, x2, x2, x1, x3, n1, n2, n3, one, one, one, pad], axis=0)
    for g in range(0, blocks, 4):
        stack = [kinds[pl.ds(b, FEATS, stride=blocks), :] for b in range(g, g + 4)]
        turned = jnp.concatenate(stack, axis=0).T.astype(BF16)
        for b in range(4):
            left[g + b] = turned[:, b * FEATS : (b + 1) * FEATS]
    if right is not None:
        y1, y2, y3 = split_three(x * scale)
        kinds[...] = jnp.concatenate([y1, y2, y1, y2, y3, y1, one, one, one, m1, m2, m3, pad], axis=0)
        for b in range(blocks):
            right[b] = kinds[pl.ds(b, FEATS, stride=blocks), :].astype(BF16)


def rows_of(packed, blocks):
    lists = packed.shape[0] - LIST_ROWS
    coords = lists - 3 * blocks
    return coords // blocks, coords, lists


def pack_kernel(
    blocks, place, tile_rows, tile_cols, tile_count, signs, coords, noise,
    lists, mine, noise_here, got_signs, got_coords, got_rows, got_cols, sems,
):
    probes, coord_row, list_row = rows_of(mine, blocks)
    first = pl.multiple_of(place[1] * probes, probes)
    moves = [
        pltpu.make_async_copy(coords, got_coords, sems.at[0]),
        pltpu.make_async_copy(signs.at[pl.ds(first, probes), :], got_signs, sems.at[1]),
        pltpu.make_async_copy(tile_rows, got_rows, sems.at[2]),
        pltpu.make_async_copy(tile_cols, got_cols, sems.at[3]),
        pltpu.make_async_copy(noise, noise_here, sems.at[4]),
    ]
    for move in moves:
        move.start()
    lists[...] = jnp.zeros(lists.shape, F32)
    lists[2:3, :] = jnp.full((1, LANES), tile_count[0], jnp.int32).astype(F32)
    for move in moves[2:4]:
        move.wait()
    lists[0:1, : tile_rows.shape[1]] = got_rows[...].astype(F32)
    lists[1:2, : tile_cols.shape[1]] = got_cols[...].astype(F32)
    mine[list_row:] = lists[...]
    moves[0].wait()
    for c in range(3):
        for b in range(blocks):
            at = coord_row + c * blocks + b
            mine[at : at + 1] = got_coords[c : c + 1, b * BLK : (b + 1) * BLK]
    moves[1].wait()
    for b in range(blocks):
        mine[b * probes : (b + 1) * probes] = got_signs[:, b * BLK : (b + 1) * BLK].astype(F32)
    moves[4].wait()


def join_kernel(sibling, old, mine):
    del old
    at = mine.shape[0] - LIST_ROWS + 3
    mine[at : at + 3] = sibling[0:3]


def first_inner_kernel(
    blocks, mine,
    held_plan, tiles, z_ref, cross, left, right, acc, vecs, plan, kinds, sem,
):
    probes, coord_row, list_row = rows_of(mine, blocks)
    lists = mine[list_row:]
    row, col, _, times, end = compact(keys(lists, blocks, False), blocks, held_plan.shape[1], 0.0)
    put_words(held_plan, row, col, times, whole(end))
    move = pltpu.make_async_copy(held_plan, plan, sem)
    move.start()
    row, col, _, times, end = compact(keys(lists, blocks, True), blocks, cross.shape[1], 0.0)
    put_plan(cross, (col, row, times, spread(end, cross.shape[1])))
    for b in range(blocks):
        vecs[b] = stack_vec(mine[b * probes : (b + 1) * probes], True)
    side_features(blocks, mine[coord_row:list_row], kinds, left, right)
    move.wait()
    fill(tiles, 0, plan, maker(left, right))
    inner_edges(acc, vecs, plan, keeper(tiles), maker(left, right))
    z_ref[...] = acc[:blocks]


def finish_apply(blocks, acc, z_of, w_ref, q_of, prev_of, beta, noise):
    probes = acc.shape[1]
    qq = jnp.zeros((probes, LANES), F32)
    qw = jnp.zeros((probes, LANES), F32)
    for b in range(blocks):
        q = q_of(b)
        part = slice(b * BLK, (b + 1) * BLK)
        w = acc[b] + z_of(b) + noise[b : b + 1] * q
        if prev_of is not None:
            w = w - beta * prev_of(b)
        w_ref[:, part] = w
        qq = qq + q * q
        qw = qw + q * w
    put_stats(
        w_ref,
        blocks * BLK,
        lambda b: w_ref[:, b * BLK : (b + 1) * BLK],
        q_of,
        jnp.sum(qq, axis=1, keepdims=True),
        jnp.sum(qw, axis=1, keepdims=True),
        blocks,
    )


def first_outer_kernel(
    blocks, inner_plan, old_tiles, mine, above, below, noise, z_ref, right, cross,
    held_plan, tiles, w_ref, left, acc, vecs, plan, kinds, sem,
):
    probes, coord_row, list_row = rows_of(mine, blocks)
    del old_tiles
    slots = held_plan.shape[1]
    row, col, one, times, end = compact(keys(below[list_row:], blocks, True), blocks, slots, cross[3:4, :LANES])
    put_words(held_plan, cross[0:1] + row + blocks * one, cross[1:2] + col, cross[2:3] + times, whole(end))
    move = pltpu.make_async_copy(held_plan, plan, sem)
    move.start()
    for part, ref in enumerate((above, below)):
        side_features(blocks, ref[coord_row:list_row], kinds, left.at[part * blocks : (part + 1) * blocks], None)
        for b in range(blocks):
            vecs[part * blocks + b] = stack_vec(ref[b * probes : (b + 1) * probes], True)
    acc[...] = jnp.zeros_like(acc)
    move.wait()
    base = total_of(inner_plan)
    fill(tiles, base, plan, maker(left, right))
    outer_edges(acc, vecs, plan, base, keeper(tiles), maker(left, right))
    finish_apply(
        blocks, acc, lambda b: z_ref[b], w_ref, lambda b: mine[b * probes : (b + 1) * probes], None, None, noise
    )


def slab_alpha(w_ref, blocks):
    sums = w_ref[:, blocks * BLK : (blocks + 1) * BLK]
    return sums[:, 0:1] / jnp.maximum(sums[:, 1:2], 1e-30)


def inner_kernel(blocks, plan, w_ref, q_own, tiles, left, right, z_ref, acc, vecs):
    alpha = slab_alpha(w_ref, blocks)
    probes = w_ref.shape[0]
    for b in range(blocks):
        vecs[b] = stack_vec(w_ref[:, b * BLK : (b + 1) * BLK] - alpha * block_of(q_own, probes, b), False)
    inner_edges(acc, vecs, plan, keeper(tiles), maker(left, right))
    z_ref[...] = acc[:blocks]


def alpha_beta(stats, points):
    qw = [s[:, 0:1] for s in stats]
    qq = [s[:, 1:2] for s in stats]
    res = [s[:, 2:3] for s in stats]
    alpha = functools.reduce(jnp.add, qw) / points
    total = jnp.zeros_like(alpha)
    for w, q, r in zip(qw, qq, res):
        gap = alpha - w / jnp.maximum(q, 1e-30)
        total = total + (r + gap * gap * q)
    return alpha, jnp.sqrt(total / points + EPSILON)


def global_alpha_beta(slabs, points, place, stats_ref):
    order = [stats_ref[lax.rem(slab - place[0] + slabs, slabs)] for slab in range(slabs)]
    return alpha_beta(order, points)


def add_ab(ref, base, old_ab, step, alpha, beta):
    shape = (alpha.shape[0], LANES)
    lane = lax.broadcasted_iota(jnp.int32, shape, 1)
    out = jnp.zeros(shape, F32) if old_ab is None else old_ab[...]
    out = jnp.where(lane == step, alpha, out)
    ref[:, base : base + LANES] = jnp.where(lane == ITERS + step, beta, out)


def block_of(ref, rows, b):
    if len(ref.shape) == 3:
        return ref[b]
    return ref[b * rows : (b + 1) * rows]


def outer_kernel(
    blocks, slabs, points, step, place, inner_plan, plan, mine, above, below, stats_ref,
    q_own, q_above, q_below, z_raw, z_old, noise, tiles, left, right, *rest,
):
    probes = mine.shape[0]
    old_ab = None
    if step > 0:
        old_ab = rest[0]
        rest = rest[1:]
    w_ref, own_ref, above_ref, below_ref, ab_ref, *z_ref, acc, vecs, held_z = rest
    alpha, beta = global_alpha_beta(slabs, points, place, stats_ref)
    scale = 1.0 / beta
    apart = alpha - slab_alpha(mine, blocks)
    add_ab(ab_ref, 0, old_ab, step, alpha, beta)
    halves = ((mine, q_own, own_ref), (above, q_above, above_ref), (below, q_below, below_ref))
    for part, (w, old, new) in enumerate(halves):
        for b in range(blocks):
            q = (w[:, b * BLK : (b + 1) * BLK] - alpha * block_of(old, probes, b)) * scale
            new[b] = q
            if part > 0:
                vecs[(part - 1) * blocks + b] = stack_vec(q, False)
            else:
                z = (z_raw[b] - apart * z_old[b]) * scale
                held_z[b] = z
                for ref in z_ref:
                    ref[b] = z
    acc[...] = jnp.zeros_like(acc)
    outer_edges(acc, vecs, plan, total_of(inner_plan), keeper(tiles), maker(left, right))
    finish_apply(
        blocks, acc, lambda b: held_z[b], w_ref, lambda b: own_ref[b], lambda b: block_of(q_own, probes, b), beta, noise
    )


def slope_kernel(inner_plan, plan, left_own, left_halo, right, after, slopes):
    del after

    def make(left):
        return lambda slot, a, c: slope_value(mxu(left[a], right[c]))

    fill(slopes, 0, inner_plan, make(left_own))
    fill(slopes, total_of(inner_plan), plan, make(left_halo))


def points_kernel(blocks, pts, pts_above, pts_below, after, pnts, halo_pnts, slack, kinds):
    del after
    _, coord_row, list_row = rows_of(pts, blocks)
    for part, ref in enumerate((pts, pts_above, pts_below)):
        raw = ref[coord_row:list_row]
        bent = jnp.tanh(raw)
        x = raw + WARP_GAIN * bent
        x1, x2, x3 = split_three(x)
        one = jnp.ones((blocks, BLK), F32)
        kinds[...] = jnp.concatenate([x1, x2, x3, one, jnp.zeros((6 * blocks, BLK), F32)], axis=0)
        if part == 0:
            slope = 1.0 + WARP_GAIN * (1.0 - bent * bent)
            slack[...] = jnp.concatenate([x, slope, jnp.zeros((6 * blocks, BLK), F32)], axis=0)
        for b in range(blocks):
            y = kinds[pl.ds(b, 16, stride=blocks), :].astype(BF16)
            y = jnp.concatenate([y, y], axis=1)
            if part == 0:
                pnts[b] = y
            else:
                halo_pnts[(part - 1) * blocks + b] = y


def last_kernel(
    blocks, slabs, points, all_probes, place, inner_plan, plan, mine, above, below, stats_ref,
    q_own, q_above, q_below, pts, pts_above, pts_below, old_ab, slopes, left_own, left_out, right, pnts, halo_pnts, slack,
    basis_ref, grad_ref, acc, form_left, halo_left, form_right, pulls,
):
    probes, _, _ = rows_of(pts, blocks)
    alpha, beta = global_alpha_beta(slabs, points, place, stats_ref)
    scale = 1.0 / beta
    add_ab(basis_ref, blocks * BLK, old_ab, ITERS - 1, alpha, beta)
    for part, (w, old, ref) in enumerate(((mine, q_own, pts), (above, q_above, pts_above), (below, q_below, pts_below))):
        for b in range(blocks):
            part_cols = slice(b * BLK, (b + 1) * BLK)
            u = (w[:, part_cols] - alpha * block_of(old, probes, b)) * scale
            v = ref[b * probes : (b + 1) * probes]
            high = u.astype(BF16).astype(F32)
            low = u - high
            turned = jnp.concatenate([high, low, v, v], axis=0).T.astype(BF16)
            if part == 0:
                basis_ref[:, part_cols] = u
                form_left[b] = turned
                form_right[b] = jnp.concatenate([v, v, high, low], axis=0).astype(BF16)
            else:
                halo_left[(part - 1) * blocks + b] = turned

    def pull(side):
        return lambda slot, a, c: stack_tile(mxu(side[a], form_right[c]) * slopes[slot])

    def pull_made(side, left):
        return lambda slot, a, c: stack_tile(mxu(side[a], form_right[c]) * slope_value(mxu(left[a], right[c])))

    base = total_of(inner_plan)
    fill(pulls, 0, inner_plan, pull(form_left))
    fill(pulls, base, plan, pull(halo_left))
    inner_edges(acc, pnts, inner_plan, keeper(pulls), pull_made(form_left, left_own))
    outer_edges(acc, halo_pnts, plan, base, keeper(pulls), pull_made(halo_left, left_out))
    for b in range(blocks):
        part_cols = slice(b * BLK, (b + 1) * BLK)
        x = slack[pl.ds(b, 8, stride=blocks), :][0:3]
        chain = slack[pl.ds(3 * blocks + b, 8, stride=blocks), :][0:3]
        sums = acc[b]
        moved = sums[0:3] + sums[3:6] + sums[6:9] - x * sums[9:10]
        grad_ref[:, part_cols] = moved * chain * (1.0 / (LENGTH_SQ * all_probes))


def close_kernel(place, own, other, grad, basis_ref, alpha_ref, beta_ref, same_grad):
    same_grad[...] = grad[...]
    probes = own.shape[0]
    width = basis_ref.shape[1]
    lower = place[1] == 0
    mine = own[...]
    theirs = other[...]
    first = jnp.where(lower, mine, theirs)
    second = jnp.where(lower, theirs, mine)
    basis_ref[:probes] = first[:, :width]
    basis_ref[probes:] = second[:, :width]
    ab = jnp.concatenate([first[:, width:], second[:, width:]], axis=0)
    turned = jnp.concatenate([ab, jnp.zeros((LANES - 2 * probes, LANES), F32)], axis=0).T
    alpha_ref[...] = turned[:ITERS, : 2 * probes]
    beta_ref[...] = turned[ITERS : 2 * ITERS, : 2 * probes]


def vmem(count):
    return [pl.BlockSpec(memory_space=pltpu.VMEM)] * count


def smem(count):
    return [pl.BlockSpec(memory_space=pltpu.SMEM)] * count


def held(array):
    return pltpu.with_memory_space_constraint(array, pltpu.VMEM)


def stays(array):
    return pltpu.with_memory_space_constraint(array, pltpu.HBM)


def in_hbm(count):
    return [pl.BlockSpec(memory_space=pltpu.HBM)] * count


def call(name, kernel, outs, ins, scratch, work, aliases=None, limit=LIMIT_MIB):
    out_shapes, out_scalars = outs
    arrays, scalars = ins
    flops, moved = work
    return pl.pallas_call(
        kernel,
        out_shape=tuple(out_shapes),
        in_specs=smem(scalars) + vmem(len(arrays) - scalars),
        out_specs=tuple(smem(out_scalars) + vmem(len(out_shapes) - out_scalars)),
        scratch_shapes=[pltpu.VMEM(*entry) if isinstance(entry, tuple) else entry for entry in scratch],
        compiler_params=pltpu.CompilerParams(vmem_limit_bytes=limit * 1024 * 1024),
        cost_estimate=pl.CostEstimate(flops=flops, bytes_accessed=moved, transcendentals=0),
        input_output_aliases=aliases or {},
        name=name,
    )(*arrays)


def shifted(value, axes, count, steps):
    return lax.ppermute(value, axes, [(source, (source + steps) % count) for source in range(count)])


def body(coords, noise_var, probe_signs, tile_rows, tile_cols, tile_count):
    slabs = lax.axis_size("blk")
    subs = lax.axis_size("sub")
    outer = lax.axis_size("probe")
    probes = probe_signs.shape[0] // subs
    width = coords.shape[1]
    blocks = width // BLK
    cap = tile_rows.shape[-1]
    points = float(width * slabs)
    all_probes = probe_signs.shape[0] * outer
    sub = lax.axis_index("sub")
    blk = lax.axis_index("blk")
    place = jnp.stack([blk, sub]).astype(jnp.int32)
    sds = jax.ShapeDtypeStruct

    left_shape = sds((blocks, BLK, FEATS), BF16)
    right_shape = sds((blocks, FEATS, BLK), BF16)
    packed = sds((blocks * (probes + 3) + LIST_ROWS, BLK), F32)
    kinds = ((blocks * FEATS, BLK), F32)
    lists, own, noise = pl.pallas_call(
        functools.partial(pack_kernel, blocks),
        out_shape=(sds((LIST_ROWS, LANES), F32), packed, sds((blocks, BLK), F32)),
        in_specs=smem(1) + in_hbm(2) + smem(1) + in_hbm(3),
        out_specs=tuple(vmem(3)),
        scratch_shapes=[
            pltpu.VMEM((probes, width), jnp.int32),
            pltpu.VMEM((3, width), F32),
            pltpu.VMEM((1, cap), jnp.int32),
            pltpu.VMEM((1, cap), jnp.int32),
            pltpu.SemaphoreType.DMA((5,)),
        ],
        compiler_params=pltpu.CompilerParams(vmem_limit_bytes=LIMIT_MIB * 1024 * 1024),
        name="pack",
    )(
        place, stays(tile_rows.reshape(1, cap)), stays(tile_cols.reshape(1, cap)), tile_count.reshape(1),
        stays(probe_signs), stays(coords), stays(noise_var.reshape(blocks, BLK)),
    )
    sibling = shifted(lists, "sub", subs, 1)
    (mine,) = call("join", join_kernel, ((packed,), 0), ((sibling, own), 0), [], (1000, 1000), {1: 0})
    above = shifted(mine, "blk", slabs, -1)
    below = shifted(mine, "blk", slabs, 1)

    ints = jnp.int32
    inner_slots = (blocks * (blocks + 1) // 2 + TAIL + LANES) // LANES * LANES
    outer_slots = (blocks * (blocks + 1) + TAIL + LANES) // LANES * LANES
    plan_shape = sds((1, inner_slots), ints)
    outer_plan_shape = sds((1, outer_slots), ints)
    inner_smem = pltpu.SMEM((1, inner_slots), ints)
    outer_smem = pltpu.SMEM((1, outer_slots), ints)
    slots = KEPT
    ext = width + LANES
    blocks_f32 = sds((blocks, probes, BLK), F32)
    tile_shape = pltpu.VMEM((slots, 2 * BLK, BLK), BF16)
    acc_shape = ((blocks, probes, BLK), F32)

    inner_plan, tiles, z, cross, left_own, right = call(
        "first_inner",
        functools.partial(first_inner_kernel, blocks),
        ((plan_shape, tile_shape, blocks_f32, sds((LIST_ROWS, outer_slots), F32), left_shape, right_shape), 0),
        ((mine,), 0),
        [
            acc_shape, ((blocks, probes, 2 * BLK), BF16), inner_smem, kinds,
            pltpu.SemaphoreType.DMA,
        ],
        (WORK_FIRST, WORK_BYTES),
    )
    outer_plan, tiles, w, left_halo = call(
        "first_outer",
        functools.partial(first_outer_kernel, blocks),
        ((outer_plan_shape, tile_shape, sds((probes, ext), F32), sds((2 * blocks, BLK, FEATS), BF16)), 0),
        ((inner_plan, held(tiles), mine, above, below, noise, z, right, cross), 1),
        [
            acc_shape, ((2 * blocks, probes, 2 * BLK), BF16), outer_smem, kinds,
            pltpu.SemaphoreType.DMA,
        ],
        (WORK_FIRST, WORK_BYTES),
        {1: 1},
    )

    def exchange(w):
        stats = w[:, width:]
        if slabs == 4:
            far = shifted(stats, "blk", slabs, 2)
        up = shifted(w, "blk", slabs, -1)
        down = shifted(w, "blk", slabs, 1)
        if slabs == 4:
            rows = jnp.stack([stats, up[:, width:], far, down[:, width:]])
        else:
            rows = lax.all_gather(stats, "blk", axis=0)
            rows = jnp.roll(rows, -blk, axis=0)
        return up, down, rows

    q = (mine, above, below)
    ab = []
    z_old = z
    for step in range(ITERS - 1):
        up, down, stats = exchange(w)
        (z_raw,) = call(
            "inner",
            functools.partial(inner_kernel, blocks),
            ((blocks_f32,), 0),
            ((inner_plan, w, q[0], held(tiles), left_own, right), 1),
            [acc_shape, ((blocks, 2 * probes, 2 * BLK), BF16)],
            (WORK_NEXT, WORK_BYTES),
        )
        w, q0, q1, q2, next_ab, *z = call(
            "outer",
            functools.partial(outer_kernel, blocks, slabs, points, step),
            (
                (
                    sds((probes, ext), F32), blocks_f32, blocks_f32, blocks_f32, sds((probes, LANES), F32),
                    *([blocks_f32] if step < ITERS - 2 else []),
                ),
                0,
            ),
            ((place, inner_plan, outer_plan, w, up, down, stats, *q, z_raw, z_old, noise, held(tiles), left_halo, right, *ab), 3),
            [acc_shape, ((2 * blocks, 2 * probes, 2 * BLK), BF16), ((blocks, probes, BLK), F32)],
            (WORK_NEXT, WORK_BYTES),
        )
        q = (q0, q1, q2)
        ab = [next_ab]
        z_old = z[0] if z else None

    up, down, stats = exchange(w)
    (slopes,) = call(
        "slopes",
        slope_kernel,
        ((pltpu.VMEM((slots, BLK, BLK), F32),), 0),
        ((inner_plan, outer_plan, left_own, left_halo, right, w), 2),
        [],
        (WORK_FIRST, WORK_BYTES),
    )
    pnts, halo_pnts, slack = call(
        "points",
        functools.partial(points_kernel, blocks),
        (
            (
                sds((blocks, 16, 2 * BLK), BF16), sds((2 * blocks, 16, 2 * BLK), BF16), sds((12 * blocks, BLK), F32),
            ),
            0,
        ),
        ((mine, above, below, w), 0),
        [((blocks * 16, BLK), F32)],
        (WORK_NEXT, WORK_BYTES),
    )
    basis, grad = call(
        "last",
        functools.partial(last_kernel, blocks, slabs, points, all_probes),
        ((sds((probes, ext), F32), sds((3, width), F32)), 0),
        (
            (
                place, inner_plan, outer_plan, w, up, down, stats, *q, mine, above, below, *ab, held(slopes), left_own, left_halo,
                right, pnts, halo_pnts, slack,
            ),
            3,
        ),
        [
            ((blocks, 16, BLK), F32),
            ((blocks, BLK, 4 * probes), BF16),
            ((2 * blocks, BLK, 4 * probes), BF16),
            ((blocks, 4 * probes, BLK), BF16),
            ((slots, 2 * BLK, BLK), BF16),
        ],
        (WORK_FIRST, WORK_BYTES),
        limit=LIMIT_MIB * 3 // 2,
    )

    if outer == 2 and subs == 2:
        axes = ("probe", "sub")
        across, diagonal, beside = (lax.ppermute(grad, axes, [(k, k ^ flip) for k in range(4)]) for flip in (2, 3, 1))
    other = shifted(basis, "sub", subs, 1)
    last_basis, alphas, betas, grad = call(
        "close",
        close_kernel,
        (
            (
                sds((subs * probes, width), F32), sds((ITERS, subs * probes), F32), sds((ITERS, subs * probes), F32),
                sds((3, width), F32),
            ),
            0,
        ),
        ((place, basis, other, grad), 1),
        [],
        (1000000, 1000000),
    )
    if outer == 2 and subs == 2:
        coord_grad = (grad + beside) + (across + diagonal)
    else:
        coord_grad = lax.psum(grad, ("probe", "sub"))
    return alphas, betas, last_basis, coord_grad


def solution(mesh):
    return jax.shard_map(
        body,
        mesh=mesh,
        in_specs=(
            P(None, ("groups", "blk")),
            P(("groups", "blk")),
            P("probe", ("groups", "blk")),
            P(("groups", "blk"), "sub", None),
            P(("groups", "blk"), "sub", None),
            P(("groups", "blk"), "sub"),
        ),
        out_specs=(
            P(None, ("groups", "probe")),
            P(None, ("groups", "probe")),
            P("probe", ("groups", "blk")),
            P(None, ("groups", "blk")),
        ),
        check_vma=False,
    )
```

```python
import functools
import math

import jax
import jax.numpy as jnp
from jax import lax
from jax.experimental import pallas as pl
from jax.experimental.pallas import tpu as pltpu
from jax.sharding import PartitionSpec as P

ITERS = 3
SIGNAL_VAR = 0.1
LENGTH_SQ = 2.0
TAPER_SQ = 16.0
WARP_GAIN = 0.4
EPSILON = 1e-06

BLK = 128
LANES = 128
FEATS = 32
GROUP = 32
TAIL = 8
LIST_ROWS = 8
LIMIT_MIB = 16
KEPT = 256
WORK_FIRST = 300000000
WORK_NEXT = 100000000
WORK_BYTES = 4000000

DECAY = TAPER_SQ / (2.0 * LENGTH_SQ)
Z_TOP = math.sqrt(SIGNAL_VAR * math.exp(-DECAY))
Z_RATE = DECAY / Z_TOP
Z_OF_D = -Z_TOP / TAPER_SQ
Z_STEP = 4.0 * LENGTH_SQ / TAPER_SQ * Z_TOP

F32 = jnp.float32
BF16 = jnp.bfloat16


def split_two(x):
    high = x.astype(BF16)
    low = (x - high.astype(F32)).astype(BF16)
    return high, low


def split_three(x):
    one = x.astype(BF16).astype(F32)
    rest = x - one
    two = rest.astype(BF16).astype(F32)
    three = (rest - two).astype(BF16).astype(F32)
    return one, two, three


def warp(x):
    return x + WARP_GAIN * jnp.tanh(x)


def mxu(a, b):
    return lax.dot_general(a, b, (((1,), (0,)), ((), ())), preferred_element_type=F32)


def put_stats(ref, base, w_of, q_of, qq, qw, blocks):
    alpha_s = qw / jnp.maximum(qq, 1e-30)
    acc = jnp.zeros((qq.shape[0], LANES), F32)
    for b in range(blocks):
        r = w_of(b) - alpha_s * q_of(b)
        acc = acc + r * r
    res = jnp.sum(acc, axis=1, keepdims=True)
    lane = lax.broadcasted_iota(jnp.int32, (qq.shape[0], LANES), 1)
    out = jnp.where(lane == 0, qw, jnp.where(lane == 1, qq, jnp.where(lane == 2, res, 0.0)))
    ref[:, base : base + LANES] = out


def mxu_turned(a, b):
    return lax.dot_general(a, b, (((1,), (1,)), ((), ())), preferred_element_type=F32)


def fold(out, probes):
    if out.shape[0] > probes:
        return out[:probes] + out[probes:]
    return out


def fold_turned(out, probes):
    total = out[:probes, :BLK] + out[:probes, BLK:]
    if out.shape[0] > probes:
        total = total + out[probes:, :BLK]
    return total


def stack_vec(q, exact):
    if exact:
        high = q.astype(BF16)
        return jnp.concatenate([high, high], axis=1)
    high, low = split_two(q)
    return jnp.concatenate(
        [jnp.concatenate([high, high], axis=1), jnp.concatenate([low, jnp.zeros_like(low)], axis=1)], axis=0
    )


def stack_tile(tile):
    return jnp.concatenate(split_two(tile), axis=0)


def ranges(first, last, body):
    long = (last - first) // GROUP
    middle = first + long * GROUP

    def big(g, carry):
        body(first + g * GROUP, GROUP)
        return carry

    def small(g, carry):
        body(middle + g * TAIL, TAIL)
        return carry

    lax.fori_loop(0, long, big, 0)
    lax.fori_loop(0, (last - middle) // TAIL, small, 0)


def kept_and_made(total, room, body, kept, made):
    first = jnp.minimum(total, room)
    ranges(0, first, functools.partial(body, kept))
    many = (total - first) // TAIL

    def rest(g, carry):
        body(made, first + g * TAIL, TAIL)
        return carry

    lax.fori_loop(0, many, rest, 0)


def entry(plan, slot):
    word = plan[0, slot]
    return word & 63, (word >> 6) & 63, (word >> 12).astype(F32)


def total_of(plan):
    return plan[0, plan.shape[1] - 1]


def inner_edges(acc, vecs, plan, kept, made):
    acc[...] = jnp.zeros_like(acc)
    size = acc.shape[1]

    def group(tile_of, start, many):
        outs = []
        for u in range(many):
            slot = start + u
            a, c, times = entry(plan, slot)
            tile = tile_of(slot, a, c)
            outs.append((c, fold(mxu(vecs[a], tile), size) * times))
            outs.append((a, fold_turned(mxu_turned(vecs[c][:, :BLK], tile), size) * times))
        for c, out in outs:
            acc[c] = acc[c] + out

    kept_and_made(total_of(plan), KEPT, group, kept, made)


def outer_edges(acc, vecs, plan, base, kept, made):
    size = acc.shape[1]

    def group(tile_of, start, many):
        outs = []
        for u in range(many):
            at = start + u
            a, c, times = entry(plan, at)
            outs.append((c, fold(mxu(vecs[a], tile_of(base + at, a, c)), size) * times))
        for c, out in outs:
            acc[c] = acc[c] + out

    kept_and_made(total_of(plan), jnp.maximum(KEPT - base, 0), group, kept, made)


def tile_value(z):
    z = jnp.maximum(z, 0.0)
    return jnp.exp(z * Z_RATE) * (z * z)


def slope_value(z):
    z = jnp.maximum(z, 0.0)
    return (jnp.exp(z * Z_RATE) * z) * (z + Z_STEP)


def fill(into, base, plan, make):
    def body(start, many):
        for u in range(many):
            at = start + u
            a, c, _ = entry(plan, at)
            into[base + at] = make(base + at, a, c)

    ranges(0, jnp.minimum(total_of(plan), jnp.maximum(KEPT - base, 0)), body)


def maker(left, right):
    return lambda slot, a, c: stack_tile(tile_value(mxu(left[a], right[c])))


def keeper(tiles):
    return lambda slot, a, c: tiles[slot]


def whole(n):
    return jnp.floor((n + (TAIL - 1)) * (1.0 / TAIL)) * TAIL


def keys(lists, blocks, cross):
    out = []
    whole_lists = lists.astype(jnp.int32)
    for at in (0, 3):
        a = whole_lists[at : at + 1]
        c = whole_lists[at + 1 : at + 2]
        live = lax.broadcasted_iota(jnp.int32, a.shape, 1) < whole_lists[at + 2 : at + 3]
        if cross:
            out.append(jnp.where(live & (c >= blocks), a * blocks + c - blocks, -1))
        else:
            out.append(jnp.where(live & (c < blocks), a * blocks + c, -1))
    return jnp.concatenate(out, axis=1)


def compact(key, blocks, slots, first):
    size = blocks * blocks
    hot = jnp.where(lax.broadcasted_iota(jnp.int32, (size, key.shape[1]), 0) == key, 1.0, 0.0).astype(BF16)
    counts = mxu(hot, jnp.ones((key.shape[1], LANES), BF16))
    flags = jnp.minimum(counts, 1.0)
    shape = (size, size)
    ahead = lax.broadcasted_iota(jnp.int32, shape, 0) > lax.broadcasted_iota(jnp.int32, shape, 1)
    place = mxu(jnp.where(ahead, 1.0, 0.0).astype(BF16), flags.astype(BF16)) + first
    index = lax.broadcasted_iota(jnp.int32, (16, size), 1).astype(F32)
    row = jnp.floor((index + 0.5) * (1.0 / blocks))
    line = lax.broadcasted_iota(jnp.int32, (16, size), 0)
    names = jnp.where(line == 0, row, jnp.where(line == 1, index - row * blocks, 1.0)).astype(BF16)
    found = []
    times = []
    for part in range(slots // LANES):
        lane = (lax.broadcasted_iota(jnp.int32, (size, LANES), 1) + part * LANES).astype(F32)
        here = (place == lane) & (flags > 0.5)
        found.append(mxu(names, jnp.where(here, 1.0, 0.0).astype(BF16)))
        times.append(mxu(names, jnp.where(here, counts, 0.0).astype(BF16))[2:3])
    found = jnp.concatenate(found, axis=1)
    end = place[size - 1 :] + flags[size - 1 :]
    return found[0:1], found[1:2], found[2:3], jnp.concatenate(times, axis=1), end


def put_plan(ref, rows):
    ref[...] = jnp.zeros(ref.shape, ref.dtype)
    for at, row in enumerate(rows):
        ref[at : at + 1, :] = row.astype(ref.dtype)


def put_words(ref, row, col, times, end):
    slots = ref.shape[1]
    last = lax.broadcasted_iota(jnp.int32, ref.shape, 1) == slots - 1
    ref[...] = jnp.where(last, spread(end, slots), row + 64.0 * col + 4096.0 * times).astype(jnp.int32)


def spread(row, width):
    return jnp.concatenate([row] * (width // LANES), axis=1)


def side_features(blocks, coords, kinds, left, right):
    x = warp(coords)
    scale = -2.0 * Z_OF_D
    square = x * x
    norm = Z_OF_D * (square[:blocks] + square[blocks : 2 * blocks] + square[2 * blocks :])
    x1, x2, x3 = split_three(x)
    n1, n2, n3 = split_three(norm)
    m1, m2, m3 = split_three(norm + Z_TOP)
    one = jnp.ones_like(norm)
    pad = jnp.zeros(((FEATS - 24) * blocks, BLK), F32)
    kinds[...] = jnp.concatenate([x1, x1, x2, x2, x1, x3, n1, n2, n3, one, one, one, pad], axis=0)
    for g in range(0, blocks, 4):
        stack = [kinds[pl.ds(b, FEATS, stride=blocks), :] for b in range(g, g + 4)]
        turned = jnp.concatenate(stack, axis=0).T.astype(BF16)
        for b in range(4):
            left[g + b] = turned[:, b * FEATS : (b + 1) * FEATS]
    if right is not None:
        y1, y2, y3 = split_three(x * scale)
        kinds[...] = jnp.concatenate([y1, y2, y1, y2, y3, y1, one, one, one, m1, m2, m3, pad], axis=0)
        for b in range(blocks):
            right[b] = kinds[pl.ds(b, FEATS, stride=blocks), :].astype(BF16)


def rows_of(packed, blocks):
    lists = packed.shape[0] - LIST_ROWS
    coords = lists - 3 * blocks
    return coords // blocks, coords, lists


def pack_kernel(
    blocks, place, tile_rows, tile_cols, tile_count, signs, coords, noise,
    lists, mine, noise_here, got_signs, got_coords, got_rows, got_cols, sems,
):
    probes, coord_row, list_row = rows_of(mine, blocks)
    first = pl.multiple_of(place[1] * probes, probes)
    moves = [
        pltpu.make_async_copy(coords, got_coords, sems.at[0]),
        pltpu.make_async_copy(signs.at[pl.ds(first, probes), :], got_signs, sems.at[1]),
        pltpu.make_async_copy(tile_rows, got_rows, sems.at[2]),
        pltpu.make_async_copy(tile_cols, got_cols, sems.at[3]),
        pltpu.make_async_copy(noise, noise_here, sems.at[4]),
    ]
    for move in moves:
        move.start()
    lists[...] = jnp.zeros(lists.shape, F32)
    lists[2:3, :] = jnp.full((1, LANES), tile_count[0], jnp.int32).astype(F32)
    for move in moves[2:4]:
        move.wait()
    lists[0:1, : tile_rows.shape[1]] = got_rows[...].astype(F32)
    lists[1:2, : tile_cols.shape[1]] = got_cols[...].astype(F32)
    mine[list_row:] = lists[...]
    moves[0].wait()
    for c in range(3):
        for b in range(blocks):
            at = coord_row + c * blocks + b
            mine[at : at + 1] = got_coords[c : c + 1, b * BLK : (b + 1) * BLK]
    moves[1].wait()
    for b in range(blocks):
        mine[b * probes : (b + 1) * probes] = got_signs[:, b * BLK : (b + 1) * BLK].astype(F32)
    moves[4].wait()


def join_kernel(sibling, old, mine):
    del old
    at = mine.shape[0] - LIST_ROWS + 3
    mine[at : at + 3] = sibling[0:3]


def first_inner_kernel(
    blocks, mine,
    held_plan, tiles, z_ref, cross, left, right, acc, vecs, plan, kinds, sem,
):
    probes, coord_row, list_row = rows_of(mine, blocks)
    lists = mine[list_row:]
    row, col, _, times, end = compact(keys(lists, blocks, False), blocks, held_plan.shape[1], 0.0)
    put_words(held_plan, row, col, times, whole(end))
    move = pltpu.make_async_copy(held_plan, plan, sem)
    move.start()
    row, col, _, times, end = compact(keys(lists, blocks, True), blocks, cross.shape[1], 0.0)
    put_plan(cross, (col, row, times, spread(end, cross.shape[1])))
    for b in range(blocks):
        vecs[b] = stack_vec(mine[b * probes : (b + 1) * probes], True)
    side_features(blocks, mine[coord_row:list_row], kinds, left, right)
    move.wait()
    fill(tiles, 0, plan, maker(left, right))
    inner_edges(acc, vecs, plan, keeper(tiles), maker(left, right))
    z_ref[...] = acc[:blocks]


def finish_apply(blocks, acc, z_of, w_ref, q_of, prev_of, beta, noise):
    probes = acc.shape[1]
    qq = jnp.zeros((probes, LANES), F32)
    qw = jnp.zeros((probes, LANES), F32)
    for b in range(blocks):
        q = q_of(b)
        part = slice(b * BLK, (b + 1) * BLK)
        w = acc[b] + z_of(b) + noise[b : b + 1] * q
        if prev_of is not None:
            w = w - beta * prev_of(b)
        w_ref[:, part] = w
        qq = qq + q * q
        qw = qw + q * w
    put_stats(
        w_ref,
        blocks * BLK,
        lambda b: w_ref[:, b * BLK : (b + 1) * BLK],
        q_of,
        jnp.sum(qq, axis=1, keepdims=True),
        jnp.sum(qw, axis=1, keepdims=True),
        blocks,
    )


def first_outer_kernel(
    blocks, inner_plan, old_tiles, mine, above, below, noise, z_ref, right, cross,
    held_plan, tiles, w_ref, left, acc, vecs, plan, kinds, sem,
):
    probes, coord_row, list_row = rows_of(mine, blocks)
    del old_tiles
    slots = held_plan.shape[1]
    row, col, one, times, end = compact(keys(below[list_row:], blocks, True), blocks, slots, cross[3:4, :LANES])
    put_words(held_plan, cross[0:1] + row + blocks * one, cross[1:2] + col, cross[2:3] + times, whole(end))
    move = pltpu.make_async_copy(held_plan, plan, sem)
    move.start()
    for part, ref in enumerate((above, below)):
        side_features(blocks, ref[coord_row:list_row], kinds, left.at[part * blocks : (part + 1) * blocks], None)
        for b in range(blocks):
            vecs[part * blocks + b] = stack_vec(ref[b * probes : (b + 1) * probes], True)
    acc[...] = jnp.zeros_like(acc)
    move.wait()
    base = total_of(inner_plan)
    fill(tiles, base, plan, maker(left, right))
    outer_edges(acc, vecs, plan, base, keeper(tiles), maker(left, right))
    finish_apply(
        blocks, acc, lambda b: z_ref[b], w_ref, lambda b: mine[b * probes : (b + 1) * probes], None, None, noise
    )


def slab_alpha(w_ref, blocks):
    sums = w_ref[:, blocks * BLK : (blocks + 1) * BLK]
    return sums[:, 0:1] / jnp.maximum(sums[:, 1:2], 1e-30)


def inner_kernel(blocks, plan, w_ref, q_own, tiles, left, right, z_ref, acc, vecs):
    alpha = slab_alpha(w_ref, blocks)
    probes = w_ref.shape[0]
    for b in range(blocks):
        vecs[b] = stack_vec(w_ref[:, b * BLK : (b + 1) * BLK] - alpha * block_of(q_own, probes, b), False)
    inner_edges(acc, vecs, plan, keeper(tiles), maker(left, right))
    z_ref[...] = acc[:blocks]


def alpha_beta(stats, points):
    qw = [s[:, 0:1] for s in stats]
    qq = [s[:, 1:2] for s in stats]
    res = [s[:, 2:3] for s in stats]
    alpha = functools.reduce(jnp.add, qw) / points
    total = jnp.zeros_like(alpha)
    for w, q, r in zip(qw, qq, res):
        gap = alpha - w / jnp.maximum(q, 1e-30)
        total = total + (r + gap * gap * q)
    return alpha, jnp.sqrt(total / points + EPSILON)


def global_alpha_beta(slabs, points, place, stats_ref):
    order = [stats_ref[lax.rem(slab - place[0] + slabs, slabs)] for slab in range(slabs)]
    return alpha_beta(order, points)


def add_ab(ref, base, old_ab, step, alpha, beta):
    shape = (alpha.shape[0], LANES)
    lane = lax.broadcasted_iota(jnp.int32, shape, 1)
    out = jnp.zeros(shape, F32) if old_ab is None else old_ab[...]
    out = jnp.where(lane == step, alpha, out)
    ref[:, base : base + LANES] = jnp.where(lane == ITERS + step, beta, out)


def block_of(ref, rows, b):
    if len(ref.shape) == 3:
        return ref[b]
    return ref[b * rows : (b + 1) * rows]


def outer_kernel(
    blocks, slabs, points, step, place, inner_plan, plan, mine, above, below, stats_ref,
    q_own, q_above, q_below, z_raw, z_old, noise, tiles, left, right, *rest,
):
    probes = mine.shape[0]
    old_ab = None
    if step > 0:
        old_ab = rest[0]
        rest = rest[1:]
    w_ref, own_ref, above_ref, below_ref, ab_ref, *z_ref, acc, vecs, held_z = rest
    alpha, beta = global_alpha_beta(slabs, points, place, stats_ref)
    scale = 1.0 / beta
    apart = alpha - slab_alpha(mine, blocks)
    add_ab(ab_ref, 0, old_ab, step, alpha, beta)
    halves = ((mine, q_own, own_ref), (above, q_above, above_ref), (below, q_below, below_ref))
    for part, (w, old, new) in enumerate(halves):
        for b in range(blocks):
            q = (w[:, b * BLK : (b + 1) * BLK] - alpha * block_of(old, probes, b)) * scale
            new[b] = q
            if part > 0:
                vecs[(part - 1) * blocks + b] = stack_vec(q, False)
            else:
                z = (z_raw[b] - apart * z_old[b]) * scale
                held_z[b] = z
                for ref in z_ref:
                    ref[b] = z
    acc[...] = jnp.zeros_like(acc)
    outer_edges(acc, vecs, plan, total_of(inner_plan), keeper(tiles), maker(left, right))
    finish_apply(
        blocks, acc, lambda b: held_z[b], w_ref, lambda b: own_ref[b], lambda b: block_of(q_own, probes, b), beta, noise
    )


def slope_kernel(inner_plan, plan, left_own, left_halo, right, after, slopes):
    del after

    def make(left):
        return lambda slot, a, c: slope_value(mxu(left[a], right[c]))

    fill(slopes, 0, inner_plan, make(left_own))
    fill(slopes, total_of(inner_plan), plan, make(left_halo))


def points_kernel(blocks, pts, pts_above, pts_below, after, pnts, halo_pnts, slack, kinds):
    del after
    _, coord_row, list_row = rows_of(pts, blocks)
    for part, ref in enumerate((pts, pts_above, pts_below)):
        raw = ref[coord_row:list_row]
        bent = jnp.tanh(raw)
        x = raw + WARP_GAIN * bent
        x1, x2, x3 = split_three(x)
        one = jnp.ones((blocks, BLK), F32)
        kinds[...] = jnp.concatenate([x1, x2, x3, one, jnp.zeros((6 * blocks, BLK), F32)], axis=0)
        if part == 0:
            slope = 1.0 + WARP_GAIN * (1.0 - bent * bent)
            slack[...] = jnp.concatenate([x, slope, jnp.zeros((6 * blocks, BLK), F32)], axis=0)
        for b in range(blocks):
            y = kinds[pl.ds(b, 16, stride=blocks), :].astype(BF16)
            y = jnp.concatenate([y, y], axis=1)
            if part == 0:
                pnts[b] = y
            else:
                halo_pnts[(part - 1) * blocks + b] = y


def last_kernel(
    blocks, slabs, points, all_probes, place, inner_plan, plan, mine, above, below, stats_ref,
    q_own, q_above, q_below, pts, pts_above, pts_below, old_ab, slopes, left_own, left_out, right, pnts, halo_pnts, slack,
    basis_ref, grad_ref, acc, form_left, halo_left, form_right, pulls,
):
    probes, _, _ = rows_of(pts, blocks)
    alpha, beta = global_alpha_beta(slabs, points, place, stats_ref)
    scale = 1.0 / beta
    add_ab(basis_ref, blocks * BLK, old_ab, ITERS - 1, alpha, beta)
    for part, (w, old, ref) in enumerate(((mine, q_own, pts), (above, q_above, pts_above), (below, q_below, pts_below))):
        for b in range(blocks):
            part_cols = slice(b * BLK, (b + 1) * BLK)
            u = (w[:, part_cols] - alpha * block_of(old, probes, b)) * scale
            v = ref[b * probes : (b + 1) * probes]
            high = u.astype(BF16).astype(F32)
            low = u - high
            turned = jnp.concatenate([high, low, v, v], axis=0).T.astype(BF16)
            if part == 0:
                basis_ref[:, part_cols] = u
                form_left[b] = turned
                form_right[b] = jnp.concatenate([v, v, high, low], axis=0).astype(BF16)
            else:
                halo_left[(part - 1) * blocks + b] = turned

    def pull(side):
        return lambda slot, a, c: stack_tile(mxu(side[a], form_right[c]) * slopes[slot])

    def pull_made(side, left):
        return lambda slot, a, c: stack_tile(mxu(side[a], form_right[c]) * slope_value(mxu(left[a], right[c])))

    base = total_of(inner_plan)
    fill(pulls, 0, inner_plan, pull(form_left))
    fill(pulls, base, plan, pull(halo_left))
    inner_edges(acc, pnts, inner_plan, keeper(pulls), pull_made(form_left, left_own))
    outer_edges(acc, halo_pnts, plan, base, keeper(pulls), pull_made(halo_left, left_out))
    for b in range(blocks):
        part_cols = slice(b * BLK, (b + 1) * BLK)
        x = slack[pl.ds(b, 8, stride=blocks), :][0:3]
        chain = slack[pl.ds(3 * blocks + b, 8, stride=blocks), :][0:3]
        sums = acc[b]
        moved = sums[0:3] + sums[3:6] + sums[6:9] - x * sums[9:10]
        grad_ref[:, part_cols] = moved * chain * (1.0 / (LENGTH_SQ * all_probes))


def close_kernel(place, own, other, grad, basis_ref, alpha_ref, beta_ref, same_grad):
    same_grad[...] = grad[...]
    probes = own.shape[0]
    width = basis_ref.shape[1]
    lower = place[1] == 0
    mine = own[...]
    theirs = other[...]
    first = jnp.where(lower, mine, theirs)
    second = jnp.where(lower, theirs, mine)
    basis_ref[:probes] = first[:, :width]
    basis_ref[probes:] = second[:, :width]
    ab = jnp.concatenate([first[:, width:], second[:, width:]], axis=0)
    turned = jnp.concatenate([ab, jnp.zeros((LANES - 2 * probes, LANES), F32)], axis=0).T
    alpha_ref[...] = turned[:ITERS, : 2 * probes]
    beta_ref[...] = turned[ITERS : 2 * ITERS, : 2 * probes]


def vmem(count):
    return [pl.BlockSpec(memory_space=pltpu.VMEM)] * count


def smem(count):
    return [pl.BlockSpec(memory_space=pltpu.SMEM)] * count


def held(array):
    return pltpu.with_memory_space_constraint(array, pltpu.VMEM)


def stays(array):
    return pltpu.with_memory_space_constraint(array, pltpu.HBM)


def in_hbm(count):
    return [pl.BlockSpec(memory_space=pltpu.HBM)] * count


def call(name, kernel, outs, ins, scratch, work, aliases=None, limit=LIMIT_MIB):
    out_shapes, out_scalars = outs
    arrays, scalars = ins
    flops, moved = work
    return pl.pallas_call(
        kernel,
        out_shape=tuple(out_shapes),
        in_specs=smem(scalars) + vmem(len(arrays) - scalars),
        out_specs=tuple(smem(out_scalars) + vmem(len(out_shapes) - out_scalars)),
        scratch_shapes=[pltpu.VMEM(*entry) if isinstance(entry, tuple) else entry for entry in scratch],
        compiler_params=pltpu.CompilerParams(vmem_limit_bytes=limit * 1024 * 1024),
        cost_estimate=pl.CostEstimate(flops=flops, bytes_accessed=moved, transcendentals=0),
        input_output_aliases=aliases or {},
        name=name,
    )(*arrays)


def shifted(value, axes, count, steps):
    return lax.ppermute(value, axes, [(source, (source + steps) % count) for source in range(count)])


def body(coords, noise_var, probe_signs, tile_rows, tile_cols, tile_count):
    slabs = lax.axis_size("blk")
    subs = lax.axis_size("sub")
    outer = lax.axis_size("probe")
    probes = probe_signs.shape[0] // subs
    width = coords.shape[1]
    blocks = width // BLK
    cap = tile_rows.shape[-1]
    points = float(width * slabs)
    all_probes = probe_signs.shape[0] * outer
    sub = lax.axis_index("sub")
    blk = lax.axis_index("blk")
    place = jnp.stack([blk, sub]).astype(jnp.int32)
    sds = jax.ShapeDtypeStruct

    left_shape = sds((blocks, BLK, FEATS), BF16)
    right_shape = sds((blocks, FEATS, BLK), BF16)
    packed = sds((blocks * (probes + 3) + LIST_ROWS, BLK), F32)
    kinds = ((blocks * FEATS, BLK), F32)
    lists, own, noise = pl.pallas_call(
        functools.partial(pack_kernel, blocks),
        out_shape=(sds((LIST_ROWS, LANES), F32), packed, sds((blocks, BLK), F32)),
        in_specs=smem(1) + in_hbm(2) + smem(1) + in_hbm(3),
        out_specs=tuple(vmem(3)),
        scratch_shapes=[
            pltpu.VMEM((probes, width), jnp.int32),
            pltpu.VMEM((3, width), F32),
            pltpu.VMEM((1, cap), jnp.int32),
            pltpu.VMEM((1, cap), jnp.int32),
            pltpu.SemaphoreType.DMA((5,)),
        ],
        compiler_params=pltpu.CompilerParams(vmem_limit_bytes=LIMIT_MIB * 1024 * 1024),
        name="pack",
    )(
        place, stays(tile_rows.reshape(1, cap)), stays(tile_cols.reshape(1, cap)), tile_count.reshape(1),
        stays(probe_signs), stays(coords), stays(noise_var.reshape(blocks, BLK)),
    )
    sibling = shifted(lists, "sub", subs, 1)
    (mine,) = call("join", join_kernel, ((packed,), 0), ((sibling, own), 0), [], (1000, 1000), {1: 0})
    above = shifted(mine, "blk", slabs, -1)
    below = shifted(mine, "blk", slabs, 1)

    ints = jnp.int32
    inner_slots = (blocks * (blocks + 1) // 2 + TAIL + LANES) // LANES * LANES
    outer_slots = (blocks * (blocks + 1) + TAIL + LANES) // LANES * LANES
    plan_shape = sds((1, inner_slots), ints)
    outer_plan_shape = sds((1, outer_slots), ints)
    inner_smem = pltpu.SMEM((1, inner_slots), ints)
    outer_smem = pltpu.SMEM((1, outer_slots), ints)
    slots = KEPT
    ext = width + LANES
    blocks_f32 = sds((blocks, probes, BLK), F32)
    tile_shape = pltpu.VMEM((slots, 2 * BLK, BLK), BF16)
    acc_shape = ((blocks, probes, BLK), F32)

    inner_plan, tiles, z, cross, left_own, right = call(
        "first_inner",
        functools.partial(first_inner_kernel, blocks),
        ((plan_shape, tile_shape, blocks_f32, sds((LIST_ROWS, outer_slots), F32), left_shape, right_shape), 0),
        ((mine,), 0),
        [
            acc_shape, ((blocks, probes, 2 * BLK), BF16), inner_smem, kinds,
            pltpu.SemaphoreType.DMA,
        ],
        (WORK_FIRST, WORK_BYTES),
    )
    outer_plan, tiles, w, left_halo = call(
        "first_outer",
        functools.partial(first_outer_kernel, blocks),
        ((outer_plan_shape, tile_shape, sds((probes, ext), F32), sds((2 * blocks, BLK, FEATS), BF16)), 0),
        ((inner_plan, held(tiles), mine, above, below, noise, z, right, cross), 1),
        [
            acc_shape, ((2 * blocks, probes, 2 * BLK), BF16), outer_smem, kinds,
            pltpu.SemaphoreType.DMA,
        ],
        (WORK_FIRST, WORK_BYTES),
        {1: 1},
    )

    def exchange(w):
        stats = w[:, width:]
        if slabs == 4:
            far = shifted(stats, "blk", slabs, 2)
        up = shifted(w, "blk", slabs, -1)
        down = shifted(w, "blk", slabs, 1)
        if slabs == 4:
            rows = jnp.stack([stats, up[:, width:], far, down[:, width:]])
        else:
            rows = lax.all_gather(stats, "blk", axis=0)
            rows = jnp.roll(rows, -blk, axis=0)
        return up, down, rows

    q = (mine, above, below)
    ab = []
    z_old = z
    for step in range(ITERS - 1):
        up, down, stats = exchange(w)
        (z_raw,) = call(
            "inner",
            functools.partial(inner_kernel, blocks),
            ((blocks_f32,), 0),
            ((inner_plan, w, q[0], held(tiles), left_own, right), 1),
            [acc_shape, ((blocks, 2 * probes, 2 * BLK), BF16)],
            (WORK_NEXT, WORK_BYTES),
        )
        w, q0, q1, q2, next_ab, *z = call(
            "outer",
            functools.partial(outer_kernel, blocks, slabs, points, step),
            (
                (
                    sds((probes, ext), F32), blocks_f32, blocks_f32, blocks_f32, sds((probes, LANES), F32),
                    *([blocks_f32] if step < ITERS - 2 else []),
                ),
                0,
            ),
            ((place, inner_plan, outer_plan, w, up, down, stats, *q, z_raw, z_old, noise, held(tiles), left_halo, right, *ab), 3),
            [acc_shape, ((2 * blocks, 2 * probes, 2 * BLK), BF16), ((blocks, probes, BLK), F32)],
            (WORK_NEXT, WORK_BYTES),
        )
        q = (q0, q1, q2)
        ab = [next_ab]
        z_old = z[0] if z else None

    up, down, stats = exchange(w)
    (slopes,) = call(
        "slopes",
        slope_kernel,
        ((pltpu.VMEM((slots, BLK, BLK), F32),), 0),
        ((inner_plan, outer_plan, left_own, left_halo, right, w), 2),
        [],
        (WORK_FIRST, WORK_BYTES),
    )
    pnts, halo_pnts, slack = call(
        "points",
        functools.partial(points_kernel, blocks),
        (
            (
                sds((blocks, 16, 2 * BLK), BF16), sds((2 * blocks, 16, 2 * BLK), BF16), sds((12 * blocks, BLK), F32),
            ),
            0,
        ),
        ((mine, above, below, w), 0),
        [((blocks * 16, BLK), F32)],
        (WORK_NEXT, WORK_BYTES),
    )
    basis, grad = call(
        "last",
        functools.partial(last_kernel, blocks, slabs, points, all_probes),
        ((sds((probes, ext), F32), sds((3, width), F32)), 0),
        (
            (
                place, inner_plan, outer_plan, w, up, down, stats, *q, mine, above, below, *ab, held(slopes), left_own, left_halo,
                right, pnts, halo_pnts, slack,
            ),
            3,
        ),
        [
            ((blocks, 16, BLK), F32),
            ((blocks, BLK, 4 * probes), BF16),
            ((2 * blocks, BLK, 4 * probes), BF16),
            ((blocks, 4 * probes, BLK), BF16),
            ((slots, 2 * BLK, BLK), BF16),
        ],
        (WORK_FIRST, WORK_BYTES),
        limit=LIMIT_MIB * 3 // 2,
    )

    if outer == 2 and subs == 2:
        axes = ("probe", "sub")
        across, diagonal, beside = (lax.ppermute(grad, axes, [(k, k ^ flip) for k in range(4)]) for flip in (2, 3, 1))
    other = shifted(basis, "sub", subs, 1)
    last_basis, alphas, betas, grad = call(
        "close",
        close_kernel,
        (
            (
                sds((subs * probes, width), F32), sds((ITERS, subs * probes), F32), sds((ITERS, subs * probes), F32),
                sds((3, width), F32),
            ),
            0,
        ),
        ((place, basis, other, grad), 1),
        [],
        (1000000, 1000000),
    )
    if outer == 2 and subs == 2:
        coord_grad = (grad + beside) + (across + diagonal)
    else:
        coord_grad = lax.psum(grad, ("probe", "sub"))
    return alphas, betas, last_basis, coord_grad


def solution(mesh):
    return jax.shard_map(
        body,
        mesh=mesh,
        in_specs=(
            P(None, ("groups", "blk")),
            P(("groups", "blk")),
            P("probe", ("groups", "blk")),
            P(("groups", "blk"), "sub", None),
            P(("groups", "blk"), "sub", None),
            P(("groups", "blk"), "sub"),
        ),
        out_specs=(
            P(None, ("groups", "probe")),
            P(None, ("groups", "probe")),
            P("probe", ("groups", "blk")),
            P(None, ("groups", "blk")),
        ),
        check_vma=False,
    )
```
